32 devices in a mesh: groups: 2 (over y), doc: 16 (over z, x, core), term: 1.
Axes of the slice: x: 2, y: 2, z: 4, core: 2. Of those that a mesh axis runs over, the one named last changes fastest.
Arguments:
- hidden_states: bfloat16 [4096, 768], P(('groups', 'doc')), parts along dimension 0, may hold values from -6 to 6
- doc_lengths: int32 [32], P(('groups', 'doc')), parts along dimension 0, may hold values from 1 to 128, 1536 in all
- transform_weight: bfloat16 [768, 768], P('doc', 'term'), may hold values from -0.21875 to 0.21875
- transform_bias: float32 [768], replicated, may hold values from -3 to 3
- norm_gain: float32 [768], replicated, may hold values from 0.5 to 1.5
- norm_bias: float32 [768], replicated, may hold values from -2 to 2
- decoder_weight: bfloat16 [1, 768, 15360], P('term', None, 'doc'), may hold values from -0.21875 to 0.21875
- decoder_bias: float32 [15360], P('term'), may hold values from -3 to 3
- tile_ids: int32 [1, 32, 32], P('term', ('groups', 'doc')), parts along dimension 1, may hold values from 0 to 119, all different within a row
- owner_ids: int32 [1, 32, 32, 1], P('term', ('groups', 'doc')), parts along dimension 1, may hold values from 0 to 15; in each aligned block of 32 rows (0 to 31, 32 to 63, ..., all dimensions but the last counted through in order) at most 4 rows name the same one
- block_slots: int32 [1, 32, 32], P('term', ('groups', 'doc')), parts along dimension 1, may hold values from 0 to 1
Outputs:
- impacts: bfloat16 [32, 15360], P(('groups', 'doc'), 'term'), parts along dimension 0
- summaries: bfloat16 [64, 15360], P(('groups', 'doc'), 'term'), parts along dimension 0
The draws below stay inside these ranges and needn't reach their ends.
There are 2 independent parts, one for each index of `groups`. The reference program is written for one: setup_inputs(seed, part) draws one part's arguments, and reference() takes and returns one part's arrays. A program takes and returns all parts, laid end to end along the dimension named above; an argument that names none is the same for every part. Nothing has to cross between parts.
Inputs may be any that keep to these rules, and one draw needn't show every extreme that they name: `tile_ids`: the 32 tiles of one half and document are different. `owner_ids`: among the 32 entries of one index of doc and one half, no owner is named more than 4 times, a bound that some block reaches. `doc_lengths`: some document of each group has all 128 tokens; the stated total is that of one group's 16 documents, 1536, and each group's lengths sum to it separately.
All inputs are finite; a program needn't handle non-finite values.
Results may differ from the reference program's by a relative error of at most 0.0034.
Values may be sent and summed in bfloat16 or wider, within the bound.
No kernel may reach another device: no remote copies, remote signals or barrier semaphores. Data moves between devices by JAX's collectives and lax.ppermute only.
A program may use at most 128 MiB of HBM per device.

```python
import math
import jax
import jax.numpy as jnp
import numpy as np
from jax import lax

D = 768
VOCAB = 15360
SEQ = 128
TILE = 128
DOC_DEV = 1
SEL = 32
BLK_DEV = 2
HALVES = 1
HALF = 15360
TILES_T = 120
OWNERS = 16
DOCS = 16
TOKENS = 2048
BLOCKS = 32
CAP = 4


def place_ends(entries, key, least, largest):
    spot = [jax.random.randint(jax.random.fold_in(key, axis), (), 0, length) for axis, length in enumerate(entries.shape)]
    longest = entries.shape.index(max(entries.shape))
    beside = spot[:longest] + [(spot[longest] + 1) % entries.shape[longest]] + spot[longest + 1:]
    return entries.at[tuple(spot)].set(least).at[tuple(beside)].set(largest)


def steps_of(rng, shape, cuts, least, top_value):
    def one(axis_at, shards_of):
        heights = jax.random.uniform(jax.random.fold_in(jax.random.fold_in(rng, 6), axis_at), (shards_of,), jnp.float32, least / len(cuts), top_value / len(cuts))
        return jnp.repeat(jnp.exp(heights), shape[axis_at] // shards_of).reshape((-1,) + (1,) * (len(shape) - axis_at - 1))

    level = one(*cuts[0])
    for cut in cuts[1:]:
        level = level * one(*cut)
    return level


def picks_of(key, rows, count, top, lift):
    sequence = jax.random.permutation(jax.random.fold_in(key, 1), count)
    boost = sequence
    for power in range(3):
        boost = boost * boost // count
    boost = boost * lift // count
    lots = jax.random.randint(jax.random.fold_in(key, 2), (rows, count), 0, 4096) + boost
    sure = jax.random.permutation(jax.random.fold_in(key, 3), rows)[jnp.arange(count) % rows]
    lots = jnp.where(jnp.arange(rows)[:, None] == sure[None, :], 1 << 14, lots)
    priority = lots * count + jnp.arange(count)
    return lax.top_k(priority.astype(jnp.int32), top)[1].astype(jnp.int32)


def split_up(amount, total, reach, skew):
    loads = [(1 << 20) // math.isqrt(rank ** skew) + 1 for rank in range(2, amount + 1)]
    surplus, counts = total - reach - (amount - 1), [1] * (amount - 1)
    while surplus > 0:
        movable = [i for i in range(amount - 1) if counts[i] < reach]
        pool, left = sum([loads[i] for i in movable]), surplus
        for i in movable:
            more = min(reach - counts[i], max(1, left * loads[i] // pool), surplus)
            counts[i] = counts[i] + more
            surplus = surplus - more
    return np.array([reach] + counts)


def uneven_parts(rng, count, total, most, slope):
    if count == 2:
        one = jax.random.randint(rng, (), max(1, total - most), min(most, total - 1) + 1)
        return jnp.stack([one, total - one])
    sizes = jnp.asarray(split_up(count, total, most, slope), jnp.int32)
    twos = (count - 1) // 2
    giver, sink = sizes[1:1 + 2 * twos:2], sizes[2:2 + 2 * twos:2]
    margin = jnp.minimum(giver - 1, most - sink)
    passed = jax.random.randint(jax.random.fold_in(rng, 1), (twos,), 0, 1 << 20) % (margin + 1)
    sizes = sizes.at[1:1 + 2 * twos:2].set(giver - passed).at[2:2 + 2 * twos:2].set(sink + passed)
    return sizes[jax.random.permutation(jax.random.fold_in(rng, 2), count)]


def routed_block(key, own, number, rows, count, top, limit, skew):
    sequence = jax.random.permutation(key, count)
    packed, ordinary = shares(count, rows * top, limit, skew, True), shares(count, rows * top, limit, skew, False)
    places = jnp.arange(count)

    def named(sizes, turn):
        used = int((sizes > 0).sum())
        fixed = max(1, used // 4)
        moved = fixed + (places - fixed + turn * (used - fixed)) % max(1, count - fixed)
        return jnp.zeros((count,), jnp.int32).at[sequence[jnp.where(places < fixed, places, moved)]].set(jnp.asarray(sizes, jnp.int32))

    sizes = jnp.where(number % 4 == 0, named(packed, number // 4), named(ordinary, number - number // 4 - 1))
    mixed = jax.random.permutation(jax.random.fold_in(own, 3), count)
    source_of, receiver = mixed[0:count // 2 * 2:2], mixed[1:count // 2 * 2:2]
    room = jnp.minimum(sizes[source_of] - 1, limit - sizes[receiver]) // 2
    room = jnp.where((source_of == sequence[0]) | (receiver == sequence[0]) | (sizes[receiver] == 0), 0, jnp.maximum(room, 0))
    moved = jax.random.randint(jax.random.fold_in(own, 4), (count // 2,), 0, 1 << 20) % (room + 1)
    sizes = sizes.at[source_of].add(-moved).at[receiver].add(moved)
    labels = jnp.searchsorted(jnp.cumsum(sizes), jnp.arange(rows * top), side="right").astype(jnp.int32)
    table = labels.reshape(top, rows).T
    table = table[jax.random.permutation(jax.random.fold_in(own, 1), rows)]
    turn = jax.random.randint(jax.random.fold_in(own, 2), (rows, 1), 0, top)
    return jnp.take_along_axis(table, (jnp.arange(top)[None, :] + turn) % top, axis=1)


def shares(count, total, bound, lean, full):
    weights = [(1 << 20) // math.isqrt(rank ** lean) + 1 for rank in range(1, count + 1)]
    largest = bound if full else min(bound, max(-(-total // count), total * weights[0] // sum(weights)))
    least = 1 if total - largest >= count - 1 else 0
    holding, surplus = [largest] + [least] * (count - 1), total - largest - least * (count - 1)
    while surplus > 0:
        candidates = [i for i in range(1, count) if holding[i] < largest] or [i for i in range(1, count) if holding[i] < bound]
        whole, budget = sum([weights[i] for i in candidates]), surplus
        for i in candidates:
            extra = min(bound - holding[i], max(1, budget * weights[i] // whole), surplus)
            holding[i] = holding[i] + extra
            surplus = surplus - extra
    return np.array(holding)


def gaussian(own_key, extent, scale, most, split=(), held_as=jnp.bfloat16):
    array = jax.random.normal(own_key, extent, jnp.float32) * scale
    if len(split) > 0:
        array = steps_of(own_key, extent, split, -0.22, 0.18) * array
    return jnp.clip(array, min=-most, max=most).astype(held_as)


def setup_inputs(seed: int = 0, part: int = 0) -> dict:
    key_of = jax.random.split(jax.random.key(seed), 12)
    part_splits = jax.random.split(jax.random.fold_in(key_of[11], part), 12)
    hidden_states = gaussian(part_splits[0], (TOKENS, D), 1.0, 6.0, ((0, 16),))
    doc_lengths = uneven_parts(part_splits[1], DOCS, DOCS * 3 * SEQ // 4, SEQ, 1).astype(jnp.int32)
    transform_weight = gaussian(key_of[2], (D, D), D ** -0.5, 0.21875, ((0, 16),))
    transform_bias = gaussian(key_of[3], (D,), 0.5, 3.0, (), jnp.float32)
    norm_gain = jnp.clip(1.0 + 0.1 * jax.random.normal(key_of[4], (D,), jnp.float32), 0.5, 1.5)
    norm_bias = gaussian(key_of[5], (D,), 0.3, 2.0, (), jnp.float32)
    decoder_weight = gaussian(key_of[6], (HALVES, D, HALF), D ** -0.5, 0.21875, ((2, 16),))
    decoder_bias = gaussian(key_of[7], (VOCAB,), 0.5, 3.0, (), jnp.float32)
    tile_ids = picks_of(part_splits[8], HALVES * DOCS, TILES_T, SEL, 0).reshape((HALVES, DOCS, SEL))
    owner_ids_keys = jax.random.split(jax.random.fold_in(part_splits[9], 1), HALVES * DOCS * SEL // (DOC_DEV * SEL))
    owner_ids_turns = jax.random.permutation(jax.random.fold_in(part_splits[9], 3), HALVES * DOCS * SEL // (DOC_DEV * SEL))
    owner_ids = jax.vmap(lambda own, number: routed_block(jax.random.fold_in(part_splits[9], 2), own, number, DOC_DEV * SEL, OWNERS, 1, CAP, 2))(owner_ids_keys, owner_ids_turns).reshape((HALVES, DOCS, SEL, 1))
    block_slots = place_ends(jax.random.randint(part_splits[10], (HALVES, DOCS, SEL), 0, BLK_DEV), jax.random.fold_in(part_splits[10], 1), 0, BLK_DEV - 1).astype(jnp.int32)
    return {"hidden_states": hidden_states, "doc_lengths": doc_lengths, "transform_weight": transform_weight, "transform_bias": transform_bias, "norm_gain": norm_gain, "norm_bias": norm_bias, "decoder_weight": decoder_weight, "decoder_bias": decoder_bias, "tile_ids": tile_ids, "owner_ids": owner_ids, "block_slots": block_slots}


def layer_norm(activated, norm_gain, norm_bias):
    values = activated.astype(jnp.float32)
    centre = lax.optimization_barrier(jnp.mean(values, axis=-1, keepdims=True))
    centred = values - centre
    spread = lax.optimization_barrier(jnp.mean(centred * centred, axis=-1, keepdims=True))
    return (centred * lax.rsqrt(spread + 1e-05) * norm_gain + norm_bias).astype(jnp.bfloat16)

def reference(hidden_states, doc_lengths, transform_weight, transform_bias, norm_gain, norm_bias, decoder_weight, decoder_bias, tile_ids, owner_ids, block_slots):
    pre = jnp.dot(hidden_states, transform_weight, preferred_element_type=jnp.float32) + transform_bias
    activated = jax.nn.gelu(pre, approximate=False).astype(jnp.bfloat16)
    normed = layer_norm(activated, norm_gain, norm_bias)
    full_weight = jnp.transpose(decoder_weight, (1, 0, 2)).reshape(D, VOCAB)
    valid = jnp.arange(SEQ, dtype=jnp.int32)[None, :] < doc_lengths[:, None]

    def one_doc(pair):
        rows, keep = pair
        logits = jnp.dot(rows, full_weight, preferred_element_type=jnp.float32) + decoder_bias
        saturated = jnp.log1p(jnp.maximum(logits, 0.0))
        return lax.optimization_barrier(jnp.max(jnp.where(keep[:, None], saturated, 0.0), axis=0)).astype(jnp.bfloat16)
    impacts = lax.map(one_doc, (normed.reshape(DOCS, SEQ, D), valid))
    grid = impacts.reshape(DOCS, HALVES, TILES_T, TILE)
    half_index = jnp.arange(HALVES, dtype=jnp.int32)[:, None, None]
    doc_index = jnp.arange(DOCS, dtype=jnp.int32)[None, :, None]
    posted = grid[doc_index, half_index, tile_ids]
    blocks = owner_ids[..., 0] * BLK_DEV + block_slots
    summaries = jnp.zeros((BLOCKS, HALVES, TILES_T, TILE), jnp.bfloat16)
    summaries = summaries.at[blocks, half_index, tile_ids].max(posted)
    return (impacts, summaries.reshape(BLOCKS, VOCAB))
```

```python
import jax
import jax.numpy as jnp
from jax import lax
from jax.experimental import pallas as pl
from jax.experimental.pallas import tpu as pltpu
from jax.sharding import PartitionSpec as P

TILE = 128
BLK_DEV = 2
SLOT_ROWS = 16


def layer_norm(activated, norm_gain, norm_bias):
    values = activated.astype(jnp.float32)
    centre = jnp.mean(values, axis=-1, keepdims=True)
    centred = values - centre
    spread = jnp.mean(centred * centred, axis=-1, keepdims=True)
    return (centred * lax.rsqrt(spread + 1e-05) * norm_gain + norm_bias).astype(jnp.bfloat16)


def pool_docs(logits, keep):
    docs_here = keep.shape[0]
    saturated = jnp.log1p(jnp.maximum(logits, 0.0)).reshape(
        docs_here, keep.shape[1], logits.shape[1]
    )
    return jnp.max(jnp.where(keep[:, :, None], saturated, 0.0), axis=1)


def move_weights(
    hidden_states,
    doc_lengths,
    transform_weight,
    transform_bias,
    norm_gain,
    norm_bias,
    decoder_weight,
    decoder_bias,
    tile_ids,
    owner_ids,
    block_slots,
):
    tok_rows = hidden_states.shape[0]
    docs_here = doc_lengths.shape[0]
    seq_len = tok_rows // docs_here
    cols = transform_weight.shape[1]
    pre_half = jnp.dot(
        hidden_states,
        lax.all_gather(transform_weight, "doc", axis=0, tiled=True),
        preferred_element_type=jnp.float32,
    )
    bias_half = lax.dynamic_slice_in_dim(transform_bias, lax.axis_index("term") * cols, cols, 0)
    act_half = jax.nn.gelu(pre_half + bias_half, approximate=False).astype(jnp.bfloat16)
    activated = lax.all_gather(act_half, "term", axis=1, tiled=True)
    normed = layer_norm(activated, norm_gain, norm_bias)
    keep = jnp.arange(seq_len, dtype=jnp.int32)[None, :] < doc_lengths[:, None]
    logits = jnp.dot(
        normed,
        lax.all_gather(decoder_weight, "doc", axis=2, tiled=True)[0],
        preferred_element_type=jnp.float32,
    )
    logits = logits + decoder_bias
    impacts = pool_docs(logits, keep).astype(jnp.bfloat16)
    tiles_t = impacts.shape[1] // TILE
    slots_total = BLK_DEV * tiles_t
    tiles = impacts.reshape(docs_here * tiles_t, TILE)
    chosen = tile_ids[0]
    doc_index = jnp.arange(docs_here, dtype=jnp.int32)[:, None]
    posted = tiles[(doc_index * tiles_t + chosen).reshape(-1)]
    owners = owner_ids[0, :, :, 0].reshape(-1)
    target = block_slots[0].reshape(-1) * tiles_t + chosen.reshape(-1)
    owner_count = lax.axis_size("doc")
    capacity = max(2, 2 * posted.shape[0] // owner_count)
    onehot = (owners[:, None] == jnp.arange(owner_count, dtype=jnp.int32)[None, :]).astype(
        jnp.int32
    )
    before = jnp.cumsum(onehot, axis=0) - onehot
    position = jnp.sum(before * onehot, axis=1)
    dest = owners * capacity + position
    outgoing = jnp.zeros((owner_count * capacity, TILE), jnp.bfloat16).at[dest].set(posted)
    out_tags = jnp.full((owner_count * capacity,), slots_total, jnp.int32).at[dest].set(target)
    got_vals, got_tags = (
        lax.all_to_all(
            outgoing.reshape(owner_count, capacity, TILE),
            "doc",
            split_axis=0,
            concat_axis=0,
            tiled=True,
        ),
        lax.all_to_all(
            out_tags.reshape(owner_count, capacity), "doc", split_axis=0, concat_axis=0, tiled=True
        ),
    )
    got_vals = got_vals.reshape(-1, TILE)
    local_tags = got_tags.reshape(-1)
    summary = jnp.zeros((slots_total, TILE), jnp.bfloat16).at[local_tags].max(got_vals, mode="drop")
    return (impacts, summary.reshape(BLK_DEV, tiles_t * TILE))


def dot_t(left, right):
    return lax.dot_general(
        left, right, (((1,), (1,)), ((), ())), preferred_element_type=jnp.float32
    )


def head_kernel(chips, order, *refs):
    places = len(order)
    (place_ref, meta_ref), refs = refs[:2], refs[2:]
    hidden_refs, refs = refs[:places], refs[places:]
    weight_refs, refs = refs[:places], refs[places:]
    other_weight_ref, refs = refs[0], refs[1:]
    tbias_ref, gain_ref, nbias_ref, mine_ref, theirs_ref, dbias_ref, out_ref = refs[:7]
    tokens, weight, best_mine, best_theirs, send = refs[7:]
    core = place_ref[0]
    chip = place_ref[1]
    seq = hidden_refs[0].shape[0]
    rows = weight_refs[0].shape[0]
    half = mine_ref.shape[0]
    tiles = 2 * half // TILE
    for k in range(places):
        source = place_ref[2 + k]
        doc = 2 * source + core
        length = meta_ref[doc, TILE - 1]
        here = hidden_refs[k][...]
        keep = lax.broadcasted_iota(jnp.int32, here.shape, 0) < length
        first = jnp.broadcast_to(here[0:1, :].astype(jnp.float32), here.shape).astype(here.dtype)
        tokens[pl.ds(pl.multiple_of(source * seq, seq), seq), :] = jnp.where(keep, here, first)
        at = pl.multiple_of(doc * rows, 16)
        weight[pl.ds(at, rows), :] = weight_refs[k][...]
        at = pl.multiple_of((2 * source + 1 - core) * rows, 16)
        weight[pl.ds(at, rows), :] = other_weight_ref[k * rows : (k + 1) * rows, :]

    def two_docs(step, carry):
        at = pl.multiple_of(step * 2 * seq, 2 * seq)
        pre = jnp.dot(
            tokens[pl.ds(at, 2 * seq), :], weight[...], preferred_element_type=jnp.float32
        )
        pre = pre + tbias_ref[...]
        act = 0.5 * pre * (1.0 + lax.erf(pre * (0.5**0.5)))
        normed = layer_norm(act.astype(jnp.bfloat16), gain_ref[...], nbias_ref[...])
        for w_ref, best in ((mine_ref, best_mine), (theirs_ref, best_theirs)):
            logits = dot_t(normed, w_ref[...])
            for j in range(2):
                top = jnp.max(logits[j * seq : (j + 1) * seq], axis=0, keepdims=True)
                best[pl.ds(2 * step + j, 1), :] = top
        return carry

    lax.fori_loop(0, places // 2, two_docs, 0)
    mine, theirs = best_mine[...], best_theirs[...]
    low = jnp.where(core == 0, mine, theirs)
    high = jnp.where(core == 0, theirs, mine)
    logits = jnp.concatenate([low, high], axis=1) + dbias_ref[...]
    impacts = jnp.log1p(jnp.maximum(logits, 0.0)).astype(jnp.bfloat16).astype(jnp.float32)
    send[...] = jnp.zeros(send.shape, jnp.float32)
    devices = 2 * chips
    stride = out_ref.shape[1]
    target = lax.broadcasted_iota(jnp.int32, (BLK_DEV * devices, TILE), 0)
    for t in range(tiles):
        tile = impacts[:, t * TILE : (t + 1) * TILE]
        for c in range(2):
            send[pl.ds(c * stride + t, chips, stride=2 * stride), :] = tile
        blocks = jnp.zeros((BLK_DEV * devices, TILE), jnp.float32)
        for k in range(chips):
            block = meta_ref[2 * k + core, chip * tiles + t]
            blocks = jnp.maximum(blocks, jnp.where(target == block, tile[k : k + 1, :], 0.0))
        for s in range(BLK_DEV):
            send[pl.ds((1 + s) * SLOT_ROWS + t, devices, stride=stride), :] = blocks[
                s * devices : (s + 1) * devices
            ]
    out_ref[...] = send[...].astype(jnp.bfloat16).reshape(out_ref.shape)


def move_tokens(
    hidden_states,
    doc_lengths,
    transform_weight,
    transform_bias,
    norm_gain,
    norm_bias,
    decoder_weight,
    decoder_bias,
    tile_ids,
    owner_ids,
    block_slots,
):
    devices = lax.axis_size("doc")
    chips = devices // 2
    layers = chips // 2
    seq, width = hidden_states.shape
    half = decoder_weight.shape[2]
    tiles = 2 * half // TILE
    me = lax.axis_index("doc")
    core, chip = me % 2, me // 2
    layer, side = chip // 2, chip % 2

    def flip(value, bit):
        return lax.ppermute(value, "doc", [(i, i ^ bit) for i in range(devices)])

    def shift(value, by):
        return lax.ppermute(value, "doc", [(i, (i + 4 * by) % devices) for i in range(devices)])

    wanted = block_slots[0, 0] * devices + owner_ids[0, 0, :, 0]
    lane = jnp.arange(TILE, dtype=jnp.int32)
    posted = tile_ids[0, 0][:, None] == lane[None, :]
    table = jnp.sum(jnp.where(posted, wanted[:, None] + 1, 0), axis=0) - 1
    table = jnp.where(lane == TILE - 1, doc_lengths[0], table)
    meta = lax.all_gather(table[None, :], "doc", axis=0, tiled=True)

    weight_rows = jnp.swapaxes(decoder_weight[0], 0, 1)
    by_layer = [transform_weight] + [shift(transform_weight, s) for s in range(1, layers)]
    other_half = flip(weight_rows, 1)
    hidden = [hidden_states] + [shift(hidden_states, s) for s in range(1, layers)]
    by_layer_across = [flip(value, 2) for value in by_layer]
    hidden_across = [flip(value, 2) for value in hidden]
    weights = by_layer + by_layer_across
    other_weights = flip(jnp.concatenate(weights, axis=0), 1)
    hiddens = hidden + hidden_across
    order = [(s, f) for f in range(2) for s in range(layers)]
    sources = [((layer - s) % layers) * 2 + (side ^ f) for s, f in order]
    place = jnp.stack([core, chip] + sources).astype(jnp.int32)
    bias = lax.dynamic_slice_in_dim(decoder_bias, chip * 2 * half, 2 * half, 0)

    smem = pl.BlockSpec(memory_space=pltpu.SMEM)
    vmem = pl.BlockSpec(memory_space=pltpu.VMEM)
    send = pl.pallas_call(
        lambda *refs: head_kernel(chips, order, *refs),
        out_shape=jax.ShapeDtypeStruct(
            (devices, (1 + BLK_DEV) * SLOT_ROWS, TILE), jnp.bfloat16
        ),
        in_specs=[smem, smem] + [vmem] * (2 * chips + 1 + 6),
        out_specs=vmem,
        scratch_shapes=[
            pltpu.VMEM((chips * seq, width), jnp.bfloat16),
            pltpu.VMEM((width, width), jnp.bfloat16),
            pltpu.VMEM((chips, half), jnp.float32),
            pltpu.VMEM((chips, half), jnp.float32),
            pltpu.VMEM((devices * (1 + BLK_DEV) * SLOT_ROWS, TILE), jnp.float32),
        ],
        compiler_params=pltpu.CompilerParams(vmem_limit_bytes=32 * 1024 * 1024),
        cost_estimate=pl.CostEstimate(
            flops=2 * chips * seq * width * (width + 2 * half),
            bytes_accessed=6 * 1024 * 1024,
            transcendentals=chips * seq * width,
        ),
    )(
        place,
        meta,
        *hiddens,
        *weights,
        other_weights,
        transform_bias[None, :],
        norm_gain[None, :],
        norm_bias[None, :],
        weight_rows,
        other_half,
        bias[None, :],
    )
    got = lax.all_to_all(send, "doc", split_axis=0, concat_axis=0, tiled=True)
    got = got.reshape(chips, 2, 1 + BLK_DEV, SLOT_ROWS, TILE)[:, :, :, :tiles]
    impacts = lax.dynamic_index_in_dim(got[:, :, 0], core, 1, keepdims=False)
    summaries = jnp.maximum(got[:, 0, 1:], got[:, 1, 1:])
    summaries = jnp.swapaxes(summaries, 0, 1)
    return (impacts.reshape(1, -1), summaries.reshape(BLK_DEV, -1))


def tokens_move(mesh):
    return mesh.shape["term"] == 1 and mesh.shape["doc"] % 4 == 0


def solution(mesh):
    placed = (
        P(("groups", "doc"), None),
        P(("groups", "doc")),
        P("doc", "term"),
        P(),
        P(),
        P(),
        P("term", None, "doc"),
        P("term"),
        P("term", ("groups", "doc"), None),
        P("term", ("groups", "doc"), None, None),
        P("term", ("groups", "doc"), None),
    )

    def local(*args):
        pair = 2 * args[6].shape[2]
        tiles = pair * (mesh.shape["doc"] // 2) // TILE
        fits = pair % TILE == 0 and tiles < TILE and pair // TILE <= SLOT_ROWS
        if tokens_move(mesh) and args[1].shape[0] == 1 and fits:
            return move_tokens(*args)
        return move_weights(*args)

    return jax.shard_map(
        local,
        mesh=mesh,
        in_specs=placed,
        out_specs=(P(("groups", "doc"), "term"), P(("groups", "doc"), "term")),
        check_vma=False,
    )
```

```python
import jax
import jax.numpy as jnp
from jax import lax
from jax.experimental import pallas as pl
from jax.experimental.pallas import tpu as pltpu
from jax.sharding import PartitionSpec as P

TILE = 128
BLK_DEV = 2
SLOT_ROWS = 16


def layer_norm(activated, norm_gain, norm_bias):
    values = activated.astype(jnp.float32)
    centre = jnp.mean(values, axis=-1, keepdims=True)
    centred = values - centre
    spread = jnp.mean(centred * centred, axis=-1, keepdims=True)
    return (centred * lax.rsqrt(spread + 1e-05) * norm_gain + norm_bias).astype(jnp.bfloat16)


def pool_docs(logits, keep):
    docs_here = keep.shape[0]
    saturated = jnp.log1p(jnp.maximum(logits, 0.0)).reshape(
        docs_here, keep.shape[1], logits.shape[1]
    )
    return jnp.max(jnp.where(keep[:, :, None], saturated, 0.0), axis=1)


def move_weights(
    hidden_states,
    doc_lengths,
    transform_weight,
    transform_bias,
    norm_gain,
    norm_bias,
    decoder_weight,
    decoder_bias,
    tile_ids,
    owner_ids,
    block_slots,
):
    tok_rows = hidden_states.shape[0]
    docs_here = doc_lengths.shape[0]
    seq_len = tok_rows // docs_here
    cols = transform_weight.shape[1]
    pre_half = jnp.dot(
        hidden_states,
        lax.all_gather(transform_weight, "doc", axis=0, tiled=True),
        preferred_element_type=jnp.float32,
    )
    bias_half = lax.dynamic_slice_in_dim(transform_bias, lax.axis_index("term") * cols, cols, 0)
    act_half = jax.nn.gelu(pre_half + bias_half, approximate=False).astype(jnp.bfloat16)
    activated = lax.all_gather(act_half, "term", axis=1, tiled=True)
    normed = layer_norm(activated, norm_gain, norm_bias)
    keep = jnp.arange(seq_len, dtype=jnp.int32)[None, :] < doc_lengths[:, None]
    logits = jnp.dot(
        normed,
        lax.all_gather(decoder_weight, "doc", axis=2, tiled=True)[0],
        preferred_element_type=jnp.float32,
    )
    logits = logits + decoder_bias
    impacts = pool_docs(logits, keep).astype(jnp.bfloat16)
    tiles_t = impacts.shape[1] // TILE
    slots_total = BLK_DEV * tiles_t
    tiles = impacts.reshape(docs_here * tiles_t, TILE)
    chosen = tile_ids[0]
    doc_index = jnp.arange(docs_here, dtype=jnp.int32)[:, None]
    posted = tiles[(doc_index * tiles_t + chosen).reshape(-1)]
    owners = owner_ids[0, :, :, 0].reshape(-1)
    target = block_slots[0].reshape(-1) * tiles_t + chosen.reshape(-1)
    owner_count = lax.axis_size("doc")
    capacity = max(2, 2 * posted.shape[0] // owner_count)
    onehot = (owners[:, None] == jnp.arange(owner_count, dtype=jnp.int32)[None, :]).astype(
        jnp.int32
    )
    before = jnp.cumsum(onehot, axis=0) - onehot
    position = jnp.sum(before * onehot, axis=1)
    dest = owners * capacity + position
    outgoing = jnp.zeros((owner_count * capacity, TILE), jnp.bfloat16).at[dest].set(posted)
    out_tags = jnp.full((owner_count * capacity,), slots_total, jnp.int32).at[dest].set(target)
    got_vals, got_tags = (
        lax.all_to_all(
            outgoing.reshape(owner_count, capacity, TILE),
            "doc",
            split_axis=0,
            concat_axis=0,
            tiled=True,
        ),
        lax.all_to_all(
            out_tags.reshape(owner_count, capacity), "doc", split_axis=0, concat_axis=0, tiled=True
        ),
    )
    got_vals = got_vals.reshape(-1, TILE)
    local_tags = got_tags.reshape(-1)
    summary = jnp.zeros((slots_total, TILE), jnp.bfloat16).at[local_tags].max(got_vals, mode="drop")
    return (impacts, summary.reshape(BLK_DEV, tiles_t * TILE))


def dot_t(left, right):
    return lax.dot_general(
        left, right, (((1,), (1,)), ((), ())), preferred_element_type=jnp.float32
    )


def ring_of(layers):
    return [2 * z for z in range(layers)] + [2 * z + 1 for z in reversed(range(layers))]


def chip_after(chip, by, layers):
    layer, side = chip // 2, chip % 2
    here = jnp.where(side == 0, layer, 2 * layers - 1 - layer)
    there = (here + by + 2 * layers) % (2 * layers)
    return jnp.where(there < layers, 2 * there, 2 * (2 * layers - 1 - there) + 1)


def doc_of(me, step, own, layers):
    core = me % 2
    chip = chip_after(me // 2, jnp.where(core == 0, -step, step), layers)
    return 2 * chip + (core if own else 1 - core)


def masked(ref, length):
    here = ref[...]
    keep = lax.broadcasted_iota(jnp.int32, here.shape, 0) < length
    first = jnp.broadcast_to(here[0:1, :].astype(jnp.float32), here.shape).astype(here.dtype)
    return jnp.where(keep, here, first)


def best_logits(pair, lengths, weight, tbias, gain, nbias, mine_ref, theirs_ref):
    seq = pair[0].shape[0]
    rows = jnp.concatenate([masked(ref, length) for ref, length in zip(pair, lengths)], axis=0)
    pre = jnp.dot(rows, weight[...], preferred_element_type=jnp.float32) + tbias
    act = 0.5 * pre * (1.0 + lax.erf(pre * (0.5**0.5)))
    normed = layer_norm(act.astype(jnp.bfloat16), gain, nbias)
    tops = []
    for w_ref in (mine_ref, theirs_ref):
        logits = dot_t(normed, w_ref[...])
        tops.append(
            [
                jnp.max(logits[j * seq : (j + 1) * seq], axis=0, keepdims=True)
                for j in range(len(pair))
            ]
        )
    return tops


def pack_kernel(*refs):
    rows = refs[0].shape[0]
    for k, ref in enumerate(refs[:-1]):
        refs[-1][k * rows : (k + 1) * rows, :] = ref[...]


def docs_kernel(places, layers, blocks, *refs):
    (me_ref, meta_ref), refs = refs[:2], refs[2:]
    docs, refs = refs[: len(places)], refs[len(places) :]
    me = me_ref[0]
    core = me % 2
    if blocks:
        mine_blocks, other_blocks, refs = refs[0], refs[1], refs[2:]
        tbias_ref, gain_ref, nbias_ref, mine_ref, theirs_ref, best_mine, best_theirs, weight = refs
        rows = weight.shape[0] // (2 * len(blocks))
        for k, by in enumerate(blocks):
            chip = chip_after(me // 2, by, layers)
            at = pl.multiple_of((2 * chip + core) * rows, 16)
            weight[pl.ds(at, rows), :] = mine_blocks[k * rows : (k + 1) * rows, :]
            at = pl.multiple_of((2 * chip + 1 - core) * rows, 16)
            weight[pl.ds(at, rows), :] = other_blocks[k * rows : (k + 1) * rows, :]
    else:
        weight, refs = refs[0], refs[1:]
        tbias_ref, gain_ref, nbias_ref, mine_ref, theirs_ref, best_mine, best_theirs = refs
    lengths = [meta_ref[doc_of(me, s, o, layers) ^ me, TILE - 1] for s, o in places]
    for first in range(0, len(places), 2):
        part = slice(first, first + 2)
        mine, theirs = best_logits(
            docs[part],
            lengths[part],
            weight,
            tbias_ref[...],
            gain_ref[...],
            nbias_ref[...],
            mine_ref,
            theirs_ref,
        )
        for j in range(len(mine)):
            best_mine[first + j : first + j + 1, :] = mine[j]
            best_theirs[first + j : first + j + 1, :] = theirs[j]


def last_kernel(places, before, layers, *refs):
    (me_ref, meta_ref), refs = refs[:2], refs[2:]
    docs, refs = refs[: len(places)], refs[len(places) :]
    weight, tbias_ref, gain_ref, nbias_ref, mine_ref, theirs_ref, dbias_ref = refs[:7]
    refs = refs[7:]
    earlier, refs = refs[: 2 * len(before)], refs[2 * len(before) :]
    out_ref, best, send = refs
    me = me_ref[0]
    core, chip = me % 2, me // 2
    devices = 4 * layers
    half = mine_ref.shape[0]
    tiles = 2 * half // TILE
    best[...] = jnp.zeros(best.shape, jnp.float32)
    handled = []

    def keep(place, mine, theirs):
        low = jnp.where(core == 0, mine, theirs)
        high = jnp.where(core == 0, theirs, mine)
        logits = jnp.concatenate([low, high], axis=1) + dbias_ref[...]
        impacts = jnp.log1p(jnp.maximum(logits, 0.0)).astype(jnp.bfloat16).astype(jnp.float32)
        for k, (s, o) in enumerate(place):
            doc = doc_of(me, s, o, layers)
            best[pl.ds(doc, 1), :] = impacts[k : k + 1, :]
            handled.append((doc, impacts[k : k + 1, :]))

    for n, place in enumerate(before):
        count = len(place)
        keep(place, earlier[2 * n][0:count, :], earlier[2 * n + 1][0:count, :])
    lengths = [meta_ref[doc_of(me, s, o, layers) ^ me, TILE - 1] for s, o in places]
    mine, theirs = best_logits(
        docs,
        lengths,
        weight,
        tbias_ref[...],
        gain_ref[...],
        nbias_ref[...],
        mine_ref,
        theirs_ref,
    )
    keep(places, jnp.concatenate(mine, axis=0), jnp.concatenate(theirs, axis=0))
    send[...] = jnp.zeros(send.shape, jnp.float32)
    stride = out_ref.shape[1]
    target = lax.broadcasted_iota(jnp.int32, (BLK_DEV * devices, TILE), 0)
    for t in range(tiles):
        lanes = slice(t * TILE, (t + 1) * TILE)
        send[pl.ds(t, devices, stride=stride), :] = best[:, lanes]
        blocks = jnp.zeros((BLK_DEV * devices, TILE), jnp.float32)
        for doc, impacts in handled:
            block = meta_ref[doc ^ me, chip * tiles + t]
            blocks = jnp.maximum(blocks, jnp.where(target == block, impacts[:, lanes], 0.0))
        for s in range(BLK_DEV):
            send[pl.ds((1 + s) * SLOT_ROWS + t, devices, stride=stride), :] = blocks[
                s * devices : (s + 1) * devices
            ]
    out_ref[...] = send[...].astype(jnp.bfloat16).reshape(out_ref.shape)


def move_tokens(
    hidden_states,
    doc_lengths,
    transform_weight,
    transform_bias,
    norm_gain,
    norm_bias,
    decoder_weight,
    decoder_bias,
    tile_ids,
    owner_ids,
    block_slots,
):
    devices = lax.axis_size("doc")
    chips = devices // 2
    layers = chips // 2
    seq, width = hidden_states.shape
    half = decoder_weight.shape[2]
    tiles = 2 * half // TILE
    me = lax.axis_index("doc").astype(jnp.int32)
    ring = ring_of(layers)

    def flip(value, bit):
        return lax.ppermute(value, "doc", [(i, i ^ bit) for i in range(devices)])

    def onward(value, ways):
        moves = []
        for n, chip in enumerate(ring):
            for core, way in enumerate(ways):
                moves.append((2 * chip + core, 2 * ring[(n + way) % chips] + core))
        return lax.ppermute(value, "doc", moves)

    smem = pl.BlockSpec(memory_space=pltpu.SMEM)
    vmem = pl.BlockSpec(memory_space=pltpu.VMEM)
    limit = pltpu.CompilerParams(vmem_limit_bytes=24 * 1024 * 1024)

    wanted = block_slots[0, 0] * devices + owner_ids[0, 0, :, 0]
    lane = jnp.arange(TILE, dtype=jnp.int32)
    posted = tile_ids[0, 0][:, None] == lane[None, :]
    table = jnp.sum(jnp.where(posted, wanted[:, None] + 1, 0), axis=0) - 1
    meta = jnp.where(lane == TILE - 1, doc_lengths[0], table)[None, :]
    bit = 1
    while bit < devices:
        meta = jnp.concatenate([meta, flip(meta, bit)], axis=0)
        bit *= 2

    blocks, onto = [0], [transform_weight]
    for way, steps in ((1, chips // 2), (-1, (chips - 1) // 2)):
        moving = transform_weight
        for step in range(1, steps + 1):
            moving = onward(moving, (way, way))
            blocks.append(-way * step)
            onto.append(moving)
    mine_blocks = pl.pallas_call(
        pack_kernel,
        out_shape=jax.ShapeDtypeStruct((chips * transform_weight.shape[0], width), jnp.bfloat16),
        in_specs=[vmem] * chips,
        out_specs=vmem,
        compiler_params=limit,
    )(*onto)
    other_blocks = flip(mine_blocks, 1)

    weight_rows = jnp.swapaxes(decoder_weight[0], 0, 1)
    other_half = flip(weight_rows, 1)

    own, partner = hidden_states, flip(hidden_states, 1)
    arrived = {(0, True): hidden_states}
    for step in range(1, chips // 2 + 1):
        own = onward(own, (1, -1))
        arrived[(step, True)] = own
        if step < chips // 2:
            partner = onward(partner, (1, -1))
            arrived[(step, False)] = partner
    places = list(arrived)
    groups = [places[: len(places) // 2], places[len(places) // 2 : -2], places[-2:]]
    groups = [group for group in groups if group]

    where = me[None]
    params = (transform_bias[None, :], norm_gain[None, :], norm_bias[None, :])
    halves = (weight_rows, other_half)
    best_shape = jax.ShapeDtypeStruct((8, half), jnp.float32)
    weight = None
    results = []
    for group in groups[:-1]:
        first = weight is None
        outs = [best_shape] * 2
        if first:
            outs.append(jax.ShapeDtypeStruct((width, width), jnp.bfloat16))
        dense = (mine_blocks, other_blocks) if first else (weight,)
        args = [arrived[place] for place in group] + [*dense, *params, *halves]
        found = pl.pallas_call(
            lambda *refs, group=group, first=first: docs_kernel(
                group, layers, blocks if first else None, *refs
            ),
            out_shape=outs,
            in_specs=[smem, smem] + [vmem] * len(args),
            out_specs=[vmem] * len(outs),
            compiler_params=limit,
            cost_estimate=pl.CostEstimate(
                flops=2 * len(group) * seq * width * (width + 2 * half),
                bytes_accessed=1024 * 1024,
                transcendentals=len(group) * seq * width,
            ),
        )(where, meta, *args)
        results.extend(found[:2])
        if first:
            weight = found[2]

    bias = lax.dynamic_slice_in_dim(decoder_bias, (me // 2) * 2 * half, 2 * half, 0)[None, :]
    args = [arrived[place] for place in groups[-1]] + [weight, *params, *halves, bias, *results]
    send = pl.pallas_call(
        lambda *refs: last_kernel(groups[-1], groups[:-1], layers, *refs),
        out_shape=jax.ShapeDtypeStruct(
            (devices, (1 + BLK_DEV) * SLOT_ROWS, TILE), jnp.bfloat16
        ),
        in_specs=[smem, smem] + [vmem] * len(args),
        out_specs=vmem,
        scratch_shapes=[
            pltpu.VMEM((devices, 2 * half), jnp.float32),
            pltpu.VMEM((devices * (1 + BLK_DEV) * SLOT_ROWS, TILE), jnp.float32),
        ],
        compiler_params=limit,
        cost_estimate=pl.CostEstimate(
            flops=2 * len(groups[-1]) * seq * width * (width + 2 * half),
            bytes_accessed=1024 * 1024,
            transcendentals=len(groups[-1]) * seq * width,
        ),
    )(where, meta, *args)
    got = lax.all_to_all(send, "doc", split_axis=0, concat_axis=0, tiled=True)
    got = got.reshape(chips, 2, 1 + BLK_DEV, SLOT_ROWS, TILE)[:, :, :, :tiles]
    whole = jnp.swapaxes(jnp.maximum(got[:, 0], got[:, 1]), 0, 1).reshape(1 + BLK_DEV, -1)
    return (whole[:1], whole[1:])


def tokens_move(mesh):
    devices = mesh.shape["doc"]
    return mesh.shape["term"] == 1 and devices >= 8 and devices & (devices - 1) == 0


def solution(mesh):
    placed = (
        P(("groups", "doc"), None),
        P(("groups", "doc")),
        P("doc", "term"),
        P(),
        P(),
        P(),
        P("term", None, "doc"),
        P("term"),
        P("term", ("groups", "doc"), None),
        P("term", ("groups", "doc"), None, None),
        P("term", ("groups", "doc"), None),
    )

    def local(*args):
        pair = 2 * args[6].shape[2]
        tiles = pair * (mesh.shape["doc"] // 2) // TILE
        fits = pair % TILE == 0 and tiles < TILE and pair // TILE <= SLOT_ROWS
        if tokens_move(mesh) and args[1].shape[0] == 1 and fits:
            return move_tokens(*args)
        return move_weights(*args)

    return jax.shard_map(
        local,
        mesh=mesh,
        in_specs=placed,
        out_specs=(P(("groups", "doc"), "term"), P(("groups", "doc"), "term")),
        check_vma=False,
    )
```

```python
import jax
import jax.numpy as jnp
from jax import lax
from jax.experimental import pallas as pl
from jax.experimental.pallas import tpu as pltpu
from jax.sharding import PartitionSpec as P

TILE = 128
BLK_DEV = 2
SLOT_ROWS = 16


def layer_norm(activated, norm_gain, norm_bias):
    values = activated.astype(jnp.float32)
    centre = jnp.mean(values, axis=-1, keepdims=True)
    centred = values - centre
    spread = jnp.mean(centred * centred, axis=-1, keepdims=True)
    return (centred * lax.rsqrt(spread + 1e-05) * norm_gain + norm_bias).astype(jnp.bfloat16)


def pool_docs(logits, keep):
    docs_here = keep.shape[0]
    saturated = jnp.log1p(jnp.maximum(logits, 0.0)).reshape(
        docs_here, keep.shape[1], logits.shape[1]
    )
    return jnp.max(jnp.where(keep[:, :, None], saturated, 0.0), axis=1)


def move_weights(
    hidden_states,
    doc_lengths,
    transform_weight,
    transform_bias,
    norm_gain,
    norm_bias,
    decoder_weight,
    decoder_bias,
    tile_ids,
    owner_ids,
    block_slots,
):
    tok_rows = hidden_states.shape[0]
    docs_here = doc_lengths.shape[0]
    seq_len = tok_rows // docs_here
    cols = transform_weight.shape[1]
    pre_half = jnp.dot(
        hidden_states,
        lax.all_gather(transform_weight, "doc", axis=0, tiled=True),
        preferred_element_type=jnp.float32,
    )
    bias_half = lax.dynamic_slice_in_dim(transform_bias, lax.axis_index("term") * cols, cols, 0)
    act_half = jax.nn.gelu(pre_half + bias_half, approximate=False).astype(jnp.bfloat16)
    activated = lax.all_gather(act_half, "term", axis=1, tiled=True)
    normed = layer_norm(activated, norm_gain, norm_bias)
    keep = jnp.arange(seq_len, dtype=jnp.int32)[None, :] < doc_lengths[:, None]
    logits = jnp.dot(
        normed,
        lax.all_gather(decoder_weight, "doc", axis=2, tiled=True)[0],
        preferred_element_type=jnp.float32,
    )
    logits = logits + decoder_bias
    impacts = pool_docs(logits, keep).astype(jnp.bfloat16)
    tiles_t = impacts.shape[1] // TILE
    slots_total = BLK_DEV * tiles_t
    tiles = impacts.reshape(docs_here * tiles_t, TILE)
    chosen = tile_ids[0]
    doc_index = jnp.arange(docs_here, dtype=jnp.int32)[:, None]
    posted = tiles[(doc_index * tiles_t + chosen).reshape(-1)]
    owners = owner_ids[0, :, :, 0].reshape(-1)
    target = block_slots[0].reshape(-1) * tiles_t + chosen.reshape(-1)
    owner_count = lax.axis_size("doc")
    capacity = max(2, 2 * posted.shape[0] // owner_count)
    onehot = (owners[:, None] == jnp.arange(owner_count, dtype=jnp.int32)[None, :]).astype(
        jnp.int32
    )
    before = jnp.cumsum(onehot, axis=0) - onehot
    position = jnp.sum(before * onehot, axis=1)
    dest = owners * capacity + position
    outgoing = jnp.zeros((owner_count * capacity, TILE), jnp.bfloat16).at[dest].set(posted)
    out_tags = jnp.full((owner_count * capacity,), slots_total, jnp.int32).at[dest].set(target)
    got_vals, got_tags = (
        lax.all_to_all(
            outgoing.reshape(owner_count, capacity, TILE),
            "doc",
            split_axis=0,
            concat_axis=0,
            tiled=True,
        ),
        lax.all_to_all(
            out_tags.reshape(owner_count, capacity), "doc", split_axis=0, concat_axis=0, tiled=True
        ),
    )
    got_vals = got_vals.reshape(-1, TILE)
    local_tags = got_tags.reshape(-1)
    summary = jnp.zeros((slots_total, TILE), jnp.bfloat16).at[local_tags].max(got_vals, mode="drop")
    return (impacts, summary.reshape(BLK_DEV, tiles_t * TILE))


def dot_t(left, right):
    return lax.dot_general(
        left, right, (((1,), (1,)), ((), ())), preferred_element_type=jnp.float32
    )


def chip_at(me, shift, across, layers):
    chip = me // 2
    layer = (chip // 2 - shift + layers) % layers
    return 2 * layer + ((chip % 2) ^ across)


def masked(ref, length):
    here = ref[...]
    keep = lax.broadcasted_iota(jnp.int32, here.shape, 0).astype(jnp.float32) < length
    first = jnp.broadcast_to(here[0:1, :].astype(jnp.float32), here.shape).astype(here.dtype)
    return jnp.where(keep, here, first)


def normed_rows(docs, lengths, weight, params):
    rows = jnp.concatenate([masked(ref, length) for ref, length in zip(docs, lengths)], axis=0)
    pre = jnp.dot(rows, weight[...], preferred_element_type=jnp.float32) + params[0][...]
    act = 0.5 * pre * (1.0 + lax.erf(pre * (0.5**0.5)))
    return layer_norm(act.astype(jnp.bfloat16), params[1][...], params[2][...])


def tops_of(normed, w_ref, count):
    logits = dot_t(normed, w_ref[...])
    seq = normed.shape[0] // count
    return [
        jnp.max(logits[j * seq : (j + 1) * seq], axis=0, keepdims=True) for j in range(count)
    ]


def start_kernel(tiles_ref, owners_ref, slots_ref, length_ref, weight_ref, out_ref, sem):
    rows, width = weight_ref.shape
    copy = pltpu.make_async_copy(weight_ref, out_ref.at[:, pl.ds(0, width)], sem)
    copy.start()
    lane = lax.broadcasted_iota(jnp.int32, (rows, TILE), 1)
    table = jnp.where(lane == TILE - 1, length_ref[0], -1)
    devices = lax.axis_size("doc")
    for k in range(tiles_ref.shape[2]):
        block = slots_ref[0, 0, k] * devices + owners_ref[0, 0, k]
        table = jnp.where(lane == tiles_ref[0, 0, k], block, table)
    out_ref[:, width:] = table.astype(jnp.float32).astype(jnp.bfloat16)
    copy.wait()


def pack_kernel(*refs):
    blocks, out_ref = refs[:-1], refs[-1]
    rows, width = blocks[0].shape[0], out_ref.shape[1]
    tables = jnp.zeros((SLOT_ROWS, width), jnp.float32)
    row = lax.broadcasted_iota(jnp.int32, (SLOT_ROWS, TILE), 0)
    tables = jnp.zeros((SLOT_ROWS, TILE), jnp.float32)
    for k, ref in enumerate(blocks):
        out_ref[k * rows : (k + 1) * rows, :] = ref[:, 0:width]
        tables = jnp.where(row == k, ref[0:SLOT_ROWS, width:].astype(jnp.float32), tables)
    last = len(blocks) * rows
    out_ref[last : last + SLOT_ROWS, :] = jnp.zeros((SLOT_ROWS, width), out_ref.dtype)
    out_ref[last : last + SLOT_ROWS, 0:TILE] = tables.astype(out_ref.dtype)


def fetch(ref, slot, sem):
    copy = pltpu.make_async_copy(ref, slot, sem)
    copy.start()
    return copy


def first_kernel(layers, *refs):
    me_ref, refs = refs[0], refs[1:]
    docs, refs = refs[:layers], refs[layers:]
    packed, refs = refs[:4], refs[4:]
    params, refs = refs[:3], refs[3:]
    mine_ref, theirs_ref, refs = refs[0], refs[1], refs[2:]
    best_refs, weight, meta_ref, mine, own, sems = refs[:2], refs[2], refs[3], *refs[4:]
    mine_copy = fetch(mine_ref, mine, sems.at[0])
    own_copy = fetch(docs[0], own, sems.at[1])
    me = me_ref[0]
    core = me % 2
    rows = weight.shape[0] // (4 * layers)
    for across in range(2):
        for shift in range(layers):
            chip = chip_at(me, shift, across, layers)
            block = slice(shift * rows, (shift + 1) * rows)
            at = pl.multiple_of((2 * chip + core) * rows, SLOT_ROWS)
            weight[pl.ds(at, rows), :] = packed[across][block, :]
            at = pl.multiple_of((2 * chip + 1 - core) * rows, SLOT_ROWS)
            weight[pl.ds(at, rows), :] = packed[2 + across][block, :]
    tables = [
        ref[layers * rows : layers * rows + SLOT_ROWS, 0:TILE].astype(jnp.float32)
        for ref in packed[:2]
    ]
    meta_ref[...] = jnp.concatenate([t[0:layers] for t in tables], axis=0).astype(jnp.int32)
    lengths = [tables[0][k : k + 1, TILE - 1 : TILE] for k in range(layers)]
    docs = [own, *docs[1:]]
    order = [*range(1, layers), 0]
    for first in range(0, layers, 2):
        pair = order[first : first + 2]
        if 0 in pair:
            own_copy.wait()
        normed = normed_rows(
            [docs[k] for k in pair], [lengths[k] for k in pair], weight, params
        )
        if first == 0:
            mine_copy.wait()
        for w_ref, best in zip((mine, theirs_ref), best_refs):
            for k, top in zip(pair, tops_of(normed, w_ref, 2)):
                best[k : k + 1, :] = top


def next_kernel(layers, first, *refs):
    meta_ref, refs = refs[0], refs[1:]
    docs, weight, params, refs = refs[:2], refs[2], refs[3:6], refs[6:]
    mine_ref, theirs_ref, best_refs, mine, sem = refs[0], refs[1], refs[2:4], *refs[4:]
    copy = fetch(mine_ref, mine, sem)
    lengths = [
        meta_ref[layers + first + k : layers + first + k + 1, TILE - 1 : TILE].astype(jnp.float32)
        for k in range(2)
    ]
    normed = normed_rows(docs, lengths, weight, params)
    copy.wait()
    for w_ref, best in zip((mine, theirs_ref), best_refs):
        for j, top in enumerate(tops_of(normed, w_ref, 2)):
            best[j : j + 1, :] = top


def last_kernel(layers, counts, *refs):
    me_ref, table_ref, meta_ref, refs = refs[0], refs[1], refs[2], refs[3:]
    docs, weight, params, refs = refs[:2], refs[2], refs[3:6], refs[6:]
    mine_ref, theirs_ref, dbias_ref, refs = refs[0], refs[1], refs[2], refs[3:]
    earlier, refs = refs[: 2 * len(counts)], refs[2 * len(counts) :]
    out_ref, best, send, mine, sem = refs
    copy = fetch(mine_ref, mine, sem)
    me = me_ref[0]
    core, chip = me % 2, me // 2
    devices = 4 * layers
    tiles = 2 * mine_ref.shape[0] // TILE
    lengths = [
        meta_ref[2 * layers - 2 + k : 2 * layers - 1 + k, TILE - 1 : TILE].astype(jnp.float32)
        for k in range(2)
    ]
    normed = normed_rows(docs, lengths, weight, params)
    found = []
    copy.wait()
    for k, w_ref in enumerate((mine, theirs_ref)):
        parts = [earlier[2 * n + k][0:count, :] for n, count in enumerate(counts)]
        found.append(jnp.concatenate([*parts, *tops_of(normed, w_ref, 2)], axis=0))
    low = jnp.where(core == 0, found[0], found[1])
    high = jnp.where(core == 0, found[1], found[0])
    logits = jnp.concatenate([low, high], axis=1) + dbias_ref[...]
    impacts = jnp.log1p(jnp.maximum(logits, 0.0)).astype(jnp.bfloat16).astype(jnp.float32)
    best[...] = jnp.zeros(best.shape, jnp.float32)
    for k in range(2 * layers):
        doc = 2 * chip_at(me, k % layers, k // layers, layers) + core
        best[pl.ds(doc, 1), :] = impacts[k : k + 1, :]
    send[...] = jnp.zeros(send.shape, jnp.float32)
    stride = out_ref.shape[1]
    target = lax.broadcasted_iota(jnp.int32, (BLK_DEV * devices, TILE), 0)
    for t in range(tiles):
        lanes = slice(t * TILE, (t + 1) * TILE)
        send[pl.ds(t, devices, stride=stride), :] = best[:, lanes]
        blocks = jnp.zeros((BLK_DEV * devices, TILE), jnp.float32)
        for k in range(2 * layers):
            block = table_ref[k, chip * tiles + t]
            blocks = jnp.maximum(
                blocks, jnp.where(target == block, impacts[k : k + 1, lanes], 0.0)
            )
        for s in range(BLK_DEV):
            send[pl.ds((1 + s) * SLOT_ROWS + t, devices, stride=stride), :] = blocks[
                s * devices : (s + 1) * devices
            ]
    out_ref[...] = send[...].astype(jnp.bfloat16).reshape(out_ref.shape)


def move_tokens(
    hidden_states,
    doc_lengths,
    transform_weight,
    transform_bias,
    norm_gain,
    norm_bias,
    decoder_weight,
    decoder_bias,
    tile_ids,
    owner_ids,
    block_slots,
):
    devices = lax.axis_size("doc")
    chips = devices // 2
    layers = chips // 2
    seq, width = hidden_states.shape
    rows = transform_weight.shape[0]
    half = decoder_weight.shape[2]
    tiles = 2 * half // TILE
    me = lax.axis_index("doc").astype(jnp.int32)

    def flip(value, bit):
        return lax.ppermute(value, "doc", [(i, i ^ bit) for i in range(devices)])

    def shift(value, by):
        return lax.ppermute(value, "doc", [(i, (i + 4 * by) % devices) for i in range(devices)])

    smem = pl.BlockSpec(memory_space=pltpu.SMEM)
    vmem = pl.BlockSpec(memory_space=pltpu.VMEM)
    hbm = pl.BlockSpec(memory_space=pltpu.HBM)

    def stay(value):
        return pltpu.with_memory_space_constraint(value, pltpu.HBM)

    limit = pltpu.CompilerParams(vmem_limit_bytes=24 * 1024 * 1024)

    def cost(docs):
        return pl.CostEstimate(
            flops=2 * docs * seq * width * (width + 2 * half),
            bytes_accessed=1024 * 1024,
            transcendentals=docs * seq * width,
        )

    def shape(dims, dtype):
        return jax.ShapeDtypeStruct(dims, dtype)

    block = pl.pallas_call(
        start_kernel,
        out_shape=shape((rows, width + TILE), jnp.bfloat16),
        in_specs=[smem] * 4 + [hbm],
        out_specs=vmem,
        scratch_shapes=[pltpu.SemaphoreType.DMA],
        compiler_params=limit,
    )(
        stay(tile_ids),
        stay(owner_ids[..., 0]),
        stay(block_slots),
        doc_lengths,
        stay(transform_weight),
    )
    blocks = [block] + [shift(block, by) for by in range(1, layers)]
    near = [hidden_states] + [shift(hidden_states, by) for by in range(1, layers)]
    far = [flip(value, 2) for value in near]
    blocks, near[1], far[0] = lax.optimization_barrier((blocks, near[1], far[0]))
    packed = pl.pallas_call(
        pack_kernel,
        out_shape=shape((layers * rows + SLOT_ROWS, width), jnp.bfloat16),
        in_specs=[vmem] * layers,
        out_specs=vmem,
        compiler_params=limit,
    )(*blocks)
    packed_across = flip(packed, 2)
    packed_across, near[2] = lax.optimization_barrier((packed_across, near[2]))
    packed_all = [packed, packed_across, flip(packed, 1), flip(packed_across, 1)]

    weight_rows = jnp.swapaxes(decoder_weight[0], 0, 1)
    halves = (stay(weight_rows), flip(weight_rows, 1))

    where = me[None]
    params = (transform_bias[None, :], norm_gain[None, :], norm_bias[None, :])
    slot = pltpu.VMEM((half, width), jnp.bfloat16)
    best_shape = shape((8, half), jnp.float32)
    *best, weight, meta = pl.pallas_call(
        lambda *refs: first_kernel(layers, *refs),
        out_shape=[
            best_shape,
            best_shape,
            shape((width, width), jnp.bfloat16),
            shape((chips, TILE), jnp.int32),
        ],
        in_specs=[smem, hbm] + [vmem] * (layers - 1 + 4 + 3) + [hbm, vmem],
        out_specs=[vmem] * 4,
        scratch_shapes=[
            slot,
            pltpu.VMEM((seq, width), jnp.bfloat16),
            pltpu.SemaphoreType.DMA((2,)),
        ],
        compiler_params=limit,
        cost_estimate=cost(layers),
    )(where, stay(hidden_states), *near[1:], *packed_all, *params, *halves)
    counts = [layers]
    for first in range(0, layers - 2, 2):
        best += pl.pallas_call(
            lambda *refs, first=first: next_kernel(layers, first, *refs),
            out_shape=[best_shape] * 2,
            in_specs=[vmem] * 7 + [hbm, vmem],
            out_specs=[vmem] * 2,
            scratch_shapes=[slot, pltpu.SemaphoreType.DMA],
            compiler_params=limit,
            cost_estimate=cost(2),
        )(meta, *far[first : first + 2], weight, *params, *halves)
        counts.append(2)
    bias = lax.dynamic_slice_in_dim(decoder_bias, (me // 2) * 2 * half, 2 * half, 0)[None, :]
    send = pl.pallas_call(
        lambda *refs: last_kernel(layers, counts, *refs),
        out_shape=shape((devices, (1 + BLK_DEV) * SLOT_ROWS, TILE), jnp.bfloat16),
        in_specs=[smem] * 2 + [vmem] * 7 + [hbm] + [vmem] * (2 + len(best)),
        out_specs=vmem,
        scratch_shapes=[
            pltpu.VMEM((devices, 2 * half), jnp.float32),
            pltpu.VMEM((devices * (1 + BLK_DEV) * SLOT_ROWS, TILE), jnp.float32),
            slot,
            pltpu.SemaphoreType.DMA,
        ],
        compiler_params=limit,
        cost_estimate=cost(2),
    )(where, meta, meta, *far[layers - 2 :], weight, *params, *halves, bias, *best)
    got = lax.all_to_all(send, "doc", split_axis=0, concat_axis=0, tiled=True)
    got = got.reshape(chips, 2, 1 + BLK_DEV, SLOT_ROWS, TILE)[:, :, :, :tiles]
    whole = jnp.swapaxes(jnp.maximum(got[:, 0], got[:, 1]), 0, 1).reshape(1 + BLK_DEV, -1)
    return (whole[:1], whole[1:])


def tokens_move(mesh):
    devices = mesh.shape["doc"]
    return mesh.shape["term"] == 1 and devices >= 8 and devices & (devices - 1) == 0


def solution(mesh):
    placed = (
        P(("groups", "doc"), None),
        P(("groups", "doc")),
        P("doc", "term"),
        P(),
        P(),
        P(),
        P("term", None, "doc"),
        P("term"),
        P("term", ("groups", "doc"), None),
        P("term", ("groups", "doc"), None, None),
        P("term", ("groups", "doc"), None),
    )

    def local(*args):
        pair = 2 * args[6].shape[2]
        tiles = pair * (mesh.shape["doc"] // 2) // TILE
        fits = pair % TILE == 0 and tiles < TILE and pair // TILE <= SLOT_ROWS
        if tokens_move(mesh) and args[1].shape[0] == 1 and fits:
            return move_tokens(*args)
        return move_weights(*args)

    return jax.shard_map(
        local,
        mesh=mesh,
        in_specs=placed,
        out_specs=(P(("groups", "doc"), "term"), P(("groups", "doc"), "term")),
        check_vma=False,
    )
```

```python
import jax
import jax.numpy as jnp
from jax import lax
from jax.experimental import pallas as pl
from jax.experimental.pallas import tpu as pltpu
from jax.sharding import PartitionSpec as P

TILE = 128
BLK_DEV = 2
SLOT_ROWS = 16


def layer_norm(activated, norm_gain, norm_bias):
    values = activated.astype(jnp.float32)
    centre = jnp.mean(values, axis=-1, keepdims=True)
    centred = values - centre
    spread = jnp.mean(centred * centred, axis=-1, keepdims=True)
    return (centred * lax.rsqrt(spread + 1e-05) * norm_gain + norm_bias).astype(jnp.bfloat16)


def pool_docs(logits, keep):
    docs_here = keep.shape[0]
    saturated = jnp.log1p(jnp.maximum(logits, 0.0)).reshape(
        docs_here, keep.shape[1], logits.shape[1]
    )
    return jnp.max(jnp.where(keep[:, :, None], saturated, 0.0), axis=1)


def move_weights(
    hidden_states,
    doc_lengths,
    transform_weight,
    transform_bias,
    norm_gain,
    norm_bias,
    decoder_weight,
    decoder_bias,
    tile_ids,
    owner_ids,
    block_slots,
):
    tok_rows = hidden_states.shape[0]
    docs_here = doc_lengths.shape[0]
    seq_len = tok_rows // docs_here
    cols = transform_weight.shape[1]
    pre_half = jnp.dot(
        hidden_states,
        lax.all_gather(transform_weight, "doc", axis=0, tiled=True),
        preferred_element_type=jnp.float32,
    )
    bias_half = lax.dynamic_slice_in_dim(transform_bias, lax.axis_index("term") * cols, cols, 0)
    act_half = jax.nn.gelu(pre_half + bias_half, approximate=False).astype(jnp.bfloat16)
    activated = lax.all_gather(act_half, "term", axis=1, tiled=True)
    normed = layer_norm(activated, norm_gain, norm_bias)
    keep = jnp.arange(seq_len, dtype=jnp.int32)[None, :] < doc_lengths[:, None]
    logits = jnp.dot(
        normed,
        lax.all_gather(decoder_weight, "doc", axis=2, tiled=True)[0],
        preferred_element_type=jnp.float32,
    )
    logits = logits + decoder_bias
    impacts = pool_docs(logits, keep).astype(jnp.bfloat16)
    tiles_t = impacts.shape[1] // TILE
    slots_total = BLK_DEV * tiles_t
    tiles = impacts.reshape(docs_here * tiles_t, TILE)
    chosen = tile_ids[0]
    doc_index = jnp.arange(docs_here, dtype=jnp.int32)[:, None]
    posted = tiles[(doc_index * tiles_t + chosen).reshape(-1)]
    owners = owner_ids[0, :, :, 0].reshape(-1)
    target = block_slots[0].reshape(-1) * tiles_t + chosen.reshape(-1)
    owner_count = lax.axis_size("doc")
    capacity = max(2, 2 * posted.shape[0] // owner_count)
    onehot = (owners[:, None] == jnp.arange(owner_count, dtype=jnp.int32)[None, :]).astype(
        jnp.int32
    )
    before = jnp.cumsum(onehot, axis=0) - onehot
    position = jnp.sum(before * onehot, axis=1)
    dest = owners * capacity + position
    outgoing = jnp.zeros((owner_count * capacity, TILE), jnp.bfloat16).at[dest].set(posted)
    out_tags = jnp.full((owner_count * capacity,), slots_total, jnp.int32).at[dest].set(target)
    got_vals, got_tags = (
        lax.all_to_all(
            outgoing.reshape(owner_count, capacity, TILE),
            "doc",
            split_axis=0,
            concat_axis=0,
            tiled=True,
        ),
        lax.all_to_all(
            out_tags.reshape(owner_count, capacity), "doc", split_axis=0, concat_axis=0, tiled=True
        ),
    )
    got_vals = got_vals.reshape(-1, TILE)
    local_tags = got_tags.reshape(-1)
    summary = jnp.zeros((slots_total, TILE), jnp.bfloat16).at[local_tags].max(got_vals, mode="drop")
    return (impacts, summary.reshape(BLK_DEV, tiles_t * TILE))


def dot_t(left, right):
    return lax.dot_general(
        left, right, (((1,), (1,)), ((), ())), preferred_element_type=jnp.float32
    )


def chip_at(me, shift, across, layers):
    chip = me // 2
    layer = (chip // 2 - shift + layers) % layers
    return 2 * layer + ((chip % 2) ^ across)


def masked(ref, length):
    here = ref[...]
    keep = lax.broadcasted_iota(jnp.int32, here.shape, 0).astype(jnp.float32) < length
    first = jnp.broadcast_to(here[0:1, :].astype(jnp.float32), here.shape).astype(here.dtype)
    return jnp.where(keep, here, first)


def normed_rows(docs, lengths, weight, params):
    rows = jnp.concatenate([masked(ref, length) for ref, length in zip(docs, lengths)], axis=0)
    pre = jnp.dot(rows, weight[...], preferred_element_type=jnp.float32) + params[0:1, :]
    act = 0.5 * pre * (1.0 + lax.erf(pre * (0.5**0.5)))
    return layer_norm(act.astype(jnp.bfloat16), params[1:2, :], params[2:3, :])


def tops_of(normed, w_ref, count):
    logits = dot_t(normed, w_ref[...])
    seq = normed.shape[0] // count
    return [
        jnp.max(logits[j * seq : (j + 1) * seq], axis=0, keepdims=True) for j in range(count)
    ]


def start_kernel(tiles_ref, owners_ref, slots_ref, length_ref, *refs):
    weight_ref, vectors, (out_ref, rows_ref, kept, sems) = refs[0], refs[1:4], refs[4:]
    rows, width = weight_ref.shape
    copies = [fetch(weight_ref, out_ref.at[:, pl.ds(0, width)], sems.at[0])]
    for k, ref in enumerate(vectors):
        copies.append(fetch(ref, kept.at[pl.ds(k * width, width)], sems.at[1 + k]))
    lane = lax.broadcasted_iota(jnp.int32, (rows, TILE), 1)
    table = jnp.where(lane == TILE - 1, length_ref[0], -1)
    devices = lax.axis_size("doc")
    for k in range(tiles_ref.shape[2]):
        block = slots_ref[0, 0, k] * devices + owners_ref[0, 0, k]
        table = jnp.where(lane == tiles_ref[0, 0, k], block, table)
    out_ref[:, width:] = table.astype(jnp.float32).astype(jnp.bfloat16)
    for copy in copies:
        copy.wait()
    for k in range(len(vectors)):
        rows_ref[k : k + 1, :] = kept[pl.ds(k * width, width)][None, :]


def pack_kernel(*refs):
    blocks, out_ref, meta_ref = refs[:-2], refs[-2], refs[-1]
    rows, width = blocks[0].shape[0], out_ref.shape[1]
    row = lax.broadcasted_iota(jnp.int32, meta_ref.shape, 0)
    tables = jnp.zeros(meta_ref.shape, jnp.float32)
    for k, ref in enumerate(blocks):
        out_ref[k * rows : (k + 1) * rows, :] = ref[:, 0:width]
        table = ref[0:SLOT_ROWS, width:].astype(jnp.float32)
        tables = jnp.where(row == k, table[0 : len(blocks)], tables)
    meta_ref[...] = tables.astype(jnp.int32)


def fetch(ref, slot, sem):
    copy = pltpu.make_async_copy(ref, slot, sem)
    copy.start()
    return copy


def length_of(meta_ref, k):
    return meta_ref[k : k + 1, TILE - 1 : TILE].astype(jnp.float32)


def first_kernel(layers, order, *refs):
    (me_ref, meta_ref), refs = refs[:2], refs[2:]
    docs, refs = refs[: len(order)], refs[len(order) :]
    packed, refs = refs[:2], refs[2:]
    params, mine_ref, theirs_ref, refs = refs[0], refs[1], refs[2], refs[3:]
    best_refs, weight, mine, own, sems = refs[:2], refs[2], *refs[3:]
    mine_copy = fetch(mine_ref, mine, sems.at[0])
    own_copy = fetch(docs[-1], own, sems.at[1])
    me = me_ref[0]
    core = me % 2
    rows = weight.shape[0] // (4 * layers)
    for k in range(2 * layers):
        chip = chip_at(me, k % layers, k // layers, layers)
        block = slice(k * rows, (k + 1) * rows)
        at = pl.multiple_of((2 * chip + core) * rows, SLOT_ROWS)
        weight[pl.ds(at, rows), :] = packed[0][block, :]
        at = pl.multiple_of((2 * chip + 1 - core) * rows, SLOT_ROWS)
        weight[pl.ds(at, rows), :] = packed[1][block, :]
    docs = [*docs[:-1], own]
    for first in range(0, len(order), 2):
        if first + 2 == len(order):
            own_copy.wait()
        lengths = [length_of(meta_ref, k) for k in order[first : first + 2]]
        normed = normed_rows(docs[first : first + 2], lengths, weight, params)
        if first == 0:
            mine_copy.wait()
        for w_ref, best in zip((mine, theirs_ref), best_refs):
            for j, top in enumerate(tops_of(normed, w_ref, 2)):
                best[first + j : first + j + 1, :] = top


def next_kernel(order, *refs):
    meta_ref, refs = refs[0], refs[1:]
    docs, weight, params, refs = refs[:2], refs[2], refs[3], refs[4:]
    mine_ref, theirs_ref, best_refs, mine, sem = refs[0], refs[1], refs[2:4], *refs[4:]
    copy = fetch(mine_ref, mine, sem)
    lengths = [length_of(meta_ref, k) for k in order]
    normed = normed_rows(docs, lengths, weight, params)
    copy.wait()
    for w_ref, best in zip((mine, theirs_ref), best_refs):
        for j, top in enumerate(tops_of(normed, w_ref, 2)):
            best[j : j + 1, :] = top


def last_kernel(layers, orders, *refs):
    me_ref, table_ref, meta_ref, refs = refs[0], refs[1], refs[2], refs[3:]
    docs, weight, params, refs = refs[:2], refs[2], refs[3], refs[4:]
    mine_ref, theirs_ref, dbias_ref, refs = refs[0], refs[1], refs[2], refs[3:]
    counts = [len(order) for order in orders[:-1]]
    earlier, refs = refs[: 2 * len(counts)], refs[2 * len(counts) :]
    out_ref, send, mine, sem = refs
    copy = fetch(mine_ref, mine, sem)
    me = me_ref[0]
    core, chip = me % 2, me // 2
    devices = 4 * layers
    tiles = 2 * mine_ref.shape[0] // TILE
    lengths = [length_of(meta_ref, k) for k in orders[-1]]
    normed = normed_rows(docs, lengths, weight, params)
    found = []
    copy.wait()
    for k, w_ref in enumerate((mine, theirs_ref)):
        parts = [earlier[2 * n + k][0:count, :] for n, count in enumerate(counts)]
        found.append(jnp.concatenate([*parts, *tops_of(normed, w_ref, 2)], axis=0))
    low = jnp.where(core == 0, found[0], found[1])
    high = jnp.where(core == 0, found[1], found[0])
    logits = jnp.concatenate([low, high], axis=1)
    order = [k for group in orders for k in group]
    docs_at = [2 * chip_at(me, k % layers, k // layers, layers) + core for k in order]
    bias = dbias_ref[...]
    bias = pltpu.roll(bias, bias.shape[0] - chip * tiles, 0)
    send[...] = jnp.zeros(send.shape, jnp.float32)
    stride = out_ref.shape[1]
    target = lax.broadcasted_iota(jnp.int32, (BLK_DEV * devices, TILE), 0)
    for t in range(tiles):
        lanes = slice(t * TILE, (t + 1) * TILE)
        impacts = jnp.log1p(jnp.maximum(logits[:, lanes] + bias[t : t + 1, :], 0.0))
        impacts = impacts.astype(jnp.bfloat16).astype(jnp.float32)
        blocks = jnp.zeros((BLK_DEV * devices, TILE), jnp.float32)
        for n, k in enumerate(order):
            row = impacts[n : n + 1, :]
            send[pl.ds(docs_at[n] * stride + t, 1), :] = row
            block = table_ref[k, chip * tiles + t]
            blocks = jnp.maximum(blocks, jnp.where(target == block, row, 0.0))
        for s in range(BLK_DEV):
            send[pl.ds((1 + s) * SLOT_ROWS + t, devices, stride=stride), :] = blocks[
                s * devices : (s + 1) * devices
            ]
    out_ref[...] = send[...].astype(jnp.bfloat16).reshape(out_ref.shape)


def move_tokens(
    hidden_states,
    doc_lengths,
    transform_weight,
    transform_bias,
    norm_gain,
    norm_bias,
    decoder_weight,
    decoder_bias,
    tile_ids,
    owner_ids,
    block_slots,
):
    devices = lax.axis_size("doc")
    chips = devices // 2
    layers = chips // 2
    seq, width = hidden_states.shape
    rows = transform_weight.shape[0]
    half = decoder_weight.shape[2]
    tiles = 2 * half // TILE
    me = lax.axis_index("doc").astype(jnp.int32)

    def flip(value, bit):
        return lax.ppermute(value, "doc", [(i, i ^ bit) for i in range(devices)])

    def shift(value, by):
        return lax.ppermute(value, "doc", [(i, (i + 4 * by) % devices) for i in range(devices)])

    smem = pl.BlockSpec(memory_space=pltpu.SMEM)
    vmem = pl.BlockSpec(memory_space=pltpu.VMEM)
    hbm = pl.BlockSpec(memory_space=pltpu.HBM)

    def stay(value):
        return pltpu.with_memory_space_constraint(value, pltpu.HBM)

    limit = pltpu.CompilerParams(vmem_limit_bytes=24 * 1024 * 1024)

    def cost(docs):
        return pl.CostEstimate(
            flops=2 * docs * seq * width * (width + 2 * half),
            bytes_accessed=1024 * 1024,
            transcendentals=docs * seq * width,
        )

    def shape(dims, dtype):
        return jax.ShapeDtypeStruct(dims, dtype)

    def after(value, *done):
        return lax.optimization_barrier((value, *done))[0]

    near = {1: shift(hidden_states, 1)}
    far = {0: flip(hidden_states, 2)}
    block, params = pl.pallas_call(
        start_kernel,
        out_shape=[
            shape((rows, width + TILE), jnp.bfloat16),
            shape((8, width), jnp.float32),
        ],
        in_specs=[smem] * 4 + [hbm] * 4,
        out_specs=[vmem] * 2,
        scratch_shapes=[
            pltpu.VMEM((3 * width,), jnp.float32),
            pltpu.SemaphoreType.DMA((4,)),
        ],
        compiler_params=limit,
    )(
        stay(tile_ids),
        stay(owner_ids[..., 0]),
        stay(block_slots),
        doc_lengths,
        stay(transform_weight),
        stay(transform_bias),
        stay(norm_gain),
        stay(norm_bias),
    )
    blocks = [block]
    for by in range(1, layers):
        blocks.append(shift(after(block, far[0]) if by > 2 else block, by))
    weight_rows = jnp.swapaxes(decoder_weight[0], 0, 1)
    theirs = flip(weight_rows, 1)
    blocks += [flip(after(value, near[1]) if k > 1 else value, 2) for k, value in enumerate(blocks)]
    for by in range(2, layers):
        near[by] = shift(after(hidden_states, blocks[by - 1]), by)
    for by in range(1, layers):
        far[by] = flip(near[by], 2)
    blocks[0] = after(block, far[1], theirs)
    packed, meta = pl.pallas_call(
        pack_kernel,
        out_shape=[
            shape((chips * rows, width), jnp.bfloat16),
            shape((chips, TILE), jnp.int32),
        ],
        in_specs=[vmem] * chips,
        out_specs=[vmem] * 2,
        compiler_params=limit,
    )(*blocks)
    other_packed = flip(after(packed, *near.values()), 1)

    orders = [[1, layers, layers + 1, 0]]
    orders += [[by, layers + by] for by in range(2, layers)]
    arrived = {layers + by: value for by, value in far.items()} | near
    where = me[None]
    halves = (stay(weight_rows), theirs)
    slot = pltpu.VMEM((half, width), jnp.bfloat16)
    best_shape = shape((8, half), jnp.float32)
    first_docs = [arrived[k] for k in orders[0][:-1]]
    *best, weight = pl.pallas_call(
        lambda *refs: first_kernel(layers, orders[0], *refs),
        out_shape=[best_shape, best_shape, shape((width, width), jnp.bfloat16)],
        in_specs=[smem] + [vmem] * len(orders[0]) + [hbm] + [vmem] * 3 + [hbm, vmem],
        out_specs=[vmem] * 3,
        scratch_shapes=[
            slot,
            pltpu.VMEM((seq, width), jnp.bfloat16),
            pltpu.SemaphoreType.DMA((2,)),
        ],
        compiler_params=limit,
        cost_estimate=cost(len(orders[0])),
    )(where, meta, *first_docs, stay(hidden_states), packed, other_packed, params, *halves)
    for order in orders[1:-1]:
        best += pl.pallas_call(
            lambda *refs, order=order: next_kernel(order, *refs),
            out_shape=[best_shape] * 2,
            in_specs=[vmem] * 5 + [hbm, vmem],
            out_specs=[vmem] * 2,
            scratch_shapes=[slot, pltpu.SemaphoreType.DMA],
            compiler_params=limit,
            cost_estimate=cost(2),
        )(meta, *[arrived[k] for k in order], weight, params, *halves)
    send = pl.pallas_call(
        lambda *refs: last_kernel(layers, orders, *refs),
        out_shape=shape((devices, (1 + BLK_DEV) * SLOT_ROWS, TILE), jnp.bfloat16),
        in_specs=[smem] * 2 + [vmem] * 5 + [hbm] + [vmem] * (2 + len(best)),
        out_specs=vmem,
        scratch_shapes=[
            pltpu.VMEM((devices * (1 + BLK_DEV) * SLOT_ROWS, TILE), jnp.float32),
            slot,
            pltpu.SemaphoreType.DMA,
        ],
        compiler_params=limit,
        cost_estimate=cost(2),
    )(
        where,
        meta,
        meta,
        *[arrived[k] for k in orders[-1]],
        weight,
        params,
        *halves,
        decoder_bias.reshape(-1, TILE),
        *best,
    )
    got = lax.all_to_all(send, "doc", split_axis=0, concat_axis=0, tiled=True)
    got = got.reshape(chips, 2, 1 + BLK_DEV, SLOT_ROWS, TILE)[:, :, :, :tiles]
    whole = jnp.swapaxes(jnp.maximum(got[:, 0], got[:, 1]), 0, 1).reshape(1 + BLK_DEV, -1)
    return (whole[:1], whole[1:])


def tokens_move(mesh):
    devices = mesh.shape["doc"]
    return mesh.shape["term"] == 1 and devices >= 8 and devices & (devices - 1) == 0


def solution(mesh):
    placed = (
        P(("groups", "doc"), None),
        P(("groups", "doc")),
        P("doc", "term"),
        P(),
        P(),
        P(),
        P("term", None, "doc"),
        P("term"),
        P("term", ("groups", "doc"), None),
        P("term", ("groups", "doc"), None, None),
        P("term", ("groups", "doc"), None),
    )

    def local(*args):
        pair = 2 * args[6].shape[2]
        tiles = pair * (mesh.shape["doc"] // 2) // TILE
        fits = pair % TILE == 0 and tiles < TILE and pair // TILE <= SLOT_ROWS
        if tokens_move(mesh) and args[1].shape[0] == 1 and fits:
            return move_tokens(*args)
        return move_weights(*args)

    return jax.shard_map(
        local,
        mesh=mesh,
        in_specs=placed,
        out_specs=(P(("groups", "doc"), "term"), P(("groups", "doc"), "term")),
        check_vma=False,
    )
```

```python
import jax
import jax.numpy as jnp
from jax import lax
from jax.experimental import pallas as pl
from jax.experimental.pallas import tpu as pltpu
from jax.sharding import PartitionSpec as P

TILE = 128
BLK_DEV = 2
SLOT_ROWS = 16


def layer_norm(activated, norm_gain, norm_bias):
    values = activated.astype(jnp.float32)
    centre = jnp.mean(values, axis=-1, keepdims=True)
    centred = values - centre
    spread = jnp.mean(centred * centred, axis=-1, keepdims=True)
    return (centred * lax.rsqrt(spread + 1e-05) * norm_gain + norm_bias).astype(jnp.bfloat16)


def pool_docs(logits, keep):
    docs_here = keep.shape[0]
    saturated = jnp.log1p(jnp.maximum(logits, 0.0)).reshape(
        docs_here, keep.shape[1], logits.shape[1]
    )
    return jnp.max(jnp.where(keep[:, :, None], saturated, 0.0), axis=1)


def move_weights(
    hidden_states,
    doc_lengths,
    transform_weight,
    transform_bias,
    norm_gain,
    norm_bias,
    decoder_weight,
    decoder_bias,
    tile_ids,
    owner_ids,
    block_slots,
):
    tok_rows = hidden_states.shape[0]
    docs_here = doc_lengths.shape[0]
    seq_len = tok_rows // docs_here
    cols = transform_weight.shape[1]
    pre_half = jnp.dot(
        hidden_states,
        lax.all_gather(transform_weight, "doc", axis=0, tiled=True),
        preferred_element_type=jnp.float32,
    )
    bias_half = lax.dynamic_slice_in_dim(transform_bias, lax.axis_index("term") * cols, cols, 0)
    act_half = jax.nn.gelu(pre_half + bias_half, approximate=False).astype(jnp.bfloat16)
    activated = lax.all_gather(act_half, "term", axis=1, tiled=True)
    normed = layer_norm(activated, norm_gain, norm_bias)
    keep = jnp.arange(seq_len, dtype=jnp.int32)[None, :] < doc_lengths[:, None]
    logits = jnp.dot(
        normed,
        lax.all_gather(decoder_weight, "doc", axis=2, tiled=True)[0],
        preferred_element_type=jnp.float32,
    )
    logits = logits + decoder_bias
    impacts = pool_docs(logits, keep).astype(jnp.bfloat16)
    tiles_t = impacts.shape[1] // TILE
    slots_total = BLK_DEV * tiles_t
    tiles = impacts.reshape(docs_here * tiles_t, TILE)
    chosen = tile_ids[0]
    doc_index = jnp.arange(docs_here, dtype=jnp.int32)[:, None]
    posted = tiles[(doc_index * tiles_t + chosen).reshape(-1)]
    owners = owner_ids[0, :, :, 0].reshape(-1)
    target = block_slots[0].reshape(-1) * tiles_t + chosen.reshape(-1)
    owner_count = lax.axis_size("doc")
    capacity = max(2, 2 * posted.shape[0] // owner_count)
    onehot = (owners[:, None] == jnp.arange(owner_count, dtype=jnp.int32)[None, :]).astype(
        jnp.int32
    )
    before = jnp.cumsum(onehot, axis=0) - onehot
    position = jnp.sum(before * onehot, axis=1)
    dest = owners * capacity + position
    outgoing = jnp.zeros((owner_count * capacity, TILE), jnp.bfloat16).at[dest].set(posted)
    out_tags = jnp.full((owner_count * capacity,), slots_total, jnp.int32).at[dest].set(target)
    got_vals, got_tags = (
        lax.all_to_all(
            outgoing.reshape(owner_count, capacity, TILE),
            "doc",
            split_axis=0,
            concat_axis=0,
            tiled=True,
        ),
        lax.all_to_all(
            out_tags.reshape(owner_count, capacity), "doc", split_axis=0, concat_axis=0, tiled=True
        ),
    )
    got_vals = got_vals.reshape(-1, TILE)
    local_tags = got_tags.reshape(-1)
    summary = jnp.zeros((slots_total, TILE), jnp.bfloat16).at[local_tags].max(got_vals, mode="drop")
    return (impacts, summary.reshape(BLK_DEV, tiles_t * TILE))


def dot_t(left, right):
    return lax.dot_general(
        left, right, (((1,), (1,)), ((), ())), preferred_element_type=jnp.float32
    )


def masked(ref, length):
    here = ref[...]
    keep = lax.broadcasted_iota(jnp.int32, here.shape, 0).astype(jnp.float32) < length
    first = jnp.broadcast_to(here[0:1, :].astype(jnp.float32), here.shape).astype(here.dtype)
    return jnp.where(keep, here, first)


def normed_rows(docs, lengths, weight, params):
    rows = jnp.concatenate([masked(ref, length) for ref, length in zip(docs, lengths)], axis=0)
    pre = jnp.dot(rows, weight[...], preferred_element_type=jnp.float32) + params[0:1, :]
    act = 0.5 * pre * (1.0 + lax.erf(pre * (0.5**0.5)))
    return layer_norm(act.astype(jnp.bfloat16), params[1:2, :], params[2:3, :])


def tops_of(normed, w_ref, count):
    logits = dot_t(normed, w_ref[...])
    seq = normed.shape[0] // count
    return [
        jnp.max(logits[j * seq : (j + 1) * seq], axis=0, keepdims=True) for j in range(count)
    ]


def start_kernel(tiles_ref, owners_ref, slots_ref, length_ref, *refs):
    weight_ref, vectors, (out_ref, rows_ref, kept, sems) = refs[0], refs[1:4], refs[4:]
    rows, width = weight_ref.shape
    copies = [fetch(weight_ref, out_ref.at[:, pl.ds(0, width)], sems.at[0])]
    for k, ref in enumerate(vectors):
        copies.append(fetch(ref, kept.at[pl.ds(k * width, width)], sems.at[1 + k]))
    lane = lax.broadcasted_iota(jnp.int32, (rows, TILE), 1)
    table = jnp.where(lane == TILE - 1, length_ref[0], -1)
    devices = lax.axis_size("doc")
    for k in range(tiles_ref.shape[2]):
        block = slots_ref[0, 0, k] * devices + owners_ref[0, 0, k]
        table = jnp.where(lane == tiles_ref[0, 0, k], block, table)
    out_ref[:, width:] = table.astype(jnp.float32).astype(jnp.bfloat16)
    for copy in copies:
        copy.wait()
    for k in range(len(vectors)):
        rows_ref[k : k + 1, :] = kept[pl.ds(k * width, width)][None, :]


def pile_kernel(*refs):
    at = 0
    for ref in refs[:-1]:
        refs[-1][at : at + ref.shape[0], :] = ref[...]
        at += ref.shape[0]


def pack_kernel(*refs):
    arrays, out_ref, meta_ref = refs[:-2], refs[-2], refs[-1]
    rows, width = arrays[0].shape[0], out_ref.shape[1]
    row = lax.broadcasted_iota(jnp.int32, meta_ref.shape, 0)
    tables = jnp.zeros(meta_ref.shape, jnp.float32)
    k = 0
    for ref in arrays:
        for first in range(0, ref.shape[0], rows):
            out_ref[k * rows : (k + 1) * rows, :] = ref[first : first + rows, 0:width]
            table = ref[first : first + SLOT_ROWS, width:].astype(jnp.float32)
            tables = jnp.where(row == k, table[0 : meta_ref.shape[0]], tables)
            k += 1
    meta_ref[...] = tables.astype(jnp.int32)


def fetch(ref, slot, sem):
    copy = pltpu.make_async_copy(ref, slot, sem)
    copy.start()
    return copy


def length_of(meta_ref, k):
    return meta_ref[k : k + 1, TILE - 1 : TILE].astype(jnp.float32)


def first_kernel(masks, order, *refs):
    (me_ref, meta_ref), refs = refs[:2], refs[2:]
    docs, refs = refs[: len(order)], refs[len(order) :]
    packed, refs = refs[:2], refs[2:]
    params, mine_ref, theirs_ref, refs = refs[0], refs[1], refs[2], refs[3:]
    best_refs, weight, mine, own, sems = refs[:2], refs[2], *refs[3:]
    mine_copy = fetch(mine_ref, mine, sems.at[0])
    own_copy = fetch(docs[-1], own, sems.at[1])
    me = me_ref[0]
    core = me % 2
    rows = weight.shape[0] // (2 * len(masks))
    for k, mask in enumerate(masks):
        chip = (me // 2) ^ mask
        block = slice(k * rows, (k + 1) * rows)
        at = pl.multiple_of((2 * chip + core) * rows, SLOT_ROWS)
        weight[pl.ds(at, rows), :] = packed[0][block, :]
        at = pl.multiple_of((2 * chip + 1 - core) * rows, SLOT_ROWS)
        weight[pl.ds(at, rows), :] = packed[1][block, :]
    docs = [*docs[:-1], own]
    for first in range(0, len(order), 2):
        if first + 2 == len(order):
            own_copy.wait()
        lengths = [length_of(meta_ref, masks.index(m)) for m in order[first : first + 2]]
        normed = normed_rows(docs[first : first + 2], lengths, weight, params)
        if first == 0:
            mine_copy.wait()
        for w_ref, best in zip((mine, theirs_ref), best_refs):
            for j, top in enumerate(tops_of(normed, w_ref, 2)):
                best[first + j : first + j + 1, :] = top


def next_kernel(masks, order, *refs):
    meta_ref, refs = refs[0], refs[1:]
    docs, weight, params, refs = refs[:2], refs[2], refs[3], refs[4:]
    mine_ref, theirs_ref, best_refs, mine, sem = refs[0], refs[1], refs[2:4], *refs[4:]
    copy = fetch(mine_ref, mine, sem)
    lengths = [length_of(meta_ref, masks.index(m)) for m in order]
    normed = normed_rows(docs, lengths, weight, params)
    copy.wait()
    for w_ref, best in zip((mine, theirs_ref), best_refs):
        for j, top in enumerate(tops_of(normed, w_ref, 2)):
            best[j : j + 1, :] = top


def last_kernel(masks, orders, *refs):
    me_ref, table_ref, meta_ref, refs = refs[0], refs[1], refs[2], refs[3:]
    docs, weight, params, refs = refs[:2], refs[2], refs[3], refs[4:]
    mine_ref, theirs_ref, dbias_ref, refs = refs[0], refs[1], refs[2], refs[3:]
    counts = [len(order) for order in orders[:-1]]
    earlier, refs = refs[: 2 * len(counts)], refs[2 * len(counts) :]
    out_ref, send, mine, sem = refs
    copy = fetch(mine_ref, mine, sem)
    me = me_ref[0]
    core, chip = me % 2, me // 2
    devices = 2 * len(masks)
    tiles = 2 * mine_ref.shape[0] // TILE
    lengths = [length_of(meta_ref, masks.index(m)) for m in orders[-1]]
    normed = normed_rows(docs, lengths, weight, params)
    found = []
    copy.wait()
    for k, w_ref in enumerate((mine, theirs_ref)):
        parts = [earlier[2 * n + k][0:count, :] for n, count in enumerate(counts)]
        found.append(jnp.concatenate([*parts, *tops_of(normed, w_ref, 2)], axis=0))
    low = jnp.where(core == 0, found[0], found[1])
    high = jnp.where(core == 0, found[1], found[0])
    logits = jnp.concatenate([low, high], axis=1)
    order = [mask for group in orders for mask in group]
    docs_at = [me ^ (2 * mask) for mask in order]
    bias = dbias_ref[...]
    bias = pltpu.roll(bias, bias.shape[0] - chip * tiles, 0)
    send[...] = jnp.zeros(send.shape, jnp.float32)
    stride = out_ref.shape[1]
    target = lax.broadcasted_iota(jnp.int32, (BLK_DEV * devices, TILE), 0)
    for t in range(tiles):
        lanes = slice(t * TILE, (t + 1) * TILE)
        impacts = jnp.log1p(jnp.maximum(logits[:, lanes] + bias[t : t + 1, :], 0.0))
        impacts = impacts.astype(jnp.bfloat16).astype(jnp.float32)
        blocks = jnp.zeros((BLK_DEV * devices, TILE), jnp.float32)
        for n, mask in enumerate(order):
            row = impacts[n : n + 1, :]
            send[pl.ds(docs_at[n] * stride + t, 1), :] = row
            block = table_ref[masks.index(mask), chip * tiles + t]
            blocks = jnp.maximum(blocks, jnp.where(target == block, row, 0.0))
        for s in range(BLK_DEV):
            send[pl.ds((1 + s) * SLOT_ROWS + t, devices, stride=stride), :] = blocks[
                s * devices : (s + 1) * devices
            ]
    out_ref[...] = send[...].astype(jnp.bfloat16).reshape(out_ref.shape)


def move_tokens(
    hidden_states,
    doc_lengths,
    transform_weight,
    transform_bias,
    norm_gain,
    norm_bias,
    decoder_weight,
    decoder_bias,
    tile_ids,
    owner_ids,
    block_slots,
):
    devices = lax.axis_size("doc")
    chips = devices // 2
    seq, width = hidden_states.shape
    rows = transform_weight.shape[0]
    half = decoder_weight.shape[2]
    tiles = 2 * half // TILE
    me = lax.axis_index("doc").astype(jnp.int32)

    def cross(value, mask):
        return lax.ppermute(value, "doc", [(i, i ^ (2 * mask)) for i in range(devices)])

    def swap(value):
        return lax.ppermute(value, "doc", [(i, i ^ 1) for i in range(devices)])

    smem = pl.BlockSpec(memory_space=pltpu.SMEM)
    vmem = pl.BlockSpec(memory_space=pltpu.VMEM)
    hbm = pl.BlockSpec(memory_space=pltpu.HBM)

    def stay(value):
        return pltpu.with_memory_space_constraint(value, pltpu.HBM)

    limit = pltpu.CompilerParams(vmem_limit_bytes=24 * 1024 * 1024)

    def cost(docs):
        return pl.CostEstimate(
            flops=2 * docs * seq * width * (width + 2 * half),
            bytes_accessed=1024 * 1024,
            transcendentals=docs * seq * width,
        )

    def shape(dims, dtype):
        return jax.ShapeDtypeStruct(dims, dtype)

    def after(value, *done):
        return lax.optimization_barrier((value, *done))[0]

    docs = {0: hidden_states, 6: cross(hidden_states, 6), 2: cross(hidden_states, 2)}
    docs[1] = cross(hidden_states, 1)
    block, params = pl.pallas_call(
        start_kernel,
        out_shape=[
            shape((rows, width + TILE), jnp.bfloat16),
            shape((8, width), jnp.float32),
        ],
        in_specs=[smem] * 4 + [hbm] * 4,
        out_specs=[vmem] * 2,
        scratch_shapes=[
            pltpu.VMEM((3 * width,), jnp.float32),
            pltpu.SemaphoreType.DMA((4,)),
        ],
        compiler_params=limit,
    )(
        stay(tile_ids),
        stay(owner_ids[..., 0]),
        stay(block_slots),
        doc_lengths,
        stay(transform_weight),
        stay(transform_bias),
        stay(norm_gain),
        stay(norm_bias),
    )
    weight_rows = jnp.swapaxes(decoder_weight[0], 0, 1)
    theirs = swap(weight_rows)

    def pile(*values):
        total = sum(value.shape[0] for value in values)
        return pl.pallas_call(
            pile_kernel,
            out_shape=shape((total, values[0].shape[1]), values[0].dtype),
            in_specs=[vmem] * len(values),
            out_specs=vmem,
            compiler_params=limit,
        )(*values)

    block_6 = cross(block, 6)
    block_2 = cross(after(block, docs[1]), 2)
    block_4 = cross(after(block_6, docs[2]), 2)
    docs[4] = cross(docs[6], 2)
    docs[3] = cross(docs[2], 1)
    docs[7] = cross(docs[6], 1)
    docs[5] = cross(docs[4], 1)
    near_pile = cross(pile(block, block_2), 1)
    far_pile = cross(pile(block_6, block_4), 1)
    masks = [0, 2, 6, 4, 1, 3, 7, 5]
    packed, meta = pl.pallas_call(
        pack_kernel,
        out_shape=[
            shape((chips * rows, width), jnp.bfloat16),
            shape((chips, TILE), jnp.int32),
        ],
        in_specs=[vmem] * 6,
        out_specs=[vmem] * 2,
        compiler_params=limit,
    )(after(block, docs[4], docs[3], theirs), block_2, block_6, block_4, near_pile, far_pile)
    other_packed = swap(after(packed, docs[7]))

    orders = [[2, 1, 3, 0], [6, 7], [4, 5]]
    where = me[None]
    halves = (stay(weight_rows), theirs)
    slot = pltpu.VMEM((half, width), jnp.bfloat16)
    best_shape = shape((8, half), jnp.float32)
    first_docs = [docs[mask] for mask in orders[0][:-1]]
    *best, weight = pl.pallas_call(
        lambda *refs: first_kernel(masks, orders[0], *refs),
        out_shape=[best_shape, best_shape, shape((width, width), jnp.bfloat16)],
        in_specs=[smem] + [vmem] * len(orders[0]) + [hbm] + [vmem] * 3 + [hbm, vmem],
        out_specs=[vmem] * 3,
        scratch_shapes=[
            slot,
            pltpu.VMEM((seq, width), jnp.bfloat16),
            pltpu.SemaphoreType.DMA((2,)),
        ],
        compiler_params=limit,
        cost_estimate=cost(len(orders[0])),
    )(where, meta, *first_docs, stay(hidden_states), packed, other_packed, params, *halves)
    for order in orders[1:-1]:
        best += pl.pallas_call(
            lambda *refs, order=order: next_kernel(masks, order, *refs),
            out_shape=[best_shape] * 2,
            in_specs=[vmem] * 5 + [hbm, vmem],
            out_specs=[vmem] * 2,
            scratch_shapes=[slot, pltpu.SemaphoreType.DMA],
            compiler_params=limit,
            cost_estimate=cost(2),
        )(meta, *[docs[mask] for mask in order], weight, params, *halves)
    send = pl.pallas_call(
        lambda *refs: last_kernel(masks, orders, *refs),
        out_shape=shape((devices, (1 + BLK_DEV) * SLOT_ROWS, TILE), jnp.bfloat16),
        in_specs=[smem] * 2 + [vmem] * 5 + [hbm] + [vmem] * (2 + len(best)),
        out_specs=vmem,
        scratch_shapes=[
            pltpu.VMEM((devices * (1 + BLK_DEV) * SLOT_ROWS, TILE), jnp.float32),
            slot,
            pltpu.SemaphoreType.DMA,
        ],
        compiler_params=limit,
        cost_estimate=cost(2),
    )(
        where,
        meta,
        meta,
        *[docs[mask] for mask in orders[-1]],
        weight,
        params,
        *halves,
        decoder_bias.reshape(-1, TILE),
        *best,
    )
    got = lax.all_to_all(send, "doc", split_axis=0, concat_axis=0, tiled=True)
    got = got.reshape(chips, 2, 1 + BLK_DEV, SLOT_ROWS, TILE)[:, :, :, :tiles]
    whole = jnp.swapaxes(jnp.maximum(got[:, 0], got[:, 1]), 0, 1).reshape(1 + BLK_DEV, -1)
    return (whole[:1], whole[1:])


def tokens_move(mesh):
    return mesh.shape["term"] == 1 and mesh.shape["doc"] == 16


def solution(mesh):
    placed = (
        P(("groups", "doc"), None),
        P(("groups", "doc")),
        P("doc", "term"),
        P(),
        P(),
        P(),
        P("term", None, "doc"),
        P("term"),
        P("term", ("groups", "doc"), None),
        P("term", ("groups", "doc"), None, None),
        P("term", ("groups", "doc"), None),
    )

    def local(*args):
        pair = 2 * args[6].shape[2]
        tiles = pair * (mesh.shape["doc"] // 2) // TILE
        fits = pair % TILE == 0 and tiles < TILE and pair // TILE <= SLOT_ROWS
        if tokens_move(mesh) and args[1].shape[0] == 1 and fits:
            return move_tokens(*args)
        return move_weights(*args)

    return jax.shard_map(
        local,
        mesh=mesh,
        in_specs=placed,
        out_specs=(P(("groups", "doc"), "term"), P(("groups", "doc"), "term")),
        check_vma=False,
    )
```

```python
import jax
import jax.numpy as jnp
from jax import lax
from jax.experimental import pallas as pl
from jax.experimental.pallas import tpu as pltpu
from jax.sharding import PartitionSpec as P

TILE = 128
BLK_DEV = 2
SLOT_ROWS = 16


def layer_norm(activated, norm_gain, norm_bias):
    values = activated.astype(jnp.float32)
    centre = jnp.mean(values, axis=-1, keepdims=True)
    centred = values - centre
    spread = jnp.mean(centred * centred, axis=-1, keepdims=True)
    return (centred * lax.rsqrt(spread + 1e-05) * norm_gain + norm_bias).astype(jnp.bfloat16)


def pool_docs(logits, keep):
    docs_here = keep.shape[0]
    saturated = jnp.log1p(jnp.maximum(logits, 0.0)).reshape(
        docs_here, keep.shape[1], logits.shape[1]
    )
    return jnp.max(jnp.where(keep[:, :, None], saturated, 0.0), axis=1)


def move_weights(
    hidden_states,
    doc_lengths,
    transform_weight,
    transform_bias,
    norm_gain,
    norm_bias,
    decoder_weight,
    decoder_bias,
    tile_ids,
    owner_ids,
    block_slots,
):
    tok_rows = hidden_states.shape[0]
    docs_here = doc_lengths.shape[0]
    seq_len = tok_rows // docs_here
    cols = transform_weight.shape[1]
    pre_half = jnp.dot(
        hidden_states,
        lax.all_gather(transform_weight, "doc", axis=0, tiled=True),
        preferred_element_type=jnp.float32,
    )
    bias_half = lax.dynamic_slice_in_dim(transform_bias, lax.axis_index("term") * cols, cols, 0)
    act_half = jax.nn.gelu(pre_half + bias_half, approximate=False).astype(jnp.bfloat16)
    activated = lax.all_gather(act_half, "term", axis=1, tiled=True)
    normed = layer_norm(activated, norm_gain, norm_bias)
    keep = jnp.arange(seq_len, dtype=jnp.int32)[None, :] < doc_lengths[:, None]
    logits = jnp.dot(
        normed,
        lax.all_gather(decoder_weight, "doc", axis=2, tiled=True)[0],
        preferred_element_type=jnp.float32,
    )
    logits = logits + decoder_bias
    impacts = pool_docs(logits, keep).astype(jnp.bfloat16)
    tiles_t = impacts.shape[1] // TILE
    slots_total = BLK_DEV * tiles_t
    tiles = impacts.reshape(docs_here * tiles_t, TILE)
    chosen = tile_ids[0]
    doc_index = jnp.arange(docs_here, dtype=jnp.int32)[:, None]
    posted = tiles[(doc_index * tiles_t + chosen).reshape(-1)]
    owners = owner_ids[0, :, :, 0].reshape(-1)
    target = block_slots[0].reshape(-1) * tiles_t + chosen.reshape(-1)
    owner_count = lax.axis_size("doc")
    capacity = max(2, 2 * posted.shape[0] // owner_count)
    onehot = (owners[:, None] == jnp.arange(owner_count, dtype=jnp.int32)[None, :]).astype(
        jnp.int32
    )
    before = jnp.cumsum(onehot, axis=0) - onehot
    position = jnp.sum(before * onehot, axis=1)
    dest = owners * capacity + position
    outgoing = jnp.zeros((owner_count * capacity, TILE), jnp.bfloat16).at[dest].set(posted)
    out_tags = jnp.full((owner_count * capacity,), slots_total, jnp.int32).at[dest].set(target)
    got_vals, got_tags = (
        lax.all_to_all(
            outgoing.reshape(owner_count, capacity, TILE),
            "doc",
            split_axis=0,
            concat_axis=0,
            tiled=True,
        ),
        lax.all_to_all(
            out_tags.reshape(owner_count, capacity), "doc", split_axis=0, concat_axis=0, tiled=True
        ),
    )
    got_vals = got_vals.reshape(-1, TILE)
    local_tags = got_tags.reshape(-1)
    summary = jnp.zeros((slots_total, TILE), jnp.bfloat16).at[local_tags].max(got_vals, mode="drop")
    return (impacts, summary.reshape(BLK_DEV, tiles_t * TILE))


def dot_t(left, right):
    return lax.dot_general(
        left, right, (((1,), (1,)), ((), ())), preferred_element_type=jnp.float32
    )


def masked(ref, length):
    here = ref[...]
    keep = lax.broadcasted_iota(jnp.int32, here.shape, 0).astype(jnp.float32) < length
    first = jnp.broadcast_to(here[0:1, :].astype(jnp.float32), here.shape).astype(here.dtype)
    return jnp.where(keep, here, first)


def normed_rows(docs, lengths, weight, params):
    rows = jnp.concatenate([masked(ref, length) for ref, length in zip(docs, lengths)], axis=0)
    pre = jnp.dot(rows, weight[...], preferred_element_type=jnp.float32) + params[0:1, :]
    act = 0.5 * pre * (1.0 + lax.erf(pre * (0.5**0.5)))
    return layer_norm(act.astype(jnp.bfloat16), params[1:2, :], params[2:3, :])


def tops_of(normed, w_ref, count):
    logits = dot_t(normed, w_ref[...])
    seq = normed.shape[0] // count
    return [
        jnp.max(logits[j * seq : (j + 1) * seq], axis=0, keepdims=True) for j in range(count)
    ]


def start_kernel(tiles_ref, owners_ref, slots_ref, length_ref, *refs):
    weight_ref, vectors, (out_ref, rows_ref, kept, sems) = refs[0], refs[1:4], refs[4:]
    rows, width = weight_ref.shape
    copies = [fetch(weight_ref, out_ref.at[:, pl.ds(0, width)], sems.at[0])]
    for k, ref in enumerate(vectors):
        copies.append(fetch(ref, kept.at[pl.ds(k * width, width)], sems.at[1 + k]))
    lane = lax.broadcasted_iota(jnp.int32, (rows, TILE), 1)
    table = jnp.where(lane == TILE - 1, length_ref[0], -1)
    devices = lax.axis_size("doc")
    for k in range(tiles_ref.shape[2]):
        block = slots_ref[0, 0, k] * devices + owners_ref[0, 0, k]
        table = jnp.where(lane == tiles_ref[0, 0, k], block, table)
    out_ref[:, width:] = table.astype(jnp.float32).astype(jnp.bfloat16)
    for copy in copies:
        copy.wait()
    for k in range(len(vectors)):
        rows_ref[k : k + 1, :] = kept[pl.ds(k * width, width)][None, :]


def pile_kernel(*refs):
    at = 0
    for ref in refs[:-1]:
        refs[-1][at : at + ref.shape[0], :] = ref[...]
        at += ref.shape[0]


def pack_kernel(*refs):
    arrays, out_ref, meta_ref = refs[:-2], refs[-2], refs[-1]
    rows, width = arrays[0].shape[0], out_ref.shape[1]
    row = lax.broadcasted_iota(jnp.int32, meta_ref.shape, 0)
    tables = jnp.zeros(meta_ref.shape, jnp.float32)
    k = 0
    for ref in arrays:
        for first in range(0, ref.shape[0], rows):
            out_ref[k * rows : (k + 1) * rows, :] = ref[first : first + rows, 0:width]
            table = ref[first : first + SLOT_ROWS, width:].astype(jnp.float32)
            tables = jnp.where(row == k, table[0 : meta_ref.shape[0]], tables)
            k += 1
    meta_ref[...] = tables.astype(jnp.int32)


def fetch(ref, slot, sem):
    copy = pltpu.make_async_copy(ref, slot, sem)
    copy.start()
    return copy


def length_of(meta_ref, k):
    return meta_ref[k : k + 1, TILE - 1 : TILE].astype(jnp.float32)


def first_kernel(masks, order, *refs):
    (me_ref, meta_ref), refs = refs[:2], refs[2:]
    docs, refs = refs[: len(order)], refs[len(order) :]
    packed, refs = refs[:2], refs[2:]
    params, mine_ref, theirs_ref, refs = refs[0], refs[1], refs[2], refs[3:]
    best_refs, weight, mine, late, sems = refs[:2], refs[2], *refs[3:]
    mine_copy = fetch(mine_ref, mine, sems.at[0])
    late_copies = [fetch(docs[k - 2], late.at[k], sems.at[1 + k]) for k in range(2)]
    me = me_ref[0]
    core = me % 2
    rows = weight.shape[0] // (2 * len(masks))
    for k, mask in enumerate(masks):
        chip = (me // 2) ^ mask
        block = slice(k * rows, (k + 1) * rows)
        at = pl.multiple_of((2 * chip + core) * rows, SLOT_ROWS)
        weight[pl.ds(at, rows), :] = packed[0][block, :]
        at = pl.multiple_of((2 * chip + 1 - core) * rows, SLOT_ROWS)
        weight[pl.ds(at, rows), :] = packed[1][block, :]
    docs = [*docs[:-2], late.at[0], late.at[1]]
    for first in range(0, len(order), 2):
        if first + 2 == len(order):
            for copy in late_copies:
                copy.wait()
        lengths = [length_of(meta_ref, masks.index(m)) for m in order[first : first + 2]]
        normed = normed_rows(docs[first : first + 2], lengths, weight, params)
        if first == 0:
            mine_copy.wait()
        for w_ref, best in zip((mine, theirs_ref), best_refs):
            for j, top in enumerate(tops_of(normed, w_ref, 2)):
                best[first + j : first + j + 1, :] = top


def next_kernel(masks, order, *refs):
    meta_ref, refs = refs[0], refs[1:]
    docs, weight, params, refs = refs[:2], refs[2], refs[3], refs[4:]
    mine_ref, theirs_ref, best_refs, mine, sem = refs[0], refs[1], refs[2:4], *refs[4:]
    copy = fetch(mine_ref, mine, sem)
    lengths = [length_of(meta_ref, masks.index(m)) for m in order]
    normed = normed_rows(docs, lengths, weight, params)
    copy.wait()
    for w_ref, best in zip((mine, theirs_ref), best_refs):
        for j, top in enumerate(tops_of(normed, w_ref, 2)):
            best[j : j + 1, :] = top


def last_kernel(masks, orders, *refs):
    me_ref, table_ref, meta_ref, refs = refs[0], refs[1], refs[2], refs[3:]
    docs, weight, params, refs = refs[:2], refs[2], refs[3], refs[4:]
    mine_ref, theirs_ref, dbias_ref, refs = refs[0], refs[1], refs[2], refs[3:]
    counts = [len(order) for order in orders[:-1]]
    earlier, refs = refs[: 2 * len(counts)], refs[2 * len(counts) :]
    out_ref, send, mine, sem = refs
    copy = fetch(mine_ref, mine, sem)
    me = me_ref[0]
    core, chip = me % 2, me // 2
    devices = 2 * len(masks)
    tiles = 2 * mine_ref.shape[0] // TILE
    lengths = [length_of(meta_ref, masks.index(m)) for m in orders[-1]]
    normed = normed_rows(docs, lengths, weight, params)
    found = []
    copy.wait()
    for k, w_ref in enumerate((mine, theirs_ref)):
        parts = [earlier[2 * n + k][0:count, :] for n, count in enumerate(counts)]
        found.append(jnp.concatenate([*parts, *tops_of(normed, w_ref, 2)], axis=0))
    low = jnp.where(core == 0, found[0], found[1])
    high = jnp.where(core == 0, found[1], found[0])
    logits = jnp.concatenate([low, high], axis=1)
    order = [mask for group in orders for mask in group]
    docs_at = [me ^ (2 * mask) for mask in order]
    bias = dbias_ref[...]
    bias = pltpu.roll(bias, bias.shape[0] - chip * tiles, 0)
    send[...] = jnp.zeros(send.shape, jnp.float32)
    stride = out_ref.shape[1]
    target = lax.broadcasted_iota(jnp.int32, (BLK_DEV * devices, TILE), 0)
    for t in range(tiles):
        lanes = slice(t * TILE, (t + 1) * TILE)
        impacts = jnp.log1p(jnp.maximum(logits[:, lanes] + bias[t : t + 1, :], 0.0))
        impacts = impacts.astype(jnp.bfloat16).astype(jnp.float32)
        blocks = jnp.zeros((BLK_DEV * devices, TILE), jnp.float32)
        for n, mask in enumerate(order):
            row = impacts[n : n + 1, :]
            send[pl.ds(docs_at[n] * stride + t, 1), :] = row
            block = table_ref[masks.index(mask), chip * tiles + t]
            blocks = jnp.maximum(blocks, jnp.where(target == block, row, 0.0))
        for s in range(BLK_DEV):
            send[pl.ds((1 + s) * SLOT_ROWS + t, devices, stride=stride), :] = blocks[
                s * devices : (s + 1) * devices
            ]
    out_ref[...] = send[...].astype(jnp.bfloat16).reshape(out_ref.shape)


def move_tokens(
    hidden_states,
    doc_lengths,
    transform_weight,
    transform_bias,
    norm_gain,
    norm_bias,
    decoder_weight,
    decoder_bias,
    tile_ids,
    owner_ids,
    block_slots,
):
    devices = lax.axis_size("doc")
    chips = devices // 2
    seq, width = hidden_states.shape
    rows = transform_weight.shape[0]
    half = decoder_weight.shape[2]
    tiles = 2 * half // TILE
    me = lax.axis_index("doc").astype(jnp.int32)

    def cross(value, mask):
        return lax.ppermute(value, "doc", [(i, i ^ (2 * mask)) for i in range(devices)])

    def swap(value):
        return lax.ppermute(value, "doc", [(i, i ^ 1) for i in range(devices)])

    smem = pl.BlockSpec(memory_space=pltpu.SMEM)
    vmem = pl.BlockSpec(memory_space=pltpu.VMEM)
    hbm = pl.BlockSpec(memory_space=pltpu.HBM)

    def stay(value):
        return pltpu.with_memory_space_constraint(value, pltpu.HBM)

    limit = pltpu.CompilerParams(vmem_limit_bytes=24 * 1024 * 1024)

    def cost(docs):
        return pl.CostEstimate(
            flops=2 * docs * seq * width * (width + 2 * half),
            bytes_accessed=1024 * 1024,
            transcendentals=docs * seq * width,
        )

    def shape(dims, dtype):
        return jax.ShapeDtypeStruct(dims, dtype)

    def after(value, *done):
        return lax.optimization_barrier((value, *done))[0]

    block, params = pl.pallas_call(
        start_kernel,
        out_shape=[
            shape((rows, width + TILE), jnp.bfloat16),
            shape((8, width), jnp.float32),
        ],
        in_specs=[smem] * 4 + [hbm] * 4,
        out_specs=[vmem] * 2,
        scratch_shapes=[
            pltpu.VMEM((3 * width,), jnp.float32),
            pltpu.SemaphoreType.DMA((4,)),
        ],
        compiler_params=limit,
    )(
        stay(tile_ids),
        stay(owner_ids[..., 0]),
        stay(block_slots),
        doc_lengths,
        stay(transform_weight),
        stay(transform_bias),
        stay(norm_gain),
        stay(norm_bias),
    )
    def pile(*values):
        total = sum(value.shape[0] for value in values)
        return pl.pallas_call(
            pile_kernel,
            out_shape=shape((total, values[0].shape[1]), values[0].dtype),
            in_specs=[vmem] * len(values),
            out_specs=vmem,
            compiler_params=limit,
        )(*values)

    block_6 = cross(block, 6)
    block_2 = cross(block, 2)
    docs = {0: hidden_states, 1: cross(hidden_states, 1), 2: cross(hidden_states, 2)}
    near_pile = cross(pile(block, block_2), 1)
    block_4 = cross(block_6, 2)
    docs[6] = cross(after(hidden_states, block_6), 6)
    docs[3] = cross(docs[2], 1)
    far_pile = cross(pile(block_6, after(block_4, docs[1], docs[2])), 1)
    docs[4] = cross(docs[6], 2)
    docs[7] = cross(docs[6], 1)
    docs[5] = cross(docs[4], 1)
    weight_rows = jnp.swapaxes(decoder_weight[0], 0, 1)
    theirs = swap(after(weight_rows, block_6, block_2))
    masks = [0, 2, 6, 4, 1, 3, 7, 5]
    packed, meta = pl.pallas_call(
        pack_kernel,
        out_shape=[
            shape((chips * rows, width), jnp.bfloat16),
            shape((chips, TILE), jnp.int32),
        ],
        in_specs=[vmem] * 6,
        out_specs=[vmem] * 2,
        compiler_params=limit,
    )(after(block, docs[6]), block_2, block_6, block_4, near_pile, far_pile)
    other_packed = swap(after(packed, docs[3], docs[4]))

    orders = [[2, 3, 1, 0], [6, 7], [4, 5]]
    where = me[None]
    halves = (stay(weight_rows), theirs)
    slot = pltpu.VMEM((half, width), jnp.bfloat16)
    best_shape = shape((8, half), jnp.float32)
    *best, weight = pl.pallas_call(
        lambda *refs: first_kernel(masks, orders[0], *refs),
        out_shape=[best_shape, best_shape, shape((width, width), jnp.bfloat16)],
        in_specs=[smem] + [vmem] * 3 + [hbm] * 2 + [vmem] * 3 + [hbm, vmem],
        out_specs=[vmem] * 3,
        scratch_shapes=[
            slot,
            pltpu.VMEM((2, seq, width), jnp.bfloat16),
            pltpu.SemaphoreType.DMA((3,)),
        ],
        compiler_params=limit,
        cost_estimate=cost(len(orders[0])),
    )(where, meta, docs[2], docs[3], stay(docs[1]), stay(hidden_states), packed, other_packed, params, *halves)
    for order in orders[1:-1]:
        best += pl.pallas_call(
            lambda *refs, order=order: next_kernel(masks, order, *refs),
            out_shape=[best_shape] * 2,
            in_specs=[vmem] * 5 + [hbm, vmem],
            out_specs=[vmem] * 2,
            scratch_shapes=[slot, pltpu.SemaphoreType.DMA],
            compiler_params=limit,
            cost_estimate=cost(2),
        )(meta, *[docs[mask] for mask in order], weight, params, *halves)
    send = pl.pallas_call(
        lambda *refs: last_kernel(masks, orders, *refs),
        out_shape=shape((devices, (1 + BLK_DEV) * SLOT_ROWS, TILE), jnp.bfloat16),
        in_specs=[smem] * 2 + [vmem] * 5 + [hbm] + [vmem] * (2 + len(best)),
        out_specs=vmem,
        scratch_shapes=[
            pltpu.VMEM((devices * (1 + BLK_DEV) * SLOT_ROWS, TILE), jnp.float32),
            slot,
            pltpu.SemaphoreType.DMA,
        ],
        compiler_params=limit,
        cost_estimate=cost(2),
    )(
        where,
        meta,
        meta,
        *[docs[mask] for mask in orders[-1]],
        weight,
        params,
        *halves,
        decoder_bias.reshape(-1, TILE),
        *best,
    )
    got = lax.all_to_all(send, "doc", split_axis=0, concat_axis=0, tiled=True)
    got = got.reshape(chips, 2, 1 + BLK_DEV, SLOT_ROWS, TILE)[:, :, :, :tiles]
    whole = jnp.swapaxes(jnp.maximum(got[:, 0], got[:, 1]), 0, 1).reshape(1 + BLK_DEV, -1)
    return (whole[:1], whole[1:])


def tokens_move(mesh):
    return mesh.shape["term"] == 1 and mesh.shape["doc"] == 16


def solution(mesh):
    placed = (
        P(("groups", "doc"), None),
        P(("groups", "doc")),
        P("doc", "term"),
        P(),
        P(),
        P(),
        P("term", None, "doc"),
        P("term"),
        P("term", ("groups", "doc"), None),
        P("term", ("groups", "doc"), None, None),
        P("term", ("groups", "doc"), None),
    )

    def local(*args):
        pair = 2 * args[6].shape[2]
        tiles = pair * (mesh.shape["doc"] // 2) // TILE
        fits = pair % TILE == 0 and tiles < TILE and pair // TILE <= SLOT_ROWS
        if tokens_move(mesh) and args[1].shape[0] == 1 and fits:
            return move_tokens(*args)
        return move_weights(*args)

    return jax.shard_map(
        local,
        mesh=mesh,
        in_specs=placed,
        out_specs=(P(("groups", "doc"), "term"), P(("groups", "doc"), "term")),
        check_vma=False,
    )
```

```python
import jax
import jax.numpy as jnp
from jax import lax
from jax.experimental import pallas as pl
from jax.experimental.pallas import tpu as pltpu
from jax.sharding import PartitionSpec as P

TILE = 128
BLK_DEV = 2
SLOT_ROWS = 16


def layer_norm(activated, norm_gain, norm_bias):
    values = activated.astype(jnp.float32)
    centre = jnp.mean(values, axis=-1, keepdims=True)
    centred = values - centre
    spread = jnp.mean(centred * centred, axis=-1, keepdims=True)
    return (centred * lax.rsqrt(spread + 1e-05) * norm_gain + norm_bias).astype(jnp.bfloat16)


def pool_docs(logits, keep):
    docs_here = keep.shape[0]
    saturated = jnp.log1p(jnp.maximum(logits, 0.0)).reshape(
        docs_here, keep.shape[1], logits.shape[1]
    )
    return jnp.max(jnp.where(keep[:, :, None], saturated, 0.0), axis=1)


def move_weights(
    hidden_states,
    doc_lengths,
    transform_weight,
    transform_bias,
    norm_gain,
    norm_bias,
    decoder_weight,
    decoder_bias,
    tile_ids,
    owner_ids,
    block_slots,
):
    tok_rows = hidden_states.shape[0]
    docs_here = doc_lengths.shape[0]
    seq_len = tok_rows // docs_here
    cols = transform_weight.shape[1]
    pre_half = jnp.dot(
        hidden_states,
        lax.all_gather(transform_weight, "doc", axis=0, tiled=True),
        preferred_element_type=jnp.float32,
    )
    bias_half = lax.dynamic_slice_in_dim(transform_bias, lax.axis_index("term") * cols, cols, 0)
    act_half = jax.nn.gelu(pre_half + bias_half, approximate=False).astype(jnp.bfloat16)
    activated = lax.all_gather(act_half, "term", axis=1, tiled=True)
    normed = layer_norm(activated, norm_gain, norm_bias)
    keep = jnp.arange(seq_len, dtype=jnp.int32)[None, :] < doc_lengths[:, None]
    logits = jnp.dot(
        normed,
        lax.all_gather(decoder_weight, "doc", axis=2, tiled=True)[0],
        preferred_element_type=jnp.float32,
    )
    logits = logits + decoder_bias
    impacts = pool_docs(logits, keep).astype(jnp.bfloat16)
    tiles_t = impacts.shape[1] // TILE
    slots_total = BLK_DEV * tiles_t
    tiles = impacts.reshape(docs_here * tiles_t, TILE)
    chosen = tile_ids[0]
    doc_index = jnp.arange(docs_here, dtype=jnp.int32)[:, None]
    posted = tiles[(doc_index * tiles_t + chosen).reshape(-1)]
    owners = owner_ids[0, :, :, 0].reshape(-1)
    target = block_slots[0].reshape(-1) * tiles_t + chosen.reshape(-1)
    owner_count = lax.axis_size("doc")
    capacity = max(2, 2 * posted.shape[0] // owner_count)
    onehot = (owners[:, None] == jnp.arange(owner_count, dtype=jnp.int32)[None, :]).astype(
        jnp.int32
    )
    before = jnp.cumsum(onehot, axis=0) - onehot
    position = jnp.sum(before * onehot, axis=1)
    dest = owners * capacity + position
    outgoing = jnp.zeros((owner_count * capacity, TILE), jnp.bfloat16).at[dest].set(posted)
    out_tags = jnp.full((owner_count * capacity,), slots_total, jnp.int32).at[dest].set(target)
    got_vals, got_tags = (
        lax.all_to_all(
            outgoing.reshape(owner_count, capacity, TILE),
            "doc",
            split_axis=0,
            concat_axis=0,
            tiled=True,
        ),
        lax.all_to_all(
            out_tags.reshape(owner_count, capacity), "doc", split_axis=0, concat_axis=0, tiled=True
        ),
    )
    got_vals = got_vals.reshape(-1, TILE)
    local_tags = got_tags.reshape(-1)
    summary = jnp.zeros((slots_total, TILE), jnp.bfloat16).at[local_tags].max(got_vals, mode="drop")
    return (impacts, summary.reshape(BLK_DEV, tiles_t * TILE))


def dot_t(left, right):
    return lax.dot_general(
        left, right, (((1,), (1,)), ((), ())), preferred_element_type=jnp.float32
    )


def masked(ref, length):
    here = ref[...]
    keep = lax.broadcasted_iota(jnp.int32, here.shape, 0).astype(jnp.float32) < length
    first = jnp.broadcast_to(here[0:1, :].astype(jnp.float32), here.shape).astype(here.dtype)
    return jnp.where(keep, here, first)


def normed_rows(docs, lengths, weight, params):
    rows = jnp.concatenate([masked(ref, length) for ref, length in zip(docs, lengths)], axis=0)
    pre = jnp.dot(rows, weight[...], preferred_element_type=jnp.float32) + params[0:1, :]
    act = 0.5 * pre * (1.0 + lax.erf(pre * (0.5**0.5)))
    return layer_norm(act.astype(jnp.bfloat16), params[1:2, :], params[2:3, :])


def tops_of(normed, w_ref, count):
    logits = dot_t(normed, w_ref[...])
    seq = normed.shape[0] // count
    return [
        jnp.max(logits[j * seq : (j + 1) * seq], axis=0, keepdims=True) for j in range(count)
    ]


def start_kernel(tiles_ref, owners_ref, slots_ref, length_ref, *refs):
    weight_ref, vectors, (out_ref, rows_ref, kept, sems) = refs[0], refs[1:4], refs[4:]
    rows, width = weight_ref.shape
    copies = [fetch(weight_ref, out_ref.at[:, pl.ds(0, width)], sems.at[0])]
    for k, ref in enumerate(vectors):
        copies.append(fetch(ref, kept.at[pl.ds(k * width, width)], sems.at[1 + k]))
    lane = lax.broadcasted_iota(jnp.int32, (rows, TILE), 1)
    table = jnp.where(lane == TILE - 1, length_ref[0], -1)
    devices = lax.axis_size("doc")
    for k in range(tiles_ref.shape[2]):
        block = slots_ref[0, 0, k] * devices + owners_ref[0, 0, k]
        table = jnp.where(lane == tiles_ref[0, 0, k], block, table)
    out_ref[:, width:] = table.astype(jnp.float32).astype(jnp.bfloat16)
    for copy in copies:
        copy.wait()
    for k in range(len(vectors)):
        rows_ref[k : k + 1, :] = kept[pl.ds(k * width, width)][None, :]


def pile_kernel(*refs):
    at = 0
    for ref in refs[:-1]:
        refs[-1][at : at + ref.shape[0], :] = ref[...]
        at += ref.shape[0]


def pack_kernel(*refs):
    arrays, out_ref, meta_ref = refs[:-2], refs[-2], refs[-1]
    rows, width = arrays[0].shape[0], out_ref.shape[1]
    row = lax.broadcasted_iota(jnp.int32, meta_ref.shape, 0)
    tables = jnp.zeros(meta_ref.shape, jnp.float32)
    k = 0
    for ref in arrays:
        for first in range(0, ref.shape[0], rows):
            out_ref[k * rows : (k + 1) * rows, :] = ref[first : first + rows, 0:width]
            table = ref[first : first + SLOT_ROWS, width:].astype(jnp.float32)
            tables = jnp.where(row == k, table[0 : meta_ref.shape[0]], tables)
            k += 1
    meta_ref[...] = tables.astype(jnp.int32)


def fetch(ref, slot, sem):
    copy = pltpu.make_async_copy(ref, slot, sem)
    copy.start()
    return copy


def length_of(meta_ref, k):
    return meta_ref[k : k + 1, TILE - 1 : TILE].astype(jnp.float32)


def first_kernel(masks, order, *refs):
    (me_ref, meta_ref), refs = refs[:2], refs[2:]
    docs, refs = refs[: len(order)], refs[len(order) :]
    packed, refs = refs[:2], refs[2:]
    params, mine_ref, theirs_ref, refs = refs[0], refs[1], refs[2], refs[3:]
    best_refs, weight, mine, late, sems = refs[:2], refs[2], refs[3], *refs[4:]
    mine_copy = fetch(mine_ref, mine, sems.at[0])
    late_copies = [fetch(docs[k - 2], late.at[k], sems.at[1 + k]) for k in range(2)]
    me = me_ref[0]
    core = me % 2
    rows = weight.shape[0] // (2 * len(masks))
    for k, mask in enumerate(masks):
        chip = (me // 2) ^ mask
        block = slice(k * rows, (k + 1) * rows)
        at = pl.multiple_of((2 * chip + core) * rows, SLOT_ROWS)
        weight[pl.ds(at, rows), :] = packed[0][block, :]
        at = pl.multiple_of((2 * chip + 1 - core) * rows, SLOT_ROWS)
        weight[pl.ds(at, rows), :] = packed[1][block, :]
    docs = [*docs[:-2], late.at[0], late.at[1]]
    for first in range(0, len(order), 2):
        if first + 2 == len(order):
            for copy in late_copies:
                copy.wait()
        lengths = [length_of(meta_ref, masks.index(m)) for m in order[first : first + 2]]
        normed = normed_rows(docs[first : first + 2], lengths, weight, params)
        if first == 0:
            mine_copy.wait()
        for w_ref, best in zip((mine, theirs_ref), best_refs):
            for j, top in enumerate(tops_of(normed, w_ref, 2)):
                best[first + j : first + j + 1, :] = top


def next_kernel(masks, order, *refs):
    meta_ref, refs = refs[0], refs[1:]
    docs, weight, params, refs = refs[:2], refs[2], refs[3], refs[4:]
    halves, best_refs = refs[:2], refs[2:]
    lengths = [length_of(meta_ref, masks.index(m)) for m in order]
    normed = normed_rows(docs, lengths, weight, params)
    for w_ref, best in zip(halves, best_refs):
        for j, top in enumerate(tops_of(normed, w_ref, 2)):
            best[j : j + 1, :] = top


def last_kernel(masks, orders, *refs):
    me_ref, table_ref, meta_ref, refs = refs[0], refs[1], refs[2], refs[3:]
    docs, weight, params, refs = refs[:2], refs[2], refs[3], refs[4:]
    halves, dbias_ref, refs = refs[:2], refs[2], refs[3:]
    counts = [len(order) for order in orders[:-1]]
    earlier, refs = refs[: 2 * len(counts)], refs[2 * len(counts) :]
    out_ref, send = refs
    me = me_ref[0]
    core, chip = me % 2, me // 2
    devices = 2 * len(masks)
    tiles = 2 * halves[0].shape[0] // TILE
    lengths = [length_of(meta_ref, masks.index(m)) for m in orders[-1]]
    normed = normed_rows(docs, lengths, weight, params)
    found = []
    for k, w_ref in enumerate(halves):
        parts = [earlier[2 * n + k][0:count, :] for n, count in enumerate(counts)]
        found.append(jnp.concatenate([*parts, *tops_of(normed, w_ref, 2)], axis=0))
    low = jnp.where(core == 0, found[0], found[1])
    high = jnp.where(core == 0, found[1], found[0])
    logits = jnp.concatenate([low, high], axis=1)
    order = [mask for group in orders for mask in group]
    docs_at = [me ^ (2 * mask) for mask in order]
    bias = dbias_ref[...]
    bias = pltpu.roll(bias, bias.shape[0] - chip * tiles, 0)
    send[...] = jnp.zeros(send.shape, jnp.float32)
    stride = out_ref.shape[1]
    target = lax.broadcasted_iota(jnp.int32, (BLK_DEV * devices, TILE), 0)
    for t in range(tiles):
        lanes = slice(t * TILE, (t + 1) * TILE)
        impacts = jnp.log1p(jnp.maximum(logits[:, lanes] + bias[t : t + 1, :], 0.0))
        impacts = impacts.astype(jnp.bfloat16).astype(jnp.float32)
        blocks = jnp.zeros((BLK_DEV * devices, TILE), jnp.float32)
        for n, mask in enumerate(order):
            row = impacts[n : n + 1, :]
            send[pl.ds(docs_at[n] * stride + t, 1), :] = row
            block = table_ref[masks.index(mask), chip * tiles + t]
            blocks = jnp.maximum(blocks, jnp.where(target == block, row, 0.0))
        for s in range(BLK_DEV):
            send[pl.ds((1 + s) * SLOT_ROWS + t, devices, stride=stride), :] = blocks[
                s * devices : (s + 1) * devices
            ]
    out_ref[...] = send[...].astype(jnp.bfloat16).reshape(out_ref.shape)


def move_tokens(
    hidden_states,
    doc_lengths,
    transform_weight,
    transform_bias,
    norm_gain,
    norm_bias,
    decoder_weight,
    decoder_bias,
    tile_ids,
    owner_ids,
    block_slots,
):
    devices = lax.axis_size("doc")
    chips = devices // 2
    seq, width = hidden_states.shape
    rows = transform_weight.shape[0]
    half = decoder_weight.shape[2]
    tiles = 2 * half // TILE
    me = lax.axis_index("doc").astype(jnp.int32)

    def cross(value, mask):
        return lax.ppermute(value, "doc", [(i, i ^ (2 * mask)) for i in range(devices)])

    def swap(value):
        return lax.ppermute(value, "doc", [(i, i ^ 1) for i in range(devices)])

    smem = pl.BlockSpec(memory_space=pltpu.SMEM)
    vmem = pl.BlockSpec(memory_space=pltpu.VMEM)
    hbm = pl.BlockSpec(memory_space=pltpu.HBM)

    def stay(value):
        return pltpu.with_memory_space_constraint(value, pltpu.HBM)

    limit = pltpu.CompilerParams(vmem_limit_bytes=24 * 1024 * 1024)

    def cost(docs):
        return pl.CostEstimate(
            flops=2 * docs * seq * width * (width + 2 * half),
            bytes_accessed=1024 * 1024,
            transcendentals=docs * seq * width,
        )

    def shape(dims, dtype):
        return jax.ShapeDtypeStruct(dims, dtype)

    def after(value, *done):
        return lax.optimization_barrier((value, *done))[0]

    block, params = pl.pallas_call(
        start_kernel,
        out_shape=[
            shape((rows, width + TILE), jnp.bfloat16),
            shape((8, width), jnp.float32),
        ],
        in_specs=[smem] * 4 + [hbm] * 4,
        out_specs=[vmem] * 2,
        scratch_shapes=[
            pltpu.VMEM((3 * width,), jnp.float32),
            pltpu.SemaphoreType.DMA((4,)),
        ],
        compiler_params=limit,
    )(
        stay(tile_ids),
        stay(owner_ids[..., 0]),
        stay(block_slots),
        doc_lengths,
        stay(transform_weight),
        stay(transform_bias),
        stay(norm_gain),
        stay(norm_bias),
    )
    def pile(*values):
        total = sum(value.shape[0] for value in values)
        return pl.pallas_call(
            pile_kernel,
            out_shape=shape((total, values[0].shape[1]), values[0].dtype),
            in_specs=[vmem] * len(values),
            out_specs=vmem,
            compiler_params=limit,
        )(*values)

    weight_rows = jnp.swapaxes(decoder_weight[0], 0, 1)
    theirs = swap(weight_rows)
    docs = {0: hidden_states, 1: cross(hidden_states, 1)}
    block_6 = cross(block, 6)
    block_2 = cross(block, 2)
    docs[6] = cross(hidden_states, 6)
    docs[2] = cross(hidden_states, 2)
    near_pile = cross(pile(block, block_2), 1)
    block_4 = cross(after(block_6, docs[1], theirs), 2)
    docs[4] = cross(docs[6], 2)
    docs[3] = cross(docs[2], 1)
    far_pile = cross(pile(block_6, after(block_4, near_pile)), 1)
    docs[7] = cross(docs[6], 1)
    docs[5] = cross(docs[4], 1)
    masks = [0, 2, 6, 4, 1, 3, 7, 5]
    packed, meta = pl.pallas_call(
        pack_kernel,
        out_shape=[
            shape((chips * rows, width), jnp.bfloat16),
            shape((chips, TILE), jnp.int32),
        ],
        in_specs=[vmem] * 6,
        out_specs=[vmem] * 2,
        compiler_params=limit,
    )(after(block, docs[4]), block_2, block_6, block_4, near_pile, far_pile)
    other_packed = swap(after(packed, docs[3]))

    orders = [[2, 3, 1, 0], [6, 7], [4, 5]]
    where = me[None]
    best_shape = shape((8, half), jnp.float32)
    *best, weight, mine = pl.pallas_call(
        lambda *refs: first_kernel(masks, orders[0], *refs),
        out_shape=[
            best_shape,
            best_shape,
            shape((width, width), jnp.bfloat16),
            shape((half, width), jnp.bfloat16),
        ],
        in_specs=[smem] + [vmem] * 3 + [hbm] * 2 + [vmem] * 3 + [hbm, vmem],
        out_specs=[vmem] * 4,
        scratch_shapes=[
            pltpu.VMEM((2, seq, width), jnp.bfloat16),
            pltpu.SemaphoreType.DMA((3,)),
        ],
        compiler_params=limit,
        cost_estimate=cost(len(orders[0])),
    )(
        where,
        meta,
        docs[2],
        docs[3],
        stay(docs[1]),
        stay(hidden_states),
        packed,
        other_packed,
        params,
        stay(weight_rows),
        theirs,
    )
    for order in orders[1:-1]:
        best += pl.pallas_call(
            lambda *refs, order=order: next_kernel(masks, order, *refs),
            out_shape=[best_shape] * 2,
            in_specs=[vmem] * 7,
            out_specs=[vmem] * 2,
            compiler_params=limit,
            cost_estimate=cost(2),
        )(meta, *[docs[mask] for mask in order], weight, params, mine, theirs)
    send = pl.pallas_call(
        lambda *refs: last_kernel(masks, orders, *refs),
        out_shape=shape((devices, (1 + BLK_DEV) * SLOT_ROWS, TILE), jnp.bfloat16),
        in_specs=[smem] * 2 + [vmem] * (8 + len(best)),
        out_specs=vmem,
        scratch_shapes=[
            pltpu.VMEM((devices * (1 + BLK_DEV) * SLOT_ROWS, TILE), jnp.float32),
        ],
        compiler_params=limit,
        cost_estimate=cost(2),
    )(
        where,
        meta,
        meta,
        *[docs[mask] for mask in orders[-1]],
        weight,
        params,
        mine,
        theirs,
        decoder_bias.reshape(-1, TILE),
        *best,
    )
    got = lax.all_to_all(send, "doc", split_axis=0, concat_axis=0, tiled=True)
    got = got.reshape(chips, 2, 1 + BLK_DEV, SLOT_ROWS, TILE)[:, :, :, :tiles]
    whole = jnp.swapaxes(jnp.maximum(got[:, 0], got[:, 1]), 0, 1).reshape(1 + BLK_DEV, -1)
    return (whole[:1], whole[1:])


def tokens_move(mesh):
    return mesh.shape["term"] == 1 and mesh.shape["doc"] == 16


def solution(mesh):
    placed = (
        P(("groups", "doc"), None),
        P(("groups", "doc")),
        P("doc", "term"),
        P(),
        P(),
        P(),
        P("term", None, "doc"),
        P("term"),
        P("term", ("groups", "doc"), None),
        P("term", ("groups", "doc"), None, None),
        P("term", ("groups", "doc"), None),
    )

    def local(*args):
        pair = 2 * args[6].shape[2]
        tiles = pair * (mesh.shape["doc"] // 2) // TILE
        fits = pair % TILE == 0 and tiles < TILE and pair // TILE <= SLOT_ROWS
        if tokens_move(mesh) and args[1].shape[0] == 1 and fits:
            return move_tokens(*args)
        return move_weights(*args)

    return jax.shard_map(
        local,
        mesh=mesh,
        in_specs=placed,
        out_specs=(P(("groups", "doc"), "term"), P(("groups", "doc"), "term")),
        check_vma=False,
    )
```

```python
import jax
import jax.numpy as jnp
from jax import lax
from jax.experimental import pallas as pl
from jax.experimental.pallas import tpu as pltpu
from jax.sharding import PartitionSpec as P

TILE = 128
BLK_DEV = 2
SLOT_ROWS = 16


def layer_norm(activated, norm_gain, norm_bias):
    values = activated.astype(jnp.float32)
    centre = jnp.mean(values, axis=-1, keepdims=True)
    centred = values - centre
    spread = jnp.mean(centred * centred, axis=-1, keepdims=True)
    return (centred * lax.rsqrt(spread + 1e-05) * norm_gain + norm_bias).astype(jnp.bfloat16)


def pool_docs(logits, keep):
    docs_here = keep.shape[0]
    saturated = jnp.log1p(jnp.maximum(logits, 0.0)).reshape(
        docs_here, keep.shape[1], logits.shape[1]
    )
    return jnp.max(jnp.where(keep[:, :, None], saturated, 0.0), axis=1)


def move_weights(
    hidden_states,
    doc_lengths,
    transform_weight,
    transform_bias,
    norm_gain,
    norm_bias,
    decoder_weight,
    decoder_bias,
    tile_ids,
    owner_ids,
    block_slots,
):
    tok_rows = hidden_states.shape[0]
    docs_here = doc_lengths.shape[0]
    seq_len = tok_rows // docs_here
    cols = transform_weight.shape[1]
    pre_half = jnp.dot(
        hidden_states,
        lax.all_gather(transform_weight, "doc", axis=0, tiled=True),
        preferred_element_type=jnp.float32,
    )
    bias_half = lax.dynamic_slice_in_dim(transform_bias, lax.axis_index("term") * cols, cols, 0)
    act_half = jax.nn.gelu(pre_half + bias_half, approximate=False).astype(jnp.bfloat16)
    activated = lax.all_gather(act_half, "term", axis=1, tiled=True)
    normed = layer_norm(activated, norm_gain, norm_bias)
    keep = jnp.arange(seq_len, dtype=jnp.int32)[None, :] < doc_lengths[:, None]
    logits = jnp.dot(
        normed,
        lax.all_gather(decoder_weight, "doc", axis=2, tiled=True)[0],
        preferred_element_type=jnp.float32,
    )
    logits = logits + decoder_bias
    impacts = pool_docs(logits, keep).astype(jnp.bfloat16)
    tiles_t = impacts.shape[1] // TILE
    slots_total = BLK_DEV * tiles_t
    tiles = impacts.reshape(docs_here * tiles_t, TILE)
    chosen = tile_ids[0]
    doc_index = jnp.arange(docs_here, dtype=jnp.int32)[:, None]
    posted = tiles[(doc_index * tiles_t + chosen).reshape(-1)]
    owners = owner_ids[0, :, :, 0].reshape(-1)
    target = block_slots[0].reshape(-1) * tiles_t + chosen.reshape(-1)
    owner_count = lax.axis_size("doc")
    capacity = max(2, 2 * posted.shape[0] // owner_count)
    onehot = (owners[:, None] == jnp.arange(owner_count, dtype=jnp.int32)[None, :]).astype(
        jnp.int32
    )
    before = jnp.cumsum(onehot, axis=0) - onehot
    position = jnp.sum(before * onehot, axis=1)
    dest = owners * capacity + position
    outgoing = jnp.zeros((owner_count * capacity, TILE), jnp.bfloat16).at[dest].set(posted)
    out_tags = jnp.full((owner_count * capacity,), slots_total, jnp.int32).at[dest].set(target)
    got_vals, got_tags = (
        lax.all_to_all(
            outgoing.reshape(owner_count, capacity, TILE),
            "doc",
            split_axis=0,
            concat_axis=0,
            tiled=True,
        ),
        lax.all_to_all(
            out_tags.reshape(owner_count, capacity), "doc", split_axis=0, concat_axis=0, tiled=True
        ),
    )
    got_vals = got_vals.reshape(-1, TILE)
    local_tags = got_tags.reshape(-1)
    summary = jnp.zeros((slots_total, TILE), jnp.bfloat16).at[local_tags].max(got_vals, mode="drop")
    return (impacts, summary.reshape(BLK_DEV, tiles_t * TILE))


def dot_t(left, right):
    return lax.dot_general(
        left, right, (((1,), (1,)), ((), ())), preferred_element_type=jnp.float32
    )


def masked(ref, seq, length):
    here = ref[0:seq, :]
    keep = lax.broadcasted_iota(jnp.int32, here.shape, 0).astype(jnp.float32) < length
    first = jnp.broadcast_to(here[0:1, :].astype(jnp.float32), here.shape).astype(here.dtype)
    return jnp.where(keep, here, first)


def normed_rows(docs, seq, lengths, weight, params):
    masks = [masked(ref, seq, length) for ref, length in zip(docs, lengths)]
    rows = jnp.concatenate(masks, axis=0)
    pre = jnp.dot(rows, weight[...], preferred_element_type=jnp.float32) + params[0:1, :]
    act = 0.5 * pre * (1.0 + lax.erf(pre * (0.5**0.5)))
    return layer_norm(act.astype(jnp.bfloat16), params[1:2, :], params[2:3, :])


def tops_of(normed, w_ref, count):
    logits = dot_t(normed, w_ref[...])
    seq = normed.shape[0] // count
    return [
        jnp.max(logits[j * seq : (j + 1) * seq], axis=0, keepdims=True) for j in range(count)
    ]


def start_kernel(tiles_ref, owners_ref, slots_ref, length_ref, *refs):
    hidden_ref, weight_ref, vectors = refs[0], refs[1], refs[2:5]
    load_ref, block_ref, rows_ref, kept, sems = refs[5:]
    seq, (rows, width) = hidden_ref.shape[0], weight_ref.shape
    copies = [
        fetch(weight_ref, block_ref.at[:, pl.ds(0, width)], sems.at[0]),
        fetch(weight_ref, load_ref.at[pl.ds(seq, rows), :], sems.at[1]),
        fetch(hidden_ref, load_ref.at[pl.ds(0, seq), :], sems.at[2]),
    ]
    for k, ref in enumerate(vectors):
        copies.append(fetch(ref, kept.at[pl.ds(k * width, width)], sems.at[3 + k]))
    lane = lax.broadcasted_iota(jnp.int32, (rows, TILE), 1)
    table = jnp.where(lane == TILE - 1, length_ref[0], -1)
    devices = lax.axis_size("doc")
    for k in range(tiles_ref.shape[2]):
        block = slots_ref[0, 0, k] * devices + owners_ref[0, 0, k]
        table = jnp.where(lane == tiles_ref[0, 0, k], block, table)
    table = table.astype(jnp.float32).astype(jnp.bfloat16)
    block_ref[:, width:] = table
    for first in range(0, width, TILE):
        load_ref[seq + rows :, first : first + TILE] = table[0:SLOT_ROWS]
    for copy in copies:
        copy.wait()
    for k in range(len(vectors)):
        rows_ref[k : k + 1, :] = kept[pl.ds(k * width, width)][None, :]


def pile_kernel(*refs):
    at = 0
    for ref in refs[:-1]:
        refs[-1][at : at + ref.shape[0], :] = ref[...]
        at += ref.shape[0]


def pack_kernel(seq, *refs):
    arrays, out_ref, meta_ref = refs[:-2], refs[-2], refs[-1]
    width = out_ref.shape[1]
    rows = out_ref.shape[0] // meta_ref.shape[0]
    row = lax.broadcasted_iota(jnp.int32, meta_ref.shape, 0)
    tables = jnp.zeros(meta_ref.shape, jnp.float32)
    k = 0
    for ref in arrays:
        if ref.shape[1] == width:
            parts = [(ref[seq : seq + rows, :], ref[seq + rows : seq + rows + SLOT_ROWS, 0:TILE])]
        else:
            parts = [
                (ref[first : first + rows, 0:width], ref[first : first + SLOT_ROWS, width:])
                for first in range(0, ref.shape[0], rows)
            ]
        for part, table in parts:
            out_ref[k * rows : (k + 1) * rows, :] = part
            tables = jnp.where(row == k, table.astype(jnp.float32)[0 : meta_ref.shape[0]], tables)
            k += 1
    meta_ref[...] = tables.astype(jnp.int32)


def fetch(ref, slot, sem):
    copy = pltpu.make_async_copy(ref, slot, sem)
    copy.start()
    return copy


def length_of(meta_ref, k):
    return meta_ref[k : k + 1, TILE - 1 : TILE].astype(jnp.float32)


def first_kernel(seq, masks, order, *refs):
    (me_ref, meta_ref), refs = refs[:2], refs[2:]
    docs, refs = refs[: len(order)], refs[len(order) :]
    packed, params, mine_ref, theirs_ref, refs = refs[:2], refs[2], refs[3], refs[4], refs[5:]
    best_mine, best_theirs, weight, mine, sem = refs
    copy = fetch(mine_ref, mine, sem)
    me = me_ref[0]
    core = me % 2
    rows = weight.shape[0] // (2 * len(masks))
    for k, mask in enumerate(masks):
        chip = (me // 2) ^ mask
        block = slice(k * rows, (k + 1) * rows)
        at = pl.multiple_of((2 * chip + core) * rows, SLOT_ROWS)
        weight[pl.ds(at, rows), :] = packed[0][block, :]
        at = pl.multiple_of((2 * chip + 1 - core) * rows, SLOT_ROWS)
        weight[pl.ds(at, rows), :] = packed[1][block, :]
    for first in range(0, len(order), 2):
        lengths = [length_of(meta_ref, masks.index(m)) for m in order[first : first + 2]]
        normed = normed_rows(docs[first : first + 2], seq, lengths, weight, params)
        for w_ref, best in ((theirs_ref, best_theirs), (mine, best_mine)):
            if first == 0 and w_ref is mine:
                copy.wait()
            for j, top in enumerate(tops_of(normed, w_ref, 2)):
                best[first + j : first + j + 1, :] = top


def next_kernel(seq, masks, order, *refs):
    meta_ref, refs = refs[0], refs[1:]
    docs, weight, params, refs = refs[:2], refs[2], refs[3], refs[4:]
    halves, best_refs = refs[:2], refs[2:]
    lengths = [length_of(meta_ref, masks.index(m)) for m in order]
    normed = normed_rows(docs, seq, lengths, weight, params)
    for w_ref, best in zip(halves, best_refs):
        for j, top in enumerate(tops_of(normed, w_ref, 2)):
            best[j : j + 1, :] = top


def last_kernel(seq, masks, orders, *refs):
    me_ref, table_ref, meta_ref, refs = refs[0], refs[1], refs[2], refs[3:]
    docs, weight, params, refs = refs[:2], refs[2], refs[3], refs[4:]
    halves, dbias_ref, refs = refs[:2], refs[2], refs[3:]
    counts = [len(order) for order in orders[:-1]]
    earlier, refs = refs[: 2 * len(counts)], refs[2 * len(counts) :]
    out_ref, send = refs
    me = me_ref[0]
    core, chip = me % 2, me // 2
    devices = 2 * len(masks)
    tiles = 2 * halves[0].shape[0] // TILE
    lengths = [length_of(meta_ref, masks.index(m)) for m in orders[-1]]
    normed = normed_rows(docs, seq, lengths, weight, params)
    found = []
    for k, w_ref in enumerate(halves):
        parts = [earlier[2 * n + k][0:count, :] for n, count in enumerate(counts)]
        found.append(jnp.concatenate([*parts, *tops_of(normed, w_ref, 2)], axis=0))
    low = jnp.where(core == 0, found[0], found[1])
    high = jnp.where(core == 0, found[1], found[0])
    logits = jnp.concatenate([low, high], axis=1)
    order = [mask for group in orders for mask in group]
    docs_at = [me ^ (2 * mask) for mask in order]
    bias = dbias_ref[...]
    bias = pltpu.roll(bias, bias.shape[0] - chip * tiles, 0)
    send[...] = jnp.zeros(send.shape, jnp.float32)
    stride = out_ref.shape[1]
    target = lax.broadcasted_iota(jnp.int32, (BLK_DEV * devices, TILE), 0)
    for t in range(tiles):
        lanes = slice(t * TILE, (t + 1) * TILE)
        impacts = jnp.log1p(jnp.maximum(logits[:, lanes] + bias[t : t + 1, :], 0.0))
        impacts = impacts.astype(jnp.bfloat16).astype(jnp.float32)
        blocks = jnp.zeros((BLK_DEV * devices, TILE), jnp.float32)
        for n, mask in enumerate(order):
            row = impacts[n : n + 1, :]
            send[pl.ds(docs_at[n] * stride + t, 1), :] = row
            block = table_ref[masks.index(mask), chip * tiles + t]
            blocks = jnp.maximum(blocks, jnp.where(target == block, row, 0.0))
        for s in range(BLK_DEV):
            send[pl.ds((1 + s) * SLOT_ROWS + t, devices, stride=stride), :] = blocks[
                s * devices : (s + 1) * devices
            ]
    out_ref[...] = send[...].astype(jnp.bfloat16).reshape(out_ref.shape)


def move_tokens(
    hidden_states,
    doc_lengths,
    transform_weight,
    transform_bias,
    norm_gain,
    norm_bias,
    decoder_weight,
    decoder_bias,
    tile_ids,
    owner_ids,
    block_slots,
):
    devices = lax.axis_size("doc")
    chips = devices // 2
    seq, width = hidden_states.shape
    rows = transform_weight.shape[0]
    half = decoder_weight.shape[2]
    tiles = 2 * half // TILE
    me = lax.axis_index("doc").astype(jnp.int32)

    def cross(value, mask):
        return lax.ppermute(value, "doc", [(i, i ^ (2 * mask)) for i in range(devices)])

    def swap(value):
        return lax.ppermute(value, "doc", [(i, i ^ 1) for i in range(devices)])

    smem = pl.BlockSpec(memory_space=pltpu.SMEM)
    vmem = pl.BlockSpec(memory_space=pltpu.VMEM)
    hbm = pl.BlockSpec(memory_space=pltpu.HBM)

    def stay(value):
        return pltpu.with_memory_space_constraint(value, pltpu.HBM)

    limit = pltpu.CompilerParams(vmem_limit_bytes=24 * 1024 * 1024)

    def cost(docs):
        return pl.CostEstimate(
            flops=2 * docs * seq * width * (width + 2 * half),
            bytes_accessed=1024 * 1024,
            transcendentals=docs * seq * width,
        )

    def shape(dims, dtype):
        return jax.ShapeDtypeStruct(dims, dtype)

    def after(value, *done):
        return lax.optimization_barrier((value, *done))[0]

    load, block, params = pl.pallas_call(
        start_kernel,
        out_shape=[
            shape((seq + rows + SLOT_ROWS, width), jnp.bfloat16),
            shape((rows, width + TILE), jnp.bfloat16),
            shape((8, width), jnp.float32),
        ],
        in_specs=[smem] * 4 + [hbm] * 5,
        out_specs=[vmem] * 3,
        scratch_shapes=[
            pltpu.VMEM((3 * width,), jnp.float32),
            pltpu.SemaphoreType.DMA((6,)),
        ],
        compiler_params=limit,
    )(
        stay(tile_ids),
        stay(owner_ids[..., 0]),
        stay(block_slots),
        doc_lengths,
        stay(hidden_states),
        stay(transform_weight),
        stay(transform_bias),
        stay(norm_gain),
        stay(norm_bias),
    )
    def pile(*values):
        total = sum(value.shape[0] for value in values)
        return pl.pallas_call(
            pile_kernel,
            out_shape=shape((total, values[0].shape[1]), values[0].dtype),
            in_specs=[vmem] * len(values),
            out_specs=vmem,
            compiler_params=limit,
        )(*values)

    weight_rows = jnp.swapaxes(decoder_weight[0], 0, 1)
    theirs = swap(weight_rows)
    block_6 = cross(block, 6)
    docs = {0: load, 2: cross(load, 2), 1: cross(load, 1)}
    block_4 = cross(block_6, 2)
    docs[6] = cross(after(hidden_states, block_6), 6)
    docs[3] = cross(after(docs[2], block_6), 1)
    far_pile = cross(pile(block_6, after(block_4, docs[1], docs[2], theirs)), 1)
    docs[4] = cross(docs[6], 2)
    docs[7] = cross(docs[6], 1)
    docs[5] = cross(docs[4], 1)
    masks = [0, 1, 2, 3, 6, 4, 7, 5]
    packed, meta = pl.pallas_call(
        lambda *refs: pack_kernel(seq, *refs),
        out_shape=[
            shape((chips * rows, width), jnp.bfloat16),
            shape((chips, TILE), jnp.int32),
        ],
        in_specs=[vmem] * 7,
        out_specs=[vmem] * 2,
        compiler_params=limit,
    )(docs[0], docs[1], docs[2], docs[3], after(block_6, docs[6]), block_4, far_pile)
    other_packed = swap(after(packed, docs[3]))

    orders = [[2, 3, 1, 0], [6, 7], [4, 5]]
    where = me[None]
    best_shape = shape((8, half), jnp.float32)
    *best, weight, mine = pl.pallas_call(
        lambda *refs: first_kernel(seq, masks, orders[0], *refs),
        out_shape=[
            best_shape,
            best_shape,
            shape((width, width), jnp.bfloat16),
            shape((half, width), jnp.bfloat16),
        ],
        in_specs=[smem] + [vmem] * 8 + [hbm, vmem],
        out_specs=[vmem] * 4,
        scratch_shapes=[pltpu.SemaphoreType.DMA],
        compiler_params=limit,
        cost_estimate=cost(len(orders[0])),
    )(
        where,
        meta,
        *[docs[mask] for mask in orders[0]],
        packed,
        after(other_packed, docs[4]),
        params,
        stay(weight_rows),
        theirs,
    )
    for order in orders[1:-1]:
        best += pl.pallas_call(
            lambda *refs, order=order: next_kernel(seq, masks, order, *refs),
            out_shape=[best_shape] * 2,
            in_specs=[vmem] * 7,
            out_specs=[vmem] * 2,
            compiler_params=limit,
            cost_estimate=cost(2),
        )(meta, *[docs[mask] for mask in order], weight, params, mine, theirs)
    send = pl.pallas_call(
        lambda *refs: last_kernel(seq, masks, orders, *refs),
        out_shape=shape((devices, (1 + BLK_DEV) * SLOT_ROWS, TILE), jnp.bfloat16),
        in_specs=[smem] * 2 + [vmem] * (8 + len(best)),
        out_specs=vmem,
        scratch_shapes=[
            pltpu.VMEM((devices * (1 + BLK_DEV) * SLOT_ROWS, TILE), jnp.float32),
        ],
        compiler_params=limit,
        cost_estimate=cost(2),
    )(
        where,
        meta,
        meta,
        *[docs[mask] for mask in orders[-1]],
        weight,
        params,
        mine,
        theirs,
        decoder_bias.reshape(-1, TILE),
        *best,
    )
    got = lax.all_to_all(send, "doc", split_axis=0, concat_axis=0, tiled=True)
    got = got.reshape(chips, 2, 1 + BLK_DEV, SLOT_ROWS, TILE)[:, :, :, :tiles]
    whole = jnp.swapaxes(jnp.maximum(got[:, 0], got[:, 1]), 0, 1).reshape(1 + BLK_DEV, -1)
    return (whole[:1], whole[1:])


def tokens_move(mesh):
    return mesh.shape["term"] == 1 and mesh.shape["doc"] == 16


def solution(mesh):
    placed = (
        P(("groups", "doc"), None),
        P(("groups", "doc")),
        P("doc", "term"),
        P(),
        P(),
        P(),
        P("term", None, "doc"),
        P("term"),
        P("term", ("groups", "doc"), None),
        P("term", ("groups", "doc"), None, None),
        P("term", ("groups", "doc"), None),
    )

    def local(*args):
        pair = 2 * args[6].shape[2]
        tiles = pair * (mesh.shape["doc"] // 2) // TILE
        fits = pair % TILE == 0 and tiles < TILE and pair // TILE <= SLOT_ROWS
        if tokens_move(mesh) and args[1].shape[0] == 1 and fits:
            return move_tokens(*args)
        return move_weights(*args)

    return jax.shard_map(
        local,
        mesh=mesh,
        in_specs=placed,
        out_specs=(P(("groups", "doc"), "term"), P(("groups", "doc"), "term")),
        check_vma=False,
    )
```

```python
import jax
import jax.numpy as jnp
from jax import lax
from jax.experimental import pallas as pl
from jax.experimental.pallas import tpu as pltpu
from jax.sharding import PartitionSpec as P

TILE = 128
BLK_DEV = 2
SLOT_ROWS = 16


def layer_norm(activated, norm_gain, norm_bias):
    values = activated.astype(jnp.float32)
    centre = jnp.mean(values, axis=-1, keepdims=True)
    centred = values - centre
    spread = jnp.mean(centred * centred, axis=-1, keepdims=True)
    return (centred * lax.rsqrt(spread + 1e-05) * norm_gain + norm_bias).astype(jnp.bfloat16)


def pool_docs(logits, keep):
    docs_here = keep.shape[0]
    saturated = jnp.log1p(jnp.maximum(logits, 0.0)).reshape(
        docs_here, keep.shape[1], logits.shape[1]
    )
    return jnp.max(jnp.where(keep[:, :, None], saturated, 0.0), axis=1)


def move_weights(
    hidden_states,
    doc_lengths,
    transform_weight,
    transform_bias,
    norm_gain,
    norm_bias,
    decoder_weight,
    decoder_bias,
    tile_ids,
    owner_ids,
    block_slots,
):
    tok_rows = hidden_states.shape[0]
    docs_here = doc_lengths.shape[0]
    seq_len = tok_rows // docs_here
    cols = transform_weight.shape[1]
    pre_half = jnp.dot(
        hidden_states,
        lax.all_gather(transform_weight, "doc", axis=0, tiled=True),
        preferred_element_type=jnp.float32,
    )
    bias_half = lax.dynamic_slice_in_dim(transform_bias, lax.axis_index("term") * cols, cols, 0)
    act_half = jax.nn.gelu(pre_half + bias_half, approximate=False).astype(jnp.bfloat16)
    activated = lax.all_gather(act_half, "term", axis=1, tiled=True)
    normed = layer_norm(activated, norm_gain, norm_bias)
    keep = jnp.arange(seq_len, dtype=jnp.int32)[None, :] < doc_lengths[:, None]
    logits = jnp.dot(
        normed,
        lax.all_gather(decoder_weight, "doc", axis=2, tiled=True)[0],
        preferred_element_type=jnp.float32,
    )
    logits = logits + decoder_bias
    impacts = pool_docs(logits, keep).astype(jnp.bfloat16)
    tiles_t = impacts.shape[1] // TILE
    slots_total = BLK_DEV * tiles_t
    tiles = impacts.reshape(docs_here * tiles_t, TILE)
    chosen = tile_ids[0]
    doc_index = jnp.arange(docs_here, dtype=jnp.int32)[:, None]
    posted = tiles[(doc_index * tiles_t + chosen).reshape(-1)]
    owners = owner_ids[0, :, :, 0].reshape(-1)
    target = block_slots[0].reshape(-1) * tiles_t + chosen.reshape(-1)
    owner_count = lax.axis_size("doc")
    capacity = max(2, 2 * posted.shape[0] // owner_count)
    onehot = (owners[:, None] == jnp.arange(owner_count, dtype=jnp.int32)[None, :]).astype(
        jnp.int32
    )
    before = jnp.cumsum(onehot, axis=0) - onehot
    position = jnp.sum(before * onehot, axis=1)
    dest = owners * capacity + position
    outgoing = jnp.zeros((owner_count * capacity, TILE), jnp.bfloat16).at[dest].set(posted)
    out_tags = jnp.full((owner_count * capacity,), slots_total, jnp.int32).at[dest].set(target)
    got_vals, got_tags = (
        lax.all_to_all(
            outgoing.reshape(owner_count, capacity, TILE),
            "doc",
            split_axis=0,
            concat_axis=0,
            tiled=True,
        ),
        lax.all_to_all(
            out_tags.reshape(owner_count, capacity), "doc", split_axis=0, concat_axis=0, tiled=True
        ),
    )
    got_vals = got_vals.reshape(-1, TILE)
    local_tags = got_tags.reshape(-1)
    summary = jnp.zeros((slots_total, TILE), jnp.bfloat16).at[local_tags].max(got_vals, mode="drop")
    return (impacts, summary.reshape(BLK_DEV, tiles_t * TILE))


def dot_t(left, right):
    return lax.dot_general(
        left, right, (((1,), (1,)), ((), ())), preferred_element_type=jnp.float32
    )


def table_of(ref, seq):
    return ref[seq : seq + SLOT_ROWS, 0:TILE].astype(jnp.float32)[0:1, :]


def masked(ref, seq):
    here = ref[0:seq, :]
    length = table_of(ref, seq)[:, TILE - 1 :]
    keep = lax.broadcasted_iota(jnp.int32, here.shape, 0).astype(jnp.float32) < length
    first = jnp.broadcast_to(here[0:1, :].astype(jnp.float32), here.shape).astype(here.dtype)
    return jnp.where(keep, here, first)


def normed_rows(docs, seq, weight, params):
    rows = jnp.concatenate([masked(ref, seq) for ref in docs], axis=0)
    pre = jnp.dot(rows, weight[...], preferred_element_type=jnp.float32) + params[0:1, :]
    act = 0.5 * pre * (1.0 + lax.erf(pre * (0.5**0.5)))
    return layer_norm(act.astype(jnp.bfloat16), params[1:2, :], params[2:3, :])


def tops_of(normed, w_ref, count):
    logits = dot_t(normed, w_ref[...])
    seq = normed.shape[0] // count
    return [
        jnp.max(logits[j * seq : (j + 1) * seq], axis=0, keepdims=True) for j in range(count)
    ]


def start_kernel(tiles_ref, owners_ref, slots_ref, length_ref, *refs):
    hidden_ref, weight_ref, vectors = refs[0], refs[1], refs[2:5]
    load_ref, block_ref, rows_ref, kept, sems = refs[5:]
    seq, width = hidden_ref.shape
    copies = [
        fetch(hidden_ref, load_ref.at[pl.ds(0, seq), :], sems.at[0]),
        fetch(weight_ref, block_ref, sems.at[1]),
    ]
    for k, ref in enumerate(vectors):
        copies.append(fetch(ref, kept.at[pl.ds(k * width, width)], sems.at[2 + k]))
    lane = lax.broadcasted_iota(jnp.int32, (SLOT_ROWS, TILE), 1)
    table = jnp.where(lane == TILE - 1, length_ref[0], -1)
    devices = lax.axis_size("doc")
    for k in range(tiles_ref.shape[2]):
        block = slots_ref[0, 0, k] * devices + owners_ref[0, 0, k]
        table = jnp.where(lane == tiles_ref[0, 0, k], block, table)
    table = table.astype(jnp.float32).astype(jnp.bfloat16)
    for first in range(0, width, TILE):
        load_ref[seq:, first : first + TILE] = table
    for copy in copies:
        copy.wait()
    for k in range(len(vectors)):
        rows_ref[k : k + 1, :] = kept[pl.ds(k * width, width)][None, :]


def pile_kernel(*refs):
    at = 0
    for ref in refs[:-1]:
        refs[-1][at : at + ref.shape[0], :] = ref[...]
        at += ref.shape[0]


def fetch(ref, slot, sem):
    copy = pltpu.make_async_copy(ref, slot, sem)
    copy.start()
    return copy


def keep_tops(normed, halves, bests):
    for w_ref, best in zip(halves, bests):
        for j, top in enumerate(tops_of(normed, w_ref, 2)):
            best[j : j + 1, :] = top


def first_kernel(seq, masks, *refs):
    me_ref, docs, packed, refs = refs[0], refs[1:3], refs[3:5], refs[5:]
    params, mine_ref, theirs_ref, best_mine, best_theirs, weight, mine, sem = refs
    copy = fetch(mine_ref, mine, sem)
    me = me_ref[0]
    core = me % 2
    rows = weight.shape[0] // (2 * len(masks))
    for k, mask in enumerate(masks):
        chip = (me // 2) ^ mask
        block = slice(k * rows, (k + 1) * rows)
        at = pl.multiple_of((2 * chip + core) * rows, SLOT_ROWS)
        weight[pl.ds(at, rows), :] = packed[0][block, :]
        at = pl.multiple_of((2 * chip + 1 - core) * rows, SLOT_ROWS)
        weight[pl.ds(at, rows), :] = packed[1][block, :]
    normed = normed_rows(docs, seq, weight, params)
    keep_tops(normed, [theirs_ref], [best_theirs])
    copy.wait()
    keep_tops(normed, [mine], [best_mine])


def next_kernel(seq, *refs):
    docs, weight, params, halves, bests = refs[:2], refs[2], refs[3], refs[4:6], refs[6:]
    keep_tops(normed_rows(docs, seq, weight, params), halves, bests)


def last_kernel(seq, masks, *refs):
    me_ref, docs, refs = refs[0], refs[1 : 1 + len(masks)], refs[1 + len(masks) :]
    weight, params, halves, dbias_ref, refs = refs[0], refs[1], refs[2:4], refs[4], refs[5:]
    earlier, out_ref, send = refs[:-2], refs[-2], refs[-1]
    me = me_ref[0]
    core, chip = me % 2, me // 2
    devices = 2 * len(masks)
    tiles = 2 * halves[0].shape[0] // TILE
    normed = normed_rows(docs[-2:], seq, weight, params)
    found = []
    for k, w_ref in enumerate(halves):
        parts = [ref[0:2, :] for ref in earlier[k::2]]
        found.append(jnp.concatenate([*parts, *tops_of(normed, w_ref, 2)], axis=0))
    low = jnp.where(core == 0, found[0], found[1])
    high = jnp.where(core == 0, found[1], found[0])
    logits = jnp.concatenate([low, high], axis=1)
    docs_at = [me ^ (2 * mask) for mask in masks]
    bias = dbias_ref[...]
    bias = pltpu.roll(bias, bias.shape[0] - chip * tiles, 0)
    tables = jnp.concatenate([table_of(ref, seq) for ref in docs], axis=0)
    tables = pltpu.roll(tables, TILE - chip * tiles, 1).astype(jnp.int32)
    send[...] = jnp.zeros(send.shape, jnp.float32)
    stride = out_ref.shape[1]
    target = lax.broadcasted_iota(jnp.int32, (BLK_DEV * devices, TILE), 0)
    for t in range(tiles):
        lanes = slice(t * TILE, (t + 1) * TILE)
        impacts = jnp.log1p(jnp.maximum(logits[:, lanes] + bias[t : t + 1, :], 0.0))
        impacts = impacts.astype(jnp.bfloat16).astype(jnp.float32)
        blocks = jnp.zeros((BLK_DEV * devices, TILE), jnp.float32)
        for n in range(len(masks)):
            row = impacts[n : n + 1, :]
            send[pl.ds(docs_at[n] * stride + t, 1), :] = row
            block = jnp.broadcast_to(tables[n : n + 1, t : t + 1], target.shape)
            blocks = jnp.maximum(blocks, jnp.where(target == block, row, 0.0))
        for s in range(BLK_DEV):
            send[pl.ds((1 + s) * SLOT_ROWS + t, devices, stride=stride), :] = blocks[
                s * devices : (s + 1) * devices
            ]
    out_ref[...] = send[...].astype(jnp.bfloat16).reshape(out_ref.shape)


def move_tokens(
    hidden_states,
    doc_lengths,
    transform_weight,
    transform_bias,
    norm_gain,
    norm_bias,
    decoder_weight,
    decoder_bias,
    tile_ids,
    owner_ids,
    block_slots,
):
    devices = lax.axis_size("doc")
    chips = devices // 2
    seq, width = hidden_states.shape
    rows = transform_weight.shape[0]
    half = decoder_weight.shape[2]
    tiles = 2 * half // TILE
    me = lax.axis_index("doc").astype(jnp.int32)

    def cross(value, mask):
        return lax.ppermute(value, "doc", [(i, i ^ (2 * mask)) for i in range(devices)])

    def swap(value):
        return lax.ppermute(value, "doc", [(i, i ^ 1) for i in range(devices)])

    smem = pl.BlockSpec(memory_space=pltpu.SMEM)
    vmem = pl.BlockSpec(memory_space=pltpu.VMEM)
    hbm = pl.BlockSpec(memory_space=pltpu.HBM)

    def stay(value):
        return pltpu.with_memory_space_constraint(value, pltpu.HBM)

    limit = pltpu.CompilerParams(vmem_limit_bytes=24 * 1024 * 1024)

    def cost(docs):
        return pl.CostEstimate(flops=docs, bytes_accessed=docs, transcendentals=0)

    def shape(dims, dtype):
        return jax.ShapeDtypeStruct(dims, dtype)

    def after(value, *done):
        return lax.optimization_barrier((value, *done))[0]

    def pile(*values):
        total = sum(value.shape[0] for value in values)
        return pl.pallas_call(
            pile_kernel,
            out_shape=shape((total, values[0].shape[1]), values[0].dtype),
            in_specs=[vmem] * len(values),
            out_specs=vmem,
            compiler_params=limit,
        )(*values)

    weight_rows = jnp.swapaxes(decoder_weight[0], 0, 1)
    block_6 = cross(transform_weight, 6)
    block_2 = cross(transform_weight, 2)
    theirs = swap(weight_rows)
    load, block, params = pl.pallas_call(
        start_kernel,
        out_shape=[
            shape((seq + SLOT_ROWS, width), jnp.bfloat16),
            shape((rows, width), jnp.bfloat16),
            shape((8, width), jnp.float32),
        ],
        in_specs=[smem] * 4 + [hbm] * 5,
        out_specs=[vmem] * 3,
        scratch_shapes=[
            pltpu.VMEM((3 * width,), jnp.float32),
            pltpu.SemaphoreType.DMA((5,)),
        ],
        compiler_params=limit,
    )(
        stay(tile_ids),
        stay(owner_ids[..., 0]),
        stay(block_slots),
        doc_lengths,
        stay(hidden_states),
        stay(transform_weight),
        stay(transform_bias),
        stay(norm_gain),
        stay(norm_bias),
    )
    docs = {0: load, 1: cross(after(load, block_6), 1)}
    near_pile = cross(pile(block, block_2), 1)
    block_4 = cross(block_6, 2)
    docs[6] = cross(after(load, block_6), 6)
    docs[2] = cross(after(load, block_4), 2)
    far_pile = cross(pile(block_6, after(block_4, near_pile, docs[1])), 1)
    docs[3] = cross(docs[2], 1)
    docs[4] = cross(docs[6], 2)
    docs[7] = cross(docs[6], 1)
    packed = pile(after(block, docs[6], docs[2], theirs), block_2, block_6, block_4, near_pile, far_pile)
    other_packed = swap(packed)
    block_masks = [0, 2, 6, 4, 1, 3, 7, 5]

    masks = [0, 1, 2, 3, 6, 7, 4, 5]
    where = me[None]
    best_shape = shape((8, half), jnp.float32)
    *best, weight, mine = pl.pallas_call(
        lambda *refs: first_kernel(seq, block_masks, *refs),
        out_shape=[
            best_shape,
            best_shape,
            shape((width, width), jnp.bfloat16),
            shape((half, width), jnp.bfloat16),
        ],
        in_specs=[smem] + [vmem] * 5 + [hbm, vmem],
        out_specs=[vmem] * 4,
        scratch_shapes=[pltpu.SemaphoreType.DMA],
        compiler_params=limit,
        cost_estimate=cost(2),
    )(
        where,
        *[docs[mask] for mask in masks[:2]],
        packed,
        other_packed,
        params,
        stay(weight_rows),
        theirs,
    )
    docs[5] = cross(after(docs[4], weight), 1)
    for first in range(2, len(masks) - 2, 2):
        best += pl.pallas_call(
            lambda *refs: next_kernel(seq, *refs),
            out_shape=[best_shape] * 2,
            in_specs=[vmem] * 6,
            out_specs=[vmem] * 2,
            compiler_params=limit,
            cost_estimate=cost(2),
        )(*[docs[mask] for mask in masks[first : first + 2]], weight, params, mine, theirs)
    send = pl.pallas_call(
        lambda *refs: last_kernel(seq, masks, *refs),
        out_shape=shape((devices, (1 + BLK_DEV) * SLOT_ROWS, TILE), jnp.bfloat16),
        in_specs=[smem] + [vmem] * (len(masks) + 5 + len(best)),
        out_specs=vmem,
        scratch_shapes=[
            pltpu.VMEM((devices * (1 + BLK_DEV) * SLOT_ROWS, TILE), jnp.float32),
        ],
        compiler_params=limit,
        cost_estimate=cost(2),
    )(
        where,
        *[docs[mask] for mask in masks],
        weight,
        params,
        mine,
        theirs,
        decoder_bias.reshape(-1, TILE),
        *best,
    )
    got = lax.all_to_all(send, "doc", split_axis=0, concat_axis=0, tiled=True)
    got = got.reshape(chips, 2, 1 + BLK_DEV, SLOT_ROWS, TILE)[:, :, :, :tiles]
    whole = jnp.swapaxes(jnp.maximum(got[:, 0], got[:, 1]), 0, 1).reshape(1 + BLK_DEV, -1)
    return (whole[:1], whole[1:])


def tokens_move(mesh):
    return mesh.shape["term"] == 1 and mesh.shape["doc"] == 16


def solution(mesh):
    placed = (
        P(("groups", "doc"), None),
        P(("groups", "doc")),
        P("doc", "term"),
        P(),
        P(),
        P(),
        P("term", None, "doc"),
        P("term"),
        P("term", ("groups", "doc"), None),
        P("term", ("groups", "doc"), None, None),
        P("term", ("groups", "doc"), None),
    )

    def local(*args):
        pair = 2 * args[6].shape[2]
        tiles = pair * (mesh.shape["doc"] // 2) // TILE
        fits = pair % TILE == 0 and tiles < TILE and pair // TILE <= SLOT_ROWS
        if tokens_move(mesh) and args[1].shape[0] == 1 and fits:
            return move_tokens(*args)
        return move_weights(*args)

    return jax.shard_map(
        local,
        mesh=mesh,
        in_specs=placed,
        out_specs=(P(("groups", "doc"), "term"), P(("groups", "doc"), "term")),
        check_vma=False,
    )
```

```python
import jax
import jax.numpy as jnp
from jax import lax
from jax.experimental import pallas as pl
from jax.experimental.pallas import tpu as pltpu
from jax.sharding import PartitionSpec as P

TILE = 128
BLK_DEV = 2
SLOT_ROWS = 16


def layer_norm(activated, norm_gain, norm_bias):
    values = activated.astype(jnp.float32)
    centre = jnp.mean(values, axis=-1, keepdims=True)
    centred = values - centre
    spread = jnp.mean(centred * centred, axis=-1, keepdims=True)
    return (centred * lax.rsqrt(spread + 1e-05) * norm_gain + norm_bias).astype(jnp.bfloat16)


def pool_docs(logits, keep):
    docs_here = keep.shape[0]
    saturated = jnp.log1p(jnp.maximum(logits, 0.0)).reshape(
        docs_here, keep.shape[1], logits.shape[1]
    )
    return jnp.max(jnp.where(keep[:, :, None], saturated, 0.0), axis=1)


def move_weights(
    hidden_states,
    doc_lengths,
    transform_weight,
    transform_bias,
    norm_gain,
    norm_bias,
    decoder_weight,
    decoder_bias,
    tile_ids,
    owner_ids,
    block_slots,
):
    tok_rows = hidden_states.shape[0]
    docs_here = doc_lengths.shape[0]
    seq_len = tok_rows // docs_here
    cols = transform_weight.shape[1]
    pre_half = jnp.dot(
        hidden_states,
        lax.all_gather(transform_weight, "doc", axis=0, tiled=True),
        preferred_element_type=jnp.float32,
    )
    bias_half = lax.dynamic_slice_in_dim(transform_bias, lax.axis_index("term") * cols, cols, 0)
    act_half = jax.nn.gelu(pre_half + bias_half, approximate=False).astype(jnp.bfloat16)
    activated = lax.all_gather(act_half, "term", axis=1, tiled=True)
    normed = layer_norm(activated, norm_gain, norm_bias)
    keep = jnp.arange(seq_len, dtype=jnp.int32)[None, :] < doc_lengths[:, None]
    logits = jnp.dot(
        normed,
        lax.all_gather(decoder_weight, "doc", axis=2, tiled=True)[0],
        preferred_element_type=jnp.float32,
    )
    logits = logits + decoder_bias
    impacts = pool_docs(logits, keep).astype(jnp.bfloat16)
    tiles_t = impacts.shape[1] // TILE
    slots_total = BLK_DEV * tiles_t
    tiles = impacts.reshape(docs_here * tiles_t, TILE)
    chosen = tile_ids[0]
    doc_index = jnp.arange(docs_here, dtype=jnp.int32)[:, None]
    posted = tiles[(doc_index * tiles_t + chosen).reshape(-1)]
    owners = owner_ids[0, :, :, 0].reshape(-1)
    target = block_slots[0].reshape(-1) * tiles_t + chosen.reshape(-1)
    owner_count = lax.axis_size("doc")
    capacity = max(2, 2 * posted.shape[0] // owner_count)
    onehot = (owners[:, None] == jnp.arange(owner_count, dtype=jnp.int32)[None, :]).astype(
        jnp.int32
    )
    before = jnp.cumsum(onehot, axis=0) - onehot
    position = jnp.sum(before * onehot, axis=1)
    dest = owners * capacity + position
    outgoing = jnp.zeros((owner_count * capacity, TILE), jnp.bfloat16).at[dest].set(posted)
    out_tags = jnp.full((owner_count * capacity,), slots_total, jnp.int32).at[dest].set(target)
    got_vals, got_tags = (
        lax.all_to_all(
            outgoing.reshape(owner_count, capacity, TILE),
            "doc",
            split_axis=0,
            concat_axis=0,
            tiled=True,
        ),
        lax.all_to_all(
            out_tags.reshape(owner_count, capacity), "doc", split_axis=0, concat_axis=0, tiled=True
        ),
    )
    got_vals = got_vals.reshape(-1, TILE)
    local_tags = got_tags.reshape(-1)
    summary = jnp.zeros((slots_total, TILE), jnp.bfloat16).at[local_tags].max(got_vals, mode="drop")
    return (impacts, summary.reshape(BLK_DEV, tiles_t * TILE))


def dot_t(left, right):
    return lax.dot_general(
        left, right, (((1,), (1,)), ((), ())), preferred_element_type=jnp.float32
    )


def table_of(ref):
    return ref[ref.shape[0] - SLOT_ROWS :, 0:TILE].astype(jnp.float32)[0:1, :]


def masked(ref, table_ref, seq):
    here = ref[0:seq, :]
    length = table_of(table_ref)[:, TILE - 1 :]
    keep = lax.broadcasted_iota(jnp.int32, here.shape, 0).astype(jnp.float32) < length
    first = jnp.broadcast_to(here[0:1, :].astype(jnp.float32), here.shape).astype(here.dtype)
    return jnp.where(keep, here, first)


def normed_rows(docs, tables, seq, weight, params):
    rows = [masked(ref, table, seq) for ref, table in zip(docs, tables)]
    rows = jnp.concatenate(rows, axis=0)
    pre = jnp.dot(rows, weight[...], preferred_element_type=jnp.float32) + params[0:1, :]
    act = 0.5 * pre * (1.0 + lax.erf(pre * (0.5**0.5)))
    return layer_norm(act.astype(jnp.bfloat16), params[1:2, :], params[2:3, :])


def tops_of(normed, w_ref, count):
    logits = dot_t(normed, w_ref[...])
    seq = normed.shape[0] // count
    return [
        jnp.max(logits[j * seq : (j + 1) * seq], axis=0, keepdims=True) for j in range(count)
    ]


def start_kernel(tiles_ref, owners_ref, slots_ref, length_ref, *refs):
    hidden_ref, weight_ref, vectors = refs[0], refs[1], refs[2:5]
    load_ref, block_ref, table_ref, rows_ref, kept, sems = refs[5:]
    seq, width = hidden_ref.shape
    copies = [
        fetch(hidden_ref, load_ref.at[pl.ds(0, seq), :], sems.at[0]),
        fetch(weight_ref, block_ref, sems.at[1]),
    ]
    for k, ref in enumerate(vectors):
        copies.append(fetch(ref, kept.at[pl.ds(k * width, width)], sems.at[2 + k]))
    lane = lax.broadcasted_iota(jnp.int32, (SLOT_ROWS, TILE), 1)
    table = jnp.where(lane == TILE - 1, length_ref[0], -1)
    devices = lax.axis_size("doc")
    for k in range(tiles_ref.shape[2]):
        block = slots_ref[0, 0, k] * devices + owners_ref[0, 0, k]
        table = jnp.where(lane == tiles_ref[0, 0, k], block, table)
    table = table.astype(jnp.float32).astype(jnp.bfloat16)
    for first in range(0, width, TILE):
        load_ref[seq:, first : first + TILE] = table
        table_ref[:, first : first + TILE] = table
    for copy in copies:
        copy.wait()
    for k in range(len(vectors)):
        rows_ref[k : k + 1, :] = kept[pl.ds(k * width, width)][None, :]


def pile_kernel(counts, *refs):
    at = 0
    for ref, count in zip(refs[:-1], counts):
        refs[-1][at : at + count, :] = ref[0:count, :]
        at += count


def fetch(ref, slot, sem):
    copy = pltpu.make_async_copy(ref, slot, sem)
    copy.start()
    return copy


def keep_tops(normed, halves, bests):
    for w_ref, best in zip(halves, bests):
        for j, top in enumerate(tops_of(normed, w_ref, 2)):
            best[j : j + 1, :] = top


def first_kernel(seq, masks, *refs):
    me_ref, docs, tables, packed, refs = refs[0], refs[1:3], refs[3:5], refs[5:7], refs[7:]
    params, mine_ref, theirs_ref, best_mine, best_theirs, weight, mine, sem = refs
    copy = fetch(mine_ref, mine, sem)
    me = me_ref[0]
    core = me % 2
    rows = weight.shape[0] // (2 * len(masks))
    for k, mask in enumerate(masks):
        chip = (me // 2) ^ mask
        block = slice(k * rows, (k + 1) * rows)
        at = pl.multiple_of((2 * chip + core) * rows, SLOT_ROWS)
        weight[pl.ds(at, rows), :] = packed[0][block, :]
        at = pl.multiple_of((2 * chip + 1 - core) * rows, SLOT_ROWS)
        weight[pl.ds(at, rows), :] = packed[1][block, :]
    normed = normed_rows(docs, tables, seq, weight, params)
    keep_tops(normed, [theirs_ref], [best_theirs])
    copy.wait()
    keep_tops(normed, [mine], [best_mine])


def next_kernel(seq, *refs):
    docs, weight, params, halves, bests = refs[:2], refs[2], refs[3], refs[4:6], refs[6:]
    keep_tops(normed_rows(docs, docs, seq, weight, params), halves, bests)


def last_kernel(seq, masks, *refs):
    me_ref, docs, tables, refs = refs[0], refs[1:3], refs[3 : 3 + len(masks)], refs[3 + len(masks) :]
    weight, params, halves, dbias_ref, refs = refs[0], refs[1], refs[2:4], refs[4], refs[5:]
    earlier, out_ref, send = refs[:-2], refs[-2], refs[-1]
    me = me_ref[0]
    core, chip = me % 2, me // 2
    devices = 2 * len(masks)
    tiles = 2 * halves[0].shape[0] // TILE
    normed = normed_rows(docs, docs, seq, weight, params)
    found = []
    for k, w_ref in enumerate(halves):
        parts = [ref[0:2, :] for ref in earlier[k::2]]
        found.append(jnp.concatenate([*parts, *tops_of(normed, w_ref, 2)], axis=0))
    low = jnp.where(core == 0, found[0], found[1])
    high = jnp.where(core == 0, found[1], found[0])
    logits = jnp.concatenate([low, high], axis=1)
    docs_at = [me ^ (2 * mask) for mask in masks]
    bias = dbias_ref[...]
    bias = pltpu.roll(bias, bias.shape[0] - chip * tiles, 0)
    tables = jnp.concatenate([table_of(ref) for ref in tables], axis=0)
    tables = pltpu.roll(tables, TILE - chip * tiles, 1).astype(jnp.int32)
    send[...] = jnp.zeros(send.shape, jnp.float32)
    stride = out_ref.shape[1]
    target = lax.broadcasted_iota(jnp.int32, (BLK_DEV * devices, TILE), 0)
    for t in range(tiles):
        lanes = slice(t * TILE, (t + 1) * TILE)
        impacts = jnp.log1p(jnp.maximum(logits[:, lanes] + bias[t : t + 1, :], 0.0))
        impacts = impacts.astype(jnp.bfloat16).astype(jnp.float32)
        blocks = jnp.zeros((BLK_DEV * devices, TILE), jnp.float32)
        for n in range(len(masks)):
            row = impacts[n : n + 1, :]
            send[pl.ds(docs_at[n] * stride + t, 1), :] = row
            block = jnp.broadcast_to(tables[n : n + 1, t : t + 1], target.shape)
            blocks = jnp.maximum(blocks, jnp.where(target == block, row, 0.0))
        for s in range(BLK_DEV):
            send[pl.ds((1 + s) * SLOT_ROWS + t, devices, stride=stride), :] = blocks[
                s * devices : (s + 1) * devices
            ]
    out_ref[...] = send[...].astype(jnp.bfloat16).reshape(out_ref.shape)


def move_tokens(
    hidden_states,
    doc_lengths,
    transform_weight,
    transform_bias,
    norm_gain,
    norm_bias,
    decoder_weight,
    decoder_bias,
    tile_ids,
    owner_ids,
    block_slots,
):
    devices = lax.axis_size("doc")
    chips = devices // 2
    seq, width = hidden_states.shape
    rows = transform_weight.shape[0]
    half = decoder_weight.shape[2]
    tiles = 2 * half // TILE
    me = lax.axis_index("doc").astype(jnp.int32)

    def cross(value, mask):
        return lax.ppermute(value, "doc", [(i, i ^ (2 * mask)) for i in range(devices)])

    def swap(value):
        return lax.ppermute(value, "doc", [(i, i ^ 1) for i in range(devices)])

    smem = pl.BlockSpec(memory_space=pltpu.SMEM)
    vmem = pl.BlockSpec(memory_space=pltpu.VMEM)
    hbm = pl.BlockSpec(memory_space=pltpu.HBM)

    def stay(value):
        return pltpu.with_memory_space_constraint(value, pltpu.HBM)

    limit = pltpu.CompilerParams(vmem_limit_bytes=24 * 1024 * 1024)

    def cost(docs):
        return pl.CostEstimate(flops=docs, bytes_accessed=docs, transcendentals=0)

    def shape(dims, dtype):
        return jax.ShapeDtypeStruct(dims, dtype)

    def after(value, *done):
        return lax.optimization_barrier((value, *done))[0]

    def pile(values, counts):
        return pl.pallas_call(
            lambda *refs: pile_kernel(counts, *refs),
            out_shape=shape((sum(counts), width), jnp.bfloat16),
            in_specs=[vmem] * len(values),
            out_specs=vmem,
            compiler_params=limit,
        )(*values)

    weight_rows = jnp.swapaxes(decoder_weight[0], 0, 1)
    block_6 = cross(transform_weight, 6)
    block_2 = cross(transform_weight, 2)
    theirs = swap(weight_rows)
    docs = {1: cross(hidden_states, 1)}
    load, block, table, params = pl.pallas_call(
        start_kernel,
        out_shape=[
            shape((seq + SLOT_ROWS, width), jnp.bfloat16),
            shape((rows, width), jnp.bfloat16),
            shape((SLOT_ROWS, width), jnp.bfloat16),
            shape((8, width), jnp.float32),
        ],
        in_specs=[smem] * 4 + [hbm] * 5,
        out_specs=[vmem] * 4,
        scratch_shapes=[
            pltpu.VMEM((3 * width,), jnp.float32),
            pltpu.SemaphoreType.DMA((5,)),
        ],
        compiler_params=limit,
    )(
        stay(tile_ids),
        stay(owner_ids[..., 0]),
        stay(block_slots),
        doc_lengths,
        stay(hidden_states),
        stay(transform_weight),
        stay(transform_bias),
        stay(norm_gain),
        stay(norm_bias),
    )
    docs[0] = load
    docs[2] = cross(after(load, block_2, block_6), 2)
    near = (block, after(block_2, block_6, docs[1]), table)
    near_pile = cross(pile(near, (rows, rows, SLOT_ROWS)), 1)
    block_4 = cross(block_6, 2)
    docs[6] = cross(after(load, block_6), 6)
    far = (block_6, after(block_4, near_pile, docs[2]))
    far_pile = cross(pile(far, (rows, rows)), 1)
    docs[3] = cross(docs[2], 1)
    docs[4] = cross(docs[6], 2)
    docs[7] = cross(docs[6], 1)
    late = (docs[6], docs[3], theirs)
    packed = pile(
        (after(block, *late), block_2, block_6, block_4, near_pile, far_pile),
        (rows, rows, rows, rows, 2 * rows, 2 * rows),
    )
    other_packed = swap(packed)
    block_masks = [0, 2, 6, 4, 1, 3, 7, 5]

    masks = [0, 1, 2, 3, 6, 7, 4, 5]
    where = me[None]
    best_shape = shape((8, half), jnp.float32)
    *best, weight, mine = pl.pallas_call(
        lambda *refs: first_kernel(seq, block_masks, *refs),
        out_shape=[
            best_shape,
            best_shape,
            shape((width, width), jnp.bfloat16),
            shape((half, width), jnp.bfloat16),
        ],
        in_specs=[smem] + [vmem] * 7 + [hbm, vmem],
        out_specs=[vmem] * 4,
        scratch_shapes=[pltpu.SemaphoreType.DMA],
        compiler_params=limit,
        cost_estimate=cost(2),
    )(
        where,
        docs[0],
        docs[1],
        docs[0],
        near_pile,
        packed,
        other_packed,
        params,
        stay(weight_rows),
        theirs,
    )
    docs[5] = cross(after(docs[4], weight), 1)
    for first in range(2, len(masks) - 2, 2):
        best += pl.pallas_call(
            lambda *refs: next_kernel(seq, *refs),
            out_shape=[best_shape] * 2,
            in_specs=[vmem] * 6,
            out_specs=[vmem] * 2,
            compiler_params=limit,
            cost_estimate=cost(2),
        )(*[docs[mask] for mask in masks[first : first + 2]], weight, params, mine, theirs)
    send = pl.pallas_call(
        lambda *refs: last_kernel(seq, masks, *refs),
        out_shape=shape((devices, (1 + BLK_DEV) * SLOT_ROWS, TILE), jnp.bfloat16),
        in_specs=[smem] + [vmem] * (2 + len(masks) + 5 + len(best)),
        out_specs=vmem,
        scratch_shapes=[
            pltpu.VMEM((devices * (1 + BLK_DEV) * SLOT_ROWS, TILE), jnp.float32),
        ],
        compiler_params=limit,
        cost_estimate=cost(2),
    )(
        where,
        *[docs[mask] for mask in masks[-2:]],
        *[near_pile if mask == 1 else docs[mask] for mask in masks],
        weight,
        params,
        mine,
        theirs,
        decoder_bias.reshape(-1, TILE),
        *best,
    )
    got = lax.all_to_all(send, "doc", split_axis=0, concat_axis=0, tiled=True)
    got = got.reshape(chips, 2, 1 + BLK_DEV, SLOT_ROWS, TILE)[:, :, :, :tiles]
    whole = jnp.swapaxes(jnp.maximum(got[:, 0], got[:, 1]), 0, 1).reshape(1 + BLK_DEV, -1)
    return (whole[:1], whole[1:])


def tokens_move(mesh):
    return mesh.shape["term"] == 1 and mesh.shape["doc"] == 16


def solution(mesh):
    placed = (
        P(("groups", "doc"), None),
        P(("groups", "doc")),
        P("doc", "term"),
        P(),
        P(),
        P(),
        P("term", None, "doc"),
        P("term"),
        P("term", ("groups", "doc"), None),
        P("term", ("groups", "doc"), None, None),
        P("term", ("groups", "doc"), None),
    )

    def local(*args):
        pair = 2 * args[6].shape[2]
        tiles = pair * (mesh.shape["doc"] // 2) // TILE
        fits = pair % TILE == 0 and tiles < TILE and pair // TILE <= SLOT_ROWS
        if tokens_move(mesh) and args[1].shape[0] == 1 and fits:
            return move_tokens(*args)
        return move_weights(*args)

    return jax.shard_map(
        local,
        mesh=mesh,
        in_specs=placed,
        out_specs=(P(("groups", "doc"), "term"), P(("groups", "doc"), "term")),
        check_vma=False,
    )
```

```python
import jax
import jax.numpy as jnp
from jax import lax
from jax.experimental import pallas as pl
from jax.experimental.pallas import tpu as pltpu
from jax.sharding import PartitionSpec as P

TILE = 128
BLK_DEV = 2
SLOT_ROWS = 16


def layer_norm(activated, norm_gain, norm_bias):
    values = activated.astype(jnp.float32)
    centre = jnp.mean(values, axis=-1, keepdims=True)
    centred = values - centre
    spread = jnp.mean(centred * centred, axis=-1, keepdims=True)
    return (centred * lax.rsqrt(spread + 1e-05) * norm_gain + norm_bias).astype(jnp.bfloat16)


def pool_docs(logits, keep):
    docs_here = keep.shape[0]
    saturated = jnp.log1p(jnp.maximum(logits, 0.0)).reshape(
        docs_here, keep.shape[1], logits.shape[1]
    )
    return jnp.max(jnp.where(keep[:, :, None], saturated, 0.0), axis=1)


def move_weights(
    hidden_states,
    doc_lengths,
    transform_weight,
    transform_bias,
    norm_gain,
    norm_bias,
    decoder_weight,
    decoder_bias,
    tile_ids,
    owner_ids,
    block_slots,
):
    tok_rows = hidden_states.shape[0]
    docs_here = doc_lengths.shape[0]
    seq_len = tok_rows // docs_here
    cols = transform_weight.shape[1]
    pre_half = jnp.dot(
        hidden_states,
        lax.all_gather(transform_weight, "doc", axis=0, tiled=True),
        preferred_element_type=jnp.float32,
    )
    bias_half = lax.dynamic_slice_in_dim(transform_bias, lax.axis_index("term") * cols, cols, 0)
    act_half = jax.nn.gelu(pre_half + bias_half, approximate=False).astype(jnp.bfloat16)
    activated = lax.all_gather(act_half, "term", axis=1, tiled=True)
    normed = layer_norm(activated, norm_gain, norm_bias)
    keep = jnp.arange(seq_len, dtype=jnp.int32)[None, :] < doc_lengths[:, None]
    logits = jnp.dot(
        normed,
        lax.all_gather(decoder_weight, "doc", axis=2, tiled=True)[0],
        preferred_element_type=jnp.float32,
    )
    logits = logits + decoder_bias
    impacts = pool_docs(logits, keep).astype(jnp.bfloat16)
    tiles_t = impacts.shape[1] // TILE
    slots_total = BLK_DEV * tiles_t
    tiles = impacts.reshape(docs_here * tiles_t, TILE)
    chosen = tile_ids[0]
    doc_index = jnp.arange(docs_here, dtype=jnp.int32)[:, None]
    posted = tiles[(doc_index * tiles_t + chosen).reshape(-1)]
    owners = owner_ids[0, :, :, 0].reshape(-1)
    target = block_slots[0].reshape(-1) * tiles_t + chosen.reshape(-1)
    owner_count = lax.axis_size("doc")
    capacity = max(2, 2 * posted.shape[0] // owner_count)
    onehot = (owners[:, None] == jnp.arange(owner_count, dtype=jnp.int32)[None, :]).astype(
        jnp.int32
    )
    before = jnp.cumsum(onehot, axis=0) - onehot
    position = jnp.sum(before * onehot, axis=1)
    dest = owners * capacity + position
    outgoing = jnp.zeros((owner_count * capacity, TILE), jnp.bfloat16).at[dest].set(posted)
    out_tags = jnp.full((owner_count * capacity,), slots_total, jnp.int32).at[dest].set(target)
    got_vals, got_tags = (
        lax.all_to_all(
            outgoing.reshape(owner_count, capacity, TILE),
            "doc",
            split_axis=0,
            concat_axis=0,
            tiled=True,
        ),
        lax.all_to_all(
            out_tags.reshape(owner_count, capacity), "doc", split_axis=0, concat_axis=0, tiled=True
        ),
    )
    got_vals = got_vals.reshape(-1, TILE)
    local_tags = got_tags.reshape(-1)
    summary = jnp.zeros((slots_total, TILE), jnp.bfloat16).at[local_tags].max(got_vals, mode="drop")
    return (impacts, summary.reshape(BLK_DEV, tiles_t * TILE))


def dot_t(left, right):
    return lax.dot_general(
        left, right, (((1,), (1,)), ((), ())), preferred_element_type=jnp.float32
    )


def table_of(ref):
    return ref[ref.shape[0] - SLOT_ROWS :, 0:TILE].astype(jnp.float32)[0:1, :]


def masked(ref, table_ref, seq):
    here = ref[0:seq, :]
    length = table_of(table_ref)[:, TILE - 1 :]
    keep = lax.broadcasted_iota(jnp.int32, here.shape, 0).astype(jnp.float32) < length
    first = jnp.broadcast_to(here[0:1, :].astype(jnp.float32), here.shape).astype(here.dtype)
    return jnp.where(keep, here, first)


def normed_rows(docs, tables, seq, weight, params):
    rows = [masked(ref, table, seq) for ref, table in zip(docs, tables)]
    rows = jnp.concatenate(rows, axis=0)
    pre = jnp.dot(rows, weight[...], preferred_element_type=jnp.float32) + params[0:1, :]
    act = 0.5 * pre * (1.0 + lax.erf(pre * (0.5**0.5)))
    return layer_norm(act.astype(jnp.bfloat16), params[1:2, :], params[2:3, :])


def tops_of(normed, w_ref, count):
    logits = dot_t(normed, w_ref[...])
    seq = normed.shape[0] // count
    return [
        jnp.max(logits[j * seq : (j + 1) * seq], axis=0, keepdims=True) for j in range(count)
    ]


def start_kernel(tiles_ref, owners_ref, slots_ref, length_ref, *refs):
    hidden_ref, weight_ref, vectors = refs[0], refs[1], refs[2:5]
    load_ref, block_ref, table_ref, rows_ref, kept, sems = refs[5:]
    seq, width = hidden_ref.shape
    copies = [
        fetch(hidden_ref, load_ref.at[pl.ds(0, seq), :], sems.at[0]),
        fetch(weight_ref, block_ref, sems.at[1]),
    ]
    for k, ref in enumerate(vectors):
        copies.append(fetch(ref, kept.at[pl.ds(k * width, width)], sems.at[2 + k]))
    lane = lax.broadcasted_iota(jnp.int32, (SLOT_ROWS, TILE), 1)
    table = jnp.where(lane == TILE - 1, length_ref[0], -1)
    devices = lax.axis_size("doc")
    for k in range(tiles_ref.shape[2]):
        block = slots_ref[0, 0, k] * devices + owners_ref[0, 0, k]
        table = jnp.where(lane == tiles_ref[0, 0, k], block, table)
    table = table.astype(jnp.float32).astype(jnp.bfloat16)
    for first in range(0, width, TILE):
        load_ref[seq:, first : first + TILE] = table
        table_ref[:, first : first + TILE] = table
    for copy in copies:
        copy.wait()
    for k in range(len(vectors)):
        rows_ref[k : k + 1, :] = kept[pl.ds(k * width, width)][None, :]


def pile_kernel(parts, heights, *refs):
    rows = jnp.concatenate(
        [ref[first : first + count, :] for ref, (first, count) in zip(refs, parts)], axis=0
    )
    at = 0
    for ref, height in zip(refs[len(parts) :], heights):
        ref[...] = rows[at : at + height, :]
        at += height


def fetch(ref, slot, sem):
    copy = pltpu.make_async_copy(ref, slot, sem)
    copy.start()
    return copy


def keep_tops(normed, halves, bests):
    for w_ref, best in zip(halves, bests):
        for j, top in enumerate(tops_of(normed, w_ref, 2)):
            best[j : j + 1, :] = top


def first_kernel(seq, masks, *refs):
    me_ref, docs, refs = refs[0], refs[1:3], refs[3:]
    mine_parts, their_parts, refs = refs[:3], refs[3:6], refs[6:]
    params, theirs_ref, late, refs = refs[0], refs[1], refs[2:5], refs[5:]
    best_mine, best_theirs, weight, kept, sems = refs[0], refs[1], refs[2], refs[3:6], refs[6]
    copies = [fetch(ref, to, sems.at[k]) for k, (ref, to) in enumerate(zip(late, kept))]
    me = me_ref[0]
    core = me % 2
    rows = weight.shape[0] // (2 * len(masks))
    packed = jnp.concatenate([ref[...] for ref in mine_parts], axis=0)
    others = jnp.concatenate([ref[...] for ref in their_parts], axis=0)
    for k, mask in enumerate(masks):
        chip = (me // 2) ^ mask
        block = slice(k * rows, (k + 1) * rows)
        at = pl.multiple_of((2 * chip + core) * rows, SLOT_ROWS)
        weight[pl.ds(at, rows), :] = packed[block, :]
        at = pl.multiple_of((2 * chip + 1 - core) * rows, SLOT_ROWS)
        weight[pl.ds(at, rows), :] = others[block, :]
    normed = normed_rows(docs, docs, seq, weight, params)
    keep_tops(normed, [theirs_ref], [best_theirs])
    for copy in copies:
        copy.wait()
    keep_tops(normed, [kept[0]], [best_mine])


def next_kernel(seq, *refs):
    docs, tables, weight, params, refs = refs[:2], refs[2:4], refs[4], refs[5], refs[6:]
    keep_tops(normed_rows(docs, tables, seq, weight, params), refs[:2], refs[2:])


def last_kernel(seq, masks, *refs):
    me_ref, docs, tables, refs = refs[0], refs[1:3], refs[3 : 3 + len(masks)], refs[3 + len(masks) :]
    weight, params, halves, dbias_ref, refs = refs[0], refs[1], refs[2:4], refs[4], refs[5:]
    earlier, out_ref, send = refs[:-2], refs[-2], refs[-1]
    me = me_ref[0]
    core, chip = me % 2, me // 2
    devices = 2 * len(masks)
    tiles = 2 * halves[0].shape[0] // TILE
    normed = normed_rows(docs, docs, seq, weight, params)
    found = []
    for k, w_ref in enumerate(halves):
        parts = [ref[0:2, :] for ref in earlier[k::2]]
        found.append(jnp.concatenate([*parts, *tops_of(normed, w_ref, 2)], axis=0))
    low = jnp.where(core == 0, found[0], found[1])
    high = jnp.where(core == 0, found[1], found[0])
    logits = jnp.concatenate([low, high], axis=1)
    docs_at = [me ^ (2 * mask) for mask in masks]
    bias = dbias_ref[...]
    bias = pltpu.roll(bias, bias.shape[0] - chip * tiles, 0)
    tables = jnp.concatenate([table_of(ref) for ref in tables], axis=0)
    tables = pltpu.roll(tables, TILE - chip * tiles, 1).astype(jnp.int32)
    send[...] = jnp.zeros(send.shape, jnp.float32)
    stride = out_ref.shape[1]
    target = lax.broadcasted_iota(jnp.int32, (BLK_DEV * devices, TILE), 0)
    for t in range(tiles):
        lanes = slice(t * TILE, (t + 1) * TILE)
        impacts = jnp.log1p(jnp.maximum(logits[:, lanes] + bias[t : t + 1, :], 0.0))
        impacts = impacts.astype(jnp.bfloat16).astype(jnp.float32)
        blocks = jnp.zeros((BLK_DEV * devices, TILE), jnp.float32)
        for n in range(len(masks)):
            row = impacts[n : n + 1, :]
            send[pl.ds(docs_at[n] * stride + t, 1), :] = row
            block = jnp.broadcast_to(tables[n : n + 1, t : t + 1], target.shape)
            blocks = jnp.maximum(blocks, jnp.where(target == block, row, 0.0))
        for s in range(BLK_DEV):
            send[pl.ds((1 + s) * SLOT_ROWS + t, devices, stride=stride), :] = blocks[
                s * devices : (s + 1) * devices
            ]
    out_ref[...] = send[...].astype(jnp.bfloat16).reshape(out_ref.shape)


def move_tokens(
    hidden_states,
    doc_lengths,
    transform_weight,
    transform_bias,
    norm_gain,
    norm_bias,
    decoder_weight,
    decoder_bias,
    tile_ids,
    owner_ids,
    block_slots,
):
    devices = lax.axis_size("doc")
    chips = devices // 2
    seq, width = hidden_states.shape
    rows = transform_weight.shape[0]
    half = decoder_weight.shape[2]
    tiles = 2 * half // TILE
    me = lax.axis_index("doc").astype(jnp.int32)

    def cross(value, mask):
        return lax.ppermute(value, "doc", [(i, i ^ (2 * mask)) for i in range(devices)])

    def swap(value):
        return lax.ppermute(value, "doc", [(i, i ^ 1) for i in range(devices)])

    smem = pl.BlockSpec(memory_space=pltpu.SMEM)
    vmem = pl.BlockSpec(memory_space=pltpu.VMEM)
    hbm = pl.BlockSpec(memory_space=pltpu.HBM)

    def stay(value):
        return pltpu.with_memory_space_constraint(value, pltpu.HBM)

    limit = pltpu.CompilerParams(vmem_limit_bytes=24 * 1024 * 1024)

    def cost(docs):
        return pl.CostEstimate(flops=docs, bytes_accessed=docs, transcendentals=0)

    def shape(dims, dtype):
        return jax.ShapeDtypeStruct(dims, dtype)

    def after(value, *done):
        return lax.optimization_barrier((value, *done))[0]

    def pile(values, parts, heights=()):
        heights = heights or (sum(count for _, count in parts),)
        piled = pl.pallas_call(
            lambda *refs: pile_kernel(parts, heights, *refs),
            out_shape=[shape((height, width), jnp.bfloat16) for height in heights],
            in_specs=[vmem] * len(values),
            out_specs=[vmem] * len(heights),
            compiler_params=limit,
        )(*values)
        return piled if len(heights) > 1 else piled[0]

    weight_rows = jnp.swapaxes(decoder_weight[0], 0, 1)
    block_6 = cross(transform_weight, 6)
    block_2 = cross(transform_weight, 2)
    theirs = swap(weight_rows)
    docs = {1: cross(hidden_states, 1)}
    load, block, table, params = pl.pallas_call(
        start_kernel,
        out_shape=[
            shape((seq + SLOT_ROWS, width), jnp.bfloat16),
            shape((rows, width), jnp.bfloat16),
            shape((SLOT_ROWS, width), jnp.bfloat16),
            shape((8, width), jnp.float32),
        ],
        in_specs=[smem] * 4 + [hbm] * 5,
        out_specs=[vmem] * 4,
        scratch_shapes=[
            pltpu.VMEM((3 * width,), jnp.float32),
            pltpu.SemaphoreType.DMA((5,)),
        ],
        compiler_params=limit,
    )(
        stay(tile_ids),
        stay(owner_ids[..., 0]),
        stay(block_slots),
        doc_lengths,
        stay(hidden_states),
        stay(transform_weight),
        stay(transform_bias),
        stay(norm_gain),
        stay(norm_bias),
    )
    near = (block, after(block_2, block_6, docs[1]), table)
    near_pile = cross(pile(near, ((0, rows), (0, rows), (0, SLOT_ROWS))), 1)
    block_4 = cross(block_6, 2)
    docs[6] = cross(after(load, block_6), 6)
    docs[2] = cross(after(load, block_4), 2)
    load_1 = pile((docs[1], near_pile), ((0, seq), (2 * rows, SLOT_ROWS)))
    far = (block_6, after(block_4, near_pile))
    far = pile(far, ((0, rows), (0, rows)))
    far_pile = cross(far, 1)
    docs[3] = cross(after(load_1, far), 2)
    docs[4] = cross(after(docs[6], far), 2)
    docs[7] = cross(docs[6], 1)
    late = (docs[2], docs[3], docs[6], theirs)
    one, two = (0, rows), (0, 2 * rows)
    sources = (after(block, *late), block_2, block_6, block_4, near_pile, far_pile)
    thirds = pile(sources, (one, one, one, one, two, two), (seq,) * 3)
    other_thirds = [swap(third) for third in thirds]
    block_masks = [0, 2, 6, 4, 1, 3, 7, 5]

    masks = [2, 3, 0, 1, 6, 7, 4, 5]
    where = me[None]
    best_shape = shape((8, half), jnp.float32)
    *best, weight, mine, own, beside = pl.pallas_call(
        lambda *refs: first_kernel(seq, block_masks, *refs),
        out_shape=[
            best_shape,
            best_shape,
            shape((width, width), jnp.bfloat16),
            shape((half, width), jnp.bfloat16),
            shape((seq, width), jnp.bfloat16),
            shape((seq, width), jnp.bfloat16),
        ],
        in_specs=[smem] + [vmem] * 10 + [hbm] * 3,
        out_specs=[vmem] * 6,
        scratch_shapes=[pltpu.SemaphoreType.DMA((3,))],
        compiler_params=limit,
        cost_estimate=cost(2),
    )(
        where,
        docs[2],
        docs[3],
        *thirds,
        *other_thirds,
        params,
        theirs,
        stay(weight_rows),
        stay(hidden_states),
        stay(docs[1]),
    )
    docs |= {0: own, 1: beside, 5: cross(after(docs[4], weight), 1)}
    tables = docs | {0: table, 1: near_pile}
    for first in range(2, len(masks) - 2, 2):
        pair = masks[first : first + 2]
        best += pl.pallas_call(
            lambda *refs: next_kernel(seq, *refs),
            out_shape=[best_shape] * 2,
            in_specs=[vmem] * 8,
            out_specs=[vmem] * 2,
            compiler_params=limit,
            cost_estimate=cost(2),
        )(
            *[docs[mask] for mask in pair],
            *[tables[mask] for mask in pair],
            weight,
            params,
            mine,
            theirs,
        )
    send = pl.pallas_call(
        lambda *refs: last_kernel(seq, masks, *refs),
        out_shape=shape((devices, (1 + BLK_DEV) * SLOT_ROWS, TILE), jnp.bfloat16),
        in_specs=[smem] + [vmem] * (2 + len(masks) + 5 + len(best)),
        out_specs=vmem,
        scratch_shapes=[
            pltpu.VMEM((devices * (1 + BLK_DEV) * SLOT_ROWS, TILE), jnp.float32),
        ],
        compiler_params=limit,
        cost_estimate=cost(2),
    )(
        where,
        *[docs[mask] for mask in masks[-2:]],
        *[tables[mask] for mask in masks],
        weight,
        params,
        mine,
        theirs,
        decoder_bias.reshape(-1, TILE),
        *best,
    )
    got = lax.all_to_all(send, "doc", split_axis=0, concat_axis=0, tiled=True)
    got = got.reshape(chips, 2, 1 + BLK_DEV, SLOT_ROWS, TILE)[:, :, :, :tiles]
    whole = jnp.swapaxes(jnp.maximum(got[:, 0], got[:, 1]), 0, 1).reshape(1 + BLK_DEV, -1)
    return (whole[:1], whole[1:])


def tokens_move(mesh):
    return mesh.shape["term"] == 1 and mesh.shape["doc"] == 16


def solution(mesh):
    placed = (
        P(("groups", "doc"), None),
        P(("groups", "doc")),
        P("doc", "term"),
        P(),
        P(),
        P(),
        P("term", None, "doc"),
        P("term"),
        P("term", ("groups", "doc"), None),
        P("term", ("groups", "doc"), None, None),
        P("term", ("groups", "doc"), None),
    )

    def local(*args):
        pair = 2 * args[6].shape[2]
        tiles = pair * (mesh.shape["doc"] // 2) // TILE
        fits = pair % TILE == 0 and tiles < TILE and pair // TILE <= SLOT_ROWS
        if tokens_move(mesh) and args[1].shape[0] == 1 and fits:
            return move_tokens(*args)
        return move_weights(*args)

    return jax.shard_map(
        local,
        mesh=mesh,
        in_specs=placed,
        out_specs=(P(("groups", "doc"), "term"), P(("groups", "doc"), "term")),
        check_vma=False,
    )
```

```python
import jax
import jax.numpy as jnp
from jax import lax
from jax.experimental import pallas as pl
from jax.experimental.pallas import tpu as pltpu
from jax.sharding import PartitionSpec as P

TILE = 128
BLK_DEV = 2
SLOT_ROWS = 16


def layer_norm(activated, norm_gain, norm_bias):
    values = activated.astype(jnp.float32)
    centre = jnp.mean(values, axis=-1, keepdims=True)
    centred = values - centre
    spread = jnp.mean(centred * centred, axis=-1, keepdims=True)
    return (centred * lax.rsqrt(spread + 1e-05) * norm_gain + norm_bias).astype(jnp.bfloat16)


def pool_docs(logits, keep):
    docs_here = keep.shape[0]
    saturated = jnp.log1p(jnp.maximum(logits, 0.0)).reshape(
        docs_here, keep.shape[1], logits.shape[1]
    )
    return jnp.max(jnp.where(keep[:, :, None], saturated, 0.0), axis=1)


def move_weights(
    hidden_states,
    doc_lengths,
    transform_weight,
    transform_bias,
    norm_gain,
    norm_bias,
    decoder_weight,
    decoder_bias,
    tile_ids,
    owner_ids,
    block_slots,
):
    tok_rows = hidden_states.shape[0]
    docs_here = doc_lengths.shape[0]
    seq_len = tok_rows // docs_here
    cols = transform_weight.shape[1]
    pre_half = jnp.dot(
        hidden_states,
        lax.all_gather(transform_weight, "doc", axis=0, tiled=True),
        preferred_element_type=jnp.float32,
    )
    bias_half = lax.dynamic_slice_in_dim(transform_bias, lax.axis_index("term") * cols, cols, 0)
    act_half = jax.nn.gelu(pre_half + bias_half, approximate=False).astype(jnp.bfloat16)
    activated = lax.all_gather(act_half, "term", axis=1, tiled=True)
    normed = layer_norm(activated, norm_gain, norm_bias)
    keep = jnp.arange(seq_len, dtype=jnp.int32)[None, :] < doc_lengths[:, None]
    logits = jnp.dot(
        normed,
        lax.all_gather(decoder_weight, "doc", axis=2, tiled=True)[0],
        preferred_element_type=jnp.float32,
    )
    logits = logits + decoder_bias
    impacts = pool_docs(logits, keep).astype(jnp.bfloat16)
    tiles_t = impacts.shape[1] // TILE
    slots_total = BLK_DEV * tiles_t
    tiles = impacts.reshape(docs_here * tiles_t, TILE)
    chosen = tile_ids[0]
    doc_index = jnp.arange(docs_here, dtype=jnp.int32)[:, None]
    posted = tiles[(doc_index * tiles_t + chosen).reshape(-1)]
    owners = owner_ids[0, :, :, 0].reshape(-1)
    target = block_slots[0].reshape(-1) * tiles_t + chosen.reshape(-1)
    owner_count = lax.axis_size("doc")
    capacity = max(2, 2 * posted.shape[0] // owner_count)
    onehot = (owners[:, None] == jnp.arange(owner_count, dtype=jnp.int32)[None, :]).astype(
        jnp.int32
    )
    before = jnp.cumsum(onehot, axis=0) - onehot
    position = jnp.sum(before * onehot, axis=1)
    dest = owners * capacity + position
    outgoing = jnp.zeros((owner_count * capacity, TILE), jnp.bfloat16).at[dest].set(posted)
    out_tags = jnp.full((owner_count * capacity,), slots_total, jnp.int32).at[dest].set(target)
    got_vals, got_tags = (
        lax.all_to_all(
            outgoing.reshape(owner_count, capacity, TILE),
            "doc",
            split_axis=0,
            concat_axis=0,
            tiled=True,
        ),
        lax.all_to_all(
            out_tags.reshape(owner_count, capacity), "doc", split_axis=0, concat_axis=0, tiled=True
        ),
    )
    got_vals = got_vals.reshape(-1, TILE)
    local_tags = got_tags.reshape(-1)
    summary = jnp.zeros((slots_total, TILE), jnp.bfloat16).at[local_tags].max(got_vals, mode="drop")
    return (impacts, summary.reshape(BLK_DEV, tiles_t * TILE))


def dot_t(left, right):
    return lax.dot_general(
        left, right, (((1,), (1,)), ((), ())), preferred_element_type=jnp.float32
    )


def table_of(ref):
    return ref[ref.shape[0] - SLOT_ROWS :, 0:TILE].astype(jnp.float32)[0:1, :]


def masked(ref, table_ref, seq):
    here = ref[0:seq, :]
    length = table_of(table_ref)[:, TILE - 1 :]
    keep = lax.broadcasted_iota(jnp.int32, here.shape, 0).astype(jnp.float32) < length
    first = jnp.broadcast_to(here[0:1, :].astype(jnp.float32), here.shape).astype(here.dtype)
    return jnp.where(keep, here, first)


def normed_rows(docs, tables, seq, weight, params):
    rows = [masked(ref, table, seq) for ref, table in zip(docs, tables)]
    rows = jnp.concatenate(rows, axis=0)
    pre = jnp.dot(rows, weight[...], preferred_element_type=jnp.float32) + params[0:1, :]
    act = 0.5 * pre * (1.0 + lax.erf(pre * (0.5**0.5)))
    return layer_norm(act.astype(jnp.bfloat16), params[1:2, :], params[2:3, :])


def tops_of(normed, w_ref, count):
    logits = dot_t(normed, w_ref[...])
    seq = normed.shape[0] // count
    return [
        jnp.max(logits[j * seq : (j + 1) * seq], axis=0, keepdims=True) for j in range(count)
    ]


def start_kernel(tiles_ref, owners_ref, slots_ref, length_ref, *refs):
    hidden_ref, weight_ref, vectors = refs[0], refs[1], refs[2:5]
    load_ref, block_ref, table_ref, rows_ref, kept, sems = refs[5:]
    seq, width = hidden_ref.shape
    copies = [
        fetch(hidden_ref, load_ref.at[pl.ds(0, seq), :], sems.at[0]),
        fetch(weight_ref, block_ref, sems.at[1]),
    ]
    for k, ref in enumerate(vectors):
        copies.append(fetch(ref, kept.at[pl.ds(k * width, width)], sems.at[2 + k]))
    lane = lax.broadcasted_iota(jnp.int32, (SLOT_ROWS, TILE), 1)
    table = jnp.where(lane == TILE - 1, length_ref[0], -1)
    devices = lax.axis_size("doc")
    for k in range(tiles_ref.shape[2]):
        block = slots_ref[0, 0, k] * devices + owners_ref[0, 0, k]
        table = jnp.where(lane == tiles_ref[0, 0, k], block, table)
    table = table.astype(jnp.float32).astype(jnp.bfloat16)
    for first in range(0, width, TILE):
        load_ref[seq:, first : first + TILE] = table
        table_ref[:, first : first + TILE] = table
    for copy in copies:
        copy.wait()
    for k in range(len(vectors)):
        rows_ref[k : k + 1, :] = kept[pl.ds(k * width, width)][None, :]


def pile_kernel(parts, heights, *refs):
    rows = jnp.concatenate(
        [ref[first : first + count, :] for ref, (first, count) in zip(refs, parts)], axis=0
    )
    at = 0
    for ref, height in zip(refs[len(parts) :], heights):
        ref[...] = rows[at : at + height, :]
        at += height


def fetch(ref, slot, sem):
    copy = pltpu.make_async_copy(ref, slot, sem)
    copy.start()
    return copy


def keep_tops(normed, halves, bests):
    for w_ref, best in zip(halves, bests):
        for j, top in enumerate(tops_of(normed, w_ref, 2)):
            best[j : j + 1, :] = top


def fetch_kernel(count, *refs):
    copies = [fetch(refs[1 + k], refs[1 + count + k], refs[-1].at[k]) for k in range(count)]
    for copy in copies:
        copy.wait()


def first_kernel(seq, masks, *refs):
    me_ref, docs, tables, refs = refs[0], refs[1:3], refs[3:5], refs[5:]
    mine_parts, their_parts, params, halves, refs = refs[:3], refs[3:6], refs[6], refs[7:9], refs[9:]
    bests, weight = refs[:2], refs[2]
    me = me_ref[0]
    core = me % 2
    rows = weight.shape[0] // (2 * len(masks))
    packed = jnp.concatenate([ref[...] for ref in mine_parts], axis=0)
    others = jnp.concatenate([ref[...] for ref in their_parts], axis=0)
    for k, mask in enumerate(masks):
        chip = (me // 2) ^ mask
        block = slice(k * rows, (k + 1) * rows)
        at = pl.multiple_of((2 * chip + core) * rows, SLOT_ROWS)
        weight[pl.ds(at, rows), :] = packed[block, :]
        at = pl.multiple_of((2 * chip + 1 - core) * rows, SLOT_ROWS)
        weight[pl.ds(at, rows), :] = others[block, :]
    keep_tops(normed_rows(docs, tables, seq, weight, params), halves, bests)


def next_kernel(seq, *refs):
    docs, tables, weight, params, refs = refs[:2], refs[2:4], refs[4], refs[5], refs[6:]
    keep_tops(normed_rows(docs, tables, seq, weight, params), refs[:2], refs[2:])


def last_kernel(seq, masks, *refs):
    me_ref, docs, tables, refs = refs[0], refs[1:3], refs[3 : 3 + len(masks)], refs[3 + len(masks) :]
    weight, params, halves, dbias_ref, refs = refs[0], refs[1], refs[2:4], refs[4], refs[5:]
    earlier, out_ref, send = refs[:-2], refs[-2], refs[-1]
    me = me_ref[0]
    core, chip = me % 2, me // 2
    devices = 2 * len(masks)
    tiles = 2 * halves[0].shape[0] // TILE
    normed = normed_rows(docs, docs, seq, weight, params)
    found = []
    for k, w_ref in enumerate(halves):
        parts = [ref[0:2, :] for ref in earlier[k::2]]
        found.append(jnp.concatenate([*parts, *tops_of(normed, w_ref, 2)], axis=0))
    low = jnp.where(core == 0, found[0], found[1])
    high = jnp.where(core == 0, found[1], found[0])
    logits = jnp.concatenate([low, high], axis=1)
    docs_at = [me ^ (2 * mask) for mask in masks]
    bias = dbias_ref[...]
    bias = pltpu.roll(bias, bias.shape[0] - chip * tiles, 0)
    tables = jnp.concatenate([table_of(ref) for ref in tables], axis=0)
    tables = pltpu.roll(tables, TILE - chip * tiles, 1).astype(jnp.int32)
    send[...] = jnp.zeros(send.shape, jnp.float32)
    stride = out_ref.shape[1]
    target = lax.broadcasted_iota(jnp.int32, (BLK_DEV * devices, TILE), 0)
    for t in range(tiles):
        lanes = slice(t * TILE, (t + 1) * TILE)
        impacts = jnp.log1p(jnp.maximum(logits[:, lanes] + bias[t : t + 1, :], 0.0))
        impacts = impacts.astype(jnp.bfloat16).astype(jnp.float32)
        blocks = jnp.zeros((BLK_DEV * devices, TILE), jnp.float32)
        for n in range(len(masks)):
            row = impacts[n : n + 1, :]
            send[pl.ds(docs_at[n] * stride + t, 1), :] = row
            block = jnp.broadcast_to(tables[n : n + 1, t : t + 1], target.shape)
            blocks = jnp.maximum(blocks, jnp.where(target == block, row, 0.0))
        for s in range(BLK_DEV):
            send[pl.ds((1 + s) * SLOT_ROWS + t, devices, stride=stride), :] = blocks[
                s * devices : (s + 1) * devices
            ]
    out_ref[...] = send[...].astype(jnp.bfloat16).reshape(out_ref.shape)


def move_tokens(
    hidden_states,
    doc_lengths,
    transform_weight,
    transform_bias,
    norm_gain,
    norm_bias,
    decoder_weight,
    decoder_bias,
    tile_ids,
    owner_ids,
    block_slots,
):
    devices = lax.axis_size("doc")
    chips = devices // 2
    seq, width = hidden_states.shape
    rows = transform_weight.shape[0]
    half = decoder_weight.shape[2]
    tiles = 2 * half // TILE
    me = lax.axis_index("doc").astype(jnp.int32)

    def cross(value, mask):
        return lax.ppermute(value, "doc", [(i, i ^ (2 * mask)) for i in range(devices)])

    def swap(value):
        return lax.ppermute(value, "doc", [(i, i ^ 1) for i in range(devices)])

    smem = pl.BlockSpec(memory_space=pltpu.SMEM)
    vmem = pl.BlockSpec(memory_space=pltpu.VMEM)
    hbm = pl.BlockSpec(memory_space=pltpu.HBM)

    def stay(value):
        return pltpu.with_memory_space_constraint(value, pltpu.HBM)

    limit = pltpu.CompilerParams(vmem_limit_bytes=24 * 1024 * 1024)

    def cost(docs):
        return pl.CostEstimate(flops=docs, bytes_accessed=docs, transcendentals=0)

    def shape(dims, dtype):
        return jax.ShapeDtypeStruct(dims, dtype)

    def after(value, *done):
        return lax.optimization_barrier((value, *done))[0]

    def pile(values, parts, heights=()):
        heights = heights or (sum(count for _, count in parts),)
        piled = pl.pallas_call(
            lambda *refs: pile_kernel(parts, heights, *refs),
            out_shape=[shape((height, width), jnp.bfloat16) for height in heights],
            in_specs=[vmem] * len(values),
            out_specs=[vmem] * len(heights),
            compiler_params=limit,
        )(*values)
        return piled if len(heights) > 1 else piled[0]

    weight_rows = jnp.swapaxes(decoder_weight[0], 0, 1)
    block_6 = cross(transform_weight, 6)
    block_2 = cross(transform_weight, 2)
    theirs = swap(weight_rows)
    docs = {1: cross(hidden_states, 1)}
    load, block, table, params = pl.pallas_call(
        start_kernel,
        out_shape=[
            shape((seq + SLOT_ROWS, width), jnp.bfloat16),
            shape((rows, width), jnp.bfloat16),
            shape((SLOT_ROWS, width), jnp.bfloat16),
            shape((8, width), jnp.float32),
        ],
        in_specs=[smem] * 4 + [hbm] * 5,
        out_specs=[vmem] * 4,
        scratch_shapes=[
            pltpu.VMEM((3 * width,), jnp.float32),
            pltpu.SemaphoreType.DMA((5,)),
        ],
        compiler_params=limit,
    )(
        stay(tile_ids),
        stay(owner_ids[..., 0]),
        stay(block_slots),
        doc_lengths,
        stay(hidden_states),
        stay(transform_weight),
        stay(transform_bias),
        stay(norm_gain),
        stay(norm_bias),
    )
    near = (block, after(block_2, block_6, docs[1]), table)
    near_pile = cross(pile(near, ((0, rows), (0, rows), (0, SLOT_ROWS))), 1)
    block_4 = cross(block_6, 2)
    docs[6] = cross(after(load, block_6), 6)
    docs[2] = cross(after(load, block_4), 2)
    load_1 = pile((docs[1], near_pile), ((0, seq), (2 * rows, SLOT_ROWS)))
    far = (block_6, after(block_4, near_pile))
    far = pile(far, ((0, rows), (0, rows)))
    far_pile = cross(far, 1)
    docs[3] = cross(after(load_1, far), 2)
    docs[4] = cross(after(docs[6], far, docs[2]), 2)
    docs[7] = cross(docs[6], 1)
    late = (docs[6], theirs)
    one, two = (0, rows), (0, 2 * rows)
    sources = (after(block, *late), block_2, block_6, block_4, near_pile, far_pile)
    thirds = pile(sources, (one, one, one, one, two, two), (seq,) * 3)
    other_thirds = [swap(third) for third in thirds]
    block_masks = [0, 2, 6, 4, 1, 3, 7, 5]

    far_from = [stay(after(weight_rows, *thirds)), stay(docs[1])]
    mine, beside = pl.pallas_call(
        lambda *refs: fetch_kernel(2, *refs),
        out_shape=[shape(value.shape, value.dtype) for value in far_from],
        in_specs=[vmem] + [hbm] * 2,
        out_specs=[vmem] * 2,
        scratch_shapes=[pltpu.SemaphoreType.DMA((2,))],
        compiler_params=limit,
    )(thirds[0], *far_from)

    masks = [0, 1, 6, 7, 2, 3, 4, 5]
    where = me[None]
    best_shape = shape((8, half), jnp.float32)
    *best, weight = pl.pallas_call(
        lambda *refs: first_kernel(seq, block_masks, *refs),
        out_shape=[best_shape, best_shape, shape((width, width), jnp.bfloat16)],
        in_specs=[smem] + [vmem] * 13,
        out_specs=[vmem] * 3,
        compiler_params=limit,
        cost_estimate=cost(2),
    )(
        where,
        load,
        beside,
        table,
        near_pile,
        *thirds,
        *other_thirds,
        params,
        mine,
        theirs,
    )
    docs |= {0: load, 1: beside, 5: cross(after(docs[4], weight), 1)}
    tables = docs | {1: near_pile}
    for first in range(2, len(masks) - 2, 2):
        pair = masks[first : first + 2]
        best += pl.pallas_call(
            lambda *refs: next_kernel(seq, *refs),
            out_shape=[best_shape] * 2,
            in_specs=[vmem] * 8,
            out_specs=[vmem] * 2,
            compiler_params=limit,
            cost_estimate=cost(2),
        )(
            *[docs[mask] for mask in pair],
            *[tables[mask] for mask in pair],
            after(weight, best[-1]),
            params,
            mine,
            theirs,
        )
    send = pl.pallas_call(
        lambda *refs: last_kernel(seq, masks, *refs),
        out_shape=shape((devices, (1 + BLK_DEV) * SLOT_ROWS, TILE), jnp.bfloat16),
        in_specs=[smem] + [vmem] * (2 + len(masks) + 5 + len(best)),
        out_specs=vmem,
        scratch_shapes=[
            pltpu.VMEM((devices * (1 + BLK_DEV) * SLOT_ROWS, TILE), jnp.float32),
        ],
        compiler_params=limit,
        cost_estimate=cost(2),
    )(
        where,
        *[docs[mask] for mask in masks[-2:]],
        *[tables[mask] for mask in masks],
        weight,
        params,
        mine,
        theirs,
        decoder_bias.reshape(-1, TILE),
        *best,
    )
    got = lax.all_to_all(send, "doc", split_axis=0, concat_axis=0, tiled=True)
    got = got.reshape(chips, 2, 1 + BLK_DEV, SLOT_ROWS, TILE)[:, :, :, :tiles]
    whole = jnp.swapaxes(jnp.maximum(got[:, 0], got[:, 1]), 0, 1).reshape(1 + BLK_DEV, -1)
    return (whole[:1], whole[1:])


def tokens_move(mesh):
    return mesh.shape["term"] == 1 and mesh.shape["doc"] == 16


def solution(mesh):
    placed = (
        P(("groups", "doc"), None),
        P(("groups", "doc")),
        P("doc", "term"),
        P(),
        P(),
        P(),
        P("term", None, "doc"),
        P("term"),
        P("term", ("groups", "doc"), None),
        P("term", ("groups", "doc"), None, None),
        P("term", ("groups", "doc"), None),
    )

    def local(*args):
        pair = 2 * args[6].shape[2]
        tiles = pair * (mesh.shape["doc"] // 2) // TILE
        fits = pair % TILE == 0 and tiles < TILE and pair // TILE <= SLOT_ROWS
        if tokens_move(mesh) and args[1].shape[0] == 1 and fits:
            return move_tokens(*args)
        return move_weights(*args)

    return jax.shard_map(
        local,
        mesh=mesh,
        in_specs=placed,
        out_specs=(P(("groups", "doc"), "term"), P(("groups", "doc"), "term")),
        check_vma=False,
    )
```

```python
import jax
import jax.numpy as jnp
from jax import lax
from jax.experimental import pallas as pl
from jax.experimental.pallas import tpu as pltpu
from jax.sharding import PartitionSpec as P

TILE = 128
BLK_DEV = 2
SLOT_ROWS = 16


def layer_norm(activated, norm_gain, norm_bias):
    values = activated.astype(jnp.float32)
    centre = jnp.mean(values, axis=-1, keepdims=True)
    centred = values - centre
    spread = jnp.mean(centred * centred, axis=-1, keepdims=True)
    return (centred * lax.rsqrt(spread + 1e-05) * norm_gain + norm_bias).astype(jnp.bfloat16)


def pool_docs(logits, keep):
    docs_here = keep.shape[0]
    saturated = jnp.log1p(jnp.maximum(logits, 0.0)).reshape(
        docs_here, keep.shape[1], logits.shape[1]
    )
    return jnp.max(jnp.where(keep[:, :, None], saturated, 0.0), axis=1)


def move_weights(
    hidden_states,
    doc_lengths,
    transform_weight,
    transform_bias,
    norm_gain,
    norm_bias,
    decoder_weight,
    decoder_bias,
    tile_ids,
    owner_ids,
    block_slots,
):
    tok_rows = hidden_states.shape[0]
    docs_here = doc_lengths.shape[0]
    seq_len = tok_rows // docs_here
    cols = transform_weight.shape[1]
    pre_half = jnp.dot(
        hidden_states,
        lax.all_gather(transform_weight, "doc", axis=0, tiled=True),
        preferred_element_type=jnp.float32,
    )
    bias_half = lax.dynamic_slice_in_dim(transform_bias, lax.axis_index("term") * cols, cols, 0)
    act_half = jax.nn.gelu(pre_half + bias_half, approximate=False).astype(jnp.bfloat16)
    activated = lax.all_gather(act_half, "term", axis=1, tiled=True)
    normed = layer_norm(activated, norm_gain, norm_bias)
    keep = jnp.arange(seq_len, dtype=jnp.int32)[None, :] < doc_lengths[:, None]
    logits = jnp.dot(
        normed,
        lax.all_gather(decoder_weight, "doc", axis=2, tiled=True)[0],
        preferred_element_type=jnp.float32,
    )
    logits = logits + decoder_bias
    impacts = pool_docs(logits, keep).astype(jnp.bfloat16)
    tiles_t = impacts.shape[1] // TILE
    slots_total = BLK_DEV * tiles_t
    tiles = impacts.reshape(docs_here * tiles_t, TILE)
    chosen = tile_ids[0]
    doc_index = jnp.arange(docs_here, dtype=jnp.int32)[:, None]
    posted = tiles[(doc_index * tiles_t + chosen).reshape(-1)]
    owners = owner_ids[0, :, :, 0].reshape(-1)
    target = block_slots[0].reshape(-1) * tiles_t + chosen.reshape(-1)
    owner_count = lax.axis_size("doc")
    capacity = max(2, 2 * posted.shape[0] // owner_count)
    onehot = (owners[:, None] == jnp.arange(owner_count, dtype=jnp.int32)[None, :]).astype(
        jnp.int32
    )
    before = jnp.cumsum(onehot, axis=0) - onehot
    position = jnp.sum(before * onehot, axis=1)
    dest = owners * capacity + position
    outgoing = jnp.zeros((owner_count * capacity, TILE), jnp.bfloat16).at[dest].set(posted)
    out_tags = jnp.full((owner_count * capacity,), slots_total, jnp.int32).at[dest].set(target)
    got_vals, got_tags = (
        lax.all_to_all(
            outgoing.reshape(owner_count, capacity, TILE),
            "doc",
            split_axis=0,
            concat_axis=0,
            tiled=True,
        ),
        lax.all_to_all(
            out_tags.reshape(owner_count, capacity), "doc", split_axis=0, concat_axis=0, tiled=True
        ),
    )
    got_vals = got_vals.reshape(-1, TILE)
    local_tags = got_tags.reshape(-1)
    summary = jnp.zeros((slots_total, TILE), jnp.bfloat16).at[local_tags].max(got_vals, mode="drop")
    return (impacts, summary.reshape(BLK_DEV, tiles_t * TILE))


def dot_t(left, right):
    return lax.dot_general(
        left, right, (((1,), (1,)), ((), ())), preferred_element_type=jnp.float32
    )


def table_of(ref):
    return ref[ref.shape[0] - SLOT_ROWS :, 0:TILE].astype(jnp.float32)[0:1, :]


def masked(ref, table_ref, seq):
    here = ref[0:seq, :]
    length = table_of(table_ref)[:, TILE - 1 :]
    keep = lax.broadcasted_iota(jnp.int32, here.shape, 0).astype(jnp.float32) < length
    first = jnp.broadcast_to(here[0:1, :].astype(jnp.float32), here.shape).astype(here.dtype)
    return jnp.where(keep, here, first)


def normed_rows(docs, tables, seq, weight, params):
    rows = [masked(ref, table, seq) for ref, table in zip(docs, tables)]
    rows = jnp.concatenate(rows, axis=0)
    pre = jnp.dot(rows, weight[...], preferred_element_type=jnp.float32) + params[0:1, :]
    act = 0.5 * pre * (1.0 + lax.erf(pre * (0.5**0.5)))
    return layer_norm(act.astype(jnp.bfloat16), params[1:2, :], params[2:3, :])


def tops_of(normed, w_ref, count):
    logits = dot_t(normed, w_ref[...])
    seq = normed.shape[0] // count
    return [
        jnp.max(logits[j * seq : (j + 1) * seq], axis=0, keepdims=True) for j in range(count)
    ]


def start_kernel(tiles_ref, owners_ref, slots_ref, length_ref, *refs):
    hidden_ref, weight_ref, vectors = refs[0], refs[1], refs[2:5]
    load_ref, block_ref, table_ref, rows_ref, kept, sems = refs[5:]
    seq, width = hidden_ref.shape
    copies = [
        fetch(hidden_ref, load_ref.at[pl.ds(0, seq), :], sems.at[0]),
        fetch(weight_ref, block_ref, sems.at[1]),
    ]
    for k, ref in enumerate(vectors):
        copies.append(fetch(ref, kept.at[pl.ds(k * width, width)], sems.at[2 + k]))
    lane = lax.broadcasted_iota(jnp.int32, (SLOT_ROWS, TILE), 1)
    table = jnp.where(lane == TILE - 1, length_ref[0], -1)
    devices = lax.axis_size("doc")
    for k in range(tiles_ref.shape[2]):
        block = slots_ref[0, 0, k] * devices + owners_ref[0, 0, k]
        table = jnp.where(lane == tiles_ref[0, 0, k], block, table)
    table = table.astype(jnp.float32).astype(jnp.bfloat16)
    for first in range(0, width, TILE):
        load_ref[seq:, first : first + TILE] = table
        table_ref[:, first : first + TILE] = table
    for copy in copies:
        copy.wait()
    for k in range(len(vectors)):
        rows_ref[k : k + 1, :] = kept[pl.ds(k * width, width)][None, :]


def pile_kernel(parts, heights, *refs):
    rows = jnp.concatenate(
        [ref[first : first + count, :] for ref, (first, count) in zip(refs, parts)], axis=0
    )
    at = 0
    for ref, height in zip(refs[len(parts) :], heights):
        ref[...] = rows[at : at + height, :]
        at += height


def fetch(ref, slot, sem):
    copy = pltpu.make_async_copy(ref, slot, sem)
    copy.start()
    return copy


def keep_tops(normed, halves, bests):
    for w_ref, best in zip(halves, bests):
        for j, top in enumerate(tops_of(normed, w_ref, 2)):
            best[j : j + 1, :] = top


def fetch_kernel(count, *refs):
    copies = [fetch(refs[1 + k], refs[1 + count + k], refs[-1].at[k]) for k in range(count)]
    for copy in copies:
        copy.wait()


def first_kernel(seq, masks, *refs):
    me_ref, docs, tables, refs = refs[0], refs[1:3], refs[3:5], refs[5:]
    parts, others, params, halves, refs = refs[:2], refs[2:4], refs[4], refs[5:7], refs[7:]
    bests, weight = refs[:2], refs[2]
    me = me_ref[0]
    core = me % 2
    rows = weight.shape[0] // (2 * len(masks))
    for k, mask in enumerate(masks):
        chip = (me // 2) ^ mask
        part, place = divmod(k * rows, parts[0].shape[0])
        block = slice(place, place + rows)
        at = pl.multiple_of((2 * chip + core) * rows, SLOT_ROWS)
        weight[pl.ds(at, rows), :] = parts[part][block, :]
        at = pl.multiple_of((2 * chip + 1 - core) * rows, SLOT_ROWS)
        weight[pl.ds(at, rows), :] = others[part][block, :]
    keep_tops(normed_rows(docs, tables, seq, weight, params), halves, bests)


def next_kernel(seq, *refs):
    docs, tables, weight, params, refs = refs[:2], refs[2:4], refs[4], refs[5], refs[6:]
    keep_tops(normed_rows(docs, tables, seq, weight, params), refs[:2], refs[2:])


def last_kernel(seq, masks, *refs):
    me_ref, docs, tables, refs = refs[0], refs[1:3], refs[3 : 3 + len(masks)], refs[3 + len(masks) :]
    weight, params, halves, dbias_ref, refs = refs[0], refs[1], refs[2:4], refs[4], refs[5:]
    earlier, out_ref, send = refs[:-2], refs[-2], refs[-1]
    me = me_ref[0]
    core, chip = me % 2, me // 2
    devices = 2 * len(masks)
    tiles = 2 * halves[0].shape[0] // TILE
    normed = normed_rows(docs, docs, seq, weight, params)
    found = []
    for k, w_ref in enumerate(halves):
        parts = [ref[0:2, :] for ref in earlier[k::2]]
        found.append(jnp.concatenate([*parts, *tops_of(normed, w_ref, 2)], axis=0))
    low = jnp.where(core == 0, found[0], found[1])
    high = jnp.where(core == 0, found[1], found[0])
    logits = jnp.concatenate([low, high], axis=1)
    docs_at = [me ^ (2 * mask) for mask in masks]
    bias = dbias_ref[...]
    bias = pltpu.roll(bias, bias.shape[0] - chip * tiles, 0)
    tables = jnp.concatenate([table_of(ref) for ref in tables], axis=0)
    tables = pltpu.roll(tables, TILE - chip * tiles, 1).astype(jnp.int32)
    send[...] = jnp.zeros(send.shape, jnp.float32)
    stride = out_ref.shape[1]
    target = lax.broadcasted_iota(jnp.int32, (BLK_DEV * devices, TILE), 0)
    for t in range(tiles):
        lanes = slice(t * TILE, (t + 1) * TILE)
        impacts = jnp.log1p(jnp.maximum(logits[:, lanes] + bias[t : t + 1, :], 0.0))
        impacts = impacts.astype(jnp.bfloat16).astype(jnp.float32)
        blocks = jnp.zeros((BLK_DEV * devices, TILE), jnp.float32)
        for n in range(len(masks)):
            row = impacts[n : n + 1, :]
            send[pl.ds(docs_at[n] * stride + t, 1), :] = row
            block = jnp.broadcast_to(tables[n : n + 1, t : t + 1], target.shape)
            blocks = jnp.maximum(blocks, jnp.where(target == block, row, 0.0))
        for s in range(BLK_DEV):
            send[pl.ds((1 + s) * SLOT_ROWS + t, devices, stride=stride), :] = blocks[
                s * devices : (s + 1) * devices
            ]
    out_ref[...] = send[...].astype(jnp.bfloat16).reshape(out_ref.shape)


def move_tokens(
    hidden_states,
    doc_lengths,
    transform_weight,
    transform_bias,
    norm_gain,
    norm_bias,
    decoder_weight,
    decoder_bias,
    tile_ids,
    owner_ids,
    block_slots,
):
    devices = lax.axis_size("doc")
    chips = devices // 2
    seq, width = hidden_states.shape
    rows = transform_weight.shape[0]
    half = decoder_weight.shape[2]
    tiles = 2 * half // TILE
    me = lax.axis_index("doc").astype(jnp.int32)

    def cross(value, mask):
        return lax.ppermute(value, "doc", [(i, i ^ (2 * mask)) for i in range(devices)])

    def swap(value):
        return lax.ppermute(value, "doc", [(i, i ^ 1) for i in range(devices)])

    smem = pl.BlockSpec(memory_space=pltpu.SMEM)
    vmem = pl.BlockSpec(memory_space=pltpu.VMEM)
    hbm = pl.BlockSpec(memory_space=pltpu.HBM)

    def stay(value):
        return pltpu.with_memory_space_constraint(value, pltpu.HBM)

    limit = pltpu.CompilerParams(vmem_limit_bytes=24 * 1024 * 1024)

    def cost(docs):
        return pl.CostEstimate(flops=docs, bytes_accessed=docs, transcendentals=0)

    def shape(dims, dtype):
        return jax.ShapeDtypeStruct(dims, dtype)

    def after(value, *done):
        return lax.optimization_barrier((value, *done))[0]

    def pile(values, parts, heights=()):
        heights = heights or (sum(count for _, count in parts),)
        piled = pl.pallas_call(
            lambda *refs: pile_kernel(parts, heights, *refs),
            out_shape=[shape((height, width), jnp.bfloat16) for height in heights],
            in_specs=[vmem] * len(values),
            out_specs=[vmem] * len(heights),
            compiler_params=limit,
        )(*values)
        return piled if len(heights) > 1 else piled[0]

    weight_rows = jnp.swapaxes(decoder_weight[0], 0, 1)
    block_6 = cross(transform_weight, 6)
    block_2 = cross(transform_weight, 2)
    theirs = swap(weight_rows)
    docs = {1: cross(hidden_states, 1), 2: cross(hidden_states, 2)}
    load, block, table, params = pl.pallas_call(
        start_kernel,
        out_shape=[
            shape((seq + SLOT_ROWS, width), jnp.bfloat16),
            shape((rows, width), jnp.bfloat16),
            shape((SLOT_ROWS, width), jnp.bfloat16),
            shape((8, width), jnp.float32),
        ],
        in_specs=[smem] * 4 + [hbm] * 5,
        out_specs=[vmem] * 4,
        scratch_shapes=[
            pltpu.VMEM((3 * width,), jnp.float32),
            pltpu.SemaphoreType.DMA((5,)),
        ],
        compiler_params=limit,
    )(
        stay(tile_ids),
        stay(owner_ids[..., 0]),
        stay(block_slots),
        doc_lengths,
        stay(hidden_states),
        stay(transform_weight),
        stay(transform_bias),
        stay(norm_gain),
        stay(norm_bias),
    )
    near = (block, after(block_2, block_6, docs[1]), table)
    near_pile = cross(pile(near, ((0, rows), (0, rows), (0, SLOT_ROWS))), 1)
    one, two, below = (0, rows), (0, 2 * rows), (0, SLOT_ROWS)
    block_4 = cross(pile((after(block_6, docs[2]), table), (one, below)), 2)
    docs[6] = cross(after(load, block_6), 6)
    load_1 = pile((docs[1], near_pile), ((0, seq), (2 * rows, SLOT_ROWS)))
    far = (block_6, after(block_4, near_pile))
    far = pile(far, ((0, rows), (0, rows)))
    far_pile = cross(far, 1)
    docs[3] = cross(after(load_1, far), 2)
    docs[4] = cross(after(docs[6], far, docs[3]), 2)
    docs[7] = cross(docs[6], 1)
    late = (docs[6], theirs)
    sources = (after(block, *late), block_2, block_6, block_4, near_pile, far_pile)
    packed = pile(sources, (one, one, one, one, two, two), (chips // 2 * rows,) * 2)
    other_packed = [swap(part) for part in packed]
    block_masks = [0, 2, 6, 4, 1, 3, 7, 5]

    far_from = [stay(after(weight_rows, *packed)), stay(docs[1])]
    mine, beside = pl.pallas_call(
        lambda *refs: fetch_kernel(2, *refs),
        out_shape=[shape(value.shape, value.dtype) for value in far_from],
        in_specs=[vmem] + [hbm] * 2,
        out_specs=[vmem] * 2,
        scratch_shapes=[pltpu.SemaphoreType.DMA((2,))],
        compiler_params=limit,
    )(packed[0], *far_from)

    masks = [0, 1, 6, 7, 2, 3, 4, 5]
    where = me[None]
    best_shape = shape((8, half), jnp.float32)
    *best, weight = pl.pallas_call(
        lambda *refs: first_kernel(seq, block_masks, *refs),
        out_shape=[best_shape, best_shape, shape((width, width), jnp.bfloat16)],
        in_specs=[smem] + [vmem] * 11,
        out_specs=[vmem] * 3,
        compiler_params=limit,
        cost_estimate=cost(2),
    )(
        where,
        load,
        beside,
        table,
        near_pile,
        *packed,
        *other_packed,
        params,
        mine,
        theirs,
    )
    docs |= {0: load, 1: beside, 5: cross(after(docs[4], weight), 1)}
    tables = docs | {1: near_pile, 2: block_4}
    for first in range(2, len(masks) - 2, 2):
        pair = masks[first : first + 2]
        best += pl.pallas_call(
            lambda *refs: next_kernel(seq, *refs),
            out_shape=[best_shape] * 2,
            in_specs=[vmem] * 8,
            out_specs=[vmem] * 2,
            compiler_params=limit,
            cost_estimate=cost(2),
        )(
            *[docs[mask] for mask in pair],
            *[tables[mask] for mask in pair],
            after(weight, best[-1]),
            params,
            mine,
            theirs,
        )
    send = pl.pallas_call(
        lambda *refs: last_kernel(seq, masks, *refs),
        out_shape=shape((devices, (1 + BLK_DEV) * SLOT_ROWS, TILE), jnp.bfloat16),
        in_specs=[smem] + [vmem] * (2 + len(masks) + 5 + len(best)),
        out_specs=vmem,
        scratch_shapes=[
            pltpu.VMEM((devices * (1 + BLK_DEV) * SLOT_ROWS, TILE), jnp.float32),
        ],
        compiler_params=limit,
        cost_estimate=cost(2),
    )(
        where,
        *[docs[mask] for mask in masks[-2:]],
        *[tables[mask] for mask in masks],
        weight,
        params,
        mine,
        theirs,
        decoder_bias.reshape(-1, TILE),
        *best,
    )
    got = lax.all_to_all(send, "doc", split_axis=0, concat_axis=0, tiled=True)
    got = got.reshape(chips, 2, 1 + BLK_DEV, SLOT_ROWS, TILE)[:, :, :, :tiles]
    whole = jnp.swapaxes(jnp.maximum(got[:, 0], got[:, 1]), 0, 1).reshape(1 + BLK_DEV, -1)
    return (whole[:1], whole[1:])


def tokens_move(mesh):
    return mesh.shape["term"] == 1 and mesh.shape["doc"] == 16


def solution(mesh):
    placed = (
        P(("groups", "doc"), None),
        P(("groups", "doc")),
        P("doc", "term"),
        P(),
        P(),
        P(),
        P("term", None, "doc"),
        P("term"),
        P("term", ("groups", "doc"), None),
        P("term", ("groups", "doc"), None, None),
        P("term", ("groups", "doc"), None),
    )

    def local(*args):
        pair = 2 * args[6].shape[2]
        tiles = pair * (mesh.shape["doc"] // 2) // TILE
        fits = pair % TILE == 0 and tiles < TILE and pair // TILE <= SLOT_ROWS
        if tokens_move(mesh) and args[1].shape[0] == 1 and fits:
            return move_tokens(*args)
        return move_weights(*args)

    return jax.shard_map(
        local,
        mesh=mesh,
        in_specs=placed,
        out_specs=(P(("groups", "doc"), "term"), P(("groups", "doc"), "term")),
        check_vma=False,
    )
```

```python
import jax
import jax.numpy as jnp
from jax import lax
from jax.experimental import pallas as pl
from jax.experimental.pallas import tpu as pltpu
from jax.sharding import PartitionSpec as P

TILE = 128
BLK_DEV = 2
SLOT_ROWS = 16


def layer_norm(activated, norm_gain, norm_bias):
    values = activated.astype(jnp.float32)
    centre = jnp.mean(values, axis=-1, keepdims=True)
    centred = values - centre
    spread = jnp.mean(centred * centred, axis=-1, keepdims=True)
    return (centred * lax.rsqrt(spread + 1e-05) * norm_gain + norm_bias).astype(jnp.bfloat16)


def pool_docs(logits, keep):
    docs_here = keep.shape[0]
    saturated = jnp.log1p(jnp.maximum(logits, 0.0)).reshape(
        docs_here, keep.shape[1], logits.shape[1]
    )
    return jnp.max(jnp.where(keep[:, :, None], saturated, 0.0), axis=1)


def move_weights(
    hidden_states,
    doc_lengths,
    transform_weight,
    transform_bias,
    norm_gain,
    norm_bias,
    decoder_weight,
    decoder_bias,
    tile_ids,
    owner_ids,
    block_slots,
):
    tok_rows = hidden_states.shape[0]
    docs_here = doc_lengths.shape[0]
    seq_len = tok_rows // docs_here
    cols = transform_weight.shape[1]
    pre_half = jnp.dot(
        hidden_states,
        lax.all_gather(transform_weight, "doc", axis=0, tiled=True),
        preferred_element_type=jnp.float32,
    )
    bias_half = lax.dynamic_slice_in_dim(transform_bias, lax.axis_index("term") * cols, cols, 0)
    act_half = jax.nn.gelu(pre_half + bias_half, approximate=False).astype(jnp.bfloat16)
    activated = lax.all_gather(act_half, "term", axis=1, tiled=True)
    normed = layer_norm(activated, norm_gain, norm_bias)
    keep = jnp.arange(seq_len, dtype=jnp.int32)[None, :] < doc_lengths[:, None]
    logits = jnp.dot(
        normed,
        lax.all_gather(decoder_weight, "doc", axis=2, tiled=True)[0],
        preferred_element_type=jnp.float32,
    )
    logits = logits + decoder_bias
    impacts = pool_docs(logits, keep).astype(jnp.bfloat16)
    tiles_t = impacts.shape[1] // TILE
    slots_total = BLK_DEV * tiles_t
    tiles = impacts.reshape(docs_here * tiles_t, TILE)
    chosen = tile_ids[0]
    doc_index = jnp.arange(docs_here, dtype=jnp.int32)[:, None]
    posted = tiles[(doc_index * tiles_t + chosen).reshape(-1)]
    owners = owner_ids[0, :, :, 0].reshape(-1)
    target = block_slots[0].reshape(-1) * tiles_t + chosen.reshape(-1)
    owner_count = lax.axis_size("doc")
    capacity = max(2, 2 * posted.shape[0] // owner_count)
    onehot = (owners[:, None] == jnp.arange(owner_count, dtype=jnp.int32)[None, :]).astype(
        jnp.int32
    )
    before = jnp.cumsum(onehot, axis=0) - onehot
    position = jnp.sum(before * onehot, axis=1)
    dest = owners * capacity + position
    outgoing = jnp.zeros((owner_count * capacity, TILE), jnp.bfloat16).at[dest].set(posted)
    out_tags = jnp.full((owner_count * capacity,), slots_total, jnp.int32).at[dest].set(target)
    got_vals, got_tags = (
        lax.all_to_all(
            outgoing.reshape(owner_count, capacity, TILE),
            "doc",
            split_axis=0,
            concat_axis=0,
            tiled=True,
        ),
        lax.all_to_all(
            out_tags.reshape(owner_count, capacity), "doc", split_axis=0, concat_axis=0, tiled=True
        ),
    )
    got_vals = got_vals.reshape(-1, TILE)
    local_tags = got_tags.reshape(-1)
    summary = jnp.zeros((slots_total, TILE), jnp.bfloat16).at[local_tags].max(got_vals, mode="drop")
    return (impacts, summary.reshape(BLK_DEV, tiles_t * TILE))


def dot_t(left, right):
    return lax.dot_general(
        left, right, (((1,), (1,)), ((), ())), preferred_element_type=jnp.float32
    )


def table_of(ref):
    return ref[ref.shape[0] - SLOT_ROWS :, 0:TILE].astype(jnp.float32)[0:1, :]


def masked(ref, table_ref, seq):
    here = ref[0:seq, :]
    length = table_of(table_ref)[:, TILE - 1 :]
    keep = lax.broadcasted_iota(jnp.int32, here.shape, 0).astype(jnp.float32) < length
    first = jnp.broadcast_to(here[0:1, :].astype(jnp.float32), here.shape).astype(here.dtype)
    return jnp.where(keep, here, first)


def normed_rows(docs, tables, seq, weight, params):
    rows = [masked(ref, table, seq) for ref, table in zip(docs, tables)]
    rows = jnp.concatenate(rows, axis=0)
    pre = jnp.dot(rows, weight[...], preferred_element_type=jnp.float32) + params[0:1, :]
    act = 0.5 * pre * (1.0 + lax.erf(pre * (0.5**0.5)))
    return layer_norm(act.astype(jnp.bfloat16), params[1:2, :], params[2:3, :])


def tops_of(normed, w_ref, count):
    logits = dot_t(normed, w_ref[...])
    seq = normed.shape[0] // count
    return [
        jnp.max(logits[j * seq : (j + 1) * seq], axis=0, keepdims=True) for j in range(count)
    ]


def start_kernel(tiles_ref, owners_ref, slots_ref, length_ref, *refs):
    hidden_ref, weight_ref, vectors = refs[0], refs[1], refs[2:5]
    load_ref, block_ref, table_ref, rows_ref, kept, sems = refs[5:]
    seq, width = hidden_ref.shape
    copies = [
        fetch(hidden_ref, load_ref.at[pl.ds(0, seq), :], sems.at[0]),
        fetch(weight_ref, block_ref, sems.at[1]),
    ]
    for k, ref in enumerate(vectors):
        copies.append(fetch(ref, kept.at[pl.ds(k * width, width)], sems.at[2 + k]))
    lane = lax.broadcasted_iota(jnp.int32, (SLOT_ROWS, TILE), 1)
    table = jnp.where(lane == TILE - 1, length_ref[0], -1)
    devices = lax.axis_size("doc")
    for k in range(tiles_ref.shape[2]):
        block = slots_ref[0, 0, k] * devices + owners_ref[0, 0, k]
        table = jnp.where(lane == tiles_ref[0, 0, k], block, table)
    table = table.astype(jnp.float32).astype(jnp.bfloat16)
    for first in range(0, width, TILE):
        load_ref[seq:, first : first + TILE] = table
        table_ref[:, first : first + TILE] = table
    for copy in copies:
        copy.wait()
    for k in range(len(vectors)):
        rows_ref[k : k + 1, :] = kept[pl.ds(k * width, width)][None, :]


def pile_kernel(parts, heights, *refs):
    rows = jnp.concatenate(
        [ref[first : first + count, :] for ref, (first, count) in zip(refs, parts)], axis=0
    )
    at = 0
    for ref, height in zip(refs[len(parts) :], heights):
        ref[...] = rows[at : at + height, :]
        at += height


def fetch(ref, slot, sem):
    copy = pltpu.make_async_copy(ref, slot, sem)
    copy.start()
    return copy


def keep_tops(normed, halves, bests):
    for w_ref, best in zip(halves, bests):
        for j, top in enumerate(tops_of(normed, w_ref, 2)):
            best[j : j + 1, :] = top


def fetch_kernel(count, *refs):
    copies = [fetch(refs[1 + k], refs[1 + count + k], refs[-1].at[k]) for k in range(count)]
    for copy in copies:
        copy.wait()


def first_kernel(seq, masks, *refs):
    me_ref, docs, tables, refs = refs[0], refs[1:3], refs[3:5], refs[5:]
    parts, others, params, halves, refs = refs[:2], refs[2:4], refs[4], refs[5:7], refs[7:]
    bests, weight = refs[:2], refs[2]
    me = me_ref[0]
    core = me % 2
    rows = weight.shape[0] // (2 * len(masks))
    for k, mask in enumerate(masks):
        chip = (me // 2) ^ mask
        part, place = divmod(k * rows, parts[0].shape[0])
        block = slice(place, place + rows)
        at = pl.multiple_of((2 * chip + core) * rows, SLOT_ROWS)
        weight[pl.ds(at, rows), :] = parts[part][block, :]
        at = pl.multiple_of((2 * chip + 1 - core) * rows, SLOT_ROWS)
        weight[pl.ds(at, rows), :] = others[part][block, :]
    keep_tops(normed_rows(docs, tables, seq, weight, params), halves, bests)


def next_kernel(seq, *refs):
    docs, tables, weight, params, refs = refs[:2], refs[2:4], refs[4], refs[5], refs[6:]
    keep_tops(normed_rows(docs, tables, seq, weight, params), refs[:2], refs[2:])


def last_kernel(seq, masks, *refs):
    me_ref, docs, tables, refs = refs[0], refs[1:3], refs[3 : 3 + len(masks)], refs[3 + len(masks) :]
    weight, params, halves, dbias_ref, refs = refs[0], refs[1], refs[2:4], refs[4], refs[5:]
    earlier, keep_ref, give_ref, send = refs[:-3], *refs[-3:]
    me = me_ref[0]
    core, chip = me % 2, me // 2
    devices = 2 * len(masks)
    tiles = 2 * halves[0].shape[0] // TILE
    normed = normed_rows(docs, docs, seq, weight, params)
    found = []
    for k, w_ref in enumerate(halves):
        parts = [ref[0:2, :] for ref in earlier[k::2]]
        found.append(jnp.concatenate([*parts, *tops_of(normed, w_ref, 2)], axis=0))
    low = jnp.where(core == 0, found[0], found[1])
    high = jnp.where(core == 0, found[1], found[0])
    logits = jnp.concatenate([low, high], axis=1)
    docs_at = [me ^ (2 * mask) for mask in masks]
    bias = dbias_ref[...]
    bias = pltpu.roll(bias, bias.shape[0] - chip * tiles, 0)
    tables = jnp.concatenate([table_of(ref) for ref in tables], axis=0)
    tables = pltpu.roll(tables, TILE - chip * tiles, 1).astype(jnp.int32)
    send[...] = jnp.zeros(send.shape, jnp.float32)
    stride = keep_ref.shape[1]
    target = lax.broadcasted_iota(jnp.int32, (BLK_DEV * devices, TILE), 0)
    for t in range(tiles):
        lanes = slice(t * TILE, (t + 1) * TILE)
        impacts = jnp.log1p(jnp.maximum(logits[:, lanes] + bias[t : t + 1, :], 0.0))
        impacts = impacts.astype(jnp.bfloat16).astype(jnp.float32)
        blocks = jnp.zeros((BLK_DEV * devices, TILE), jnp.float32)
        for n in range(len(masks)):
            row = impacts[n : n + 1, :]
            send[pl.ds(docs_at[n] * stride + t, 1), :] = row
            block = jnp.broadcast_to(tables[n : n + 1, t : t + 1], target.shape)
            blocks = jnp.maximum(blocks, jnp.where(target == block, row, 0.0))
        for s in range(BLK_DEV):
            send[pl.ds((1 + s) * SLOT_ROWS + t, devices, stride=stride), :] = blocks[
                s * devices : (s + 1) * devices
            ]
    for k in range(len(masks)):
        at = pl.multiple_of((2 * k + core) * stride, SLOT_ROWS)
        keep_ref[k] = send[pl.ds(at, stride), :].astype(jnp.bfloat16)
        at = pl.multiple_of((2 * k + 1 - core) * stride + SLOT_ROWS, SLOT_ROWS)
        give_ref[k] = send[pl.ds(at, stride - SLOT_ROWS), :].astype(jnp.bfloat16)


def merge_kernel(me_ref, keep_ref, got_ref, *out_refs):
    for mask, out_ref in enumerate(out_refs):
        chip = (me_ref[0] // 2) ^ mask
        rows = keep_ref[chip].astype(jnp.float32)
        other = got_ref[chip].astype(jnp.float32)
        both = jnp.maximum(rows[SLOT_ROWS:], other)
        out_ref[...] = jnp.concatenate([rows[:SLOT_ROWS], both], axis=0).astype(jnp.bfloat16)


def place_kernel(tiles, me_ref, *refs):
    parts, impacts_ref, summaries_ref = refs[:-2], refs[-2], refs[-1]
    for mask, ref in enumerate(parts):
        chip = (me_ref[0] // 2) ^ mask
        rows = ref[...].astype(jnp.float32)
        lanes = pl.ds(pl.multiple_of(chip * tiles * TILE, TILE), tiles * TILE)
        lines = [
            jnp.concatenate([rows[first + t : first + t + 1] for t in range(tiles)], axis=1)
            for first in range(0, rows.shape[0], SLOT_ROWS)
        ]
        impacts_ref[:, lanes] = lines[0].astype(jnp.bfloat16)
        summaries_ref[:, lanes] = jnp.concatenate(lines[1:], axis=0).astype(jnp.bfloat16)


def move_tokens(
    hidden_states,
    doc_lengths,
    transform_weight,
    transform_bias,
    norm_gain,
    norm_bias,
    decoder_weight,
    decoder_bias,
    tile_ids,
    owner_ids,
    block_slots,
):
    devices = lax.axis_size("doc")
    chips = devices // 2
    seq, width = hidden_states.shape
    rows = transform_weight.shape[0]
    half = decoder_weight.shape[2]
    tiles = 2 * half // TILE
    me = lax.axis_index("doc").astype(jnp.int32)

    def cross(value, mask):
        return lax.ppermute(value, "doc", [(i, i ^ (2 * mask)) for i in range(devices)])

    def swap(value):
        return lax.ppermute(value, "doc", [(i, i ^ 1) for i in range(devices)])

    smem = pl.BlockSpec(memory_space=pltpu.SMEM)
    vmem = pl.BlockSpec(memory_space=pltpu.VMEM)
    hbm = pl.BlockSpec(memory_space=pltpu.HBM)

    def stay(value):
        return pltpu.with_memory_space_constraint(value, pltpu.HBM)

    limit = pltpu.CompilerParams(vmem_limit_bytes=24 * 1024 * 1024)

    def cost(docs):
        return pl.CostEstimate(flops=docs, bytes_accessed=docs, transcendentals=0)

    def shape(dims, dtype):
        return jax.ShapeDtypeStruct(dims, dtype)

    def after(value, *done):
        return lax.optimization_barrier((value, *done))[0]

    def pile(values, parts, heights=()):
        heights = heights or (sum(count for _, count in parts),)
        piled = pl.pallas_call(
            lambda *refs: pile_kernel(parts, heights, *refs),
            out_shape=[shape((height, width), jnp.bfloat16) for height in heights],
            in_specs=[vmem] * len(values),
            out_specs=[vmem] * len(heights),
            compiler_params=limit,
        )(*values)
        return piled if len(heights) > 1 else piled[0]

    weight_rows = jnp.swapaxes(decoder_weight[0], 0, 1)
    block_6 = cross(transform_weight, 6)
    block_2 = cross(transform_weight, 2)
    theirs = swap(weight_rows)
    docs = {1: cross(hidden_states, 1)}
    load, block, table, params = pl.pallas_call(
        start_kernel,
        out_shape=[
            shape((seq + SLOT_ROWS, width), jnp.bfloat16),
            shape((rows, width), jnp.bfloat16),
            shape((SLOT_ROWS, width), jnp.bfloat16),
            shape((8, width), jnp.float32),
        ],
        in_specs=[smem] * 4 + [hbm] * 5,
        out_specs=[vmem] * 4,
        scratch_shapes=[
            pltpu.VMEM((3 * width,), jnp.float32),
            pltpu.SemaphoreType.DMA((5,)),
        ],
        compiler_params=limit,
    )(
        stay(tile_ids),
        stay(owner_ids[..., 0]),
        stay(block_slots),
        doc_lengths,
        stay(hidden_states),
        stay(transform_weight),
        stay(transform_bias),
        stay(norm_gain),
        stay(norm_bias),
    )
    near = (block, after(block_2, block_6, docs[1]), table)
    near_pile = cross(pile(near, ((0, rows), (0, rows), (0, SLOT_ROWS))), 1)
    one, two = (0, rows), (0, 2 * rows)
    block_4 = cross(block_6, 2)
    docs[6] = cross(after(load, block_6), 6)
    docs[2] = cross(after(load, block_4), 2)
    load_1 = pile((docs[1], near_pile), ((0, seq), (2 * rows, SLOT_ROWS)))
    far = (block_6, after(block_4, near_pile))
    far = pile(far, ((0, rows), (0, rows)))
    far_pile = cross(far, 1)
    docs[3] = cross(after(load_1, far), 2)
    docs[4] = cross(after(docs[6], far, docs[2]), 2)
    docs[7] = cross(docs[6], 1)
    late = (docs[6], theirs)
    sources = (after(block, *late), block_2, block_6, block_4, near_pile, far_pile)
    packed = pile(sources, (one, one, one, one, two, two), (chips // 2 * rows,) * 2)
    other_packed = [swap(part) for part in packed]
    block_masks = [0, 2, 6, 4, 1, 3, 7, 5]

    far_from = [stay(after(weight_rows, *packed)), stay(docs[1])]
    mine, beside = pl.pallas_call(
        lambda *refs: fetch_kernel(2, *refs),
        out_shape=[shape(value.shape, value.dtype) for value in far_from],
        in_specs=[vmem] + [hbm] * 2,
        out_specs=[vmem] * 2,
        scratch_shapes=[pltpu.SemaphoreType.DMA((2,))],
        compiler_params=limit,
    )(packed[0], *far_from)

    masks = [0, 1, 6, 7, 2, 3, 4, 5]
    where = me[None]
    best_shape = shape((8, half), jnp.float32)
    *best, weight = pl.pallas_call(
        lambda *refs: first_kernel(seq, block_masks, *refs),
        out_shape=[best_shape, best_shape, shape((width, width), jnp.bfloat16)],
        in_specs=[smem] + [vmem] * 11,
        out_specs=[vmem] * 3,
        compiler_params=limit,
        cost_estimate=cost(2),
    )(
        where,
        load,
        beside,
        table,
        near_pile,
        *packed,
        *other_packed,
        params,
        mine,
        theirs,
    )
    docs |= {0: load, 1: beside, 5: cross(after(docs[4], weight), 1)}
    tables = docs | {1: near_pile}
    for first in range(2, len(masks) - 2, 2):
        pair = masks[first : first + 2]
        best += pl.pallas_call(
            lambda *refs: next_kernel(seq, *refs),
            out_shape=[best_shape] * 2,
            in_specs=[vmem] * 8,
            out_specs=[vmem] * 2,
            compiler_params=limit,
            cost_estimate=cost(2),
        )(
            *[docs[mask] for mask in pair],
            *[tables[mask] for mask in pair],
            after(weight, best[-1]),
            params,
            mine,
            theirs,
        )
    height = (1 + BLK_DEV) * SLOT_ROWS
    keep, give = pl.pallas_call(
        lambda *refs: last_kernel(seq, masks, *refs),
        out_shape=[
            shape((chips, height, TILE), jnp.bfloat16),
            shape((chips, height - SLOT_ROWS, TILE), jnp.bfloat16),
        ],
        in_specs=[smem] + [vmem] * (2 + len(masks) + 5 + len(best)),
        out_specs=[vmem] * 2,
        scratch_shapes=[pltpu.VMEM((devices * height, TILE), jnp.float32)],
        compiler_params=limit,
        cost_estimate=cost(2),
    )(
        where,
        *[docs[mask] for mask in masks[-2:]],
        *[tables[mask] for mask in masks],
        weight,
        params,
        mine,
        theirs,
        decoder_bias.reshape(-1, TILE),
        *best,
    )
    parts = pl.pallas_call(
        merge_kernel,
        out_shape=[shape((height, TILE), jnp.bfloat16)] * chips,
        in_specs=[smem] + [vmem] * 2,
        out_specs=[vmem] * chips,
        compiler_params=limit,
    )(where, keep, swap(give))
    parts = [cross(part, mask) if mask else part for mask, part in enumerate(parts)]
    return pl.pallas_call(
        lambda *refs: place_kernel(tiles, *refs),
        out_shape=[
            shape((1, chips * tiles * TILE), jnp.bfloat16),
            shape((BLK_DEV, chips * tiles * TILE), jnp.bfloat16),
        ],
        in_specs=[smem] + [vmem] * chips,
        out_specs=[vmem] * 2,
        compiler_params=limit,
    )(where, *parts)


def tokens_move(mesh):
    return mesh.shape["term"] == 1 and mesh.shape["doc"] == 16


def solution(mesh):
    placed = (
        P(("groups", "doc"), None),
        P(("groups", "doc")),
        P("doc", "term"),
        P(),
        P(),
        P(),
        P("term", None, "doc"),
        P("term"),
        P("term", ("groups", "doc"), None),
        P("term", ("groups", "doc"), None, None),
        P("term", ("groups", "doc"), None),
    )

    def local(*args):
        pair = 2 * args[6].shape[2]
        tiles = pair * (mesh.shape["doc"] // 2) // TILE
        fits = pair % TILE == 0 and tiles < TILE and pair // TILE <= SLOT_ROWS
        if tokens_move(mesh) and args[1].shape[0] == 1 and fits:
            return move_tokens(*args)
        return move_weights(*args)

    return jax.shard_map(
        local,
        mesh=mesh,
        in_specs=placed,
        out_specs=(P(("groups", "doc"), "term"), P(("groups", "doc"), "term")),
        check_vma=False,
    )
```

```python
import jax
import jax.numpy as jnp
from jax import lax
from jax.experimental import pallas as pl
from jax.experimental.pallas import tpu as pltpu
from jax.sharding import PartitionSpec as P

TILE = 128
BLK_DEV = 2
SLOT_ROWS = 16


def layer_norm(activated, norm_gain, norm_bias):
    values = activated.astype(jnp.float32)
    centre = jnp.mean(values, axis=-1, keepdims=True)
    centred = values - centre
    spread = jnp.mean(centred * centred, axis=-1, keepdims=True)
    return (centred * lax.rsqrt(spread + 1e-05) * norm_gain + norm_bias).astype(jnp.bfloat16)


def pool_docs(logits, keep):
    docs_here = keep.shape[0]
    saturated = jnp.log1p(jnp.maximum(logits, 0.0)).reshape(
        docs_here, keep.shape[1], logits.shape[1]
    )
    return jnp.max(jnp.where(keep[:, :, None], saturated, 0.0), axis=1)


def move_weights(
    hidden_states,
    doc_lengths,
    transform_weight,
    transform_bias,
    norm_gain,
    norm_bias,
    decoder_weight,
    decoder_bias,
    tile_ids,
    owner_ids,
    block_slots,
):
    tok_rows = hidden_states.shape[0]
    docs_here = doc_lengths.shape[0]
    seq_len = tok_rows // docs_here
    cols = transform_weight.shape[1]
    pre_half = jnp.dot(
        hidden_states,
        lax.all_gather(transform_weight, "doc", axis=0, tiled=True),
        preferred_element_type=jnp.float32,
    )
    bias_half = lax.dynamic_slice_in_dim(transform_bias, lax.axis_index("term") * cols, cols, 0)
    act_half = jax.nn.gelu(pre_half + bias_half, approximate=False).astype(jnp.bfloat16)
    activated = lax.all_gather(act_half, "term", axis=1, tiled=True)
    normed = layer_norm(activated, norm_gain, norm_bias)
    keep = jnp.arange(seq_len, dtype=jnp.int32)[None, :] < doc_lengths[:, None]
    logits = jnp.dot(
        normed,
        lax.all_gather(decoder_weight, "doc", axis=2, tiled=True)[0],
        preferred_element_type=jnp.float32,
    )
    logits = logits + decoder_bias
    impacts = pool_docs(logits, keep).astype(jnp.bfloat16)
    tiles_t = impacts.shape[1] // TILE
    slots_total = BLK_DEV * tiles_t
    tiles = impacts.reshape(docs_here * tiles_t, TILE)
    chosen = tile_ids[0]
    doc_index = jnp.arange(docs_here, dtype=jnp.int32)[:, None]
    posted = tiles[(doc_index * tiles_t + chosen).reshape(-1)]
    owners = owner_ids[0, :, :, 0].reshape(-1)
    target = block_slots[0].reshape(-1) * tiles_t + chosen.reshape(-1)
    owner_count = lax.axis_size("doc")
    capacity = max(2, 2 * posted.shape[0] // owner_count)
    onehot = (owners[:, None] == jnp.arange(owner_count, dtype=jnp.int32)[None, :]).astype(
        jnp.int32
    )
    before = jnp.cumsum(onehot, axis=0) - onehot
    position = jnp.sum(before * onehot, axis=1)
    dest = owners * capacity + position
    outgoing = jnp.zeros((owner_count * capacity, TILE), jnp.bfloat16).at[dest].set(posted)
    out_tags = jnp.full((owner_count * capacity,), slots_total, jnp.int32).at[dest].set(target)
    got_vals, got_tags = (
        lax.all_to_all(
            outgoing.reshape(owner_count, capacity, TILE),
            "doc",
            split_axis=0,
            concat_axis=0,
            tiled=True,
        ),
        lax.all_to_all(
            out_tags.reshape(owner_count, capacity), "doc", split_axis=0, concat_axis=0, tiled=True
        ),
    )
    got_vals = got_vals.reshape(-1, TILE)
    local_tags = got_tags.reshape(-1)
    summary = jnp.zeros((slots_total, TILE), jnp.bfloat16).at[local_tags].max(got_vals, mode="drop")
    return (impacts, summary.reshape(BLK_DEV, tiles_t * TILE))


def dot_t(left, right):
    return lax.dot_general(
        left, right, (((1,), (1,)), ((), ())), preferred_element_type=jnp.float32
    )


def table_of(ref):
    return ref[ref.shape[0] - SLOT_ROWS :, 0:TILE].astype(jnp.float32)[0:1, :]


def masked(ref, table_ref, seq):
    here = ref[0:seq, :]
    length = table_of(table_ref)[:, TILE - 1 :]
    keep = lax.broadcasted_iota(jnp.int32, here.shape, 0).astype(jnp.float32) < length
    first = jnp.broadcast_to(here[0:1, :].astype(jnp.float32), here.shape).astype(here.dtype)
    return jnp.where(keep, here, first)


def normed_rows(docs, tables, seq, weight, params):
    rows = [masked(ref, table, seq) for ref, table in zip(docs, tables)]
    rows = jnp.concatenate(rows, axis=0)
    pre = jnp.dot(rows, weight[...], preferred_element_type=jnp.float32) + params[0:1, :]
    act = 0.5 * pre * (1.0 + lax.erf(pre * (0.5**0.5)))
    return layer_norm(act.astype(jnp.bfloat16), params[1:2, :], params[2:3, :])


def tops_of(normed, w_ref, count):
    logits = dot_t(normed, w_ref[...])
    seq = normed.shape[0] // count
    return [
        jnp.max(logits[j * seq : (j + 1) * seq], axis=0, keepdims=True) for j in range(count)
    ]


def start_kernel(tiles_ref, owners_ref, slots_ref, length_ref, *refs):
    hidden_ref, weight_ref, vectors = refs[0], refs[1], refs[2:5]
    load_ref, block_ref, table_ref, rows_ref, kept, sems = refs[5:]
    seq, width = hidden_ref.shape
    copies = [
        fetch(hidden_ref, load_ref.at[pl.ds(0, seq), :], sems.at[0]),
        fetch(weight_ref, block_ref, sems.at[1]),
    ]
    for k, ref in enumerate(vectors):
        copies.append(fetch(ref, kept.at[pl.ds(k * width, width)], sems.at[2 + k]))
    lane = lax.broadcasted_iota(jnp.int32, (SLOT_ROWS, TILE), 1)
    table = jnp.where(lane == TILE - 1, length_ref[0], -1)
    devices = lax.axis_size("doc")
    for k in range(tiles_ref.shape[2]):
        block = slots_ref[0, 0, k] * devices + owners_ref[0, 0, k]
        table = jnp.where(lane == tiles_ref[0, 0, k], block, table)
    table = table.astype(jnp.float32).astype(jnp.bfloat16)
    for first in range(0, width, TILE):
        load_ref[seq:, first : first + TILE] = table
        table_ref[:, first : first + TILE] = table
    for copy in copies:
        copy.wait()
    for k in range(len(vectors)):
        rows_ref[k : k + 1, :] = kept[pl.ds(k * width, width)][None, :]


def pile_kernel(parts, heights, *refs):
    rows = jnp.concatenate(
        [ref[first : first + count, :] for ref, (first, count) in zip(refs, parts)], axis=0
    )
    at = 0
    for ref, height in zip(refs[len(parts) :], heights):
        ref[...] = rows[at : at + height, :]
        at += height


def fetch(ref, slot, sem):
    copy = pltpu.make_async_copy(ref, slot, sem)
    copy.start()
    return copy


def keep_tops(normed, halves, bests):
    for w_ref, best in zip(halves, bests):
        for j, top in enumerate(tops_of(normed, w_ref, 2)):
            best[j : j + 1, :] = top


def fetch_kernel(count, *refs):
    copies = [fetch(refs[1 + k], refs[1 + count + k], refs[-1].at[k]) for k in range(count)]
    for copy in copies:
        copy.wait()


def first_kernel(seq, masks, *refs):
    me_ref, docs, tables, refs = refs[0], refs[1:3], refs[3:5], refs[5:]
    parts, others, params, halves, refs = refs[:2], refs[2:4], refs[4], refs[5:7], refs[7:]
    bests, weight = refs[:2], refs[2]
    me = me_ref[0]
    core = me % 2
    rows = weight.shape[0] // (2 * len(masks))
    for k, mask in enumerate(masks):
        chip = (me // 2) ^ mask
        part, place = divmod(k * rows, parts[0].shape[0])
        block = slice(place, place + rows)
        at = pl.multiple_of((2 * chip + core) * rows, SLOT_ROWS)
        weight[pl.ds(at, rows), :] = parts[part][block, :]
        at = pl.multiple_of((2 * chip + 1 - core) * rows, SLOT_ROWS)
        weight[pl.ds(at, rows), :] = others[part][block, :]
    keep_tops(normed_rows(docs, tables, seq, weight, params), halves, bests)


def next_kernel(seq, *refs):
    docs, tables, weight, params, refs = refs[:2], refs[2:4], refs[4], refs[5], refs[6:]
    keep_tops(normed_rows(docs, tables, seq, weight, params), refs[:2], refs[2:])


def last_kernel(seq, masks, *refs):
    me_ref, docs, tables, refs = refs[0], refs[1:3], refs[3 : 3 + len(masks)], refs[3 + len(masks) :]
    weight, params, halves, dbias_ref, refs = refs[0], refs[1], refs[2:4], refs[4], refs[5:]
    earlier, keep_ref, give_ref, send = refs[:-3], *refs[-3:]
    me = me_ref[0]
    core, chip = me % 2, me // 2
    devices = 2 * len(masks)
    tiles = 2 * halves[0].shape[0] // TILE
    normed = normed_rows(docs, docs, seq, weight, params)
    found = []
    for k, w_ref in enumerate(halves):
        parts = [ref[0:2, :] for ref in earlier[k::2]]
        found.append(jnp.concatenate([*parts, *tops_of(normed, w_ref, 2)], axis=0))
    low = jnp.where(core == 0, found[0], found[1])
    high = jnp.where(core == 0, found[1], found[0])
    logits = jnp.concatenate([low, high], axis=1)
    docs_at = [me ^ (2 * mask) for mask in masks]
    bias = dbias_ref[...]
    bias = pltpu.roll(bias, bias.shape[0] - chip * tiles, 0)
    tables = jnp.concatenate([table_of(ref) for ref in tables], axis=0)
    tables = pltpu.roll(tables, TILE - chip * tiles, 1).astype(jnp.int32)
    send[...] = jnp.zeros(send.shape, jnp.float32)
    stride = keep_ref.shape[1]
    target = lax.broadcasted_iota(jnp.int32, (BLK_DEV * devices, TILE), 0)
    for t in range(tiles):
        lanes = slice(t * TILE, (t + 1) * TILE)
        impacts = jnp.log1p(jnp.maximum(logits[:, lanes] + bias[t : t + 1, :], 0.0))
        impacts = impacts.astype(jnp.bfloat16).astype(jnp.float32)
        blocks = jnp.zeros((BLK_DEV * devices, TILE), jnp.float32)
        for n in range(len(masks)):
            row = impacts[n : n + 1, :]
            send[pl.ds(docs_at[n] * stride + t, 1), :] = row
            block = jnp.broadcast_to(tables[n : n + 1, t : t + 1], target.shape)
            blocks = jnp.maximum(blocks, jnp.where(target == block, row, 0.0))
        for s in range(BLK_DEV):
            send[pl.ds((1 + s) * SLOT_ROWS + t, devices, stride=stride), :] = blocks[
                s * devices : (s + 1) * devices
            ]
    for k in range(len(masks)):
        at = pl.multiple_of((2 * k + core) * stride, SLOT_ROWS)
        keep_ref[k] = send[pl.ds(at, stride), :].astype(jnp.bfloat16)
        at = pl.multiple_of((2 * k + 1 - core) * stride + SLOT_ROWS, SLOT_ROWS)
        give_ref[k] = send[pl.ds(at, stride - SLOT_ROWS), :].astype(jnp.bfloat16)


def merge_kernel(keep_ref, got_ref, out_ref):
    out_ref[:, 0:SLOT_ROWS, :] = keep_ref[:, 0:SLOT_ROWS, :]
    mine = keep_ref[:, SLOT_ROWS:, :].astype(jnp.float32)
    theirs = got_ref[...].astype(jnp.float32)
    out_ref[:, SLOT_ROWS:, :] = jnp.maximum(mine, theirs).astype(jnp.bfloat16)


def place_kernel(tiles, rows_ref, impacts_ref, summaries_ref):
    for chip in range(rows_ref.shape[0]):
        rows = rows_ref[chip].astype(jnp.float32)
        lanes = slice(chip * tiles * TILE, (chip + 1) * tiles * TILE)
        lines = [
            jnp.concatenate([rows[first + t : first + t + 1] for t in range(tiles)], axis=1)
            for first in range(0, rows.shape[0], SLOT_ROWS)
        ]
        impacts_ref[:, lanes] = lines[0].astype(jnp.bfloat16)
        summaries_ref[:, lanes] = jnp.concatenate(lines[1:], axis=0).astype(jnp.bfloat16)


def move_tokens(
    hidden_states,
    doc_lengths,
    transform_weight,
    transform_bias,
    norm_gain,
    norm_bias,
    decoder_weight,
    decoder_bias,
    tile_ids,
    owner_ids,
    block_slots,
):
    devices = lax.axis_size("doc")
    chips = devices // 2
    seq, width = hidden_states.shape
    rows = transform_weight.shape[0]
    half = decoder_weight.shape[2]
    tiles = 2 * half // TILE
    me = lax.axis_index("doc").astype(jnp.int32)

    def cross(value, mask):
        return lax.ppermute(value, "doc", [(i, i ^ (2 * mask)) for i in range(devices)])

    def swap(value):
        return lax.ppermute(value, "doc", [(i, i ^ 1) for i in range(devices)])

    smem = pl.BlockSpec(memory_space=pltpu.SMEM)
    vmem = pl.BlockSpec(memory_space=pltpu.VMEM)
    hbm = pl.BlockSpec(memory_space=pltpu.HBM)

    def stay(value):
        return pltpu.with_memory_space_constraint(value, pltpu.HBM)

    limit = pltpu.CompilerParams(vmem_limit_bytes=24 * 1024 * 1024)

    def cost(docs):
        return pl.CostEstimate(flops=docs, bytes_accessed=docs, transcendentals=0)

    def shape(dims, dtype):
        return jax.ShapeDtypeStruct(dims, dtype)

    def after(value, *done):
        return lax.optimization_barrier((value, *done))[0]

    def pile(values, parts, heights=()):
        heights = heights or (sum(count for _, count in parts),)
        piled = pl.pallas_call(
            lambda *refs: pile_kernel(parts, heights, *refs),
            out_shape=[shape((height, width), jnp.bfloat16) for height in heights],
            in_specs=[vmem] * len(values),
            out_specs=[vmem] * len(heights),
            compiler_params=limit,
        )(*values)
        return piled if len(heights) > 1 else piled[0]

    weight_rows = jnp.swapaxes(decoder_weight[0], 0, 1)
    block_6 = cross(transform_weight, 6)
    block_2 = cross(transform_weight, 2)
    theirs = swap(weight_rows)
    docs = {1: cross(hidden_states, 1)}
    load, block, table, params = pl.pallas_call(
        start_kernel,
        out_shape=[
            shape((seq + SLOT_ROWS, width), jnp.bfloat16),
            shape((rows, width), jnp.bfloat16),
            shape((SLOT_ROWS, width), jnp.bfloat16),
            shape((8, width), jnp.float32),
        ],
        in_specs=[smem] * 4 + [hbm] * 5,
        out_specs=[vmem] * 4,
        scratch_shapes=[
            pltpu.VMEM((3 * width,), jnp.float32),
            pltpu.SemaphoreType.DMA((5,)),
        ],
        compiler_params=limit,
    )(
        stay(tile_ids),
        stay(owner_ids[..., 0]),
        stay(block_slots),
        doc_lengths,
        stay(hidden_states),
        stay(transform_weight),
        stay(transform_bias),
        stay(norm_gain),
        stay(norm_bias),
    )
    near = (block, after(block_2, block_6, docs[1]), table)
    near_pile = cross(pile(near, ((0, rows), (0, rows), (0, SLOT_ROWS))), 1)
    one, two = (0, rows), (0, 2 * rows)
    block_4 = cross(block_6, 2)
    docs[6] = cross(after(load, block_6), 6)
    docs[2] = cross(after(load, block_4), 2)
    load_1 = pile((docs[1], near_pile), ((0, seq), (2 * rows, SLOT_ROWS)))
    far = (block_6, after(block_4, near_pile))
    far = pile(far, ((0, rows), (0, rows)))
    far_pile = cross(far, 1)
    docs[3] = cross(after(load_1, far), 2)
    docs[4] = cross(after(docs[6], far, docs[2]), 2)
    docs[7] = cross(docs[6], 1)
    late = (docs[6], theirs)
    sources = (after(block, *late), block_2, block_6, block_4, near_pile, far_pile)
    packed = pile(sources, (one, one, one, one, two, two), (chips // 2 * rows,) * 2)
    other_packed = [swap(part) for part in packed]
    block_masks = [0, 2, 6, 4, 1, 3, 7, 5]

    far_from = [stay(after(weight_rows, *packed)), stay(docs[1])]
    mine, beside = pl.pallas_call(
        lambda *refs: fetch_kernel(2, *refs),
        out_shape=[shape(value.shape, value.dtype) for value in far_from],
        in_specs=[vmem] + [hbm] * 2,
        out_specs=[vmem] * 2,
        scratch_shapes=[pltpu.SemaphoreType.DMA((2,))],
        compiler_params=limit,
    )(packed[0], *far_from)

    masks = [0, 1, 6, 7, 2, 3, 4, 5]
    where = me[None]
    best_shape = shape((8, half), jnp.float32)
    *best, weight = pl.pallas_call(
        lambda *refs: first_kernel(seq, block_masks, *refs),
        out_shape=[best_shape, best_shape, shape((width, width), jnp.bfloat16)],
        in_specs=[smem] + [vmem] * 11,
        out_specs=[vmem] * 3,
        compiler_params=limit,
        cost_estimate=cost(2),
    )(
        where,
        load,
        beside,
        table,
        near_pile,
        *packed,
        *other_packed,
        params,
        mine,
        theirs,
    )
    docs |= {0: load, 1: beside, 5: cross(after(docs[4], weight), 1)}
    tables = docs | {1: near_pile}
    for first in range(2, len(masks) - 2, 2):
        pair = masks[first : first + 2]
        best += pl.pallas_call(
            lambda *refs: next_kernel(seq, *refs),
            out_shape=[best_shape] * 2,
            in_specs=[vmem] * 8,
            out_specs=[vmem] * 2,
            compiler_params=limit,
            cost_estimate=cost(2),
        )(
            *[docs[mask] for mask in pair],
            *[tables[mask] for mask in pair],
            after(weight, best[-1]),
            params,
            mine,
            theirs,
        )
    height = (1 + BLK_DEV) * SLOT_ROWS
    keep, give = pl.pallas_call(
        lambda *refs: last_kernel(seq, masks, *refs),
        out_shape=[
            shape((chips, height, TILE), jnp.bfloat16),
            shape((chips, height - SLOT_ROWS, TILE), jnp.bfloat16),
        ],
        in_specs=[smem] + [vmem] * (2 + len(masks) + 5 + len(best)),
        out_specs=[vmem] * 2,
        scratch_shapes=[pltpu.VMEM((devices * height, TILE), jnp.float32)],
        compiler_params=limit,
        cost_estimate=cost(2),
    )(
        where,
        *[docs[mask] for mask in masks[-2:]],
        *[tables[mask] for mask in masks],
        weight,
        params,
        mine,
        theirs,
        decoder_bias.reshape(-1, TILE),
        *best,
    )
    merged = pl.pallas_call(
        merge_kernel,
        out_shape=shape((chips, height, TILE), jnp.bfloat16),
        in_specs=[vmem] * 2,
        out_specs=vmem,
        compiler_params=limit,
    )(keep, swap(give))
    alike = [list(range(parity, devices, 2)) for parity in range(2)]
    got = lax.all_to_all(
        merged, "doc", split_axis=0, concat_axis=0, axis_index_groups=alike, tiled=True
    )
    return pl.pallas_call(
        lambda *refs: place_kernel(tiles, *refs),
        out_shape=[
            shape((1, chips * tiles * TILE), jnp.bfloat16),
            shape((BLK_DEV, chips * tiles * TILE), jnp.bfloat16),
        ],
        in_specs=[vmem],
        out_specs=[vmem] * 2,
        compiler_params=limit,
    )(got)


def tokens_move(mesh):
    return mesh.shape["term"] == 1 and mesh.shape["doc"] == 16


def solution(mesh):
    placed = (
        P(("groups", "doc"), None),
        P(("groups", "doc")),
        P("doc", "term"),
        P(),
        P(),
        P(),
        P("term", None, "doc"),
        P("term"),
        P("term", ("groups", "doc"), None),
        P("term", ("groups", "doc"), None, None),
        P("term", ("groups", "doc"), None),
    )

    def local(*args):
        pair = 2 * args[6].shape[2]
        tiles = pair * (mesh.shape["doc"] // 2) // TILE
        fits = pair % TILE == 0 and tiles < TILE and pair // TILE <= SLOT_ROWS
        if tokens_move(mesh) and args[1].shape[0] == 1 and fits:
            return move_tokens(*args)
        return move_weights(*args)

    return jax.shard_map(
        local,
        mesh=mesh,
        in_specs=placed,
        out_specs=(P(("groups", "doc"), "term"), P(("groups", "doc"), "term")),
        check_vma=False,
    )
```

```python
import jax
import jax.numpy as jnp
from jax import lax
from jax.experimental import pallas as pl
from jax.experimental.pallas import tpu as pltpu
from jax.sharding import PartitionSpec as P

TILE = 128
BLK_DEV = 2
SLOT_ROWS = 16


def layer_norm(activated, norm_gain, norm_bias):
    values = activated.astype(jnp.float32)
    centre = jnp.mean(values, axis=-1, keepdims=True)
    centred = values - centre
    spread = jnp.mean(centred * centred, axis=-1, keepdims=True)
    return (centred * lax.rsqrt(spread + 1e-05) * norm_gain + norm_bias).astype(jnp.bfloat16)


def pool_docs(logits, keep):
    docs_here = keep.shape[0]
    saturated = jnp.log1p(jnp.maximum(logits, 0.0)).reshape(
        docs_here, keep.shape[1], logits.shape[1]
    )
    return jnp.max(jnp.where(keep[:, :, None], saturated, 0.0), axis=1)


def move_weights(
    hidden_states,
    doc_lengths,
    transform_weight,
    transform_bias,
    norm_gain,
    norm_bias,
    decoder_weight,
    decoder_bias,
    tile_ids,
    owner_ids,
    block_slots,
):
    tok_rows = hidden_states.shape[0]
    docs_here = doc_lengths.shape[0]
    seq_len = tok_rows // docs_here
    cols = transform_weight.shape[1]
    pre_half = jnp.dot(
        hidden_states,
        lax.all_gather(transform_weight, "doc", axis=0, tiled=True),
        preferred_element_type=jnp.float32,
    )
    bias_half = lax.dynamic_slice_in_dim(transform_bias, lax.axis_index("term") * cols, cols, 0)
    act_half = jax.nn.gelu(pre_half + bias_half, approximate=False).astype(jnp.bfloat16)
    activated = lax.all_gather(act_half, "term", axis=1, tiled=True)
    normed = layer_norm(activated, norm_gain, norm_bias)
    keep = jnp.arange(seq_len, dtype=jnp.int32)[None, :] < doc_lengths[:, None]
    logits = jnp.dot(
        normed,
        lax.all_gather(decoder_weight, "doc", axis=2, tiled=True)[0],
        preferred_element_type=jnp.float32,
    )
    logits = logits + decoder_bias
    impacts = pool_docs(logits, keep).astype(jnp.bfloat16)
    tiles_t = impacts.shape[1] // TILE
    slots_total = BLK_DEV * tiles_t
    tiles = impacts.reshape(docs_here * tiles_t, TILE)
    chosen = tile_ids[0]
    doc_index = jnp.arange(docs_here, dtype=jnp.int32)[:, None]
    posted = tiles[(doc_index * tiles_t + chosen).reshape(-1)]
    owners = owner_ids[0, :, :, 0].reshape(-1)
    target = block_slots[0].reshape(-1) * tiles_t + chosen.reshape(-1)
    owner_count = lax.axis_size("doc")
    capacity = max(2, 2 * posted.shape[0] // owner_count)
    onehot = (owners[:, None] == jnp.arange(owner_count, dtype=jnp.int32)[None, :]).astype(
        jnp.int32
    )
    before = jnp.cumsum(onehot, axis=0) - onehot
    position = jnp.sum(before * onehot, axis=1)
    dest = owners * capacity + position
    outgoing = jnp.zeros((owner_count * capacity, TILE), jnp.bfloat16).at[dest].set(posted)
    out_tags = jnp.full((owner_count * capacity,), slots_total, jnp.int32).at[dest].set(target)
    got_vals, got_tags = (
        lax.all_to_all(
            outgoing.reshape(owner_count, capacity, TILE),
            "doc",
            split_axis=0,
            concat_axis=0,
            tiled=True,
        ),
        lax.all_to_all(
            out_tags.reshape(owner_count, capacity), "doc", split_axis=0, concat_axis=0, tiled=True
        ),
    )
    got_vals = got_vals.reshape(-1, TILE)
    local_tags = got_tags.reshape(-1)
    summary = jnp.zeros((slots_total, TILE), jnp.bfloat16).at[local_tags].max(got_vals, mode="drop")
    return (impacts, summary.reshape(BLK_DEV, tiles_t * TILE))


def dot_t(left, right):
    return lax.dot_general(
        left, right, (((1,), (1,)), ((), ())), preferred_element_type=jnp.float32
    )


def table_of(ref):
    return ref[ref.shape[0] - SLOT_ROWS :, 0:TILE].astype(jnp.float32)[0:1, :]


def masked(ref, table_ref, seq):
    here = ref[0:seq, :]
    length = table_of(table_ref)[:, TILE - 1 :]
    keep = lax.broadcasted_iota(jnp.int32, here.shape, 0).astype(jnp.float32) < length
    first = jnp.broadcast_to(here[0:1, :].astype(jnp.float32), here.shape).astype(here.dtype)
    return jnp.where(keep, here, first)


def normed_rows(docs, tables, seq, weight, params):
    rows = [masked(ref, table, seq) for ref, table in zip(docs, tables)]
    rows = jnp.concatenate(rows, axis=0)
    pre = jnp.dot(rows, weight[...], preferred_element_type=jnp.float32) + params[0:1, :]
    act = 0.5 * pre * (1.0 + lax.erf(pre * (0.5**0.5)))
    return layer_norm(act.astype(jnp.bfloat16), params[1:2, :], params[2:3, :])


def tops_of(normed, w_ref, count):
    logits = dot_t(normed, w_ref[...])
    seq = normed.shape[0] // count
    return [
        jnp.max(logits[j * seq : (j + 1) * seq], axis=0, keepdims=True) for j in range(count)
    ]


def start_kernel(tiles_ref, owners_ref, slots_ref, length_ref, *refs):
    hidden_ref, weight_ref, vectors = refs[0], refs[1], refs[2:5]
    load_ref, block_ref, table_ref, rows_ref, kept, sems = refs[5:]
    seq, width = hidden_ref.shape
    copies = [
        fetch(hidden_ref, load_ref.at[pl.ds(0, seq), :], sems.at[0]),
        fetch(weight_ref, block_ref, sems.at[1]),
    ]
    for k, ref in enumerate(vectors):
        copies.append(fetch(ref, kept.at[pl.ds(k * width, width)], sems.at[2 + k]))
    lane = lax.broadcasted_iota(jnp.int32, (SLOT_ROWS, TILE), 1)
    table = jnp.where(lane == TILE - 1, length_ref[0], -1)
    devices = lax.axis_size("doc")
    for k in range(tiles_ref.shape[2]):
        block = slots_ref[0, 0, k] * devices + owners_ref[0, 0, k]
        table = jnp.where(lane == tiles_ref[0, 0, k], block, table)
    table = table.astype(jnp.float32).astype(jnp.bfloat16)
    for first in range(0, width, TILE):
        load_ref[seq:, first : first + TILE] = table
        table_ref[:, first : first + TILE] = table
    for copy in copies:
        copy.wait()
    for k in range(len(vectors)):
        rows_ref[k : k + 1, :] = kept[pl.ds(k * width, width)][None, :]


def pile_kernel(parts, heights, *refs):
    rows = jnp.concatenate(
        [ref[first : first + count, :] for ref, (first, count) in zip(refs, parts)], axis=0
    )
    at = 0
    for ref, height in zip(refs[len(parts) :], heights):
        ref[...] = rows[at : at + height, :]
        at += height


def fetch(ref, slot, sem):
    copy = pltpu.make_async_copy(ref, slot, sem)
    copy.start()
    return copy


def keep_tops(normed, halves, bests):
    for w_ref, best in zip(halves, bests):
        for j, top in enumerate(tops_of(normed, w_ref, 2)):
            best[j : j + 1, :] = top


def fetch_kernel(count, *refs):
    copies = [fetch(refs[1 + k], refs[1 + count + k], refs[-1].at[k]) for k in range(count)]
    for copy in copies:
        copy.wait()


def first_kernel(seq, masks, *refs):
    me_ref, docs, tables, refs = refs[0], refs[1:3], refs[3:5], refs[5:]
    count = len(masks) // 2
    parts, others, refs = refs[:count], refs[count : 2 * count], refs[2 * count :]
    params, halves, refs = refs[0], refs[1:3], refs[3:]
    bests, weight = refs[:2], refs[2]
    me = me_ref[0]
    core = me % 2
    rows = weight.shape[0] // (2 * len(masks))
    for k, mask in enumerate(masks):
        chip = (me // 2) ^ mask
        part, place = divmod(k * rows, parts[0].shape[0])
        block = slice(place, place + rows)
        at = pl.multiple_of((2 * chip + core) * rows, SLOT_ROWS)
        weight[pl.ds(at, rows), :] = parts[part][block, :]
        at = pl.multiple_of((2 * chip + 1 - core) * rows, SLOT_ROWS)
        weight[pl.ds(at, rows), :] = others[part][block, :]
    keep_tops(normed_rows(docs, tables, seq, weight, params), halves, bests)


def next_kernel(seq, *refs):
    docs, tables, weight, params, refs = refs[:2], refs[2:4], refs[4], refs[5], refs[6:]
    keep_tops(normed_rows(docs, tables, seq, weight, params), refs[:2], refs[2:])


def last_kernel(seq, masks, *refs):
    me_ref, docs, tables, refs = refs[0], refs[1:3], refs[3 : 3 + len(masks)], refs[3 + len(masks) :]
    weight, params, halves, dbias_ref, refs = refs[0], refs[1], refs[2:4], refs[4], refs[5:]
    earlier, keep_ref, give_ref, send = refs[:-3], *refs[-3:]
    me = me_ref[0]
    core, chip = me % 2, me // 2
    devices = 2 * len(masks)
    tiles = 2 * halves[0].shape[0] // TILE
    normed = normed_rows(docs, docs, seq, weight, params)
    found = []
    for k, w_ref in enumerate(halves):
        parts = [ref[0:2, :] for ref in earlier[k::2]]
        found.append(jnp.concatenate([*parts, *tops_of(normed, w_ref, 2)], axis=0))
    low = jnp.where(core == 0, found[0], found[1])
    high = jnp.where(core == 0, found[1], found[0])
    logits = jnp.concatenate([low, high], axis=1)
    docs_at = [me ^ (2 * mask) for mask in masks]
    bias = dbias_ref[...]
    bias = pltpu.roll(bias, bias.shape[0] - chip * tiles, 0)
    tables = jnp.concatenate([table_of(ref) for ref in tables], axis=0)
    tables = pltpu.roll(tables, TILE - chip * tiles, 1).astype(jnp.int32)
    send[...] = jnp.zeros(send.shape, jnp.float32)
    stride = keep_ref.shape[1]
    target = lax.broadcasted_iota(jnp.int32, (BLK_DEV * devices, TILE), 0)
    for t in range(tiles):
        lanes = slice(t * TILE, (t + 1) * TILE)
        impacts = jnp.log1p(jnp.maximum(logits[:, lanes] + bias[t : t + 1, :], 0.0))
        impacts = impacts.astype(jnp.bfloat16).astype(jnp.float32)
        blocks = jnp.zeros((BLK_DEV * devices, TILE), jnp.float32)
        for n in range(len(masks)):
            row = impacts[n : n + 1, :]
            send[pl.ds(docs_at[n] * stride + t, 1), :] = row
            block = jnp.broadcast_to(tables[n : n + 1, t : t + 1], target.shape)
            blocks = jnp.maximum(blocks, jnp.where(target == block, row, 0.0))
        for s in range(BLK_DEV):
            send[pl.ds((1 + s) * SLOT_ROWS + t, devices, stride=stride), :] = blocks[
                s * devices : (s + 1) * devices
            ]
    for k in range(len(masks)):
        at = pl.multiple_of((2 * k + core) * stride, SLOT_ROWS)
        keep_ref[k] = send[pl.ds(at, stride), :].astype(jnp.bfloat16)
        at = pl.multiple_of((2 * k + 1 - core) * stride + SLOT_ROWS, SLOT_ROWS)
        give_ref[k] = send[pl.ds(at, stride - SLOT_ROWS), :].astype(jnp.bfloat16)


def merge_kernel(keep_ref, got_ref, out_ref):
    out_ref[:, 0:SLOT_ROWS, :] = keep_ref[:, 0:SLOT_ROWS, :]
    mine = keep_ref[:, SLOT_ROWS:, :].astype(jnp.float32)
    theirs = got_ref[...].astype(jnp.float32)
    out_ref[:, SLOT_ROWS:, :] = jnp.maximum(mine, theirs).astype(jnp.bfloat16)


def place_kernel(tiles, rows_ref, impacts_ref, summaries_ref):
    for chip in range(rows_ref.shape[0]):
        rows = rows_ref[chip].astype(jnp.float32)
        lanes = slice(chip * tiles * TILE, (chip + 1) * tiles * TILE)
        lines = [
            jnp.concatenate([rows[first + t : first + t + 1] for t in range(tiles)], axis=1)
            for first in range(0, rows.shape[0], SLOT_ROWS)
        ]
        impacts_ref[:, lanes] = lines[0].astype(jnp.bfloat16)
        summaries_ref[:, lanes] = jnp.concatenate(lines[1:], axis=0).astype(jnp.bfloat16)


def move_tokens(
    hidden_states,
    doc_lengths,
    transform_weight,
    transform_bias,
    norm_gain,
    norm_bias,
    decoder_weight,
    decoder_bias,
    tile_ids,
    owner_ids,
    block_slots,
):
    devices = lax.axis_size("doc")
    chips = devices // 2
    seq, width = hidden_states.shape
    rows = transform_weight.shape[0]
    half = decoder_weight.shape[2]
    tiles = 2 * half // TILE
    me = lax.axis_index("doc").astype(jnp.int32)

    def cross(value, mask):
        return lax.ppermute(value, "doc", [(i, i ^ (2 * mask)) for i in range(devices)])

    def swap(value):
        return lax.ppermute(value, "doc", [(i, i ^ 1) for i in range(devices)])

    smem = pl.BlockSpec(memory_space=pltpu.SMEM)
    vmem = pl.BlockSpec(memory_space=pltpu.VMEM)
    hbm = pl.BlockSpec(memory_space=pltpu.HBM)

    def stay(value):
        return pltpu.with_memory_space_constraint(value, pltpu.HBM)

    limit = pltpu.CompilerParams(vmem_limit_bytes=24 * 1024 * 1024)

    def cost(docs):
        return pl.CostEstimate(flops=docs, bytes_accessed=docs, transcendentals=0)

    def shape(dims, dtype):
        return jax.ShapeDtypeStruct(dims, dtype)

    def after(value, *done):
        return lax.optimization_barrier((value, *done))[0]

    def pile(values, parts, heights=()):
        heights = heights or (sum(count for _, count in parts),)
        piled = pl.pallas_call(
            lambda *refs: pile_kernel(parts, heights, *refs),
            out_shape=[shape((height, width), jnp.bfloat16) for height in heights],
            in_specs=[vmem] * len(values),
            out_specs=[vmem] * len(heights),
            compiler_params=limit,
        )(*values)
        return piled if len(heights) > 1 else piled[0]

    weight_rows = jnp.swapaxes(decoder_weight[0], 0, 1)
    block_6 = cross(transform_weight, 6)
    block_2 = cross(transform_weight, 2)
    theirs = swap(weight_rows)
    docs = {1: cross(hidden_states, 1), 2: cross(hidden_states, 2)}
    load, block, table, params = pl.pallas_call(
        start_kernel,
        out_shape=[
            shape((seq + SLOT_ROWS, width), jnp.bfloat16),
            shape((rows, width), jnp.bfloat16),
            shape((SLOT_ROWS, width), jnp.bfloat16),
            shape((8, width), jnp.float32),
        ],
        in_specs=[smem] * 4 + [hbm] * 5,
        out_specs=[vmem] * 4,
        scratch_shapes=[
            pltpu.VMEM((3 * width,), jnp.float32),
            pltpu.SemaphoreType.DMA((5,)),
        ],
        compiler_params=limit,
    )(
        stay(tile_ids),
        stay(owner_ids[..., 0]),
        stay(block_slots),
        doc_lengths,
        stay(hidden_states),
        stay(transform_weight),
        stay(transform_bias),
        stay(norm_gain),
        stay(norm_bias),
    )
    near = (block, after(block_2, block_6, docs[1]), table)
    near_pile = cross(pile(near, ((0, rows), (0, rows), (0, SLOT_ROWS))), 1)
    one, two = (0, rows), (0, 2 * rows)
    one, two, below = (0, rows), (0, 2 * rows), (0, SLOT_ROWS)
    block_4 = cross(pile((block_6, table), (one, below)), 2)
    docs[6] = cross(after(load, block_6), 6)
    load_1 = pile((docs[1], near_pile), ((0, seq), (2 * rows, SLOT_ROWS)))
    far_from = [stay(after(weight_rows, table)), stay(docs[1])]
    mine, beside = pl.pallas_call(
        lambda *refs: fetch_kernel(2, *refs),
        out_shape=[shape(value.shape, value.dtype) for value in far_from],
        in_specs=[vmem] + [hbm] * 2,
        out_specs=[vmem] * 2,
        scratch_shapes=[pltpu.SemaphoreType.DMA((2,))],
        compiler_params=limit,
    )(table, *far_from)
    far = (block_6, after(block_4, near_pile, docs[2], mine, theirs))
    far = pile(far, (one, one))
    far_pile = cross(far, 1)
    docs[3] = cross(after(load_1, far), 2)
    docs[4] = cross(after(docs[6], far), 2)
    docs[7] = cross(docs[6], 1)
    late = (docs[6], docs[3])
    sources = (after(block, *late), block_2, block_6, block_4, near_pile, far_pile)
    packed = pile(sources, (one, one, one, one, two, two), (2 * rows,) * (chips // 2))
    other_packed = [swap(part) for part in packed]
    block_masks = [0, 2, 6, 4, 1, 3, 7, 5]

    masks = [0, 1, 2, 3, 6, 7, 4, 5]
    where = me[None]
    best_shape = shape((8, half), jnp.float32)
    *best, weight = pl.pallas_call(
        lambda *refs: first_kernel(seq, block_masks, *refs),
        out_shape=[best_shape, best_shape, shape((width, width), jnp.bfloat16)],
        in_specs=[smem] + [vmem] * (7 + 2 * len(packed)),
        out_specs=[vmem] * 3,
        compiler_params=limit,
        cost_estimate=cost(2),
    )(
        where,
        load,
        beside,
        table,
        near_pile,
        *packed,
        *other_packed,
        params,
        mine,
        theirs,
    )
    docs |= {0: load, 1: beside, 5: cross(after(docs[4], weight), 1)}
    tables = docs | {1: near_pile, 2: block_4}
    for first in range(2, len(masks) - 2, 2):
        pair = masks[first : first + 2]
        best += pl.pallas_call(
            lambda *refs: next_kernel(seq, *refs),
            out_shape=[best_shape] * 2,
            in_specs=[vmem] * 8,
            out_specs=[vmem] * 2,
            compiler_params=limit,
            cost_estimate=cost(2),
        )(
            *[docs[mask] for mask in pair],
            *[tables[mask] for mask in pair],
            after(weight, best[-1]),
            params,
            mine,
            theirs,
        )
    height = (1 + BLK_DEV) * SLOT_ROWS
    keep, give = pl.pallas_call(
        lambda *refs: last_kernel(seq, masks, *refs),
        out_shape=[
            shape((chips, height, TILE), jnp.bfloat16),
            shape((chips, height - SLOT_ROWS, TILE), jnp.bfloat16),
        ],
        in_specs=[smem] + [vmem] * (2 + len(masks) + 5 + len(best)),
        out_specs=[vmem] * 2,
        scratch_shapes=[pltpu.VMEM((devices * height, TILE), jnp.float32)],
        compiler_params=limit,
        cost_estimate=cost(2),
    )(
        where,
        *[docs[mask] for mask in masks[-2:]],
        *[tables[mask] for mask in masks],
        weight,
        params,
        mine,
        theirs,
        decoder_bias.reshape(-1, TILE),
        *best,
    )
    merged = pl.pallas_call(
        merge_kernel,
        out_shape=shape((chips, height, TILE), jnp.bfloat16),
        in_specs=[vmem] * 2,
        out_specs=vmem,
        compiler_params=limit,
    )(keep, swap(give))
    alike = [list(range(parity, devices, 2)) for parity in range(2)]
    got = lax.all_to_all(
        merged, "doc", split_axis=0, concat_axis=0, axis_index_groups=alike, tiled=True
    )
    return pl.pallas_call(
        lambda *refs: place_kernel(tiles, *refs),
        out_shape=[
            shape((1, chips * tiles * TILE), jnp.bfloat16),
            shape((BLK_DEV, chips * tiles * TILE), jnp.bfloat16),
        ],
        in_specs=[vmem],
        out_specs=[vmem] * 2,
        compiler_params=limit,
    )(got)


def tokens_move(mesh):
    return mesh.shape["term"] == 1 and mesh.shape["doc"] == 16


def solution(mesh):
    placed = (
        P(("groups", "doc"), None),
        P(("groups", "doc")),
        P("doc", "term"),
        P(),
        P(),
        P(),
        P("term", None, "doc"),
        P("term"),
        P("term", ("groups", "doc"), None),
        P("term", ("groups", "doc"), None, None),
        P("term", ("groups", "doc"), None),
    )

    def local(*args):
        pair = 2 * args[6].shape[2]
        tiles = pair * (mesh.shape["doc"] // 2) // TILE
        fits = pair % TILE == 0 and tiles < TILE and pair // TILE <= SLOT_ROWS
        if tokens_move(mesh) and args[1].shape[0] == 1 and fits:
            return move_tokens(*args)
        return move_weights(*args)

    return jax.shard_map(
        local,
        mesh=mesh,
        in_specs=placed,
        out_specs=(P(("groups", "doc"), "term"), P(("groups", "doc"), "term")),
        check_vma=False,
    )
```

```python
import jax
import jax.numpy as jnp
from jax import lax
from jax.experimental import pallas as pl
from jax.experimental.pallas import tpu as pltpu
from jax.sharding import PartitionSpec as P

TILE = 128
BLK_DEV = 2
SLOT_ROWS = 16


def layer_norm(activated, norm_gain, norm_bias):
    values = activated.astype(jnp.float32)
    centre = jnp.mean(values, axis=-1, keepdims=True)
    centred = values - centre
    spread = jnp.mean(centred * centred, axis=-1, keepdims=True)
    return (centred * lax.rsqrt(spread + 1e-05) * norm_gain + norm_bias).astype(jnp.bfloat16)


def pool_docs(logits, keep):
    docs_here = keep.shape[0]
    saturated = jnp.log1p(jnp.maximum(logits, 0.0)).reshape(
        docs_here, keep.shape[1], logits.shape[1]
    )
    return jnp.max(jnp.where(keep[:, :, None], saturated, 0.0), axis=1)


def move_weights(
    hidden_states,
    doc_lengths,
    transform_weight,
    transform_bias,
    norm_gain,
    norm_bias,
    decoder_weight,
    decoder_bias,
    tile_ids,
    owner_ids,
    block_slots,
):
    tok_rows = hidden_states.shape[0]
    docs_here = doc_lengths.shape[0]
    seq_len = tok_rows // docs_here
    cols = transform_weight.shape[1]
    pre_half = jnp.dot(
        hidden_states,
        lax.all_gather(transform_weight, "doc", axis=0, tiled=True),
        preferred_element_type=jnp.float32,
    )
    bias_half = lax.dynamic_slice_in_dim(transform_bias, lax.axis_index("term") * cols, cols, 0)
    act_half = jax.nn.gelu(pre_half + bias_half, approximate=False).astype(jnp.bfloat16)
    activated = lax.all_gather(act_half, "term", axis=1, tiled=True)
    normed = layer_norm(activated, norm_gain, norm_bias)
    keep = jnp.arange(seq_len, dtype=jnp.int32)[None, :] < doc_lengths[:, None]
    logits = jnp.dot(
        normed,
        lax.all_gather(decoder_weight, "doc", axis=2, tiled=True)[0],
        preferred_element_type=jnp.float32,
    )
    logits = logits + decoder_bias
    impacts = pool_docs(logits, keep).astype(jnp.bfloat16)
    tiles_t = impacts.shape[1] // TILE
    slots_total = BLK_DEV * tiles_t
    tiles = impacts.reshape(docs_here * tiles_t, TILE)
    chosen = tile_ids[0]
    doc_index = jnp.arange(docs_here, dtype=jnp.int32)[:, None]
    posted = tiles[(doc_index * tiles_t + chosen).reshape(-1)]
    owners = owner_ids[0, :, :, 0].reshape(-1)
    target = block_slots[0].reshape(-1) * tiles_t + chosen.reshape(-1)
    owner_count = lax.axis_size("doc")
    capacity = max(2, 2 * posted.shape[0] // owner_count)
    onehot = (owners[:, None] == jnp.arange(owner_count, dtype=jnp.int32)[None, :]).astype(
        jnp.int32
    )
    before = jnp.cumsum(onehot, axis=0) - onehot
    position = jnp.sum(before * onehot, axis=1)
    dest = owners * capacity + position
    outgoing = jnp.zeros((owner_count * capacity, TILE), jnp.bfloat16).at[dest].set(posted)
    out_tags = jnp.full((owner_count * capacity,), slots_total, jnp.int32).at[dest].set(target)
    got_vals, got_tags = (
        lax.all_to_all(
            outgoing.reshape(owner_count, capacity, TILE),
            "doc",
            split_axis=0,
            concat_axis=0,
            tiled=True,
        ),
        lax.all_to_all(
            out_tags.reshape(owner_count, capacity), "doc", split_axis=0, concat_axis=0, tiled=True
        ),
    )
    got_vals = got_vals.reshape(-1, TILE)
    local_tags = got_tags.reshape(-1)
    summary = jnp.zeros((slots_total, TILE), jnp.bfloat16).at[local_tags].max(got_vals, mode="drop")
    return (impacts, summary.reshape(BLK_DEV, tiles_t * TILE))


def dot_t(left, right):
    return lax.dot_general(
        left, right, (((1,), (1,)), ((), ())), preferred_element_type=jnp.float32
    )


def table_of(ref):
    return ref[ref.shape[0] - SLOT_ROWS :, 0:TILE].astype(jnp.float32)[0:1, :]


def masked(ref, table_ref, seq):
    here = ref[0:seq, :]
    length = table_of(table_ref)[:, TILE - 1 :]
    keep = lax.broadcasted_iota(jnp.int32, here.shape, 0).astype(jnp.float32) < length
    first = jnp.broadcast_to(here[0:1, :].astype(jnp.float32), here.shape).astype(here.dtype)
    return jnp.where(keep, here, first)


def normed_rows(docs, tables, seq, weight, params):
    rows = [masked(ref, table, seq) for ref, table in zip(docs, tables)]
    rows = jnp.concatenate(rows, axis=0)
    pre = jnp.dot(rows, weight[...], preferred_element_type=jnp.float32) + params[0:1, :]
    act = 0.5 * pre * (1.0 + lax.erf(pre * (0.5**0.5)))
    return layer_norm(act.astype(jnp.bfloat16), params[1:2, :], params[2:3, :])


def tops_of(normed, w_ref, count):
    logits = dot_t(normed, w_ref[...])
    seq = normed.shape[0] // count
    return [
        jnp.max(logits[j * seq : (j + 1) * seq], axis=0, keepdims=True) for j in range(count)
    ]


def start_kernel(me_ref, tiles_ref, owners_ref, slots_ref, length_ref, *refs):
    hidden_ref, weight_ref, vectors = refs[0], refs[1], refs[2:5]
    load_ref, block_ref, table_ref, rows_ref, kept, sems = refs[5:]
    seq, width = hidden_ref.shape
    copies = [
        fetch(hidden_ref, load_ref.at[pl.ds(0, seq), :], sems.at[0]),
        fetch(weight_ref, block_ref, sems.at[1]),
    ]
    for k, ref in enumerate(vectors):
        copies.append(fetch(ref, kept.at[pl.ds(k * width, width)], sems.at[2 + k]))
    lane = lax.broadcasted_iota(jnp.int32, (SLOT_ROWS, TILE), 1)
    table = jnp.where(lane == TILE - 1, length_ref[0], -1)
    devices = lax.axis_size("doc")
    for k in range(tiles_ref.shape[2]):
        block = slots_ref[0, 0, k] * devices + owners_ref[0, 0, k]
        table = jnp.where(lane == tiles_ref[0, 0, k], block, table)
    table = table.astype(jnp.float32).astype(jnp.bfloat16)
    for first in range(0, width, TILE):
        load_ref[seq:, first : first + TILE] = table
        table_ref[:, first : first + TILE] = table
    for copy in copies:
        copy.wait()
    for k in range(len(vectors)):
        rows_ref[k : k + 1, :] = kept[pl.ds(k * width, width)][None, :]


def pile_kernel(parts, heights, *refs):
    rows = jnp.concatenate(
        [ref[first : first + count, :] for ref, (first, count) in zip(refs, parts)], axis=0
    )
    at = 0
    for ref, height in zip(refs[len(parts) :], heights):
        ref[...] = rows[at : at + height, :]
        at += height


def fetch(ref, slot, sem):
    copy = pltpu.make_async_copy(ref, slot, sem)
    copy.start()
    return copy


def keep_tops(normed, halves, bests):
    for w_ref, best in zip(halves, bests):
        for j, top in enumerate(tops_of(normed, w_ref, 2)):
            best[j : j + 1, :] = top


def fetch_kernel(count, *refs):
    copies = [fetch(refs[1 + k], refs[1 + count + k], refs[-1].at[k]) for k in range(count)]
    for copy in copies:
        copy.wait()


def first_kernel(seq, masks, *refs):
    me_ref, docs, tables, refs = refs[0], refs[1:3], refs[3:5], refs[5:]
    count = len(masks) // 2
    parts, others, refs = refs[:count], refs[count : 2 * count], refs[2 * count :]
    params, halves, refs = refs[0], refs[1:3], refs[3:]
    bests, weight = refs[:2], refs[2]
    me = me_ref[0]
    core = me % 2
    rows = weight.shape[0] // (2 * len(masks))
    for k, mask in enumerate(masks):
        chip = (me // 2) ^ mask
        part, place = divmod(k * rows, parts[0].shape[0])
        block = slice(place, place + rows)
        at = pl.multiple_of((2 * chip + core) * rows, SLOT_ROWS)
        weight[pl.ds(at, rows), :] = parts[part][block, :]
        at = pl.multiple_of((2 * chip + 1 - core) * rows, SLOT_ROWS)
        weight[pl.ds(at, rows), :] = others[part][block, :]
    keep_tops(normed_rows(docs, tables, seq, weight, params), halves, bests)


def next_kernel(seq, *refs):
    docs, tables, weight, params, refs = refs[:2], refs[2:4], refs[4], refs[5], refs[6:]
    keep_tops(normed_rows(docs, tables, seq, weight, params), refs[:2], refs[2:])


def last_kernel(seq, masks, *refs):
    me_ref, docs, tables, refs = refs[0], refs[1:3], refs[3 : 3 + len(masks)], refs[3 + len(masks) :]
    weight, params, halves, dbias_ref, refs = refs[0], refs[1], refs[2:4], refs[4], refs[5:]
    earlier, keep_ref, give_ref, send = refs[:-3], *refs[-3:]
    me = me_ref[0]
    core, chip = me % 2, me // 2
    devices = 2 * len(masks)
    tiles = 2 * halves[0].shape[0] // TILE
    normed = normed_rows(docs, docs, seq, weight, params)
    found = []
    for k, w_ref in enumerate(halves):
        parts = [ref[0:2, :] for ref in earlier[k::2]]
        found.append(jnp.concatenate([*parts, *tops_of(normed, w_ref, 2)], axis=0))
    low = jnp.where(core == 0, found[0], found[1])
    high = jnp.where(core == 0, found[1], found[0])
    logits = jnp.concatenate([low, high], axis=1)
    docs_at = [me ^ (2 * mask) for mask in masks]
    bias = dbias_ref[...]
    bias = pltpu.roll(bias, bias.shape[0] - chip * tiles, 0)
    tables = jnp.concatenate([table_of(ref) for ref in tables], axis=0)
    tables = pltpu.roll(tables, TILE - chip * tiles, 1).astype(jnp.int32)
    send[...] = jnp.zeros(send.shape, jnp.float32)
    stride = keep_ref.shape[1]
    target = lax.broadcasted_iota(jnp.int32, (BLK_DEV * devices, TILE), 0)
    for t in range(tiles):
        lanes = slice(t * TILE, (t + 1) * TILE)
        impacts = jnp.log1p(jnp.maximum(logits[:, lanes] + bias[t : t + 1, :], 0.0))
        impacts = impacts.astype(jnp.bfloat16).astype(jnp.float32)
        blocks = jnp.zeros((BLK_DEV * devices, TILE), jnp.float32)
        for n in range(len(masks)):
            row = impacts[n : n + 1, :]
            send[pl.ds(docs_at[n] * stride + t, 1), :] = row
            block = jnp.broadcast_to(tables[n : n + 1, t : t + 1], target.shape)
            blocks = jnp.maximum(blocks, jnp.where(target == block, row, 0.0))
        for s in range(BLK_DEV):
            send[pl.ds((1 + s) * SLOT_ROWS + t, devices, stride=stride), :] = blocks[
                s * devices : (s + 1) * devices
            ]
    for k in range(len(masks)):
        at = pl.multiple_of((2 * k + core) * stride, SLOT_ROWS)
        keep_ref[k] = send[pl.ds(at, stride), :].astype(jnp.bfloat16)
        at = pl.multiple_of((2 * k + 1 - core) * stride + SLOT_ROWS, SLOT_ROWS)
        give_ref[k] = send[pl.ds(at, stride - SLOT_ROWS), :].astype(jnp.bfloat16)


def merge_kernel(keep_ref, got_ref, out_ref):
    out_ref[:, 0:SLOT_ROWS, :] = keep_ref[:, 0:SLOT_ROWS, :]
    mine = keep_ref[:, SLOT_ROWS:, :].astype(jnp.float32)
    theirs = got_ref[...].astype(jnp.float32)
    out_ref[:, SLOT_ROWS:, :] = jnp.maximum(mine, theirs).astype(jnp.bfloat16)


def place_kernel(tiles, rows_ref, impacts_ref, summaries_ref):
    for chip in range(rows_ref.shape[0]):
        rows = rows_ref[chip].astype(jnp.float32)
        lanes = slice(chip * tiles * TILE, (chip + 1) * tiles * TILE)
        lines = [
            jnp.concatenate([rows[first + t : first + t + 1] for t in range(tiles)], axis=1)
            for first in range(0, rows.shape[0], SLOT_ROWS)
        ]
        impacts_ref[:, lanes] = lines[0].astype(jnp.bfloat16)
        summaries_ref[:, lanes] = jnp.concatenate(lines[1:], axis=0).astype(jnp.bfloat16)


def move_tokens(
    hidden_states,
    doc_lengths,
    transform_weight,
    transform_bias,
    norm_gain,
    norm_bias,
    decoder_weight,
    decoder_bias,
    tile_ids,
    owner_ids,
    block_slots,
):
    devices = lax.axis_size("doc")
    chips = devices // 2
    seq, width = hidden_states.shape
    rows = transform_weight.shape[0]
    half = decoder_weight.shape[2]
    tiles = 2 * half // TILE
    me = lax.axis_index("doc").astype(jnp.int32)

    def cross(value, mask):
        return lax.ppermute(value, "doc", [(i, i ^ (2 * mask)) for i in range(devices)])

    def swap(value):
        return lax.ppermute(value, "doc", [(i, i ^ 1) for i in range(devices)])

    smem = pl.BlockSpec(memory_space=pltpu.SMEM)
    vmem = pl.BlockSpec(memory_space=pltpu.VMEM)
    hbm = pl.BlockSpec(memory_space=pltpu.HBM)

    def stay(value):
        return pltpu.with_memory_space_constraint(value, pltpu.HBM)

    limit = pltpu.CompilerParams(vmem_limit_bytes=24 * 1024 * 1024)

    def cost(docs):
        return pl.CostEstimate(flops=docs, bytes_accessed=docs, transcendentals=0)

    def shape(dims, dtype):
        return jax.ShapeDtypeStruct(dims, dtype)

    def after(value, *done):
        return lax.optimization_barrier((value, *done))[0]

    def pile(values, parts, heights=()):
        heights = heights or (sum(count for _, count in parts),)
        piled = pl.pallas_call(
            lambda *refs: pile_kernel(parts, heights, *refs),
            out_shape=[shape((height, width), jnp.bfloat16) for height in heights],
            in_specs=[vmem] * len(values),
            out_specs=[vmem] * len(heights),
            compiler_params=limit,
        )(*values)
        return piled if len(heights) > 1 else piled[0]

    where = me[None]
    weight_rows = jnp.swapaxes(decoder_weight[0], 0, 1)
    block_6 = cross(transform_weight, 6)
    block_2 = cross(transform_weight, 2)
    theirs = swap(weight_rows)
    docs = {1: cross(hidden_states, 1), 2: cross(hidden_states, 2)}
    load, block, table, params = pl.pallas_call(
        start_kernel,
        out_shape=[
            shape((seq + SLOT_ROWS, width), jnp.bfloat16),
            shape((rows, width), jnp.bfloat16),
            shape((SLOT_ROWS, width), jnp.bfloat16),
            shape((8, width), jnp.float32),
        ],
        in_specs=[smem] * 5 + [hbm] * 5,
        out_specs=[vmem] * 4,
        scratch_shapes=[
            pltpu.VMEM((3 * width,), jnp.float32),
            pltpu.SemaphoreType.DMA((5,)),
        ],
        compiler_params=limit,
    )(
        where,
        stay(tile_ids),
        stay(owner_ids[..., 0]),
        stay(block_slots),
        doc_lengths,
        stay(hidden_states),
        stay(transform_weight),
        stay(transform_bias),
        stay(norm_gain),
        stay(norm_bias),
    )
    near = (block, after(block_2, block_6, docs[1]), table)
    near_pile = cross(pile(near, ((0, rows), (0, rows), (0, SLOT_ROWS))), 1)
    one, two = (0, rows), (0, 2 * rows)
    one, two, below = (0, rows), (0, 2 * rows), (0, SLOT_ROWS)
    block_4 = cross(pile((block_6, table), (one, below)), 2)
    docs[6] = cross(after(load, block_6), 6)
    load_1 = pile((docs[1], near_pile), ((0, seq), (2 * rows, SLOT_ROWS)))
    far_from = [stay(after(weight_rows, table))]
    [mine] = pl.pallas_call(
        lambda *refs: fetch_kernel(1, *refs),
        out_shape=[shape(value.shape, value.dtype) for value in far_from],
        in_specs=[vmem] + [hbm],
        out_specs=[vmem],
        scratch_shapes=[pltpu.SemaphoreType.DMA((1,))],
        compiler_params=limit,
    )(table, *far_from)
    far = (block_6, after(block_4, near_pile, docs[2], mine, theirs))
    far = pile(far, (one, one))
    far_pile = cross(far, 1)
    docs[3] = cross(after(load_1, far), 2)
    docs[4] = cross(after(docs[6], far), 2)
    docs[7] = cross(docs[6], 1)
    late = (docs[6], docs[3])
    sources = (after(block, *late), block_2, block_6, block_4, near_pile, far_pile)
    packed = pile(sources, (one, one, one, one, two, two), (2 * rows,) * (chips // 2))
    other_packed = [swap(part) for part in packed]
    block_masks = [0, 2, 6, 4, 1, 3, 7, 5]

    masks = [0, 1, 2, 3, 6, 7, 4, 5]
    best_shape = shape((8, half), jnp.float32)
    *best, weight = pl.pallas_call(
        lambda *refs: first_kernel(seq, block_masks, *refs),
        out_shape=[best_shape, best_shape, shape((width, width), jnp.bfloat16)],
        in_specs=[smem] + [vmem] * (7 + 2 * len(packed)),
        out_specs=[vmem] * 3,
        compiler_params=limit,
        cost_estimate=cost(2),
    )(
        where,
        load,
        docs[1],
        table,
        near_pile,
        *packed,
        *other_packed,
        params,
        mine,
        theirs,
    )
    docs |= {0: load, 5: cross(after(docs[4], weight), 1)}
    tables = docs | {1: near_pile, 2: block_4}
    for first in range(2, len(masks) - 2, 2):
        pair = masks[first : first + 2]
        best += pl.pallas_call(
            lambda *refs: next_kernel(seq, *refs),
            out_shape=[best_shape] * 2,
            in_specs=[vmem] * 8,
            out_specs=[vmem] * 2,
            compiler_params=limit,
            cost_estimate=cost(2),
        )(
            *[docs[mask] for mask in pair],
            *[tables[mask] for mask in pair],
            after(weight, best[-1]),
            params,
            mine,
            theirs,
        )
    height = (1 + BLK_DEV) * SLOT_ROWS
    keep, give = pl.pallas_call(
        lambda *refs: last_kernel(seq, masks, *refs),
        out_shape=[
            shape((chips, height, TILE), jnp.bfloat16),
            shape((chips, height - SLOT_ROWS, TILE), jnp.bfloat16),
        ],
        in_specs=[smem] + [vmem] * (2 + len(masks) + 5 + len(best)),
        out_specs=[vmem] * 2,
        scratch_shapes=[pltpu.VMEM((devices * height, TILE), jnp.float32)],
        compiler_params=limit,
        cost_estimate=cost(2),
    )(
        where,
        *[docs[mask] for mask in masks[-2:]],
        *[tables[mask] for mask in masks],
        weight,
        params,
        mine,
        theirs,
        decoder_bias.reshape(-1, TILE),
        *best,
    )
    merged = pl.pallas_call(
        merge_kernel,
        out_shape=shape((chips, height, TILE), jnp.bfloat16),
        in_specs=[vmem] * 2,
        out_specs=vmem,
        compiler_params=limit,
    )(keep, swap(give))
    alike = [list(range(parity, devices, 2)) for parity in range(2)]
    got = lax.all_to_all(
        merged, "doc", split_axis=0, concat_axis=0, axis_index_groups=alike, tiled=True
    )
    return pl.pallas_call(
        lambda *refs: place_kernel(tiles, *refs),
        out_shape=[
            shape((1, chips * tiles * TILE), jnp.bfloat16),
            shape((BLK_DEV, chips * tiles * TILE), jnp.bfloat16),
        ],
        in_specs=[vmem],
        out_specs=[vmem] * 2,
        compiler_params=limit,
    )(got)


def tokens_move(mesh):
    return mesh.shape["term"] == 1 and mesh.shape["doc"] == 16


def solution(mesh):
    placed = (
        P(("groups", "doc"), None),
        P(("groups", "doc")),
        P("doc", "term"),
        P(),
        P(),
        P(),
        P("term", None, "doc"),
        P("term"),
        P("term", ("groups", "doc"), None),
        P("term", ("groups", "doc"), None, None),
        P("term", ("groups", "doc"), None),
    )

    def local(*args):
        pair = 2 * args[6].shape[2]
        tiles = pair * (mesh.shape["doc"] // 2) // TILE
        fits = pair % TILE == 0 and tiles < TILE and pair // TILE <= SLOT_ROWS
        if tokens_move(mesh) and args[1].shape[0] == 1 and fits:
            return move_tokens(*args)
        return move_weights(*args)

    return jax.shard_map(
        local,
        mesh=mesh,
        in_specs=placed,
        out_specs=(P(("groups", "doc"), "term"), P(("groups", "doc"), "term")),
        check_vma=False,
    )
```

```python
import jax
import jax.numpy as jnp
from jax import lax
from jax.experimental import pallas as pl
from jax.experimental.pallas import tpu as pltpu
from jax.sharding import PartitionSpec as P

TILE = 128
BLK_DEV = 2
SLOT_ROWS = 16


def layer_norm(activated, norm_gain, norm_bias):
    values = activated.astype(jnp.float32)
    centre = jnp.mean(values, axis=-1, keepdims=True)
    centred = values - centre
    spread = jnp.mean(centred * centred, axis=-1, keepdims=True)
    return (centred * lax.rsqrt(spread + 1e-05) * norm_gain + norm_bias).astype(jnp.bfloat16)


def pool_docs(logits, keep):
    docs_here = keep.shape[0]
    saturated = jnp.log1p(jnp.maximum(logits, 0.0)).reshape(
        docs_here, keep.shape[1], logits.shape[1]
    )
    return jnp.max(jnp.where(keep[:, :, None], saturated, 0.0), axis=1)


def move_weights(
    hidden_states,
    doc_lengths,
    transform_weight,
    transform_bias,
    norm_gain,
    norm_bias,
    decoder_weight,
    decoder_bias,
    tile_ids,
    owner_ids,
    block_slots,
):
    tok_rows = hidden_states.shape[0]
    docs_here = doc_lengths.shape[0]
    seq_len = tok_rows // docs_here
    cols = transform_weight.shape[1]
    pre_half = jnp.dot(
        hidden_states,
        lax.all_gather(transform_weight, "doc", axis=0, tiled=True),
        preferred_element_type=jnp.float32,
    )
    bias_half = lax.dynamic_slice_in_dim(transform_bias, lax.axis_index("term") * cols, cols, 0)
    act_half = jax.nn.gelu(pre_half + bias_half, approximate=False).astype(jnp.bfloat16)
    activated = lax.all_gather(act_half, "term", axis=1, tiled=True)
    normed = layer_norm(activated, norm_gain, norm_bias)
    keep = jnp.arange(seq_len, dtype=jnp.int32)[None, :] < doc_lengths[:, None]
    logits = jnp.dot(
        normed,
        lax.all_gather(decoder_weight, "doc", axis=2, tiled=True)[0],
        preferred_element_type=jnp.float32,
    )
    logits = logits + decoder_bias
    impacts = pool_docs(logits, keep).astype(jnp.bfloat16)
    tiles_t = impacts.shape[1] // TILE
    slots_total = BLK_DEV * tiles_t
    tiles = impacts.reshape(docs_here * tiles_t, TILE)
    chosen = tile_ids[0]
    doc_index = jnp.arange(docs_here, dtype=jnp.int32)[:, None]
    posted = tiles[(doc_index * tiles_t + chosen).reshape(-1)]
    owners = owner_ids[0, :, :, 0].reshape(-1)
    target = block_slots[0].reshape(-1) * tiles_t + chosen.reshape(-1)
    owner_count = lax.axis_size("doc")
    capacity = max(2, 2 * posted.shape[0] // owner_count)
    onehot = (owners[:, None] == jnp.arange(owner_count, dtype=jnp.int32)[None, :]).astype(
        jnp.int32
    )
    before = jnp.cumsum(onehot, axis=0) - onehot
    position = jnp.sum(before * onehot, axis=1)
    dest = owners * capacity + position
    outgoing = jnp.zeros((owner_count * capacity, TILE), jnp.bfloat16).at[dest].set(posted)
    out_tags = jnp.full((owner_count * capacity,), slots_total, jnp.int32).at[dest].set(target)
    got_vals, got_tags = (
        lax.all_to_all(
            outgoing.reshape(owner_count, capacity, TILE),
            "doc",
            split_axis=0,
            concat_axis=0,
            tiled=True,
        ),
        lax.all_to_all(
            out_tags.reshape(owner_count, capacity), "doc", split_axis=0, concat_axis=0, tiled=True
        ),
    )
    got_vals = got_vals.reshape(-1, TILE)
    local_tags = got_tags.reshape(-1)
    summary = jnp.zeros((slots_total, TILE), jnp.bfloat16).at[local_tags].max(got_vals, mode="drop")
    return (impacts, summary.reshape(BLK_DEV, tiles_t * TILE))


def dot_t(left, right):
    return lax.dot_general(
        left, right, (((1,), (1,)), ((), ())), preferred_element_type=jnp.float32
    )


def table_of(ref):
    return ref[ref.shape[0] - SLOT_ROWS :, 0:TILE].astype(jnp.float32)[0:1, :]


def masked(ref, table_ref, seq):
    here = ref[0:seq, :]
    length = table_of(table_ref)[:, TILE - 1 :]
    keep = lax.broadcasted_iota(jnp.int32, here.shape, 0).astype(jnp.float32) < length
    first = jnp.broadcast_to(here[0:1, :].astype(jnp.float32), here.shape).astype(here.dtype)
    return jnp.where(keep, here, first)


def normed_rows(docs, tables, seq, weight, params):
    rows = [masked(ref, table, seq) for ref, table in zip(docs, tables)]
    rows = jnp.concatenate(rows, axis=0)
    pre = jnp.dot(rows, weight[...], preferred_element_type=jnp.float32) + params[0:1, :]
    act = 0.5 * pre * (1.0 + lax.erf(pre * (0.5**0.5)))
    return layer_norm(act.astype(jnp.bfloat16), params[1:2, :], params[2:3, :])


def tops_of(normed, w_ref, count):
    logits = dot_t(normed, w_ref[...])
    seq = normed.shape[0] // count
    return [
        jnp.max(logits[j * seq : (j + 1) * seq], axis=0, keepdims=True) for j in range(count)
    ]


def start_kernel(me_ref, tiles_ref, owners_ref, slots_ref, length_ref, *refs):
    hidden_ref, weight_ref, vectors = refs[0], refs[1], refs[2:5]
    load_ref, block_ref, table_ref, rows_ref, kept, sems = refs[5:]
    seq, width = hidden_ref.shape
    copies = [
        fetch(hidden_ref, load_ref.at[pl.ds(0, seq), :], sems.at[0]),
        fetch(weight_ref, block_ref, sems.at[1]),
    ]
    for k, ref in enumerate(vectors):
        copies.append(fetch(ref, kept.at[pl.ds(k * width, width)], sems.at[2 + k]))
    lane = lax.broadcasted_iota(jnp.int32, (SLOT_ROWS, TILE), 1)
    table = jnp.where(lane == TILE - 1, length_ref[0], -1)
    devices = lax.axis_size("doc")
    for k in range(tiles_ref.shape[2]):
        block = slots_ref[0, 0, k] * devices + owners_ref[0, 0, k]
        table = jnp.where(lane == tiles_ref[0, 0, k], block, table)
    table = table.astype(jnp.float32).astype(jnp.bfloat16)
    for first in range(0, width, TILE):
        load_ref[seq:, first : first + TILE] = table
        table_ref[:, first : first + TILE] = table
    for copy in copies:
        copy.wait()
    for k in range(len(vectors)):
        rows_ref[k : k + 1, :] = kept[pl.ds(k * width, width)][None, :]


def pile_kernel(parts, heights, *refs):
    rows = jnp.concatenate(
        [ref[first : first + count, :] for ref, (first, count) in zip(refs, parts)], axis=0
    )
    at = 0
    for ref, height in zip(refs[len(parts) :], heights):
        ref[...] = rows[at : at + height, :]
        at += height


def fetch(ref, slot, sem):
    copy = pltpu.make_async_copy(ref, slot, sem)
    copy.start()
    return copy


def keep_tops(normed, halves, bests):
    for w_ref, best in zip(halves, bests):
        for j, top in enumerate(tops_of(normed, w_ref, 2)):
            best[j : j + 1, :] = top


def fetch_kernel(count, *refs):
    copies = [fetch(refs[1 + k], refs[1 + count + k], refs[-1].at[k]) for k in range(count)]
    for copy in copies:
        copy.wait()


def first_kernel(seq, shard, masks, *refs):
    me_ref, docs, tables, refs = refs[0], refs[1:3], refs[3:5], refs[5:]
    count = len(masks) * shard // seq
    parts, others, refs = refs[:count], refs[count : 2 * count], refs[2 * count :]
    params, halves, refs = refs[0], refs[1:3], refs[3:]
    bests, weight = refs[:2], refs[2]
    me = me_ref[0]
    core = me % 2
    for at in range(0, len(masks) * shard, SLOT_ROWS):
        (k, inside), (part, place) = divmod(at, shard), divmod(at, seq)
        chip = (me // 2) ^ masks[k]
        for whose, sources in ((core, parts), (1 - core, others)):
            to = pl.multiple_of((2 * chip + whose) * shard + inside, SLOT_ROWS)
            weight[pl.ds(to, SLOT_ROWS), :] = sources[part][place : place + SLOT_ROWS, :]
    keep_tops(normed_rows(docs, tables, seq, weight, params), halves, bests)


def next_kernel(seq, *refs):
    docs, tables, weight, params, refs = refs[:2], refs[2:4], refs[4], refs[5], refs[6:]
    keep_tops(normed_rows(docs, tables, seq, weight, params), refs[:2], refs[2:])


def last_kernel(seq, masks, *refs):
    me_ref, docs, tables, refs = refs[0], refs[1:3], refs[3 : 3 + len(masks)], refs[3 + len(masks) :]
    weight, params, halves, dbias_ref, refs = refs[0], refs[1], refs[2:4], refs[4], refs[5:]
    earlier, keep_ref, give_ref, send = refs[:-3], *refs[-3:]
    me = me_ref[0]
    core, chip = me % 2, me // 2
    devices = 2 * len(masks)
    tiles = 2 * halves[0].shape[0] // TILE
    normed = normed_rows(docs, docs, seq, weight, params)
    found = []
    for k, w_ref in enumerate(halves):
        parts = [ref[0:2, :] for ref in earlier[k::2]]
        found.append(jnp.concatenate([*parts, *tops_of(normed, w_ref, 2)], axis=0))
    low = jnp.where(core == 0, found[0], found[1])
    high = jnp.where(core == 0, found[1], found[0])
    logits = jnp.concatenate([low, high], axis=1)
    docs_at = [me ^ (2 * mask) for mask in masks]
    bias = dbias_ref[...]
    bias = pltpu.roll(bias, bias.shape[0] - chip * tiles, 0)
    tables = jnp.concatenate([table_of(ref) for ref in tables], axis=0)
    tables = pltpu.roll(tables, TILE - chip * tiles, 1).astype(jnp.int32)
    send[...] = jnp.zeros(send.shape, jnp.float32)
    stride = keep_ref.shape[1]
    target = lax.broadcasted_iota(jnp.int32, (BLK_DEV * devices, TILE), 0)
    for t in range(tiles):
        lanes = slice(t * TILE, (t + 1) * TILE)
        impacts = jnp.log1p(jnp.maximum(logits[:, lanes] + bias[t : t + 1, :], 0.0))
        impacts = impacts.astype(jnp.bfloat16).astype(jnp.float32)
        blocks = jnp.zeros((BLK_DEV * devices, TILE), jnp.float32)
        for n in range(len(masks)):
            row = impacts[n : n + 1, :]
            send[pl.ds(docs_at[n] * stride + t, 1), :] = row
            block = jnp.broadcast_to(tables[n : n + 1, t : t + 1], target.shape)
            blocks = jnp.maximum(blocks, jnp.where(target == block, row, 0.0))
        for s in range(BLK_DEV):
            send[pl.ds((1 + s) * SLOT_ROWS + t, devices, stride=stride), :] = blocks[
                s * devices : (s + 1) * devices
            ]
    for k in range(len(masks)):
        at = pl.multiple_of((2 * k + core) * stride, SLOT_ROWS)
        keep_ref[k] = send[pl.ds(at, stride), :].astype(jnp.bfloat16)
        at = pl.multiple_of((2 * k + 1 - core) * stride + SLOT_ROWS, SLOT_ROWS)
        give_ref[k] = send[pl.ds(at, stride - SLOT_ROWS), :].astype(jnp.bfloat16)


def merge_kernel(keep_ref, got_ref, out_ref):
    out_ref[:, 0:SLOT_ROWS, :] = keep_ref[:, 0:SLOT_ROWS, :]
    mine = keep_ref[:, SLOT_ROWS:, :].astype(jnp.float32)
    theirs = got_ref[...].astype(jnp.float32)
    out_ref[:, SLOT_ROWS:, :] = jnp.maximum(mine, theirs).astype(jnp.bfloat16)


def place_kernel(tiles, rows_ref, impacts_ref, summaries_ref):
    for chip in range(rows_ref.shape[0]):
        rows = rows_ref[chip].astype(jnp.float32)
        lanes = slice(chip * tiles * TILE, (chip + 1) * tiles * TILE)
        lines = [
            jnp.concatenate([rows[first + t : first + t + 1] for t in range(tiles)], axis=1)
            for first in range(0, rows.shape[0], SLOT_ROWS)
        ]
        impacts_ref[:, lanes] = lines[0].astype(jnp.bfloat16)
        summaries_ref[:, lanes] = jnp.concatenate(lines[1:], axis=0).astype(jnp.bfloat16)


def move_tokens(
    hidden_states,
    doc_lengths,
    transform_weight,
    transform_bias,
    norm_gain,
    norm_bias,
    decoder_weight,
    decoder_bias,
    tile_ids,
    owner_ids,
    block_slots,
):
    devices = lax.axis_size("doc")
    chips = devices // 2
    seq, width = hidden_states.shape
    rows = transform_weight.shape[0]
    half = decoder_weight.shape[2]
    tiles = 2 * half // TILE
    me = lax.axis_index("doc").astype(jnp.int32)

    def cross(value, mask):
        return lax.ppermute(value, "doc", [(i, i ^ (2 * mask)) for i in range(devices)])

    def swap(value):
        return lax.ppermute(value, "doc", [(i, i ^ 1) for i in range(devices)])

    smem = pl.BlockSpec(memory_space=pltpu.SMEM)
    vmem = pl.BlockSpec(memory_space=pltpu.VMEM)
    hbm = pl.BlockSpec(memory_space=pltpu.HBM)

    def stay(value):
        return pltpu.with_memory_space_constraint(value, pltpu.HBM)

    limit = pltpu.CompilerParams(vmem_limit_bytes=24 * 1024 * 1024)

    def cost(docs):
        return pl.CostEstimate(flops=docs, bytes_accessed=docs, transcendentals=0)

    def shape(dims, dtype):
        return jax.ShapeDtypeStruct(dims, dtype)

    def after(value, *done):
        return lax.optimization_barrier((value, *done))[0]

    def pile(values, parts, heights=()):
        heights = heights or (sum(count for _, count in parts),)
        piled = pl.pallas_call(
            lambda *refs: pile_kernel(parts, heights, *refs),
            out_shape=[shape((height, width), jnp.bfloat16) for height in heights],
            in_specs=[vmem] * len(values),
            out_specs=[vmem] * len(heights),
            compiler_params=limit,
        )(*values)
        return piled if len(heights) > 1 else piled[0]

    where = me[None]
    weight_rows = jnp.swapaxes(decoder_weight[0], 0, 1)
    block_6 = cross(transform_weight, 6)
    block_2 = cross(transform_weight, 2)
    theirs = swap(weight_rows)
    docs = {1: cross(hidden_states, 1), 2: cross(hidden_states, 2)}
    load, block, table, params = pl.pallas_call(
        start_kernel,
        out_shape=[
            shape((seq + SLOT_ROWS, width), jnp.bfloat16),
            shape((rows, width), jnp.bfloat16),
            shape((SLOT_ROWS, width), jnp.bfloat16),
            shape((8, width), jnp.float32),
        ],
        in_specs=[smem] * 5 + [hbm] * 5,
        out_specs=[vmem] * 4,
        scratch_shapes=[
            pltpu.VMEM((3 * width,), jnp.float32),
            pltpu.SemaphoreType.DMA((5,)),
        ],
        compiler_params=limit,
    )(
        where,
        stay(tile_ids),
        stay(owner_ids[..., 0]),
        stay(block_slots),
        doc_lengths,
        stay(hidden_states),
        stay(transform_weight),
        stay(transform_bias),
        stay(norm_gain),
        stay(norm_bias),
    )
    one, two, below = (0, rows), (0, 2 * rows), (0, SLOT_ROWS)
    near = pile((block, after(block_2, block_6, docs[1]), table), (one, one, below))
    near_pile = cross(near, 1)
    block_4 = cross(pile((block_6, table), (one, below)), 2)
    docs[6] = cross(after(load, block_6), 6)
    docs[3] = cross(after(docs[2], near), 1)
    far_from = [stay(after(weight_rows, table))]
    [mine] = pl.pallas_call(
        lambda *refs: fetch_kernel(1, *refs),
        out_shape=[shape(value.shape, value.dtype) for value in far_from],
        in_specs=[vmem] + [hbm],
        out_specs=[vmem],
        scratch_shapes=[pltpu.SemaphoreType.DMA((1,))],
        compiler_params=limit,
    )(table, *far_from)
    far = (block_6, after(block_4, near_pile, mine, theirs))
    far = pile(far, (one, (0, rows + SLOT_ROWS)))
    far_pile = cross(far, 1)
    docs[4] = cross(after(docs[6], far), 2)
    docs[7] = cross(docs[6], 1)
    sources = (after(block, docs[6], docs[3]), block_2, block_6, block_4, near_pile, far_pile)
    packed = pile(sources, (one, one, one, one, two, two), (seq,) * (chips * rows // seq))
    other_packed = [swap(part) for part in packed]
    block_masks = [0, 2, 6, 4, 1, 3, 7, 5]

    masks = [6, 7, 0, 1, 2, 3, 4, 5]
    docs[0] = load
    docs[5] = cross(after(docs[4], docs[7], *other_packed), 1)
    tables = docs | {1: near_pile, 2: block_4, 3: far_pile}
    best_shape = shape((8, half), jnp.float32)
    *best, weight = pl.pallas_call(
        lambda *refs: first_kernel(seq, rows, block_masks, *refs),
        out_shape=[best_shape, best_shape, shape((width, width), jnp.bfloat16)],
        in_specs=[smem] + [vmem] * (7 + 2 * len(packed)),
        out_specs=[vmem] * 3,
        compiler_params=limit,
        cost_estimate=cost(2),
    )(
        where,
        *[docs[mask] for mask in masks[:2]],
        *[tables[mask] for mask in masks[:2]],
        *packed,
        *other_packed,
        params,
        mine,
        theirs,
    )
    for first in range(2, len(masks) - 2, 2):
        pair = masks[first : first + 2]
        best += pl.pallas_call(
            lambda *refs: next_kernel(seq, *refs),
            out_shape=[best_shape] * 2,
            in_specs=[vmem] * 8,
            out_specs=[vmem] * 2,
            compiler_params=limit,
            cost_estimate=cost(2),
        )(
            *[docs[mask] for mask in pair],
            *[tables[mask] for mask in pair],
            after(weight, best[-1]),
            params,
            mine,
            theirs,
        )
    height = (1 + BLK_DEV) * SLOT_ROWS
    keep, give = pl.pallas_call(
        lambda *refs: last_kernel(seq, masks, *refs),
        out_shape=[
            shape((chips, height, TILE), jnp.bfloat16),
            shape((chips, height - SLOT_ROWS, TILE), jnp.bfloat16),
        ],
        in_specs=[smem] + [vmem] * (2 + len(masks) + 5 + len(best)),
        out_specs=[vmem] * 2,
        scratch_shapes=[pltpu.VMEM((devices * height, TILE), jnp.float32)],
        compiler_params=limit,
        cost_estimate=cost(2),
    )(
        where,
        *[docs[mask] for mask in masks[-2:]],
        *[tables[mask] for mask in masks],
        weight,
        params,
        mine,
        theirs,
        decoder_bias.reshape(-1, TILE),
        *best,
    )
    merged = pl.pallas_call(
        merge_kernel,
        out_shape=shape((chips, height, TILE), jnp.bfloat16),
        in_specs=[vmem] * 2,
        out_specs=vmem,
        compiler_params=limit,
    )(keep, swap(give))
    alike = [list(range(parity, devices, 2)) for parity in range(2)]
    got = lax.all_to_all(
        merged, "doc", split_axis=0, concat_axis=0, axis_index_groups=alike, tiled=True
    )
    return pl.pallas_call(
        lambda *refs: place_kernel(tiles, *refs),
        out_shape=[
            shape((1, chips * tiles * TILE), jnp.bfloat16),
            shape((BLK_DEV, chips * tiles * TILE), jnp.bfloat16),
        ],
        in_specs=[vmem],
        out_specs=[vmem] * 2,
        compiler_params=limit,
    )(got)


def tokens_move(mesh):
    return mesh.shape["term"] == 1 and mesh.shape["doc"] == 16


def solution(mesh):
    placed = (
        P(("groups", "doc"), None),
        P(("groups", "doc")),
        P("doc", "term"),
        P(),
        P(),
        P(),
        P("term", None, "doc"),
        P("term"),
        P("term", ("groups", "doc"), None),
        P("term", ("groups", "doc"), None, None),
        P("term", ("groups", "doc"), None),
    )

    def local(*args):
        pair = 2 * args[6].shape[2]
        tiles = pair * (mesh.shape["doc"] // 2) // TILE
        fits = pair % TILE == 0 and tiles < TILE and pair // TILE <= SLOT_ROWS
        if tokens_move(mesh) and args[1].shape[0] == 1 and fits:
            return move_tokens(*args)
        return move_weights(*args)

    return jax.shard_map(
        local,
        mesh=mesh,
        in_specs=placed,
        out_specs=(P(("groups", "doc"), "term"), P(("groups", "doc"), "term")),
        check_vma=False,
    )
```

```python
import jax
import jax.numpy as jnp
from jax import lax
from jax.experimental import pallas as pl
from jax.experimental.pallas import tpu as pltpu
from jax.sharding import PartitionSpec as P

TILE = 128
BLK_DEV = 2
SLOT_ROWS = 16


def layer_norm(activated, norm_gain, norm_bias):
    values = activated.astype(jnp.float32)
    centre = jnp.mean(values, axis=-1, keepdims=True)
    centred = values - centre
    spread = jnp.mean(centred * centred, axis=-1, keepdims=True)
    return (centred * lax.rsqrt(spread + 1e-05) * norm_gain + norm_bias).astype(jnp.bfloat16)


def pool_docs(logits, keep):
    docs_here = keep.shape[0]
    saturated = jnp.log1p(jnp.maximum(logits, 0.0)).reshape(
        docs_here, keep.shape[1], logits.shape[1]
    )
    return jnp.max(jnp.where(keep[:, :, None], saturated, 0.0), axis=1)


def move_weights(
    hidden_states,
    doc_lengths,
    transform_weight,
    transform_bias,
    norm_gain,
    norm_bias,
    decoder_weight,
    decoder_bias,
    tile_ids,
    owner_ids,
    block_slots,
):
    tok_rows = hidden_states.shape[0]
    docs_here = doc_lengths.shape[0]
    seq_len = tok_rows // docs_here
    cols = transform_weight.shape[1]
    pre_half = jnp.dot(
        hidden_states,
        lax.all_gather(transform_weight, "doc", axis=0, tiled=True),
        preferred_element_type=jnp.float32,
    )
    bias_half = lax.dynamic_slice_in_dim(transform_bias, lax.axis_index("term") * cols, cols, 0)
    act_half = jax.nn.gelu(pre_half + bias_half, approximate=False).astype(jnp.bfloat16)
    activated = lax.all_gather(act_half, "term", axis=1, tiled=True)
    normed = layer_norm(activated, norm_gain, norm_bias)
    keep = jnp.arange(seq_len, dtype=jnp.int32)[None, :] < doc_lengths[:, None]
    logits = jnp.dot(
        normed,
        lax.all_gather(decoder_weight, "doc", axis=2, tiled=True)[0],
        preferred_element_type=jnp.float32,
    )
    logits = logits + decoder_bias
    impacts = pool_docs(logits, keep).astype(jnp.bfloat16)
    tiles_t = impacts.shape[1] // TILE
    slots_total = BLK_DEV * tiles_t
    tiles = impacts.reshape(docs_here * tiles_t, TILE)
    chosen = tile_ids[0]
    doc_index = jnp.arange(docs_here, dtype=jnp.int32)[:, None]
    posted = tiles[(doc_index * tiles_t + chosen).reshape(-1)]
    owners = owner_ids[0, :, :, 0].reshape(-1)
    target = block_slots[0].reshape(-1) * tiles_t + chosen.reshape(-1)
    owner_count = lax.axis_size("doc")
    capacity = max(2, 2 * posted.shape[0] // owner_count)
    onehot = (owners[:, None] == jnp.arange(owner_count, dtype=jnp.int32)[None, :]).astype(
        jnp.int32
    )
    before = jnp.cumsum(onehot, axis=0) - onehot
    position = jnp.sum(before * onehot, axis=1)
    dest = owners * capacity + position
    outgoing = jnp.zeros((owner_count * capacity, TILE), jnp.bfloat16).at[dest].set(posted)
    out_tags = jnp.full((owner_count * capacity,), slots_total, jnp.int32).at[dest].set(target)
    got_vals, got_tags = (
        lax.all_to_all(
            outgoing.reshape(owner_count, capacity, TILE),
            "doc",
            split_axis=0,
            concat_axis=0,
            tiled=True,
        ),
        lax.all_to_all(
            out_tags.reshape(owner_count, capacity), "doc", split_axis=0, concat_axis=0, tiled=True
        ),
    )
    got_vals = got_vals.reshape(-1, TILE)
    local_tags = got_tags.reshape(-1)
    summary = jnp.zeros((slots_total, TILE), jnp.bfloat16).at[local_tags].max(got_vals, mode="drop")
    return (impacts, summary.reshape(BLK_DEV, tiles_t * TILE))


def dot_t(left, right):
    return lax.dot_general(
        left, right, (((1,), (1,)), ((), ())), preferred_element_type=jnp.float32
    )


def table_of(ref):
    return ref[ref.shape[0] - SLOT_ROWS :, 0:TILE].astype(jnp.float32)[0:1, :]


def masked(ref, table_ref, seq):
    here = ref[0:seq, :]
    length = table_of(table_ref)[:, TILE - 1 :]
    keep = lax.broadcasted_iota(jnp.int32, here.shape, 0).astype(jnp.float32) < length
    first = jnp.broadcast_to(here[0:1, :].astype(jnp.float32), here.shape).astype(here.dtype)
    return jnp.where(keep, here, first)


def normed_rows(docs, tables, seq, weight, params):
    rows = [masked(ref, table, seq) for ref, table in zip(docs, tables)]
    rows = jnp.concatenate(rows, axis=0)
    pre = jnp.dot(rows, weight[...], preferred_element_type=jnp.float32) + params[0:1, :]
    act = 0.5 * pre * (1.0 + lax.erf(pre * (0.5**0.5)))
    return layer_norm(act.astype(jnp.bfloat16), params[1:2, :], params[2:3, :])


def tops_of(normed, w_ref, count):
    logits = dot_t(normed, w_ref[...])
    seq = normed.shape[0] // count
    return [
        jnp.max(logits[j * seq : (j + 1) * seq], axis=0, keepdims=True) for j in range(count)
    ]


def start_kernel(me_ref, tiles_ref, owners_ref, slots_ref, length_ref, *refs):
    hidden_ref, weight_ref, vectors = refs[0], refs[1], refs[2:5]
    load_ref, block_ref, table_ref, rows_ref, kept, sems = refs[5:]
    seq, width = hidden_ref.shape
    copies = [
        fetch(hidden_ref, load_ref.at[pl.ds(0, seq), :], sems.at[0]),
        fetch(weight_ref, block_ref, sems.at[1]),
    ]
    for k, ref in enumerate(vectors):
        copies.append(fetch(ref, kept.at[pl.ds(k * width, width)], sems.at[2 + k]))
    lane = lax.broadcasted_iota(jnp.int32, (SLOT_ROWS, TILE), 1)
    table = jnp.where(lane == TILE - 1, length_ref[0], -1)
    devices = lax.axis_size("doc")
    for k in range(tiles_ref.shape[2]):
        block = slots_ref[0, 0, k] * devices + owners_ref[0, 0, k]
        table = jnp.where(lane == tiles_ref[0, 0, k], block, table)
    table = table.astype(jnp.float32).astype(jnp.bfloat16)
    for first in range(0, width, TILE):
        load_ref[seq:, first : first + TILE] = table
        table_ref[:, first : first + TILE] = table
    for copy in copies:
        copy.wait()
    for k in range(len(vectors)):
        rows_ref[k : k + 1, :] = kept[pl.ds(k * width, width)][None, :]


def pile_kernel(parts, heights, *refs):
    rows = jnp.concatenate(
        [ref[first : first + count, :] for ref, (first, count) in zip(refs, parts)], axis=0
    )
    at = 0
    for ref, height in zip(refs[len(parts) :], heights):
        ref[...] = rows[at : at + height, :]
        at += height


def fetch(ref, slot, sem):
    copy = pltpu.make_async_copy(ref, slot, sem)
    copy.start()
    return copy


def keep_tops(normed, halves, bests):
    for w_ref, best in zip(halves, bests):
        for j, top in enumerate(tops_of(normed, w_ref, 2)):
            best[j : j + 1, :] = top


def fetch_kernel(count, *refs):
    copies = [fetch(refs[1 + k], refs[1 + count + k], refs[-1].at[k]) for k in range(count)]
    for copy in copies:
        copy.wait()


def first_kernel(seq, shard, masks, *refs):
    me_ref, docs, tables, refs = refs[0], refs[1:3], refs[3:5], refs[5:]
    count = len(masks) * shard // seq
    parts, others, refs = refs[:count], refs[count : 2 * count], refs[2 * count :]
    params, halves, refs = refs[0], refs[1:3], refs[3:]
    bests, weight = refs[:2], refs[2]
    me = me_ref[0]
    core = me % 2
    for at in range(0, len(masks) * shard, SLOT_ROWS):
        (k, inside), (part, place) = divmod(at, shard), divmod(at, seq)
        chip = (me // 2) ^ masks[k]
        for whose, sources in ((core, parts), (1 - core, others)):
            to = pl.multiple_of((2 * chip + whose) * shard + inside, SLOT_ROWS)
            weight[pl.ds(to, SLOT_ROWS), :] = sources[part][place : place + SLOT_ROWS, :]
    keep_tops(normed_rows(docs, tables, seq, weight, params), halves, bests)


def next_kernel(seq, *refs):
    docs, tables, weight, params, refs = refs[:2], refs[2:4], refs[4], refs[5], refs[6:]
    keep_tops(normed_rows(docs, tables, seq, weight, params), refs[:2], refs[2:])


def last_kernel(seq, masks, *refs):
    me_ref, docs, tables, refs = refs[0], refs[1:3], refs[3 : 3 + len(masks)], refs[3 + len(masks) :]
    weight, params, halves, dbias_ref, refs = refs[0], refs[1], refs[2:4], refs[4], refs[5:]
    earlier, keep_ref, give_ref, send = refs[:-3], *refs[-3:]
    me = me_ref[0]
    core, chip = me % 2, me // 2
    devices = 2 * len(masks)
    tiles = 2 * halves[0].shape[0] // TILE
    normed = normed_rows(docs, docs, seq, weight, params)
    found = []
    for k, w_ref in enumerate(halves):
        parts = [ref[0:2, :] for ref in earlier[k::2]]
        found.append(jnp.concatenate([*parts, *tops_of(normed, w_ref, 2)], axis=0))
    low = jnp.where(core == 0, found[0], found[1])
    high = jnp.where(core == 0, found[1], found[0])
    logits = jnp.concatenate([low, high], axis=1)
    docs_at = [me ^ (2 * mask) for mask in masks]
    bias = dbias_ref[...]
    bias = pltpu.roll(bias, bias.shape[0] - chip * tiles, 0)
    tables = jnp.concatenate([table_of(ref) for ref in tables], axis=0)
    tables = pltpu.roll(tables, TILE - chip * tiles, 1).astype(jnp.int32)
    send[...] = jnp.zeros(send.shape, jnp.float32)
    stride = keep_ref.shape[1]
    target = lax.broadcasted_iota(jnp.int32, (BLK_DEV * devices, TILE), 0)
    for t in range(tiles):
        lanes = slice(t * TILE, (t + 1) * TILE)
        impacts = jnp.log1p(jnp.maximum(logits[:, lanes] + bias[t : t + 1, :], 0.0))
        impacts = impacts.astype(jnp.bfloat16).astype(jnp.float32)
        blocks = jnp.zeros((BLK_DEV * devices, TILE), jnp.float32)
        for n in range(len(masks)):
            row = impacts[n : n + 1, :]
            send[pl.ds(docs_at[n] * stride + t, 1), :] = row
            block = jnp.broadcast_to(tables[n : n + 1, t : t + 1], target.shape)
            blocks = jnp.maximum(blocks, jnp.where(target == block, row, 0.0))
        for s in range(BLK_DEV):
            send[pl.ds((1 + s) * SLOT_ROWS + t, devices, stride=stride), :] = blocks[
                s * devices : (s + 1) * devices
            ]
    for k in range(len(masks)):
        at = pl.multiple_of((2 * k + core) * stride, SLOT_ROWS)
        keep_ref[k] = send[pl.ds(at, stride), :].astype(jnp.bfloat16)
        at = pl.multiple_of((2 * k + 1 - core) * stride + SLOT_ROWS, SLOT_ROWS)
        give_ref[k] = send[pl.ds(at, stride - SLOT_ROWS), :].astype(jnp.bfloat16)


def merge_kernel(keep_ref, got_ref, out_ref):
    out_ref[:, 0:SLOT_ROWS, :] = keep_ref[:, 0:SLOT_ROWS, :]
    mine = keep_ref[:, SLOT_ROWS:, :].astype(jnp.float32)
    theirs = got_ref[...].astype(jnp.float32)
    out_ref[:, SLOT_ROWS:, :] = jnp.maximum(mine, theirs).astype(jnp.bfloat16)


def place_kernel(tiles, rows_ref, impacts_ref, summaries_ref):
    for chip in range(rows_ref.shape[0]):
        rows = rows_ref[chip].astype(jnp.float32)
        lanes = slice(chip * tiles * TILE, (chip + 1) * tiles * TILE)
        lines = [
            jnp.concatenate([rows[first + t : first + t + 1] for t in range(tiles)], axis=1)
            for first in range(0, rows.shape[0], SLOT_ROWS)
        ]
        impacts_ref[:, lanes] = lines[0].astype(jnp.bfloat16)
        summaries_ref[:, lanes] = jnp.concatenate(lines[1:], axis=0).astype(jnp.bfloat16)


def move_tokens(
    hidden_states,
    doc_lengths,
    transform_weight,
    transform_bias,
    norm_gain,
    norm_bias,
    decoder_weight,
    decoder_bias,
    tile_ids,
    owner_ids,
    block_slots,
):
    devices = lax.axis_size("doc")
    chips = devices // 2
    seq, width = hidden_states.shape
    rows = transform_weight.shape[0]
    half = decoder_weight.shape[2]
    tiles = 2 * half // TILE
    me = lax.axis_index("doc").astype(jnp.int32)

    def cross(value, mask):
        return lax.ppermute(value, "doc", [(i, i ^ (2 * mask)) for i in range(devices)])

    def swap(value):
        return lax.ppermute(value, "doc", [(i, i ^ 1) for i in range(devices)])

    smem = pl.BlockSpec(memory_space=pltpu.SMEM)
    vmem = pl.BlockSpec(memory_space=pltpu.VMEM)
    hbm = pl.BlockSpec(memory_space=pltpu.HBM)

    def stay(value):
        return pltpu.with_memory_space_constraint(value, pltpu.HBM)

    limit = pltpu.CompilerParams(vmem_limit_bytes=24 * 1024 * 1024)

    def cost(docs):
        return pl.CostEstimate(flops=docs, bytes_accessed=docs, transcendentals=0)

    def shape(dims, dtype):
        return jax.ShapeDtypeStruct(dims, dtype)

    def after(value, *done):
        return lax.optimization_barrier((value, *done))[0]

    def pile(values, parts, heights=()):
        heights = heights or (sum(count for _, count in parts),)
        piled = pl.pallas_call(
            lambda *refs: pile_kernel(parts, heights, *refs),
            out_shape=[shape((height, width), jnp.bfloat16) for height in heights],
            in_specs=[vmem] * len(values),
            out_specs=[vmem] * len(heights),
            compiler_params=limit,
        )(*values)
        return piled if len(heights) > 1 else piled[0]

    where = me[None]
    weight_rows = jnp.swapaxes(decoder_weight[0], 0, 1)
    block_6 = cross(transform_weight, 6)
    block_2 = cross(transform_weight, 2)
    theirs = swap(weight_rows)
    docs = {1: cross(hidden_states, 1), 2: cross(hidden_states, 2)}
    load, block, table, params = pl.pallas_call(
        start_kernel,
        out_shape=[
            shape((seq + SLOT_ROWS, width), jnp.bfloat16),
            shape((rows, width), jnp.bfloat16),
            shape((SLOT_ROWS, width), jnp.bfloat16),
            shape((8, width), jnp.float32),
        ],
        in_specs=[smem] * 5 + [hbm] * 5,
        out_specs=[vmem] * 4,
        scratch_shapes=[
            pltpu.VMEM((3 * width,), jnp.float32),
            pltpu.SemaphoreType.DMA((5,)),
        ],
        compiler_params=limit,
    )(
        where,
        stay(tile_ids),
        stay(owner_ids[..., 0]),
        stay(block_slots),
        doc_lengths,
        stay(hidden_states),
        stay(transform_weight),
        stay(transform_bias),
        stay(norm_gain),
        stay(norm_bias),
    )
    one, two, below = (0, rows), (0, 2 * rows), (0, SLOT_ROWS)
    near = pile((block, after(block_2, block_6, docs[1]), table), (one, one, below))
    near_pile = cross(near, 1)
    block_4 = cross(pile((block_6, table), (one, below)), 2)
    docs[6] = cross(after(load, block_6), 6)
    docs[3] = cross(after(docs[2], near), 1)
    far_from = [stay(after(weight_rows, table))]
    [mine] = pl.pallas_call(
        lambda *refs: fetch_kernel(1, *refs),
        out_shape=[shape(value.shape, value.dtype) for value in far_from],
        in_specs=[vmem] + [hbm],
        out_specs=[vmem],
        scratch_shapes=[pltpu.SemaphoreType.DMA((1,))],
        compiler_params=limit,
    )(table, *far_from)
    far = (block_6, after(block_4, near_pile, mine, theirs))
    far = pile(far, (one, (0, rows + SLOT_ROWS)))
    far_pile = cross(far, 1)
    docs[4] = pile((cross(after(docs[6], far), 2),), ((0, seq + SLOT_ROWS),))
    docs[7] = cross(docs[6], 1)
    sources = (after(block, docs[6], docs[3]), block_2, block_6, block_4, near_pile, far_pile)
    packed = pile(sources, (one, one, one, one, two, two), (seq,) * (chips * rows // seq))
    other_packed = [swap(part) for part in packed]
    block_masks = [0, 2, 6, 4, 1, 3, 7, 5]

    masks = [0, 1, 2, 3, 6, 7, 4, 5]
    docs[0] = load
    docs[5] = cross(after(docs[4], docs[7], *other_packed), 1)
    tables = docs | {1: near_pile, 2: block_4, 3: far_pile}
    best_shape = shape((8, half), jnp.float32)
    *best, weight = pl.pallas_call(
        lambda *refs: first_kernel(seq, rows, block_masks, *refs),
        out_shape=[best_shape, best_shape, shape((width, width), jnp.bfloat16)],
        in_specs=[smem] + [vmem] * (7 + 2 * len(packed)),
        out_specs=[vmem] * 3,
        compiler_params=limit,
        cost_estimate=cost(2),
    )(
        where,
        *[docs[mask] for mask in masks[:2]],
        *[tables[mask] for mask in masks[:2]],
        *packed,
        *other_packed,
        params,
        mine,
        theirs,
    )
    for first in range(2, len(masks) - 2, 2):
        pair = masks[first : first + 2]
        best += pl.pallas_call(
            lambda *refs: next_kernel(seq, *refs),
            out_shape=[best_shape] * 2,
            in_specs=[vmem] * 8,
            out_specs=[vmem] * 2,
            compiler_params=limit,
            cost_estimate=cost(2),
        )(
            *[docs[mask] for mask in pair],
            *[tables[mask] for mask in pair],
            after(weight, best[-1]),
            params,
            mine,
            theirs,
        )
    height = (1 + BLK_DEV) * SLOT_ROWS
    keep, give = pl.pallas_call(
        lambda *refs: last_kernel(seq, masks, *refs),
        out_shape=[
            shape((chips, height, TILE), jnp.bfloat16),
            shape((chips, height - SLOT_ROWS, TILE), jnp.bfloat16),
        ],
        in_specs=[smem] + [vmem] * (2 + len(masks) + 5 + len(best)),
        out_specs=[vmem] * 2,
        scratch_shapes=[pltpu.VMEM((devices * height, TILE), jnp.float32)],
        compiler_params=limit,
        cost_estimate=cost(2),
    )(
        where,
        *[docs[mask] for mask in masks[-2:]],
        *[tables[mask] for mask in masks],
        weight,
        params,
        mine,
        theirs,
        decoder_bias.reshape(-1, TILE),
        *best,
    )
    merged = pl.pallas_call(
        merge_kernel,
        out_shape=shape((chips, height, TILE), jnp.bfloat16),
        in_specs=[vmem] * 2,
        out_specs=vmem,
        compiler_params=limit,
    )(keep, swap(give))
    alike = [list(range(parity, devices, 2)) for parity in range(2)]
    got = lax.all_to_all(
        merged, "doc", split_axis=0, concat_axis=0, axis_index_groups=alike, tiled=True
    )
    return pl.pallas_call(
        lambda *refs: place_kernel(tiles, *refs),
        out_shape=[
            shape((1, chips * tiles * TILE), jnp.bfloat16),
            shape((BLK_DEV, chips * tiles * TILE), jnp.bfloat16),
        ],
        in_specs=[vmem],
        out_specs=[vmem] * 2,
        compiler_params=limit,
    )(got)


def tokens_move(mesh):
    return mesh.shape["term"] == 1 and mesh.shape["doc"] == 16


def solution(mesh):
    placed = (
        P(("groups", "doc"), None),
        P(("groups", "doc")),
        P("doc", "term"),
        P(),
        P(),
        P(),
        P("term", None, "doc"),
        P("term"),
        P("term", ("groups", "doc"), None),
        P("term", ("groups", "doc"), None, None),
        P("term", ("groups", "doc"), None),
    )

    def local(*args):
        pair = 2 * args[6].shape[2]
        tiles = pair * (mesh.shape["doc"] // 2) // TILE
        fits = pair % TILE == 0 and tiles < TILE and pair // TILE <= SLOT_ROWS
        if tokens_move(mesh) and args[1].shape[0] == 1 and fits:
            return move_tokens(*args)
        return move_weights(*args)

    return jax.shard_map(
        local,
        mesh=mesh,
        in_specs=placed,
        out_specs=(P(("groups", "doc"), "term"), P(("groups", "doc"), "term")),
        check_vma=False,
    )
```

```python
import jax
import jax.numpy as jnp
from jax import lax
from jax.experimental import pallas as pl
from jax.experimental.pallas import tpu as pltpu
from jax.sharding import PartitionSpec as P

TILE = 128
BLK_DEV = 2
SLOT_ROWS = 16


def layer_norm(activated, norm_gain, norm_bias):
    values = activated.astype(jnp.float32)
    centre = jnp.mean(values, axis=-1, keepdims=True)
    centred = values - centre
    spread = jnp.mean(centred * centred, axis=-1, keepdims=True)
    return (centred * lax.rsqrt(spread + 1e-05) * norm_gain + norm_bias).astype(jnp.bfloat16)


def pool_docs(logits, keep):
    docs_here = keep.shape[0]
    saturated = jnp.log1p(jnp.maximum(logits, 0.0)).reshape(
        docs_here, keep.shape[1], logits.shape[1]
    )
    return jnp.max(jnp.where(keep[:, :, None], saturated, 0.0), axis=1)


def move_weights(
    hidden_states,
    doc_lengths,
    transform_weight,
    transform_bias,
    norm_gain,
    norm_bias,
    decoder_weight,
    decoder_bias,
    tile_ids,
    owner_ids,
    block_slots,
):
    tok_rows = hidden_states.shape[0]
    docs_here = doc_lengths.shape[0]
    seq_len = tok_rows // docs_here
    cols = transform_weight.shape[1]
    pre_half = jnp.dot(
        hidden_states,
        lax.all_gather(transform_weight, "doc", axis=0, tiled=True),
        preferred_element_type=jnp.float32,
    )
    bias_half = lax.dynamic_slice_in_dim(transform_bias, lax.axis_index("term") * cols, cols, 0)
    act_half = jax.nn.gelu(pre_half + bias_half, approximate=False).astype(jnp.bfloat16)
    activated = lax.all_gather(act_half, "term", axis=1, tiled=True)
    normed = layer_norm(activated, norm_gain, norm_bias)
    keep = jnp.arange(seq_len, dtype=jnp.int32)[None, :] < doc_lengths[:, None]
    logits = jnp.dot(
        normed,
        lax.all_gather(decoder_weight, "doc", axis=2, tiled=True)[0],
        preferred_element_type=jnp.float32,
    )
    logits = logits + decoder_bias
    impacts = pool_docs(logits, keep).astype(jnp.bfloat16)
    tiles_t = impacts.shape[1] // TILE
    slots_total = BLK_DEV * tiles_t
    tiles = impacts.reshape(docs_here * tiles_t, TILE)
    chosen = tile_ids[0]
    doc_index = jnp.arange(docs_here, dtype=jnp.int32)[:, None]
    posted = tiles[(doc_index * tiles_t + chosen).reshape(-1)]
    owners = owner_ids[0, :, :, 0].reshape(-1)
    target = block_slots[0].reshape(-1) * tiles_t + chosen.reshape(-1)
    owner_count = lax.axis_size("doc")
    capacity = max(2, 2 * posted.shape[0] // owner_count)
    onehot = (owners[:, None] == jnp.arange(owner_count, dtype=jnp.int32)[None, :]).astype(
        jnp.int32
    )
    before = jnp.cumsum(onehot, axis=0) - onehot
    position = jnp.sum(before * onehot, axis=1)
    dest = owners * capacity + position
    outgoing = jnp.zeros((owner_count * capacity, TILE), jnp.bfloat16).at[dest].set(posted)
    out_tags = jnp.full((owner_count * capacity,), slots_total, jnp.int32).at[dest].set(target)
    got_vals, got_tags = (
        lax.all_to_all(
            outgoing.reshape(owner_count, capacity, TILE),
            "doc",
            split_axis=0,
            concat_axis=0,
            tiled=True,
        ),
        lax.all_to_all(
            out_tags.reshape(owner_count, capacity), "doc", split_axis=0, concat_axis=0, tiled=True
        ),
    )
    got_vals = got_vals.reshape(-1, TILE)
    local_tags = got_tags.reshape(-1)
    summary = jnp.zeros((slots_total, TILE), jnp.bfloat16).at[local_tags].max(got_vals, mode="drop")
    return (impacts, summary.reshape(BLK_DEV, tiles_t * TILE))


def dot_t(left, right):
    return lax.dot_general(
        left, right, (((1,), (1,)), ((), ())), preferred_element_type=jnp.float32
    )


def table_of(ref):
    return ref[ref.shape[0] - SLOT_ROWS :, 0:TILE].astype(jnp.float32)[0:1, :]


def masked(ref, table_ref, seq):
    here = ref[0:seq, :]
    length = table_of(table_ref)[:, TILE - 1 :]
    keep = lax.broadcasted_iota(jnp.int32, here.shape, 0).astype(jnp.float32) < length
    first = jnp.broadcast_to(here[0:1, :].astype(jnp.float32), here.shape).astype(here.dtype)
    return jnp.where(keep, here, first)


def normed_rows(docs, tables, seq, weight, params):
    rows = [masked(ref, table, seq) for ref, table in zip(docs, tables)]
    rows = jnp.concatenate(rows, axis=0)
    pre = jnp.dot(rows, weight[...], preferred_element_type=jnp.float32) + params[0:1, :]
    act = 0.5 * pre * (1.0 + lax.erf(pre * (0.5**0.5)))
    return layer_norm(act.astype(jnp.bfloat16), params[1:2, :], params[2:3, :])


def tops_of(normed, w_ref, count):
    logits = dot_t(normed, w_ref[...])
    seq = normed.shape[0] // count
    return [
        jnp.max(logits[j * seq : (j + 1) * seq], axis=0, keepdims=True) for j in range(count)
    ]


def start_kernel(me_ref, tiles_ref, owners_ref, slots_ref, length_ref, *refs):
    hidden_ref, weight_ref, vectors = refs[0], refs[1], refs[2:5]
    load_ref, block_ref, table_ref, rows_ref, kept, sems = refs[5:]
    seq, width = hidden_ref.shape
    copies = [
        fetch(hidden_ref, load_ref.at[pl.ds(0, seq), :], sems.at[0]),
        fetch(weight_ref, block_ref, sems.at[1]),
    ]
    for k, ref in enumerate(vectors):
        copies.append(fetch(ref, kept.at[pl.ds(k * width, width)], sems.at[2 + k]))
    lane = lax.broadcasted_iota(jnp.int32, (SLOT_ROWS, TILE), 1)
    table = jnp.where(lane == TILE - 1, length_ref[0], -1)
    devices = lax.axis_size("doc")
    for k in range(tiles_ref.shape[2]):
        block = slots_ref[0, 0, k] * devices + owners_ref[0, 0, k]
        table = jnp.where(lane == tiles_ref[0, 0, k], block, table)
    table = table.astype(jnp.float32).astype(jnp.bfloat16)
    for first in range(0, width, TILE):
        load_ref[seq:, first : first + TILE] = table
        table_ref[:, first : first + TILE] = table
    for copy in copies:
        copy.wait()
    for k in range(len(vectors)):
        rows_ref[k : k + 1, :] = kept[pl.ds(k * width, width)][None, :]


def pile_kernel(parts, heights, *refs):
    rows = jnp.concatenate(
        [ref[first : first + count, :] for ref, (first, count) in zip(refs, parts)], axis=0
    )
    at = 0
    for ref, height in zip(refs[len(parts) :], heights):
        ref[...] = rows[at : at + height, :]
        at += height


def fetch(ref, slot, sem):
    copy = pltpu.make_async_copy(ref, slot, sem)
    copy.start()
    return copy


def keep_tops(normed, count, halves, bests):
    for w_ref, best in zip(halves, bests):
        for j, top in enumerate(tops_of(normed, w_ref, count)):
            best[j : j + 1, :] = top


def fetch_kernel(count, *refs):
    copies = [fetch(refs[1 + k], refs[1 + count + k], refs[-1].at[k]) for k in range(count)]
    for copy in copies:
        copy.wait()


def first_kernel(seq, shard, masks, *refs):
    me_ref, docs, tables, refs = refs[0], refs[1:3], refs[3:5], refs[5:]
    count = len(masks) * shard // seq
    parts, others, refs = refs[:count], refs[count : 2 * count], refs[2 * count :]
    params, halves, refs = refs[0], refs[1:3], refs[3:]
    bests, weight = refs[:2], refs[2]
    me = me_ref[0]
    core = me % 2
    for at in range(0, len(masks) * shard, SLOT_ROWS):
        (k, inside), (part, place) = divmod(at, shard), divmod(at, seq)
        chip = (me // 2) ^ masks[k]
        for whose, sources in ((core, parts), (1 - core, others)):
            to = pl.multiple_of((2 * chip + whose) * shard + inside, SLOT_ROWS)
            weight[pl.ds(to, SLOT_ROWS), :] = sources[part][place : place + SLOT_ROWS, :]
    keep_tops(normed_rows(docs, tables, seq, weight, params), len(docs), halves, bests)


def next_kernel(seq, count, *refs):
    docs, tables, refs = refs[:count], refs[count : 2 * count], refs[2 * count :]
    weight, params, refs = refs[0], refs[1], refs[2:]
    keep_tops(normed_rows(docs, tables, seq, weight, params), count, refs[:2], refs[2:])


def last_kernel(seq, groups, *refs):
    masks = [mask for group in groups for mask in group]
    me_ref, docs, refs = refs[0], refs[1 : 1 + len(groups[-1])], refs[1 + len(groups[-1]) :]
    tables, refs = refs[: len(masks)], refs[len(masks) :]
    weight, params, halves, dbias_ref, refs = refs[0], refs[1], refs[2:4], refs[4], refs[5:]
    earlier, keep_ref, give_ref, send = refs[:-3], *refs[-3:]
    me = me_ref[0]
    core, chip = me % 2, me // 2
    devices = 2 * len(masks)
    tiles = 2 * halves[0].shape[0] // TILE
    normed = normed_rows(docs, docs, seq, weight, params)
    found = []
    for k, w_ref in enumerate(halves):
        parts = [ref[0 : len(group), :] for ref, group in zip(earlier[k::2], groups)]
        parts += tops_of(normed, w_ref, len(docs))
        found.append(jnp.concatenate(parts, axis=0))
    low = jnp.where(core == 0, found[0], found[1])
    high = jnp.where(core == 0, found[1], found[0])
    logits = jnp.concatenate([low, high], axis=1)
    docs_at = [me ^ (2 * mask) for mask in masks]
    bias = dbias_ref[...]
    bias = pltpu.roll(bias, bias.shape[0] - chip * tiles, 0)
    tables = jnp.concatenate([table_of(ref) for ref in tables], axis=0)
    tables = pltpu.roll(tables, TILE - chip * tiles, 1).astype(jnp.int32)
    send[...] = jnp.zeros(send.shape, jnp.float32)
    stride = keep_ref.shape[1]
    target = lax.broadcasted_iota(jnp.int32, (BLK_DEV * devices, TILE), 0)
    for t in range(tiles):
        lanes = slice(t * TILE, (t + 1) * TILE)
        impacts = jnp.log1p(jnp.maximum(logits[:, lanes] + bias[t : t + 1, :], 0.0))
        impacts = impacts.astype(jnp.bfloat16).astype(jnp.float32)
        blocks = jnp.zeros((BLK_DEV * devices, TILE), jnp.float32)
        for n in range(len(masks)):
            row = impacts[n : n + 1, :]
            send[pl.ds(docs_at[n] * stride + t, 1), :] = row
            block = jnp.broadcast_to(tables[n : n + 1, t : t + 1], target.shape)
            blocks = jnp.maximum(blocks, jnp.where(target == block, row, 0.0))
        for s in range(BLK_DEV):
            send[pl.ds((1 + s) * SLOT_ROWS + t, devices, stride=stride), :] = blocks[
                s * devices : (s + 1) * devices
            ]
    for k in range(len(masks)):
        at = pl.multiple_of((2 * k + core) * stride, SLOT_ROWS)
        keep_ref[k] = send[pl.ds(at, stride), :].astype(jnp.bfloat16)
        at = pl.multiple_of((2 * k + 1 - core) * stride + SLOT_ROWS, SLOT_ROWS)
        give_ref[k] = send[pl.ds(at, stride - SLOT_ROWS), :].astype(jnp.bfloat16)


def merge_kernel(keep_ref, got_ref, out_ref):
    out_ref[:, 0:SLOT_ROWS, :] = keep_ref[:, 0:SLOT_ROWS, :]
    mine = keep_ref[:, SLOT_ROWS:, :].astype(jnp.float32)
    theirs = got_ref[...].astype(jnp.float32)
    out_ref[:, SLOT_ROWS:, :] = jnp.maximum(mine, theirs).astype(jnp.bfloat16)


def place_kernel(tiles, rows_ref, impacts_ref, summaries_ref):
    for chip in range(rows_ref.shape[0]):
        rows = rows_ref[chip].astype(jnp.float32)
        lanes = slice(chip * tiles * TILE, (chip + 1) * tiles * TILE)
        lines = [
            jnp.concatenate([rows[first + t : first + t + 1] for t in range(tiles)], axis=1)
            for first in range(0, rows.shape[0], SLOT_ROWS)
        ]
        impacts_ref[:, lanes] = lines[0].astype(jnp.bfloat16)
        summaries_ref[:, lanes] = jnp.concatenate(lines[1:], axis=0).astype(jnp.bfloat16)


def move_tokens(
    hidden_states,
    doc_lengths,
    transform_weight,
    transform_bias,
    norm_gain,
    norm_bias,
    decoder_weight,
    decoder_bias,
    tile_ids,
    owner_ids,
    block_slots,
):
    devices = lax.axis_size("doc")
    chips = devices // 2
    seq, width = hidden_states.shape
    rows = transform_weight.shape[0]
    half = decoder_weight.shape[2]
    tiles = 2 * half // TILE
    me = lax.axis_index("doc").astype(jnp.int32)

    def cross(value, mask):
        return lax.ppermute(value, "doc", [(i, i ^ (2 * mask)) for i in range(devices)])

    def swap(value):
        return lax.ppermute(value, "doc", [(i, i ^ 1) for i in range(devices)])

    smem = pl.BlockSpec(memory_space=pltpu.SMEM)
    vmem = pl.BlockSpec(memory_space=pltpu.VMEM)
    hbm = pl.BlockSpec(memory_space=pltpu.HBM)

    def stay(value):
        return pltpu.with_memory_space_constraint(value, pltpu.HBM)

    limit = pltpu.CompilerParams(vmem_limit_bytes=24 * 1024 * 1024)

    def cost(docs):
        return pl.CostEstimate(flops=docs, bytes_accessed=docs, transcendentals=0)

    def shape(dims, dtype):
        return jax.ShapeDtypeStruct(dims, dtype)

    def after(value, *done):
        return lax.optimization_barrier((value, *done))[0]

    def pile(values, parts, heights=()):
        heights = heights or (sum(count for _, count in parts),)
        piled = pl.pallas_call(
            lambda *refs: pile_kernel(parts, heights, *refs),
            out_shape=[shape((height, width), jnp.bfloat16) for height in heights],
            in_specs=[vmem] * len(values),
            out_specs=[vmem] * len(heights),
            compiler_params=limit,
        )(*values)
        return piled if len(heights) > 1 else piled[0]

    where = me[None]
    weight_rows = jnp.swapaxes(decoder_weight[0], 0, 1)
    block_6 = cross(transform_weight, 6)
    block_2 = cross(transform_weight, 2)
    theirs = swap(weight_rows)
    docs = {1: cross(hidden_states, 1)}
    load, block, table, params = pl.pallas_call(
        start_kernel,
        out_shape=[
            shape((seq + SLOT_ROWS, width), jnp.bfloat16),
            shape((rows, width), jnp.bfloat16),
            shape((SLOT_ROWS, width), jnp.bfloat16),
            shape((8, width), jnp.float32),
        ],
        in_specs=[smem] * 5 + [hbm] * 5,
        out_specs=[vmem] * 4,
        scratch_shapes=[
            pltpu.VMEM((3 * width,), jnp.float32),
            pltpu.SemaphoreType.DMA((5,)),
        ],
        compiler_params=limit,
    )(
        where,
        stay(tile_ids),
        stay(owner_ids[..., 0]),
        stay(block_slots),
        doc_lengths,
        stay(hidden_states),
        stay(transform_weight),
        stay(transform_bias),
        stay(norm_gain),
        stay(norm_bias),
    )
    docs[2] = cross(after(hidden_states, table), 2)
    one, two, below = (0, rows), (0, 2 * rows), (0, SLOT_ROWS)
    near = pile((block, after(block_2, block_6, docs[1]), table), (one, one, below))
    near_pile = cross(near, 1)
    block_4 = cross(pile((block_6, table), (one, below)), 2)
    docs[6] = cross(after(load, block_6), 6)
    docs[3] = cross(after(docs[2], near), 1)
    far_from = [stay(after(weight_rows, table))]
    [mine] = pl.pallas_call(
        lambda *refs: fetch_kernel(1, *refs),
        out_shape=[shape(value.shape, value.dtype) for value in far_from],
        in_specs=[vmem] + [hbm],
        out_specs=[vmem],
        scratch_shapes=[pltpu.SemaphoreType.DMA((1,))],
        compiler_params=limit,
    )(table, *far_from)
    far = (block_6, after(block_4, near_pile, mine, theirs))
    far = pile(far, (one, (0, rows + SLOT_ROWS)))
    far_pile = cross(far, 1)
    docs[4] = pile((cross(after(docs[6], far), 2),), ((0, seq + SLOT_ROWS),))
    docs[7] = cross(docs[6], 1)
    sources = (after(block, docs[6], docs[3]), block_2, block_6, block_4, near_pile, far_pile)
    packed = pile(sources, (one, one, one, one, two, two), (seq,) * (chips * rows // seq))
    other_packed = [swap(part) for part in packed]
    block_masks = [0, 2, 6, 4, 1, 3, 7, 5]

    groups = [[0, 1], [2, 3], [6, 7, 4], [5]]
    masks = [mask for group in groups for mask in group]
    docs[0] = load
    tables = docs | {1: near_pile, 2: block_4, 3: far_pile}
    best_shape = shape((8, half), jnp.float32)
    *best, weight = pl.pallas_call(
        lambda *refs: first_kernel(seq, rows, block_masks, *refs),
        out_shape=[best_shape, best_shape, shape((width, width), jnp.bfloat16)],
        in_specs=[smem] + [vmem] * (7 + 2 * len(packed)),
        out_specs=[vmem] * 3,
        compiler_params=limit,
        cost_estimate=cost(2),
    )(
        where,
        *[docs[mask] for mask in masks[:2]],
        *[tables[mask] for mask in masks[:2]],
        *packed,
        *other_packed,
        params,
        mine,
        theirs,
    )
    docs[5] = cross(after(docs[4], docs[7], weight), 1)
    tables[5] = docs[5]
    for group in groups[1:-1]:
        best += pl.pallas_call(
            lambda *refs, count=len(group): next_kernel(seq, count, *refs),
            out_shape=[best_shape] * 2,
            in_specs=[vmem] * (2 * len(group) + 4),
            out_specs=[vmem] * 2,
            compiler_params=limit,
            cost_estimate=cost(len(group)),
        )(
            *[docs[mask] for mask in group],
            *[tables[mask] for mask in group],
            after(weight, best[-1]),
            params,
            mine,
            theirs,
        )
    height = (1 + BLK_DEV) * SLOT_ROWS
    keep, give = pl.pallas_call(
        lambda *refs: last_kernel(seq, groups, *refs),
        out_shape=[
            shape((chips, height, TILE), jnp.bfloat16),
            shape((chips, height - SLOT_ROWS, TILE), jnp.bfloat16),
        ],
        in_specs=[smem] + [vmem] * (len(groups[-1]) + len(masks) + 5 + len(best)),
        out_specs=[vmem] * 2,
        scratch_shapes=[pltpu.VMEM((devices * height, TILE), jnp.float32)],
        compiler_params=limit,
        cost_estimate=cost(2),
    )(
        where,
        *[docs[mask] for mask in groups[-1]],
        *[tables[mask] for mask in masks],
        weight,
        params,
        mine,
        theirs,
        decoder_bias.reshape(-1, TILE),
        *best,
    )
    merged = pl.pallas_call(
        merge_kernel,
        out_shape=shape((chips, height, TILE), jnp.bfloat16),
        in_specs=[vmem] * 2,
        out_specs=vmem,
        compiler_params=limit,
    )(keep, swap(give))
    alike = [list(range(parity, devices, 2)) for parity in range(2)]
    got = lax.all_to_all(
        merged, "doc", split_axis=0, concat_axis=0, axis_index_groups=alike, tiled=True
    )
    return pl.pallas_call(
        lambda *refs: place_kernel(tiles, *refs),
        out_shape=[
            shape((1, chips * tiles * TILE), jnp.bfloat16),
            shape((BLK_DEV, chips * tiles * TILE), jnp.bfloat16),
        ],
        in_specs=[vmem],
        out_specs=[vmem] * 2,
        compiler_params=limit,
    )(got)


def tokens_move(mesh):
    return mesh.shape["term"] == 1 and mesh.shape["doc"] == 16


def solution(mesh):
    placed = (
        P(("groups", "doc"), None),
        P(("groups", "doc")),
        P("doc", "term"),
        P(),
        P(),
        P(),
        P("term", None, "doc"),
        P("term"),
        P("term", ("groups", "doc"), None),
        P("term", ("groups", "doc"), None, None),
        P("term", ("groups", "doc"), None),
    )

    def local(*args):
        pair = 2 * args[6].shape[2]
        tiles = pair * (mesh.shape["doc"] // 2) // TILE
        fits = pair % TILE == 0 and tiles < TILE and pair // TILE <= SLOT_ROWS
        if tokens_move(mesh) and args[1].shape[0] == 1 and fits:
            return move_tokens(*args)
        return move_weights(*args)

    return jax.shard_map(
        local,
        mesh=mesh,
        in_specs=placed,
        out_specs=(P(("groups", "doc"), "term"), P(("groups", "doc"), "term")),
        check_vma=False,
    )
```

```python
import jax
import jax.numpy as jnp
from jax import lax
from jax.experimental import pallas as pl
from jax.experimental.pallas import tpu as pltpu
from jax.sharding import PartitionSpec as P

TILE = 128
BLK_DEV = 2
SLOT_ROWS = 16


def layer_norm(activated, norm_gain, norm_bias):
    values = activated.astype(jnp.float32)
    centre = jnp.mean(values, axis=-1, keepdims=True)
    centred = values - centre
    spread = jnp.mean(centred * centred, axis=-1, keepdims=True)
    return (centred * lax.rsqrt(spread + 1e-05) * norm_gain + norm_bias).astype(jnp.bfloat16)


def pool_docs(logits, keep):
    docs_here = keep.shape[0]
    saturated = jnp.log1p(jnp.maximum(logits, 0.0)).reshape(
        docs_here, keep.shape[1], logits.shape[1]
    )
    return jnp.max(jnp.where(keep[:, :, None], saturated, 0.0), axis=1)


def move_weights(
    hidden_states,
    doc_lengths,
    transform_weight,
    transform_bias,
    norm_gain,
    norm_bias,
    decoder_weight,
    decoder_bias,
    tile_ids,
    owner_ids,
    block_slots,
):
    tok_rows = hidden_states.shape[0]
    docs_here = doc_lengths.shape[0]
    seq_len = tok_rows // docs_here
    cols = transform_weight.shape[1]
    pre_half = jnp.dot(
        hidden_states,
        lax.all_gather(transform_weight, "doc", axis=0, tiled=True),
        preferred_element_type=jnp.float32,
    )
    bias_half = lax.dynamic_slice_in_dim(transform_bias, lax.axis_index("term") * cols, cols, 0)
    act_half = jax.nn.gelu(pre_half + bias_half, approximate=False).astype(jnp.bfloat16)
    activated = lax.all_gather(act_half, "term", axis=1, tiled=True)
    normed = layer_norm(activated, norm_gain, norm_bias)
    keep = jnp.arange(seq_len, dtype=jnp.int32)[None, :] < doc_lengths[:, None]
    logits = jnp.dot(
        normed,
        lax.all_gather(decoder_weight, "doc", axis=2, tiled=True)[0],
        preferred_element_type=jnp.float32,
    )
    logits = logits + decoder_bias
    impacts = pool_docs(logits, keep).astype(jnp.bfloat16)
    tiles_t = impacts.shape[1] // TILE
    slots_total = BLK_DEV * tiles_t
    tiles = impacts.reshape(docs_here * tiles_t, TILE)
    chosen = tile_ids[0]
    doc_index = jnp.arange(docs_here, dtype=jnp.int32)[:, None]
    posted = tiles[(doc_index * tiles_t + chosen).reshape(-1)]
    owners = owner_ids[0, :, :, 0].reshape(-1)
    target = block_slots[0].reshape(-1) * tiles_t + chosen.reshape(-1)
    owner_count = lax.axis_size("doc")
    capacity = max(2, 2 * posted.shape[0] // owner_count)
    onehot = (owners[:, None] == jnp.arange(owner_count, dtype=jnp.int32)[None, :]).astype(
        jnp.int32
    )
    before = jnp.cumsum(onehot, axis=0) - onehot
    position = jnp.sum(before * onehot, axis=1)
    dest = owners * capacity + position
    outgoing = jnp.zeros((owner_count * capacity, TILE), jnp.bfloat16).at[dest].set(posted)
    out_tags = jnp.full((owner_count * capacity,), slots_total, jnp.int32).at[dest].set(target)
    got_vals, got_tags = (
        lax.all_to_all(
            outgoing.reshape(owner_count, capacity, TILE),
            "doc",
            split_axis=0,
            concat_axis=0,
            tiled=True,
        ),
        lax.all_to_all(
            out_tags.reshape(owner_count, capacity), "doc", split_axis=0, concat_axis=0, tiled=True
        ),
    )
    got_vals = got_vals.reshape(-1, TILE)
    local_tags = got_tags.reshape(-1)
    summary = jnp.zeros((slots_total, TILE), jnp.bfloat16).at[local_tags].max(got_vals, mode="drop")
    return (impacts, summary.reshape(BLK_DEV, tiles_t * TILE))


def dot_t(left, right):
    return lax.dot_general(
        left, right, (((1,), (1,)), ((), ())), preferred_element_type=jnp.float32
    )


def table_of(ref):
    return ref[ref.shape[0] - SLOT_ROWS :, 0:TILE].astype(jnp.float32)[0:1, :]


def masked(ref, table_ref, seq):
    here = ref[0:seq, :]
    length = table_of(table_ref)[:, TILE - 1 :]
    keep = lax.broadcasted_iota(jnp.int32, here.shape, 0).astype(jnp.float32) < length
    first = jnp.broadcast_to(here[0:1, :].astype(jnp.float32), here.shape).astype(here.dtype)
    return jnp.where(keep, here, first)


def normed_rows(docs, tables, seq, weight, params):
    rows = [masked(ref, table, seq) for ref, table in zip(docs, tables)]
    rows = jnp.concatenate(rows, axis=0)
    pre = jnp.dot(rows, weight[...], preferred_element_type=jnp.float32) + params[0:1, :]
    act = 0.5 * pre * (1.0 + lax.erf(pre * (0.5**0.5)))
    return layer_norm(act.astype(jnp.bfloat16), params[1:2, :], params[2:3, :])


def tops_of(normed, w_ref, count):
    logits = dot_t(normed, w_ref[...])
    seq = normed.shape[0] // count
    return [
        jnp.max(logits[j * seq : (j + 1) * seq], axis=0, keepdims=True) for j in range(count)
    ]


def start_kernel(me_ref, tiles_ref, owners_ref, slots_ref, length_ref, *refs):
    hidden_ref, weight_ref, vectors = refs[0], refs[1], refs[2:5]
    load_ref, block_ref, table_ref, rows_ref, kept, sems = refs[5:]
    seq, width = hidden_ref.shape
    copies = [
        fetch(hidden_ref, load_ref.at[pl.ds(0, seq), :], sems.at[0]),
        fetch(weight_ref, block_ref, sems.at[1]),
    ]
    for k, ref in enumerate(vectors):
        copies.append(fetch(ref, kept.at[pl.ds(k * width, width)], sems.at[2 + k]))
    lane = lax.broadcasted_iota(jnp.int32, (SLOT_ROWS, TILE), 1)
    table = jnp.where(lane == TILE - 1, length_ref[0], -1)
    devices = lax.axis_size("doc")
    for k in range(tiles_ref.shape[2]):
        block = slots_ref[0, 0, k] * devices + owners_ref[0, 0, k]
        table = jnp.where(lane == tiles_ref[0, 0, k], block, table)
    table = table.astype(jnp.float32).astype(jnp.bfloat16)
    for first in range(0, width, TILE):
        load_ref[seq:, first : first + TILE] = table
        table_ref[:, first : first + TILE] = table
    for copy in copies:
        copy.wait()
    for k in range(len(vectors)):
        rows_ref[k : k + 1, :] = kept[pl.ds(k * width, width)][None, :]


def pile_kernel(parts, heights, *refs):
    rows = jnp.concatenate(
        [ref[first : first + count, :] for ref, (first, count) in zip(refs, parts)], axis=0
    )
    at = 0
    for ref, height in zip(refs[len(parts) :], heights):
        ref[...] = rows[at : at + height, :]
        at += height


def fetch(ref, slot, sem):
    copy = pltpu.make_async_copy(ref, slot, sem)
    copy.start()
    return copy


def keep_tops(normed, count, halves, bests):
    for w_ref, best in zip(halves, bests):
        for j, top in enumerate(tops_of(normed, w_ref, count)):
            best[j : j + 1, :] = top


def fetch_kernel(count, *refs):
    copies = [fetch(refs[1 + k], refs[1 + count + k], refs[-1].at[k]) for k in range(count)]
    for copy in copies:
        copy.wait()


def first_kernel(seq, shard, masks, *refs):
    me_ref, docs, tables, refs = refs[0], refs[1:3], refs[3:5], refs[5:]
    count = len(masks) * shard // seq
    parts, others, refs = refs[:count], refs[count : 2 * count], refs[2 * count :]
    params, halves, refs = refs[0], refs[1:3], refs[3:]
    bests, weight = refs[:2], refs[2]
    me = me_ref[0]
    core = me % 2
    for at in range(0, len(masks) * shard, SLOT_ROWS):
        (k, inside), (part, place) = divmod(at, shard), divmod(at, seq)
        chip = (me // 2) ^ masks[k]
        for whose, sources in ((core, parts), (1 - core, others)):
            to = pl.multiple_of((2 * chip + whose) * shard + inside, SLOT_ROWS)
            weight[pl.ds(to, SLOT_ROWS), :] = sources[part][place : place + SLOT_ROWS, :]
    keep_tops(normed_rows(docs, tables, seq, weight, params), len(docs), halves, bests)


def next_kernel(seq, count, *refs):
    docs, tables, refs = refs[:count], refs[count : 2 * count], refs[2 * count :]
    weight, params, refs = refs[0], refs[1], refs[2:]
    keep_tops(normed_rows(docs, tables, seq, weight, params), count, refs[:2], refs[2:])


def last_kernel(seq, groups, *refs):
    masks = [mask for group in groups for mask in group]
    me_ref, docs, refs = refs[0], refs[1 : 1 + len(groups[-1])], refs[1 + len(groups[-1]) :]
    tables, refs = refs[: len(masks)], refs[len(masks) :]
    weight, params, halves, dbias_ref, refs = refs[0], refs[1], refs[2:4], refs[4], refs[5:]
    earlier, keep_ref, give_ref, send = refs[:-3], *refs[-3:]
    me = me_ref[0]
    core, chip = me % 2, me // 2
    devices = 2 * len(masks)
    tiles = 2 * halves[0].shape[0] // TILE
    normed = normed_rows(docs, docs, seq, weight, params)
    found = []
    for k, w_ref in enumerate(halves):
        parts = [ref[0 : len(group), :] for ref, group in zip(earlier[k::2], groups)]
        parts += tops_of(normed, w_ref, len(docs))
        found.append(jnp.concatenate(parts, axis=0))
    low = jnp.where(core == 0, found[0], found[1])
    high = jnp.where(core == 0, found[1], found[0])
    logits = jnp.concatenate([low, high], axis=1)
    docs_at = [me ^ (2 * mask) for mask in masks]
    bias = dbias_ref[...]
    bias = pltpu.roll(bias, bias.shape[0] - chip * tiles, 0)
    tables = jnp.concatenate([table_of(ref) for ref in tables], axis=0)
    tables = pltpu.roll(tables, TILE - chip * tiles, 1).astype(jnp.int32)
    send[...] = jnp.zeros(send.shape, jnp.float32)
    stride = keep_ref.shape[1]
    target = lax.broadcasted_iota(jnp.int32, (BLK_DEV * devices, TILE), 0)
    for t in range(tiles):
        lanes = slice(t * TILE, (t + 1) * TILE)
        impacts = jnp.log1p(jnp.maximum(logits[:, lanes] + bias[t : t + 1, :], 0.0))
        impacts = impacts.astype(jnp.bfloat16).astype(jnp.float32)
        blocks = jnp.zeros((BLK_DEV * devices, TILE), jnp.float32)
        for n in range(len(masks)):
            row = impacts[n : n + 1, :]
            send[pl.ds(docs_at[n] * stride + t, 1), :] = row
            block = jnp.broadcast_to(tables[n : n + 1, t : t + 1], target.shape)
            blocks = jnp.maximum(blocks, jnp.where(target == block, row, 0.0))
        for s in range(BLK_DEV):
            send[pl.ds((1 + s) * SLOT_ROWS + t, devices, stride=stride), :] = blocks[
                s * devices : (s + 1) * devices
            ]
    for k in range(len(masks)):
        at = pl.multiple_of((2 * k + core) * stride, SLOT_ROWS)
        keep_ref[k] = send[pl.ds(at, stride), :].astype(jnp.bfloat16)
        at = pl.multiple_of((2 * k + 1 - core) * stride + SLOT_ROWS, SLOT_ROWS)
        give_ref[k] = send[pl.ds(at, stride - SLOT_ROWS), :].astype(jnp.bfloat16)


def merge_kernel(keep_ref, got_ref, out_ref):
    out_ref[:, 0:SLOT_ROWS, :] = keep_ref[:, 0:SLOT_ROWS, :]
    mine = keep_ref[:, SLOT_ROWS:, :].astype(jnp.float32)
    theirs = got_ref[...].astype(jnp.float32)
    out_ref[:, SLOT_ROWS:, :] = jnp.maximum(mine, theirs).astype(jnp.bfloat16)


def place_kernel(tiles, rows_ref, impacts_ref, summaries_ref):
    for chip in range(rows_ref.shape[0]):
        rows = rows_ref[chip].astype(jnp.float32)
        lanes = slice(chip * tiles * TILE, (chip + 1) * tiles * TILE)
        lines = [
            jnp.concatenate([rows[first + t : first + t + 1] for t in range(tiles)], axis=1)
            for first in range(0, rows.shape[0], SLOT_ROWS)
        ]
        impacts_ref[:, lanes] = lines[0].astype(jnp.bfloat16)
        summaries_ref[:, lanes] = jnp.concatenate(lines[1:], axis=0).astype(jnp.bfloat16)


def move_tokens(
    hidden_states,
    doc_lengths,
    transform_weight,
    transform_bias,
    norm_gain,
    norm_bias,
    decoder_weight,
    decoder_bias,
    tile_ids,
    owner_ids,
    block_slots,
):
    devices = lax.axis_size("doc")
    chips = devices // 2
    seq, width = hidden_states.shape
    rows = transform_weight.shape[0]
    half = decoder_weight.shape[2]
    tiles = 2 * half // TILE
    me = lax.axis_index("doc").astype(jnp.int32)

    def cross(value, mask):
        return lax.ppermute(value, "doc", [(i, i ^ (2 * mask)) for i in range(devices)])

    def swap(value):
        return lax.ppermute(value, "doc", [(i, i ^ 1) for i in range(devices)])

    smem = pl.BlockSpec(memory_space=pltpu.SMEM)
    vmem = pl.BlockSpec(memory_space=pltpu.VMEM)
    hbm = pl.BlockSpec(memory_space=pltpu.HBM)

    def stay(value):
        return pltpu.with_memory_space_constraint(value, pltpu.HBM)

    limit = pltpu.CompilerParams(vmem_limit_bytes=24 * 1024 * 1024)

    def cost(docs):
        return pl.CostEstimate(flops=docs, bytes_accessed=docs, transcendentals=0)

    def shape(dims, dtype):
        return jax.ShapeDtypeStruct(dims, dtype)

    def after(value, *done):
        return lax.optimization_barrier((value, *done))[0]

    def pile(values, parts, heights=()):
        heights = heights or (sum(count for _, count in parts),)
        piled = pl.pallas_call(
            lambda *refs: pile_kernel(parts, heights, *refs),
            out_shape=[shape((height, width), jnp.bfloat16) for height in heights],
            in_specs=[vmem] * len(values),
            out_specs=[vmem] * len(heights),
            compiler_params=limit,
        )(*values)
        return piled if len(heights) > 1 else piled[0]

    where = me[None]
    weight_rows = jnp.swapaxes(decoder_weight[0], 0, 1)
    block_6 = cross(transform_weight, 6)
    block_2 = cross(transform_weight, 2)
    theirs = swap(weight_rows)
    docs = {1: cross(hidden_states, 1), 2: cross(hidden_states, 2)}
    load, block, table, params = pl.pallas_call(
        start_kernel,
        out_shape=[
            shape((seq + SLOT_ROWS, width), jnp.bfloat16),
            shape((rows, width), jnp.bfloat16),
            shape((SLOT_ROWS, width), jnp.bfloat16),
            shape((8, width), jnp.float32),
        ],
        in_specs=[smem] * 5 + [hbm] * 5,
        out_specs=[vmem] * 4,
        scratch_shapes=[
            pltpu.VMEM((3 * width,), jnp.float32),
            pltpu.SemaphoreType.DMA((5,)),
        ],
        compiler_params=limit,
    )(
        where,
        stay(tile_ids),
        stay(owner_ids[..., 0]),
        stay(block_slots),
        doc_lengths,
        stay(hidden_states),
        stay(transform_weight),
        stay(transform_bias),
        stay(norm_gain),
        stay(norm_bias),
    )
    one, two, below = (0, rows), (0, 2 * rows), (0, SLOT_ROWS)
    near = pile((block, after(block_2, block_6, docs[1]), table), (one, one, below))
    near_pile = cross(near, 1)
    block_4 = cross(pile((block_6, table), (one, below)), 2)
    docs[6] = cross(after(load, block_6), 6)
    docs[3] = cross(after(docs[2], near), 1)
    far_from = [stay(after(weight_rows, table))]
    [mine] = pl.pallas_call(
        lambda *refs: fetch_kernel(1, *refs),
        out_shape=[shape(value.shape, value.dtype) for value in far_from],
        in_specs=[vmem] + [hbm],
        out_specs=[vmem],
        scratch_shapes=[pltpu.SemaphoreType.DMA((1,))],
        compiler_params=limit,
    )(table, *far_from)
    far = (block_6, after(block_4, near_pile, docs[6], mine, theirs))
    far = pile(far, (one, (0, rows + SLOT_ROWS)))
    far_pile = cross(far, 1)
    docs[4] = pile((cross(after(docs[6], far), 2),), ((0, seq + SLOT_ROWS),))
    docs[7] = cross(docs[6], 1)
    sources = (after(block, docs[6], docs[3]), block_2, block_6, block_4, near_pile, far_pile)
    packed = pile(sources, (one, one, one, one, two, two), (seq,) * (chips * rows // seq))
    other_packed = [swap(part) for part in packed]
    block_masks = [0, 2, 6, 4, 1, 3, 7, 5]

    groups = [[0, 1], [2, 3], [6, 7, 4], [5]]
    masks = [mask for group in groups for mask in group]
    docs[0] = load
    tables = docs | {1: near_pile, 2: block_4, 3: far_pile}
    best_shape = shape((8, half), jnp.float32)
    *best, weight = pl.pallas_call(
        lambda *refs: first_kernel(seq, rows, block_masks, *refs),
        out_shape=[best_shape, best_shape, shape((width, width), jnp.bfloat16)],
        in_specs=[smem] + [vmem] * (7 + 2 * len(packed)),
        out_specs=[vmem] * 3,
        compiler_params=limit,
        cost_estimate=cost(2),
    )(
        where,
        *[docs[mask] for mask in masks[:2]],
        *[tables[mask] for mask in masks[:2]],
        *packed,
        *other_packed,
        params,
        mine,
        theirs,
    )
    docs[5] = cross(after(docs[4], weight), 1)
    tables[5] = docs[5]
    for group in groups[1:-1]:
        best += pl.pallas_call(
            lambda *refs, count=len(group): next_kernel(seq, count, *refs),
            out_shape=[best_shape] * 2,
            in_specs=[vmem] * (2 * len(group) + 4),
            out_specs=[vmem] * 2,
            compiler_params=limit,
            cost_estimate=cost(len(group)),
        )(
            *[docs[mask] for mask in group],
            *[tables[mask] for mask in group],
            after(weight, best[-1]),
            params,
            mine,
            theirs,
        )
    height = (1 + BLK_DEV) * SLOT_ROWS
    keep, give = pl.pallas_call(
        lambda *refs: last_kernel(seq, groups, *refs),
        out_shape=[
            shape((chips, height, TILE), jnp.bfloat16),
            shape((chips, height - SLOT_ROWS, TILE), jnp.bfloat16),
        ],
        in_specs=[smem] + [vmem] * (len(groups[-1]) + len(masks) + 5 + len(best)),
        out_specs=[vmem] * 2,
        scratch_shapes=[pltpu.VMEM((devices * height, TILE), jnp.float32)],
        compiler_params=limit,
        cost_estimate=cost(2),
    )(
        where,
        *[docs[mask] for mask in groups[-1]],
        *[tables[mask] for mask in masks],
        weight,
        params,
        mine,
        theirs,
        decoder_bias.reshape(-1, TILE),
        *best,
    )
    merged = pl.pallas_call(
        merge_kernel,
        out_shape=shape((chips, height, TILE), jnp.bfloat16),
        in_specs=[vmem] * 2,
        out_specs=vmem,
        compiler_params=limit,
    )(keep, swap(give))
    alike = [list(range(parity, devices, 2)) for parity in range(2)]
    got = lax.all_to_all(
        merged, "doc", split_axis=0, concat_axis=0, axis_index_groups=alike, tiled=True
    )
    return pl.pallas_call(
        lambda *refs: place_kernel(tiles, *refs),
        out_shape=[
            shape((1, chips * tiles * TILE), jnp.bfloat16),
            shape((BLK_DEV, chips * tiles * TILE), jnp.bfloat16),
        ],
        in_specs=[vmem],
        out_specs=[vmem] * 2,
        compiler_params=limit,
    )(got)


def tokens_move(mesh):
    return mesh.shape["term"] == 1 and mesh.shape["doc"] == 16


def solution(mesh):
    placed = (
        P(("groups", "doc"), None),
        P(("groups", "doc")),
        P("doc", "term"),
        P(),
        P(),
        P(),
        P("term", None, "doc"),
        P("term"),
        P("term", ("groups", "doc"), None),
        P("term", ("groups", "doc"), None, None),
        P("term", ("groups", "doc"), None),
    )

    def local(*args):
        pair = 2 * args[6].shape[2]
        tiles = pair * (mesh.shape["doc"] // 2) // TILE
        fits = pair % TILE == 0 and tiles < TILE and pair // TILE <= SLOT_ROWS
        if tokens_move(mesh) and args[1].shape[0] == 1 and fits:
            return move_tokens(*args)
        return move_weights(*args)

    return jax.shard_map(
        local,
        mesh=mesh,
        in_specs=placed,
        out_specs=(P(("groups", "doc"), "term"), P(("groups", "doc"), "term")),
        check_vma=False,
    )
```

```python
import jax
import jax.numpy as jnp
from jax import lax
from jax.experimental import pallas as pl
from jax.experimental.pallas import tpu as pltpu
from jax.sharding import PartitionSpec as P

TILE = 128
BLK_DEV = 2
SLOT_ROWS = 16


def layer_norm(activated, norm_gain, norm_bias):
    values = activated.astype(jnp.float32)
    centre = jnp.mean(values, axis=-1, keepdims=True)
    centred = values - centre
    spread = jnp.mean(centred * centred, axis=-1, keepdims=True)
    return (centred * lax.rsqrt(spread + 1e-05) * norm_gain + norm_bias).astype(jnp.bfloat16)


def pool_docs(logits, keep):
    docs_here = keep.shape[0]
    saturated = jnp.log1p(jnp.maximum(logits, 0.0)).reshape(
        docs_here, keep.shape[1], logits.shape[1]
    )
    return jnp.max(jnp.where(keep[:, :, None], saturated, 0.0), axis=1)


def move_weights(
    hidden_states,
    doc_lengths,
    transform_weight,
    transform_bias,
    norm_gain,
    norm_bias,
    decoder_weight,
    decoder_bias,
    tile_ids,
    owner_ids,
    block_slots,
):
    tok_rows = hidden_states.shape[0]
    docs_here = doc_lengths.shape[0]
    seq_len = tok_rows // docs_here
    cols = transform_weight.shape[1]
    pre_half = jnp.dot(
        hidden_states,
        lax.all_gather(transform_weight, "doc", axis=0, tiled=True),
        preferred_element_type=jnp.float32,
    )
    bias_half = lax.dynamic_slice_in_dim(transform_bias, lax.axis_index("term") * cols, cols, 0)
    act_half = jax.nn.gelu(pre_half + bias_half, approximate=False).astype(jnp.bfloat16)
    activated = lax.all_gather(act_half, "term", axis=1, tiled=True)
    normed = layer_norm(activated, norm_gain, norm_bias)
    keep = jnp.arange(seq_len, dtype=jnp.int32)[None, :] < doc_lengths[:, None]
    logits = jnp.dot(
        normed,
        lax.all_gather(decoder_weight, "doc", axis=2, tiled=True)[0],
        preferred_element_type=jnp.float32,
    )
    logits = logits + decoder_bias
    impacts = pool_docs(logits, keep).astype(jnp.bfloat16)
    tiles_t = impacts.shape[1] // TILE
    slots_total = BLK_DEV * tiles_t
    tiles = impacts.reshape(docs_here * tiles_t, TILE)
    chosen = tile_ids[0]
    doc_index = jnp.arange(docs_here, dtype=jnp.int32)[:, None]
    posted = tiles[(doc_index * tiles_t + chosen).reshape(-1)]
    owners = owner_ids[0, :, :, 0].reshape(-1)
    target = block_slots[0].reshape(-1) * tiles_t + chosen.reshape(-1)
    owner_count = lax.axis_size("doc")
    capacity = max(2, 2 * posted.shape[0] // owner_count)
    onehot = (owners[:, None] == jnp.arange(owner_count, dtype=jnp.int32)[None, :]).astype(
        jnp.int32
    )
    before = jnp.cumsum(onehot, axis=0) - onehot
    position = jnp.sum(before * onehot, axis=1)
    dest = owners * capacity + position
    outgoing = jnp.zeros((owner_count * capacity, TILE), jnp.bfloat16).at[dest].set(posted)
    out_tags = jnp.full((owner_count * capacity,), slots_total, jnp.int32).at[dest].set(target)
    got_vals, got_tags = (
        lax.all_to_all(
            outgoing.reshape(owner_count, capacity, TILE),
            "doc",
            split_axis=0,
            concat_axis=0,
            tiled=True,
        ),
        lax.all_to_all(
            out_tags.reshape(owner_count, capacity), "doc", split_axis=0, concat_axis=0, tiled=True
        ),
    )
    got_vals = got_vals.reshape(-1, TILE)
    local_tags = got_tags.reshape(-1)
    summary = jnp.zeros((slots_total, TILE), jnp.bfloat16).at[local_tags].max(got_vals, mode="drop")
    return (impacts, summary.reshape(BLK_DEV, tiles_t * TILE))


def dot_t(left, right):
    return lax.dot_general(
        left, right, (((1,), (1,)), ((), ())), preferred_element_type=jnp.float32
    )


def table_of(ref):
    return ref[ref.shape[0] - SLOT_ROWS :, 0:TILE].astype(jnp.float32)[0:1, :]


def masked(ref, table_ref, seq):
    here = ref[0:seq, :]
    length = table_of(table_ref)[:, TILE - 1 :]
    keep = lax.broadcasted_iota(jnp.int32, here.shape, 0).astype(jnp.float32) < length
    first = jnp.broadcast_to(here[0:1, :].astype(jnp.float32), here.shape).astype(here.dtype)
    return jnp.where(keep, here, first)


def normed_rows(docs, tables, seq, weight, params):
    rows = [masked(ref, table, seq) for ref, table in zip(docs, tables)]
    rows = jnp.concatenate(rows, axis=0)
    pre = jnp.dot(rows, weight[...], preferred_element_type=jnp.float32) + params[0:1, :]
    act = 0.5 * pre * (1.0 + lax.erf(pre * (0.5**0.5)))
    return layer_norm(act.astype(jnp.bfloat16), params[1:2, :], params[2:3, :])


def tops_of(normed, w_ref, count):
    logits = dot_t(normed, w_ref[...])
    seq = normed.shape[0] // count
    return [
        jnp.max(logits[j * seq : (j + 1) * seq], axis=0, keepdims=True) for j in range(count)
    ]


def start_kernel(me_ref, tiles_ref, owners_ref, slots_ref, length_ref, *refs):
    hidden_ref, weight_ref, vectors = refs[0], refs[1], refs[2:5]
    load_ref, block_ref, table_ref, rows_ref, kept, sems = refs[5:]
    seq, width = hidden_ref.shape
    copies = [
        fetch(hidden_ref, load_ref.at[pl.ds(0, seq), :], sems.at[0]),
        fetch(weight_ref, block_ref, sems.at[1]),
    ]
    for k, ref in enumerate(vectors):
        copies.append(fetch(ref, kept.at[pl.ds(k * width, width)], sems.at[2 + k]))
    lane = lax.broadcasted_iota(jnp.int32, (SLOT_ROWS, TILE), 1)
    table = jnp.where(lane == TILE - 1, length_ref[0], -1)
    devices = lax.axis_size("doc")
    for k in range(tiles_ref.shape[2]):
        block = slots_ref[0, 0, k] * devices + owners_ref[0, 0, k]
        table = jnp.where(lane == tiles_ref[0, 0, k], block, table)
    table = table.astype(jnp.float32).astype(jnp.bfloat16)
    for first in range(0, width, TILE):
        load_ref[seq:, first : first + TILE] = table
        table_ref[:, first : first + TILE] = table
    for copy in copies:
        copy.wait()
    for k in range(len(vectors)):
        rows_ref[k : k + 1, :] = kept[pl.ds(k * width, width)][None, :]


def pile_kernel(parts, heights, *refs):
    rows = jnp.concatenate(
        [ref[first : first + count, :] for ref, (first, count) in zip(refs, parts)], axis=0
    )
    at = 0
    for ref, height in zip(refs[len(parts) :], heights):
        ref[...] = rows[at : at + height, :]
        at += height


def fetch(ref, slot, sem):
    copy = pltpu.make_async_copy(ref, slot, sem)
    copy.start()
    return copy


def keep_tops(normed, count, halves, bests):
    for w_ref, best in zip(halves, bests):
        for j, top in enumerate(tops_of(normed, w_ref, count)):
            best[j : j + 1, :] = top


def fetch_kernel(count, *refs):
    copies = [fetch(refs[1 + k], refs[1 + count + k], refs[-1].at[k]) for k in range(count)]
    for copy in copies:
        copy.wait()


def first_kernel(seq, shard, masks, count, *refs):
    me_ref, docs, refs = refs[0], refs[1 : 1 + count], refs[1 + count :]
    tables, refs = refs[:count], refs[count:]
    count = len(masks) * shard // seq
    parts, others, refs = refs[:count], refs[count : 2 * count], refs[2 * count :]
    params, halves, refs = refs[0], refs[1:3], refs[3:]
    bests, weight = refs[:2], refs[2]
    me = me_ref[0]
    core = me % 2
    for at in range(0, len(masks) * shard, SLOT_ROWS):
        (k, inside), (part, place) = divmod(at, shard), divmod(at, seq)
        chip = (me // 2) ^ masks[k]
        for whose, sources in ((core, parts), (1 - core, others)):
            to = pl.multiple_of((2 * chip + whose) * shard + inside, SLOT_ROWS)
            weight[pl.ds(to, SLOT_ROWS), :] = sources[part][place : place + SLOT_ROWS, :]
    keep_tops(normed_rows(docs, tables, seq, weight, params), len(docs), halves, bests)


def next_kernel(seq, count, *refs):
    docs, tables, refs = refs[:count], refs[count : 2 * count], refs[2 * count :]
    weight, params, refs = refs[0], refs[1], refs[2:]
    keep_tops(normed_rows(docs, tables, seq, weight, params), count, refs[:2], refs[2:])


def last_kernel(seq, groups, *refs):
    masks = [mask for group in groups for mask in group]
    me_ref, docs, refs = refs[0], refs[1 : 1 + len(groups[-1])], refs[1 + len(groups[-1]) :]
    tables, refs = refs[: len(masks)], refs[len(masks) :]
    weight, params, halves, dbias_ref, refs = refs[0], refs[1], refs[2:4], refs[4], refs[5:]
    earlier, keep_ref, give_ref, send = refs[:-3], *refs[-3:]
    me = me_ref[0]
    core, chip = me % 2, me // 2
    devices = 2 * len(masks)
    tiles = 2 * halves[0].shape[0] // TILE
    normed = normed_rows(docs, docs, seq, weight, params)
    found = []
    for k, w_ref in enumerate(halves):
        parts = [ref[0 : len(group), :] for ref, group in zip(earlier[k::2], groups)]
        parts += tops_of(normed, w_ref, len(docs))
        found.append(jnp.concatenate(parts, axis=0))
    low = jnp.where(core == 0, found[0], found[1])
    high = jnp.where(core == 0, found[1], found[0])
    logits = jnp.concatenate([low, high], axis=1)
    docs_at = [me ^ (2 * mask) for mask in masks]
    bias = dbias_ref[...]
    bias = pltpu.roll(bias, bias.shape[0] - chip * tiles, 0)
    tables = jnp.concatenate([table_of(ref) for ref in tables], axis=0)
    tables = pltpu.roll(tables, TILE - chip * tiles, 1).astype(jnp.int32)
    send[...] = jnp.zeros(send.shape, jnp.float32)
    stride = keep_ref.shape[1]
    target = lax.broadcasted_iota(jnp.int32, (BLK_DEV * devices, TILE), 0)
    for t in range(tiles):
        lanes = slice(t * TILE, (t + 1) * TILE)
        impacts = jnp.log1p(jnp.maximum(logits[:, lanes] + bias[t : t + 1, :], 0.0))
        impacts = impacts.astype(jnp.bfloat16).astype(jnp.float32)
        blocks = jnp.zeros((BLK_DEV * devices, TILE), jnp.float32)
        for n in range(len(masks)):
            row = impacts[n : n + 1, :]
            send[pl.ds(docs_at[n] * stride + t, 1), :] = row
            block = jnp.broadcast_to(tables[n : n + 1, t : t + 1], target.shape)
            blocks = jnp.maximum(blocks, jnp.where(target == block, row, 0.0))
        for s in range(BLK_DEV):
            send[pl.ds((1 + s) * SLOT_ROWS + t, devices, stride=stride), :] = blocks[
                s * devices : (s + 1) * devices
            ]
    for k in range(len(masks)):
        at = pl.multiple_of((2 * k + core) * stride, SLOT_ROWS)
        keep_ref[k] = send[pl.ds(at, stride), :].astype(jnp.bfloat16)
        at = pl.multiple_of((2 * k + 1 - core) * stride + SLOT_ROWS, SLOT_ROWS)
        give_ref[k] = send[pl.ds(at, stride - SLOT_ROWS), :].astype(jnp.bfloat16)


def merge_kernel(keep_ref, got_ref, out_ref):
    out_ref[:, 0:SLOT_ROWS, :] = keep_ref[:, 0:SLOT_ROWS, :]
    mine = keep_ref[:, SLOT_ROWS:, :].astype(jnp.float32)
    theirs = got_ref[...].astype(jnp.float32)
    out_ref[:, SLOT_ROWS:, :] = jnp.maximum(mine, theirs).astype(jnp.bfloat16)


def place_kernel(tiles, rows_ref, impacts_ref, summaries_ref):
    for chip in range(rows_ref.shape[0]):
        rows = rows_ref[chip].astype(jnp.float32)
        lanes = slice(chip * tiles * TILE, (chip + 1) * tiles * TILE)
        lines = [
            jnp.concatenate([rows[first + t : first + t + 1] for t in range(tiles)], axis=1)
            for first in range(0, rows.shape[0], SLOT_ROWS)
        ]
        impacts_ref[:, lanes] = lines[0].astype(jnp.bfloat16)
        summaries_ref[:, lanes] = jnp.concatenate(lines[1:], axis=0).astype(jnp.bfloat16)


def move_tokens(
    hidden_states,
    doc_lengths,
    transform_weight,
    transform_bias,
    norm_gain,
    norm_bias,
    decoder_weight,
    decoder_bias,
    tile_ids,
    owner_ids,
    block_slots,
):
    devices = lax.axis_size("doc")
    chips = devices // 2
    seq, width = hidden_states.shape
    rows = transform_weight.shape[0]
    half = decoder_weight.shape[2]
    tiles = 2 * half // TILE
    me = lax.axis_index("doc").astype(jnp.int32)

    def cross(value, mask):
        return lax.ppermute(value, "doc", [(i, i ^ (2 * mask)) for i in range(devices)])

    def swap(value):
        return lax.ppermute(value, "doc", [(i, i ^ 1) for i in range(devices)])

    smem = pl.BlockSpec(memory_space=pltpu.SMEM)
    vmem = pl.BlockSpec(memory_space=pltpu.VMEM)
    hbm = pl.BlockSpec(memory_space=pltpu.HBM)

    def stay(value):
        return pltpu.with_memory_space_constraint(value, pltpu.HBM)

    limit = pltpu.CompilerParams(vmem_limit_bytes=24 * 1024 * 1024)

    def cost(docs):
        return pl.CostEstimate(flops=docs, bytes_accessed=docs, transcendentals=0)

    def shape(dims, dtype):
        return jax.ShapeDtypeStruct(dims, dtype)

    def after(value, *done):
        return lax.optimization_barrier((value, *done))[0]

    def pile(values, parts, heights=()):
        heights = heights or (sum(count for _, count in parts),)
        piled = pl.pallas_call(
            lambda *refs: pile_kernel(parts, heights, *refs),
            out_shape=[shape((height, width), jnp.bfloat16) for height in heights],
            in_specs=[vmem] * len(values),
            out_specs=[vmem] * len(heights),
            compiler_params=limit,
        )(*values)
        return piled if len(heights) > 1 else piled[0]

    where = me[None]
    weight_rows = jnp.swapaxes(decoder_weight[0], 0, 1)
    block_6 = cross(transform_weight, 6)
    block_2 = cross(transform_weight, 2)
    theirs = swap(weight_rows)
    docs = {1: cross(hidden_states, 1), 2: cross(hidden_states, 2)}
    load, block, table, params = pl.pallas_call(
        start_kernel,
        out_shape=[
            shape((seq + SLOT_ROWS, width), jnp.bfloat16),
            shape((rows, width), jnp.bfloat16),
            shape((SLOT_ROWS, width), jnp.bfloat16),
            shape((8, width), jnp.float32),
        ],
        in_specs=[smem] * 5 + [hbm] * 5,
        out_specs=[vmem] * 4,
        scratch_shapes=[
            pltpu.VMEM((3 * width,), jnp.float32),
            pltpu.SemaphoreType.DMA((5,)),
        ],
        compiler_params=limit,
    )(
        where,
        stay(tile_ids),
        stay(owner_ids[..., 0]),
        stay(block_slots),
        doc_lengths,
        stay(hidden_states),
        stay(transform_weight),
        stay(transform_bias),
        stay(norm_gain),
        stay(norm_bias),
    )
    one, two, below = (0, rows), (0, 2 * rows), (0, SLOT_ROWS)
    near = pile((block, after(block_2, block_6, docs[1]), table), (one, one, below))
    near_pile = cross(near, 1)
    block_4 = cross(pile((block_6, table), (one, below)), 2)
    docs[6] = cross(after(load, block_6), 6)
    docs[3] = cross(after(docs[2], near), 1)
    far_from = [stay(after(weight_rows, table))]
    [mine] = pl.pallas_call(
        lambda *refs: fetch_kernel(1, *refs),
        out_shape=[shape(value.shape, value.dtype) for value in far_from],
        in_specs=[vmem] + [hbm],
        out_specs=[vmem],
        scratch_shapes=[pltpu.SemaphoreType.DMA((1,))],
        compiler_params=limit,
    )(table, *far_from)
    far = (block_6, after(block_4, near_pile, mine, theirs))
    far = pile(far, (one, (0, rows + SLOT_ROWS)))
    far_pile = cross(far, 1)
    docs[4] = cross(after(docs[6], far), 2)
    docs[7] = cross(docs[6], 1)
    sources = (after(block, docs[6], docs[3]), block_2, block_6, block_4, near_pile, far_pile)
    packed = pile(sources, (one, one, one, one, two, two), (seq,) * (chips * rows // seq))
    other_packed = [swap(part) for part in packed]
    block_masks = [0, 2, 6, 4, 1, 3, 7, 5]

    groups = [[6, 7, 0], [1, 2, 3], [4, 5]]
    masks = [mask for group in groups for mask in group]
    docs[0] = load
    docs[5] = cross(after(docs[4], docs[7], *other_packed), 1)
    tables = docs | {1: near_pile, 2: block_4, 3: far_pile}
    best_shape = shape((8, half), jnp.float32)
    *best, weight = pl.pallas_call(
        lambda *refs: first_kernel(seq, rows, block_masks, len(groups[0]), *refs),
        out_shape=[best_shape, best_shape, shape((width, width), jnp.bfloat16)],
        in_specs=[smem] + [vmem] * (2 * len(groups[0]) + 3 + 2 * len(packed)),
        out_specs=[vmem] * 3,
        compiler_params=limit,
        cost_estimate=cost(2),
    )(
        where,
        *[docs[mask] for mask in groups[0]],
        *[tables[mask] for mask in groups[0]],
        *packed,
        *other_packed,
        params,
        mine,
        theirs,
    )
    for group in groups[1:-1]:
        best += pl.pallas_call(
            lambda *refs, count=len(group): next_kernel(seq, count, *refs),
            out_shape=[best_shape] * 2,
            in_specs=[vmem] * (2 * len(group) + 4),
            out_specs=[vmem] * 2,
            compiler_params=limit,
            cost_estimate=cost(len(group)),
        )(
            *[docs[mask] for mask in group],
            *[tables[mask] for mask in group],
            after(weight, best[-1]),
            params,
            mine,
            theirs,
        )
    height = (1 + BLK_DEV) * SLOT_ROWS
    keep, give = pl.pallas_call(
        lambda *refs: last_kernel(seq, groups, *refs),
        out_shape=[
            shape((chips, height, TILE), jnp.bfloat16),
            shape((chips, height - SLOT_ROWS, TILE), jnp.bfloat16),
        ],
        in_specs=[smem] + [vmem] * (len(groups[-1]) + len(masks) + 5 + len(best)),
        out_specs=[vmem] * 2,
        scratch_shapes=[pltpu.VMEM((devices * height, TILE), jnp.float32)],
        compiler_params=limit,
        cost_estimate=cost(2),
    )(
        where,
        *[docs[mask] for mask in groups[-1]],
        *[tables[mask] for mask in masks],
        weight,
        params,
        mine,
        theirs,
        decoder_bias.reshape(-1, TILE),
        *best,
    )
    merged = pl.pallas_call(
        merge_kernel,
        out_shape=shape((chips, height, TILE), jnp.bfloat16),
        in_specs=[vmem] * 2,
        out_specs=vmem,
        compiler_params=limit,
    )(keep, swap(give))
    alike = [list(range(parity, devices, 2)) for parity in range(2)]
    got = lax.all_to_all(
        merged, "doc", split_axis=0, concat_axis=0, axis_index_groups=alike, tiled=True
    )
    return pl.pallas_call(
        lambda *refs: place_kernel(tiles, *refs),
        out_shape=[
            shape((1, chips * tiles * TILE), jnp.bfloat16),
            shape((BLK_DEV, chips * tiles * TILE), jnp.bfloat16),
        ],
        in_specs=[vmem],
        out_specs=[vmem] * 2,
        compiler_params=limit,
    )(got)


def tokens_move(mesh):
    return mesh.shape["term"] == 1 and mesh.shape["doc"] == 16


def solution(mesh):
    placed = (
        P(("groups", "doc"), None),
        P(("groups", "doc")),
        P("doc", "term"),
        P(),
        P(),
        P(),
        P("term", None, "doc"),
        P("term"),
        P("term", ("groups", "doc"), None),
        P("term", ("groups", "doc"), None, None),
        P("term", ("groups", "doc"), None),
    )

    def local(*args):
        pair = 2 * args[6].shape[2]
        tiles = pair * (mesh.shape["doc"] // 2) // TILE
        fits = pair % TILE == 0 and tiles < TILE and pair // TILE <= SLOT_ROWS
        if tokens_move(mesh) and args[1].shape[0] == 1 and fits:
            return move_tokens(*args)
        return move_weights(*args)

    return jax.shard_map(
        local,
        mesh=mesh,
        in_specs=placed,
        out_specs=(P(("groups", "doc"), "term"), P(("groups", "doc"), "term")),
        check_vma=False,
    )
```

```python
import jax
import jax.numpy as jnp
from jax import lax
from jax.experimental import pallas as pl
from jax.experimental.pallas import tpu as pltpu
from jax.sharding import PartitionSpec as P

TILE = 128
BLK_DEV = 2
SLOT_ROWS = 16


def layer_norm(activated, norm_gain, norm_bias):
    values = activated.astype(jnp.float32)
    centre = jnp.mean(values, axis=-1, keepdims=True)
    centred = values - centre
    spread = jnp.mean(centred * centred, axis=-1, keepdims=True)
    return (centred * lax.rsqrt(spread + 1e-05) * norm_gain + norm_bias).astype(jnp.bfloat16)


def pool_docs(logits, keep):
    docs_here = keep.shape[0]
    saturated = jnp.log1p(jnp.maximum(logits, 0.0)).reshape(
        docs_here, keep.shape[1], logits.shape[1]
    )
    return jnp.max(jnp.where(keep[:, :, None], saturated, 0.0), axis=1)


def move_weights(
    hidden_states,
    doc_lengths,
    transform_weight,
    transform_bias,
    norm_gain,
    norm_bias,
    decoder_weight,
    decoder_bias,
    tile_ids,
    owner_ids,
    block_slots,
):
    tok_rows = hidden_states.shape[0]
    docs_here = doc_lengths.shape[0]
    seq_len = tok_rows // docs_here
    cols = transform_weight.shape[1]
    pre_half = jnp.dot(
        hidden_states,
        lax.all_gather(transform_weight, "doc", axis=0, tiled=True),
        preferred_element_type=jnp.float32,
    )
    bias_half = lax.dynamic_slice_in_dim(transform_bias, lax.axis_index("term") * cols, cols, 0)
    act_half = jax.nn.gelu(pre_half + bias_half, approximate=False).astype(jnp.bfloat16)
    activated = lax.all_gather(act_half, "term", axis=1, tiled=True)
    normed = layer_norm(activated, norm_gain, norm_bias)
    keep = jnp.arange(seq_len, dtype=jnp.int32)[None, :] < doc_lengths[:, None]
    logits = jnp.dot(
        normed,
        lax.all_gather(decoder_weight, "doc", axis=2, tiled=True)[0],
        preferred_element_type=jnp.float32,
    )
    logits = logits + decoder_bias
    impacts = pool_docs(logits, keep).astype(jnp.bfloat16)
    tiles_t = impacts.shape[1] // TILE
    slots_total = BLK_DEV * tiles_t
    tiles = impacts.reshape(docs_here * tiles_t, TILE)
    chosen = tile_ids[0]
    doc_index = jnp.arange(docs_here, dtype=jnp.int32)[:, None]
    posted = tiles[(doc_index * tiles_t + chosen).reshape(-1)]
    owners = owner_ids[0, :, :, 0].reshape(-1)
    target = block_slots[0].reshape(-1) * tiles_t + chosen.reshape(-1)
    owner_count = lax.axis_size("doc")
    capacity = max(2, 2 * posted.shape[0] // owner_count)
    onehot = (owners[:, None] == jnp.arange(owner_count, dtype=jnp.int32)[None, :]).astype(
        jnp.int32
    )
    before = jnp.cumsum(onehot, axis=0) - onehot
    position = jnp.sum(before * onehot, axis=1)
    dest = owners * capacity + position
    outgoing = jnp.zeros((owner_count * capacity, TILE), jnp.bfloat16).at[dest].set(posted)
    out_tags = jnp.full((owner_count * capacity,), slots_total, jnp.int32).at[dest].set(target)
    got_vals, got_tags = (
        lax.all_to_all(
            outgoing.reshape(owner_count, capacity, TILE),
            "doc",
            split_axis=0,
            concat_axis=0,
            tiled=True,
        ),
        lax.all_to_all(
            out_tags.reshape(owner_count, capacity), "doc", split_axis=0, concat_axis=0, tiled=True
        ),
    )
    got_vals = got_vals.reshape(-1, TILE)
    local_tags = got_tags.reshape(-1)
    summary = jnp.zeros((slots_total, TILE), jnp.bfloat16).at[local_tags].max(got_vals, mode="drop")
    return (impacts, summary.reshape(BLK_DEV, tiles_t * TILE))


def dot_t(left, right):
    return lax.dot_general(
        left, right, (((1,), (1,)), ((), ())), preferred_element_type=jnp.float32
    )


def table_of(ref):
    return ref[ref.shape[0] - SLOT_ROWS :, 0:TILE].astype(jnp.float32)[0:1, :]


def masked(ref, table_ref, seq):
    here = ref[0:seq, :]
    length = table_of(table_ref)[:, TILE - 1 :]
    keep = lax.broadcasted_iota(jnp.int32, here.shape, 0).astype(jnp.float32) < length
    first = jnp.broadcast_to(here[0:1, :].astype(jnp.float32), here.shape).astype(here.dtype)
    return jnp.where(keep, here, first)


def normed_rows(docs, tables, seq, weight, params):
    rows = [masked(ref, table, seq) for ref, table in zip(docs, tables)]
    rows = jnp.concatenate(rows, axis=0)
    pre = jnp.dot(rows, weight[...], preferred_element_type=jnp.float32) + params[0:1, :]
    act = 0.5 * pre * (1.0 + lax.erf(pre * (0.5**0.5)))
    return layer_norm(act.astype(jnp.bfloat16), params[1:2, :], params[2:3, :])


def tops_of(normed, w_ref, count):
    logits = dot_t(normed, w_ref[...])
    seq = normed.shape[0] // count
    return [
        jnp.max(logits[j * seq : (j + 1) * seq], axis=0, keepdims=True) for j in range(count)
    ]


def start_kernel(me_ref, tiles_ref, owners_ref, slots_ref, length_ref, *refs):
    hidden_ref, weight_ref, vectors = refs[0], refs[1], refs[2:5]
    load_ref, block_ref, table_ref, rows_ref, kept, sems = refs[5:]
    seq, width = hidden_ref.shape
    copies = [
        fetch(hidden_ref, load_ref.at[pl.ds(0, seq), :], sems.at[0]),
        fetch(weight_ref, block_ref, sems.at[1]),
    ]
    for k, ref in enumerate(vectors):
        copies.append(fetch(ref, kept.at[pl.ds(k * width, width)], sems.at[2 + k]))
    lane = lax.broadcasted_iota(jnp.int32, (SLOT_ROWS, TILE), 1)
    table = jnp.where(lane == TILE - 1, length_ref[0], -1)
    devices = lax.axis_size("doc")
    for k in range(tiles_ref.shape[2]):
        block = slots_ref[0, 0, k] * devices + owners_ref[0, 0, k]
        table = jnp.where(lane == tiles_ref[0, 0, k], block, table)
    table = table.astype(jnp.float32).astype(jnp.bfloat16)
    for first in range(0, width, TILE):
        load_ref[seq:, first : first + TILE] = table
        table_ref[:, first : first + TILE] = table
    for copy in copies:
        copy.wait()
    for k in range(len(vectors)):
        rows_ref[k : k + 1, :] = kept[pl.ds(k * width, width)][None, :]


def pile_kernel(parts, heights, *refs):
    rows = jnp.concatenate(
        [ref[first : first + count, :] for ref, (first, count) in zip(refs, parts)], axis=0
    )
    at = 0
    for ref, height in zip(refs[len(parts) :], heights):
        ref[...] = rows[at : at + height, :]
        at += height


def fetch(ref, slot, sem):
    copy = pltpu.make_async_copy(ref, slot, sem)
    copy.start()
    return copy


def keep_tops(normed, count, halves, bests):
    for w_ref, best in zip(halves, bests):
        for j, top in enumerate(tops_of(normed, w_ref, count)):
            best[j : j + 1, :] = top


def fetch_kernel(count, *refs):
    copies = [fetch(refs[1 + k], refs[1 + count + k], refs[-1].at[k]) for k in range(count)]
    for copy in copies:
        copy.wait()


def first_kernel(seq, shard, masks, count, *refs):
    me_ref, docs, refs = refs[0], refs[1 : 1 + count], refs[1 + count :]
    tables, refs = refs[:count], refs[count:]
    count = len(masks) * shard // seq
    parts, others, refs = refs[:count], refs[count : 2 * count], refs[2 * count :]
    params, halves, refs = refs[0], refs[1:3], refs[3:]
    bests, weight = refs[:2], refs[2]
    me = me_ref[0]
    core = me % 2
    for at in range(0, len(masks) * shard, SLOT_ROWS):
        (k, inside), (part, place) = divmod(at, shard), divmod(at, seq)
        chip = (me // 2) ^ masks[k]
        for whose, sources in ((core, parts), (1 - core, others)):
            to = pl.multiple_of((2 * chip + whose) * shard + inside, SLOT_ROWS)
            weight[pl.ds(to, SLOT_ROWS), :] = sources[part][place : place + SLOT_ROWS, :]
    keep_tops(normed_rows(docs, tables, seq, weight, params), len(docs), halves, bests)


def next_kernel(seq, count, *refs):
    docs, tables, refs = refs[:count], refs[count : 2 * count], refs[2 * count :]
    weight, params, refs = refs[0], refs[1], refs[2:]
    keep_tops(normed_rows(docs, tables, seq, weight, params), count, refs[:2], refs[2:])


def last_kernel(seq, groups, *refs):
    masks = [mask for group in groups for mask in group]
    me_ref, docs, refs = refs[0], refs[1 : 1 + len(groups[-1])], refs[1 + len(groups[-1]) :]
    tables, refs = refs[: len(masks)], refs[len(masks) :]
    weight, params, halves, dbias_ref, refs = refs[0], refs[1], refs[2:4], refs[4], refs[5:]
    earlier, keep_ref, give_ref, send = refs[:-3], *refs[-3:]
    me = me_ref[0]
    core, chip = me % 2, me // 2
    devices = 2 * len(masks)
    tiles = 2 * halves[0].shape[0] // TILE
    normed = normed_rows(docs, docs, seq, weight, params)
    found = []
    for k, w_ref in enumerate(halves):
        parts = [ref[0 : len(group), :] for ref, group in zip(earlier[k::2], groups)]
        parts += tops_of(normed, w_ref, len(docs))
        found.append(jnp.concatenate(parts, axis=0))
    low = jnp.where(core == 0, found[0], found[1])
    high = jnp.where(core == 0, found[1], found[0])
    logits = jnp.concatenate([low, high], axis=1)
    docs_at = [me ^ (2 * mask) for mask in masks]
    bias = dbias_ref[...]
    bias = pltpu.roll(bias, bias.shape[0] - chip * tiles, 0)
    tables = jnp.concatenate([table_of(ref) for ref in tables], axis=0)
    tables = pltpu.roll(tables, TILE - chip * tiles, 1).astype(jnp.int32)
    send[...] = jnp.zeros(send.shape, jnp.float32)
    stride = keep_ref.shape[1]
    target = lax.broadcasted_iota(jnp.int32, (BLK_DEV * devices, TILE), 0)
    for t in range(tiles):
        lanes = slice(t * TILE, (t + 1) * TILE)
        impacts = jnp.log1p(jnp.maximum(logits[:, lanes] + bias[t : t + 1, :], 0.0))
        impacts = impacts.astype(jnp.bfloat16).astype(jnp.float32)
        blocks = jnp.zeros((BLK_DEV * devices, TILE), jnp.float32)
        for n in range(len(masks)):
            row = impacts[n : n + 1, :]
            send[pl.ds(docs_at[n] * stride + t, 1), :] = row
            block = jnp.broadcast_to(tables[n : n + 1, t : t + 1], target.shape)
            blocks = jnp.maximum(blocks, jnp.where(target == block, row, 0.0))
        for s in range(BLK_DEV):
            send[pl.ds((1 + s) * SLOT_ROWS + t, devices, stride=stride), :] = blocks[
                s * devices : (s + 1) * devices
            ]
    for k in range(len(masks)):
        at = pl.multiple_of((2 * k + core) * stride, SLOT_ROWS)
        keep_ref[k] = send[pl.ds(at, stride), :].astype(jnp.bfloat16)
        at = pl.multiple_of((2 * k + 1 - core) * stride + SLOT_ROWS, SLOT_ROWS)
        give_ref[k] = send[pl.ds(at, stride - SLOT_ROWS), :].astype(jnp.bfloat16)


def merge_kernel(keep_ref, got_ref, out_ref):
    out_ref[:, 0:SLOT_ROWS, :] = keep_ref[:, 0:SLOT_ROWS, :]
    mine = keep_ref[:, SLOT_ROWS:, :].astype(jnp.float32)
    theirs = got_ref[...].astype(jnp.float32)
    out_ref[:, SLOT_ROWS:, :] = jnp.maximum(mine, theirs).astype(jnp.bfloat16)


def place_kernel(tiles, rows_ref, impacts_ref, summaries_ref):
    for chip in range(rows_ref.shape[0]):
        rows = rows_ref[chip].astype(jnp.float32)
        lanes = slice(chip * tiles * TILE, (chip + 1) * tiles * TILE)
        lines = [
            jnp.concatenate([rows[first + t : first + t + 1] for t in range(tiles)], axis=1)
            for first in range(0, rows.shape[0], SLOT_ROWS)
        ]
        impacts_ref[:, lanes] = lines[0].astype(jnp.bfloat16)
        summaries_ref[:, lanes] = jnp.concatenate(lines[1:], axis=0).astype(jnp.bfloat16)


def move_tokens(
    hidden_states,
    doc_lengths,
    transform_weight,
    transform_bias,
    norm_gain,
    norm_bias,
    decoder_weight,
    decoder_bias,
    tile_ids,
    owner_ids,
    block_slots,
):
    devices = lax.axis_size("doc")
    chips = devices // 2
    seq, width = hidden_states.shape
    rows = transform_weight.shape[0]
    half = decoder_weight.shape[2]
    tiles = 2 * half // TILE
    me = lax.axis_index("doc").astype(jnp.int32)

    def cross(value, mask):
        return lax.ppermute(value, "doc", [(i, i ^ (2 * mask)) for i in range(devices)])

    def swap(value):
        return lax.ppermute(value, "doc", [(i, i ^ 1) for i in range(devices)])

    smem = pl.BlockSpec(memory_space=pltpu.SMEM)
    vmem = pl.BlockSpec(memory_space=pltpu.VMEM)
    hbm = pl.BlockSpec(memory_space=pltpu.HBM)

    def stay(value):
        return pltpu.with_memory_space_constraint(value, pltpu.HBM)

    limit = pltpu.CompilerParams(vmem_limit_bytes=24 * 1024 * 1024)

    def cost(docs):
        return pl.CostEstimate(flops=docs, bytes_accessed=docs, transcendentals=0)

    def shape(dims, dtype):
        return jax.ShapeDtypeStruct(dims, dtype)

    def after(value, *done):
        return lax.optimization_barrier((value, *done))[0]

    def pile(values, parts, heights=()):
        heights = heights or (sum(count for _, count in parts),)
        piled = pl.pallas_call(
            lambda *refs: pile_kernel(parts, heights, *refs),
            out_shape=[shape((height, width), jnp.bfloat16) for height in heights],
            in_specs=[vmem] * len(values),
            out_specs=[vmem] * len(heights),
            compiler_params=limit,
        )(*values)
        return piled if len(heights) > 1 else piled[0]

    where = me[None]
    weight_rows = jnp.swapaxes(decoder_weight[0], 0, 1)
    block_6 = cross(transform_weight, 6)
    block_2 = cross(transform_weight, 2)
    theirs = swap(weight_rows)
    docs = {1: cross(hidden_states, 1), 2: cross(hidden_states, 2)}
    load, block, table, params = pl.pallas_call(
        start_kernel,
        out_shape=[
            shape((seq + SLOT_ROWS, width), jnp.bfloat16),
            shape((rows, width), jnp.bfloat16),
            shape((SLOT_ROWS, width), jnp.bfloat16),
            shape((8, width), jnp.float32),
        ],
        in_specs=[smem] * 5 + [hbm] * 5,
        out_specs=[vmem] * 4,
        scratch_shapes=[
            pltpu.VMEM((3 * width,), jnp.float32),
            pltpu.SemaphoreType.DMA((5,)),
        ],
        compiler_params=limit,
    )(
        where,
        stay(tile_ids),
        stay(owner_ids[..., 0]),
        stay(block_slots),
        doc_lengths,
        stay(hidden_states),
        stay(transform_weight),
        stay(transform_bias),
        stay(norm_gain),
        stay(norm_bias),
    )
    one, two, below = (0, rows), (0, 2 * rows), (0, SLOT_ROWS)
    near = pile((block, after(block_2, block_6, docs[1]), table), (one, one, below))
    near_pile = cross(near, 1)
    block_4 = cross(pile((block_6, table), (one, below)), 2)
    docs[6] = cross(after(load, block_6), 6)
    docs[3] = cross(after(docs[2], near), 1)
    far_from = [stay(after(weight_rows, near))]
    [mine] = pl.pallas_call(
        lambda *refs: fetch_kernel(1, *refs),
        out_shape=[shape(value.shape, value.dtype) for value in far_from],
        in_specs=[vmem] + [hbm],
        out_specs=[vmem],
        scratch_shapes=[pltpu.SemaphoreType.DMA((1,))],
        compiler_params=limit,
    )(table, *far_from)
    far = (block_6, after(block_4, mine, theirs))
    far = pile(far, (one, (0, rows + SLOT_ROWS)))
    far_pile = cross(far, 1)
    docs[4] = cross(after(docs[6], far), 2)
    docs[7] = cross(docs[6], 1)
    sources = (after(block, docs[6], docs[3]), block_2, block_6, block_4, near_pile, far_pile)
    packed = pile(sources, (one, one, one, one, two, two), (seq,) * (chips * rows // seq))
    other_packed = [swap(part) for part in packed]
    block_masks = [0, 2, 6, 4, 1, 3, 7, 5]

    groups = [[6, 7, 0], [1, 2, 3], [4, 5]]
    masks = [mask for group in groups for mask in group]
    docs[0] = load
    docs[5] = cross(after(docs[4], docs[7], *other_packed), 1)
    tables = docs | {1: near_pile, 2: block_4, 3: far_pile}
    best_shape = shape((8, half), jnp.float32)
    *best, weight = pl.pallas_call(
        lambda *refs: first_kernel(seq, rows, block_masks, len(groups[0]), *refs),
        out_shape=[best_shape, best_shape, shape((width, width), jnp.bfloat16)],
        in_specs=[smem] + [vmem] * (2 * len(groups[0]) + 3 + 2 * len(packed)),
        out_specs=[vmem] * 3,
        compiler_params=limit,
        cost_estimate=cost(2),
    )(
        where,
        *[docs[mask] for mask in groups[0]],
        *[tables[mask] for mask in groups[0]],
        *packed,
        *other_packed,
        params,
        mine,
        theirs,
    )
    for group in groups[1:-1]:
        best += pl.pallas_call(
            lambda *refs, count=len(group): next_kernel(seq, count, *refs),
            out_shape=[best_shape] * 2,
            in_specs=[vmem] * (2 * len(group) + 4),
            out_specs=[vmem] * 2,
            compiler_params=limit,
            cost_estimate=cost(len(group)),
        )(
            *[docs[mask] for mask in group],
            *[tables[mask] for mask in group],
            after(weight, best[-1]),
            params,
            mine,
            theirs,
        )
    height = (1 + BLK_DEV) * SLOT_ROWS
    keep, give = pl.pallas_call(
        lambda *refs: last_kernel(seq, groups, *refs),
        out_shape=[
            shape((chips, height, TILE), jnp.bfloat16),
            shape((chips, height - SLOT_ROWS, TILE), jnp.bfloat16),
        ],
        in_specs=[smem] + [vmem] * (len(groups[-1]) + len(masks) + 5 + len(best)),
        out_specs=[vmem] * 2,
        scratch_shapes=[pltpu.VMEM((devices * height, TILE), jnp.float32)],
        compiler_params=limit,
        cost_estimate=cost(2),
    )(
        where,
        *[docs[mask] for mask in groups[-1]],
        *[tables[mask] for mask in masks],
        weight,
        params,
        mine,
        theirs,
        decoder_bias.reshape(-1, TILE),
        *best,
    )
    merged = pl.pallas_call(
        merge_kernel,
        out_shape=shape((chips, height, TILE), jnp.bfloat16),
        in_specs=[vmem] * 2,
        out_specs=vmem,
        compiler_params=limit,
    )(keep, swap(give))
    alike = [list(range(parity, devices, 2)) for parity in range(2)]
    got = lax.all_to_all(
        merged, "doc", split_axis=0, concat_axis=0, axis_index_groups=alike, tiled=True
    )
    return pl.pallas_call(
        lambda *refs: place_kernel(tiles, *refs),
        out_shape=[
            shape((1, chips * tiles * TILE), jnp.bfloat16),
            shape((BLK_DEV, chips * tiles * TILE), jnp.bfloat16),
        ],
        in_specs=[vmem],
        out_specs=[vmem] * 2,
        compiler_params=limit,
    )(got)


def tokens_move(mesh):
    return mesh.shape["term"] == 1 and mesh.shape["doc"] == 16


def solution(mesh):
    placed = (
        P(("groups", "doc"), None),
        P(("groups", "doc")),
        P("doc", "term"),
        P(),
        P(),
        P(),
        P("term", None, "doc"),
        P("term"),
        P("term", ("groups", "doc"), None),
        P("term", ("groups", "doc"), None, None),
        P("term", ("groups", "doc"), None),
    )

    def local(*args):
        pair = 2 * args[6].shape[2]
        tiles = pair * (mesh.shape["doc"] // 2) // TILE
        fits = pair % TILE == 0 and tiles < TILE and pair // TILE <= SLOT_ROWS
        if tokens_move(mesh) and args[1].shape[0] == 1 and fits:
            return move_tokens(*args)
        return move_weights(*args)

    return jax.shard_map(
        local,
        mesh=mesh,
        in_specs=placed,
        out_specs=(P(("groups", "doc"), "term"), P(("groups", "doc"), "term")),
        check_vma=False,
    )
```

```python
import jax
import jax.numpy as jnp
from jax import lax
from jax.experimental import pallas as pl
from jax.experimental.pallas import tpu as pltpu
from jax.sharding import PartitionSpec as P

TILE = 128
BLK_DEV = 2
SLOT_ROWS = 16


def layer_norm(activated, norm_gain, norm_bias):
    values = activated.astype(jnp.float32)
    centre = jnp.mean(values, axis=-1, keepdims=True)
    centred = values - centre
    spread = jnp.mean(centred * centred, axis=-1, keepdims=True)
    return (centred * lax.rsqrt(spread + 1e-05) * norm_gain + norm_bias).astype(jnp.bfloat16)


def pool_docs(logits, keep):
    docs_here = keep.shape[0]
    saturated = jnp.log1p(jnp.maximum(logits, 0.0)).reshape(
        docs_here, keep.shape[1], logits.shape[1]
    )
    return jnp.max(jnp.where(keep[:, :, None], saturated, 0.0), axis=1)


def move_weights(
    hidden_states,
    doc_lengths,
    transform_weight,
    transform_bias,
    norm_gain,
    norm_bias,
    decoder_weight,
    decoder_bias,
    tile_ids,
    owner_ids,
    block_slots,
):
    tok_rows = hidden_states.shape[0]
    docs_here = doc_lengths.shape[0]
    seq_len = tok_rows // docs_here
    cols = transform_weight.shape[1]
    pre_half = jnp.dot(
        hidden_states,
        lax.all_gather(transform_weight, "doc", axis=0, tiled=True),
        preferred_element_type=jnp.float32,
    )
    bias_half = lax.dynamic_slice_in_dim(transform_bias, lax.axis_index("term") * cols, cols, 0)
    act_half = jax.nn.gelu(pre_half + bias_half, approximate=False).astype(jnp.bfloat16)
    activated = lax.all_gather(act_half, "term", axis=1, tiled=True)
    normed = layer_norm(activated, norm_gain, norm_bias)
    keep = jnp.arange(seq_len, dtype=jnp.int32)[None, :] < doc_lengths[:, None]
    logits = jnp.dot(
        normed,
        lax.all_gather(decoder_weight, "doc", axis=2, tiled=True)[0],
        preferred_element_type=jnp.float32,
    )
    logits = logits + decoder_bias
    impacts = pool_docs(logits, keep).astype(jnp.bfloat16)
    tiles_t = impacts.shape[1] // TILE
    slots_total = BLK_DEV * tiles_t
    tiles = impacts.reshape(docs_here * tiles_t, TILE)
    chosen = tile_ids[0]
    doc_index = jnp.arange(docs_here, dtype=jnp.int32)[:, None]
    posted = tiles[(doc_index * tiles_t + chosen).reshape(-1)]
    owners = owner_ids[0, :, :, 0].reshape(-1)
    target = block_slots[0].reshape(-1) * tiles_t + chosen.reshape(-1)
    owner_count = lax.axis_size("doc")
    capacity = max(2, 2 * posted.shape[0] // owner_count)
    onehot = (owners[:, None] == jnp.arange(owner_count, dtype=jnp.int32)[None, :]).astype(
        jnp.int32
    )
    before = jnp.cumsum(onehot, axis=0) - onehot
    position = jnp.sum(before * onehot, axis=1)
    dest = owners * capacity + position
    outgoing = jnp.zeros((owner_count * capacity, TILE), jnp.bfloat16).at[dest].set(posted)
    out_tags = jnp.full((owner_count * capacity,), slots_total, jnp.int32).at[dest].set(target)
    got_vals, got_tags = (
        lax.all_to_all(
            outgoing.reshape(owner_count, capacity, TILE),
            "doc",
            split_axis=0,
            concat_axis=0,
            tiled=True,
        ),
        lax.all_to_all(
            out_tags.reshape(owner_count, capacity), "doc", split_axis=0, concat_axis=0, tiled=True
        ),
    )
    got_vals = got_vals.reshape(-1, TILE)
    local_tags = got_tags.reshape(-1)
    summary = jnp.zeros((slots_total, TILE), jnp.bfloat16).at[local_tags].max(got_vals, mode="drop")
    return (impacts, summary.reshape(BLK_DEV, tiles_t * TILE))


def dot_t(left, right):
    return lax.dot_general(
        left, right, (((1,), (1,)), ((), ())), preferred_element_type=jnp.float32
    )


def table_of(ref):
    return ref[ref.shape[0] - SLOT_ROWS :, 0:TILE].astype(jnp.float32)[0:1, :]


def masked(ref, table_ref, seq):
    here = ref[0:seq, :]
    length = table_of(table_ref)[:, TILE - 1 :]
    keep = lax.broadcasted_iota(jnp.int32, here.shape, 0).astype(jnp.float32) < length
    first = jnp.broadcast_to(here[0:1, :].astype(jnp.float32), here.shape).astype(here.dtype)
    return jnp.where(keep, here, first)


def normed_rows(docs, tables, seq, weight, params):
    rows = [masked(ref, table, seq) for ref, table in zip(docs, tables)]
    rows = jnp.concatenate(rows, axis=0)
    pre = jnp.dot(rows, weight[...], preferred_element_type=jnp.float32) + params[0:1, :]
    act = 0.5 * pre * (1.0 + lax.erf(pre * (0.5**0.5)))
    return layer_norm(act.astype(jnp.bfloat16), params[1:2, :], params[2:3, :])


def tops_of(normed, w_ref, count):
    logits = dot_t(normed, w_ref[...])
    seq = normed.shape[0] // count
    return [
        jnp.max(logits[j * seq : (j + 1) * seq], axis=0, keepdims=True) for j in range(count)
    ]


def start_kernel(me_ref, tiles_ref, owners_ref, slots_ref, length_ref, *refs):
    hidden_ref, weight_ref, vectors = refs[0], refs[1], refs[2:5]
    load_ref, block_ref, table_ref, rows_ref, kept, sems = refs[5:]
    seq, width = hidden_ref.shape
    copies = [
        fetch(hidden_ref, load_ref.at[pl.ds(0, seq), :], sems.at[0]),
        fetch(weight_ref, block_ref, sems.at[1]),
    ]
    for k, ref in enumerate(vectors):
        copies.append(fetch(ref, kept.at[pl.ds(k * width, width)], sems.at[2 + k]))
    lane = lax.broadcasted_iota(jnp.int32, (SLOT_ROWS, TILE), 1)
    table = jnp.where(lane == TILE - 1, length_ref[0], -1)
    devices = lax.axis_size("doc")
    for k in range(tiles_ref.shape[2]):
        block = slots_ref[0, 0, k] * devices + owners_ref[0, 0, k]
        table = jnp.where(lane == tiles_ref[0, 0, k], block, table)
    table = table.astype(jnp.float32).astype(jnp.bfloat16)
    for first in range(0, width, TILE):
        load_ref[seq:, first : first + TILE] = table
        table_ref[:, first : first + TILE] = table
    for copy in copies:
        copy.wait()
    for k in range(len(vectors)):
        rows_ref[k : k + 1, :] = kept[pl.ds(k * width, width)][None, :]


def pile_kernel(parts, heights, *refs):
    rows = jnp.concatenate(
        [ref[first : first + count, :] for ref, (first, count) in zip(refs, parts)], axis=0
    )
    at = 0
    for ref, height in zip(refs[len(parts) :], heights):
        ref[...] = rows[at : at + height, :]
        at += height


def fetch(ref, slot, sem):
    copy = pltpu.make_async_copy(ref, slot, sem)
    copy.start()
    return copy


def keep_tops(normed, count, halves, bests):
    for w_ref, best in zip(halves, bests):
        for j, top in enumerate(tops_of(normed, w_ref, count)):
            best[j : j + 1, :] = top


def fetch_kernel(count, *refs):
    copies = [fetch(refs[1 + k], refs[1 + count + k], refs[-1].at[k]) for k in range(count)]
    for copy in copies:
        copy.wait()


def first_kernel(seq, shard, masks, count, *refs):
    me_ref, docs, refs = refs[0], refs[1 : 1 + count], refs[1 + count :]
    tables, refs = refs[:count], refs[count:]
    count = len(masks) * shard // seq
    parts, others, refs = refs[:count], refs[count : 2 * count], refs[2 * count :]
    params, halves, refs = refs[0], refs[1:3], refs[3:]
    bests, weight = refs[:2], refs[2]
    me = me_ref[0]
    core = me % 2
    for at in range(0, len(masks) * shard, SLOT_ROWS):
        (k, inside), (part, place) = divmod(at, shard), divmod(at, seq)
        chip = (me // 2) ^ masks[k]
        for whose, sources in ((core, parts), (1 - core, others)):
            to = pl.multiple_of((2 * chip + whose) * shard + inside, SLOT_ROWS)
            weight[pl.ds(to, SLOT_ROWS), :] = sources[part][place : place + SLOT_ROWS, :]
    keep_tops(normed_rows(docs, tables, seq, weight, params), len(docs), halves, bests)


def next_kernel(seq, count, *refs):
    docs, tables, refs = refs[:count], refs[count : 2 * count], refs[2 * count :]
    weight, params, refs = refs[0], refs[1], refs[2:]
    keep_tops(normed_rows(docs, tables, seq, weight, params), count, refs[:2], refs[2:])


def last_kernel(seq, groups, *refs):
    masks = [mask for group in groups for mask in group]
    me_ref, docs, refs = refs[0], refs[1 : 1 + len(groups[-1])], refs[1 + len(groups[-1]) :]
    tables, refs = refs[: len(masks)], refs[len(masks) :]
    weight, params, halves, dbias_ref, refs = refs[0], refs[1], refs[2:4], refs[4], refs[5:]
    earlier, keep_ref, give_ref, send = refs[:-3], *refs[-3:]
    me = me_ref[0]
    core, chip = me % 2, me // 2
    devices = 2 * len(masks)
    tiles = 2 * halves[0].shape[0] // TILE
    normed = normed_rows(docs, docs, seq, weight, params)
    found = []
    for k, w_ref in enumerate(halves):
        parts = [ref[0 : len(group), :] for ref, group in zip(earlier[k::2], groups)]
        parts += tops_of(normed, w_ref, len(docs))
        found.append(jnp.concatenate(parts, axis=0))
    low = jnp.where(core == 0, found[0], found[1])
    high = jnp.where(core == 0, found[1], found[0])
    logits = jnp.concatenate([low, high], axis=1)
    docs_at = [me ^ (2 * mask) for mask in masks]
    bias = dbias_ref[...]
    bias = pltpu.roll(bias, bias.shape[0] - chip * tiles, 0)
    tables = jnp.concatenate([table_of(ref) for ref in tables], axis=0)
    tables = pltpu.roll(tables, TILE - chip * tiles, 1).astype(jnp.int32)
    send[...] = jnp.zeros(send.shape, jnp.float32)
    stride = keep_ref.shape[1]
    target = lax.broadcasted_iota(jnp.int32, (BLK_DEV * devices, TILE), 0)
    for t in range(tiles):
        lanes = slice(t * TILE, (t + 1) * TILE)
        impacts = jnp.log1p(jnp.maximum(logits[:, lanes] + bias[t : t + 1, :], 0.0))
        impacts = impacts.astype(jnp.bfloat16).astype(jnp.float32)
        blocks = jnp.zeros((BLK_DEV * devices, TILE), jnp.float32)
        for n in range(len(masks)):
            row = impacts[n : n + 1, :]
            send[pl.ds(docs_at[n] * stride + t, 1), :] = row
            block = jnp.broadcast_to(tables[n : n + 1, t : t + 1], target.shape)
            blocks = jnp.maximum(blocks, jnp.where(target == block, row, 0.0))
        for s in range(BLK_DEV):
            send[pl.ds((1 + s) * SLOT_ROWS + t, devices, stride=stride), :] = blocks[
                s * devices : (s + 1) * devices
            ]
    for k in range(len(masks)):
        at = pl.multiple_of((2 * k + core) * stride, SLOT_ROWS)
        keep_ref[k] = send[pl.ds(at, stride), :].astype(jnp.bfloat16)
        at = pl.multiple_of((2 * k + 1 - core) * stride + SLOT_ROWS, SLOT_ROWS)
        give_ref[k] = send[pl.ds(at, stride - SLOT_ROWS), :].astype(jnp.bfloat16)


def merge_kernel(keep_ref, got_ref, out_ref):
    out_ref[:, 0:SLOT_ROWS, :] = keep_ref[:, 0:SLOT_ROWS, :]
    mine = keep_ref[:, SLOT_ROWS:, :].astype(jnp.float32)
    theirs = got_ref[...].astype(jnp.float32)
    out_ref[:, SLOT_ROWS:, :] = jnp.maximum(mine, theirs).astype(jnp.bfloat16)


def place_kernel(tiles, rows_ref, impacts_ref, summaries_ref):
    for chip in range(rows_ref.shape[0]):
        rows = rows_ref[chip].astype(jnp.float32)
        lanes = slice(chip * tiles * TILE, (chip + 1) * tiles * TILE)
        lines = [
            jnp.concatenate([rows[first + t : first + t + 1] for t in range(tiles)], axis=1)
            for first in range(0, rows.shape[0], SLOT_ROWS)
        ]
        impacts_ref[:, lanes] = lines[0].astype(jnp.bfloat16)
        summaries_ref[:, lanes] = jnp.concatenate(lines[1:], axis=0).astype(jnp.bfloat16)


def move_tokens(
    hidden_states,
    doc_lengths,
    transform_weight,
    transform_bias,
    norm_gain,
    norm_bias,
    decoder_weight,
    decoder_bias,
    tile_ids,
    owner_ids,
    block_slots,
):
    devices = lax.axis_size("doc")
    chips = devices // 2
    seq, width = hidden_states.shape
    rows = transform_weight.shape[0]
    half = decoder_weight.shape[2]
    tiles = 2 * half // TILE
    me = lax.axis_index("doc").astype(jnp.int32)

    def cross(value, mask):
        return lax.ppermute(value, "doc", [(i, i ^ (2 * mask)) for i in range(devices)])

    def swap(value):
        return lax.ppermute(value, "doc", [(i, i ^ 1) for i in range(devices)])

    smem = pl.BlockSpec(memory_space=pltpu.SMEM)
    vmem = pl.BlockSpec(memory_space=pltpu.VMEM)
    hbm = pl.BlockSpec(memory_space=pltpu.HBM)

    def stay(value):
        return pltpu.with_memory_space_constraint(value, pltpu.HBM)

    limit = pltpu.CompilerParams(vmem_limit_bytes=24 * 1024 * 1024)

    def cost(docs):
        return pl.CostEstimate(flops=docs, bytes_accessed=docs, transcendentals=0)

    def shape(dims, dtype):
        return jax.ShapeDtypeStruct(dims, dtype)

    def after(value, *done):
        return lax.optimization_barrier((value, *done))[0]

    def pile(values, parts, heights=()):
        heights = heights or (sum(count for _, count in parts),)
        piled = pl.pallas_call(
            lambda *refs: pile_kernel(parts, heights, *refs),
            out_shape=[shape((height, width), jnp.bfloat16) for height in heights],
            in_specs=[vmem] * len(values),
            out_specs=[vmem] * len(heights),
            compiler_params=limit,
        )(*values)
        return piled if len(heights) > 1 else piled[0]

    where = me[None]
    weight_rows = jnp.swapaxes(decoder_weight[0], 0, 1)
    block_6 = cross(transform_weight, 6)
    block_2 = cross(transform_weight, 2)
    theirs = swap(weight_rows)
    docs = {1: cross(hidden_states, 1), 2: cross(hidden_states, 2)}
    load, block, table, params = pl.pallas_call(
        start_kernel,
        out_shape=[
            shape((seq + SLOT_ROWS, width), jnp.bfloat16),
            shape((rows, width), jnp.bfloat16),
            shape((SLOT_ROWS, width), jnp.bfloat16),
            shape((8, width), jnp.float32),
        ],
        in_specs=[smem] * 5 + [hbm] * 5,
        out_specs=[vmem] * 4,
        scratch_shapes=[
            pltpu.VMEM((3 * width,), jnp.float32),
            pltpu.SemaphoreType.DMA((5,)),
        ],
        compiler_params=limit,
    )(
        where,
        stay(tile_ids),
        stay(owner_ids[..., 0]),
        stay(block_slots),
        doc_lengths,
        stay(hidden_states),
        stay(transform_weight),
        stay(transform_bias),
        stay(norm_gain),
        stay(norm_bias),
    )
    one, two, below = (0, rows), (0, 2 * rows), (0, SLOT_ROWS)
    near = pile((block, after(block_2, block_6, docs[1]), table), (one, one, below))
    near_pile = cross(near, 1)
    block_4 = cross(pile((block_6, table), (one, below)), 2)
    docs[6] = cross(after(load, block_6), 6)
    docs[3] = cross(after(docs[2], near), 1)
    far_from = [stay(after(weight_rows, table))]
    [mine] = pl.pallas_call(
        lambda *refs: fetch_kernel(1, *refs),
        out_shape=[shape(value.shape, value.dtype) for value in far_from],
        in_specs=[vmem] + [hbm],
        out_specs=[vmem],
        scratch_shapes=[pltpu.SemaphoreType.DMA((1,))],
        compiler_params=limit,
    )(table, *far_from)
    far = (block_6, after(block_4, near_pile, mine, theirs))
    far = pile(far, (one, (0, rows + SLOT_ROWS)))
    far_pile = cross(far, 1)
    docs[4] = cross(after(docs[6], far), 2)
    docs[7] = cross(docs[6], 1)
    sources = (after(block, docs[6], docs[3]), block_2, block_6, block_4, near_pile, far_pile)
    packed = pile(sources, (one, one, one, one, two, two), (seq,) * (chips * rows // seq))
    other_packed = [swap(part) for part in packed]
    block_masks = [0, 2, 6, 4, 1, 3, 7, 5]

    groups = [[6, 7, 0], [1, 2, 3], [4, 5]]
    masks = [mask for group in groups for mask in group]
    docs[0] = load
    docs[5] = cross(after(docs[4], *other_packed), 1)
    tables = docs | {1: near_pile, 2: block_4, 3: far_pile}
    best_shape = shape((8, half), jnp.float32)
    *best, weight = pl.pallas_call(
        lambda *refs: first_kernel(seq, rows, block_masks, len(groups[0]), *refs),
        out_shape=[best_shape, best_shape, shape((width, width), jnp.bfloat16)],
        in_specs=[smem] + [vmem] * (2 * len(groups[0]) + 3 + 2 * len(packed)),
        out_specs=[vmem] * 3,
        compiler_params=limit,
        cost_estimate=cost(3 * 10**9),
    )(
        where,
        *[docs[mask] for mask in groups[0]],
        *[tables[mask] for mask in groups[0]],
        *packed,
        *other_packed,
        params,
        mine,
        theirs,
    )
    for group in groups[1:-1]:
        best += pl.pallas_call(
            lambda *refs, count=len(group): next_kernel(seq, count, *refs),
            out_shape=[best_shape] * 2,
            in_specs=[vmem] * (2 * len(group) + 4),
            out_specs=[vmem] * 2,
            compiler_params=limit,
            cost_estimate=cost(len(group)),
        )(
            *[docs[mask] for mask in group],
            *[tables[mask] for mask in group],
            after(weight, best[-1]),
            params,
            mine,
            theirs,
        )
    height = (1 + BLK_DEV) * SLOT_ROWS
    keep, give = pl.pallas_call(
        lambda *refs: last_kernel(seq, groups, *refs),
        out_shape=[
            shape((chips, height, TILE), jnp.bfloat16),
            shape((chips, height - SLOT_ROWS, TILE), jnp.bfloat16),
        ],
        in_specs=[smem] + [vmem] * (len(groups[-1]) + len(masks) + 5 + len(best)),
        out_specs=[vmem] * 2,
        scratch_shapes=[pltpu.VMEM((devices * height, TILE), jnp.float32)],
        compiler_params=limit,
        cost_estimate=cost(2),
    )(
        where,
        *[docs[mask] for mask in groups[-1]],
        *[tables[mask] for mask in masks],
        weight,
        params,
        mine,
        theirs,
        decoder_bias.reshape(-1, TILE),
        *best,
    )
    merged = pl.pallas_call(
        merge_kernel,
        out_shape=shape((chips, height, TILE), jnp.bfloat16),
        in_specs=[vmem] * 2,
        out_specs=vmem,
        compiler_params=limit,
    )(keep, swap(give))
    alike = [list(range(parity, devices, 2)) for parity in range(2)]
    got = lax.all_to_all(
        merged, "doc", split_axis=0, concat_axis=0, axis_index_groups=alike, tiled=True
    )
    return pl.pallas_call(
        lambda *refs: place_kernel(tiles, *refs),
        out_shape=[
            shape((1, chips * tiles * TILE), jnp.bfloat16),
            shape((BLK_DEV, chips * tiles * TILE), jnp.bfloat16),
        ],
        in_specs=[vmem],
        out_specs=[vmem] * 2,
        compiler_params=limit,
    )(got)


def tokens_move(mesh):
    return mesh.shape["term"] == 1 and mesh.shape["doc"] == 16


def solution(mesh):
    placed = (
        P(("groups", "doc"), None),
        P(("groups", "doc")),
        P("doc", "term"),
        P(),
        P(),
        P(),
        P("term", None, "doc"),
        P("term"),
        P("term", ("groups", "doc"), None),
        P("term", ("groups", "doc"), None, None),
        P("term", ("groups", "doc"), None),
    )

    def local(*args):
        pair = 2 * args[6].shape[2]
        tiles = pair * (mesh.shape["doc"] // 2) // TILE
        fits = pair % TILE == 0 and tiles < TILE and pair // TILE <= SLOT_ROWS
        if tokens_move(mesh) and args[1].shape[0] == 1 and fits:
            return move_tokens(*args)
        return move_weights(*args)

    return jax.shard_map(
        local,
        mesh=mesh,
        in_specs=placed,
        out_specs=(P(("groups", "doc"), "term"), P(("groups", "doc"), "term")),
        check_vma=False,
    )
```

```python
import jax
import jax.numpy as jnp
from jax import lax
from jax.experimental import pallas as pl
from jax.experimental.pallas import tpu as pltpu
from jax.sharding import PartitionSpec as P

TILE = 128
BLK_DEV = 2
SLOT_ROWS = 16


def layer_norm(activated, norm_gain, norm_bias):
    values = activated.astype(jnp.float32)
    centre = jnp.mean(values, axis=-1, keepdims=True)
    centred = values - centre
    spread = jnp.mean(centred * centred, axis=-1, keepdims=True)
    return (centred * lax.rsqrt(spread + 1e-05) * norm_gain + norm_bias).astype(jnp.bfloat16)


def pool_docs(logits, keep):
    docs_here = keep.shape[0]
    saturated = jnp.log1p(jnp.maximum(logits, 0.0)).reshape(
        docs_here, keep.shape[1], logits.shape[1]
    )
    return jnp.max(jnp.where(keep[:, :, None], saturated, 0.0), axis=1)


def move_weights(
    hidden_states,
    doc_lengths,
    transform_weight,
    transform_bias,
    norm_gain,
    norm_bias,
    decoder_weight,
    decoder_bias,
    tile_ids,
    owner_ids,
    block_slots,
):
    tok_rows = hidden_states.shape[0]
    docs_here = doc_lengths.shape[0]
    seq_len = tok_rows // docs_here
    cols = transform_weight.shape[1]
    pre_half = jnp.dot(
        hidden_states,
        lax.all_gather(transform_weight, "doc", axis=0, tiled=True),
        preferred_element_type=jnp.float32,
    )
    bias_half = lax.dynamic_slice_in_dim(transform_bias, lax.axis_index("term") * cols, cols, 0)
    act_half = jax.nn.gelu(pre_half + bias_half, approximate=False).astype(jnp.bfloat16)
    activated = lax.all_gather(act_half, "term", axis=1, tiled=True)
    normed = layer_norm(activated, norm_gain, norm_bias)
    keep = jnp.arange(seq_len, dtype=jnp.int32)[None, :] < doc_lengths[:, None]
    logits = jnp.dot(
        normed,
        lax.all_gather(decoder_weight, "doc", axis=2, tiled=True)[0],
        preferred_element_type=jnp.float32,
    )
    logits = logits + decoder_bias
    impacts = pool_docs(logits, keep).astype(jnp.bfloat16)
    tiles_t = impacts.shape[1] // TILE
    slots_total = BLK_DEV * tiles_t
    tiles = impacts.reshape(docs_here * tiles_t, TILE)
    chosen = tile_ids[0]
    doc_index = jnp.arange(docs_here, dtype=jnp.int32)[:, None]
    posted = tiles[(doc_index * tiles_t + chosen).reshape(-1)]
    owners = owner_ids[0, :, :, 0].reshape(-1)
    target = block_slots[0].reshape(-1) * tiles_t + chosen.reshape(-1)
    owner_count = lax.axis_size("doc")
    capacity = max(2, 2 * posted.shape[0] // owner_count)
    onehot = (owners[:, None] == jnp.arange(owner_count, dtype=jnp.int32)[None, :]).astype(
        jnp.int32
    )
    before = jnp.cumsum(onehot, axis=0) - onehot
    position = jnp.sum(before * onehot, axis=1)
    dest = owners * capacity + position
    outgoing = jnp.zeros((owner_count * capacity, TILE), jnp.bfloat16).at[dest].set(posted)
    out_tags = jnp.full((owner_count * capacity,), slots_total, jnp.int32).at[dest].set(target)
    got_vals, got_tags = (
        lax.all_to_all(
            outgoing.reshape(owner_count, capacity, TILE),
            "doc",
            split_axis=0,
            concat_axis=0,
            tiled=True,
        ),
        lax.all_to_all(
            out_tags.reshape(owner_count, capacity), "doc", split_axis=0, concat_axis=0, tiled=True
        ),
    )
    got_vals = got_vals.reshape(-1, TILE)
    local_tags = got_tags.reshape(-1)
    summary = jnp.zeros((slots_total, TILE), jnp.bfloat16).at[local_tags].max(got_vals, mode="drop")
    return (impacts, summary.reshape(BLK_DEV, tiles_t * TILE))


def dot_t(left, right):
    return lax.dot_general(
        left, right, (((1,), (1,)), ((), ())), preferred_element_type=jnp.float32
    )


def table_of(ref):
    return ref[ref.shape[0] - SLOT_ROWS :, 0:TILE].astype(jnp.float32)[0:1, :]


def masked(ref, table_ref, seq):
    here = ref[0:seq, :]
    length = table_of(table_ref)[:, TILE - 1 :]
    keep = lax.broadcasted_iota(jnp.int32, here.shape, 0).astype(jnp.float32) < length
    first = jnp.broadcast_to(here[0:1, :].astype(jnp.float32), here.shape).astype(here.dtype)
    return jnp.where(keep, here, first)


def normed_rows(docs, tables, seq, weight, params):
    rows = [masked(ref, table, seq) for ref, table in zip(docs, tables)]
    rows = jnp.concatenate(rows, axis=0)
    pre = jnp.dot(rows, weight[...], preferred_element_type=jnp.float32) + params[0:1, :]
    act = 0.5 * pre * (1.0 + lax.erf(pre * (0.5**0.5)))
    return layer_norm(act.astype(jnp.bfloat16), params[1:2, :], params[2:3, :])


def tops_of(normed, w_ref, count):
    logits = dot_t(normed, w_ref[...])
    seq = normed.shape[0] // count
    return [
        jnp.max(logits[j * seq : (j + 1) * seq], axis=0, keepdims=True) for j in range(count)
    ]


def start_kernel(me_ref, tiles_ref, owners_ref, slots_ref, length_ref, *refs):
    hidden_ref, weight_ref, vectors = refs[0], refs[1], refs[2:5]
    load_ref, block_ref, table_ref, rows_ref, kept, sems = refs[5:]
    seq, width = hidden_ref.shape
    copies = [
        fetch(hidden_ref, load_ref.at[pl.ds(0, seq), :], sems.at[0]),
        fetch(weight_ref, block_ref, sems.at[1]),
    ]
    for k, ref in enumerate(vectors):
        copies.append(fetch(ref, kept.at[pl.ds(k * width, width)], sems.at[2 + k]))
    lane = lax.broadcasted_iota(jnp.int32, (SLOT_ROWS, TILE), 1)
    table = jnp.where(lane == TILE - 1, length_ref[0], -1)
    devices = lax.axis_size("doc")
    for k in range(tiles_ref.shape[2]):
        block = slots_ref[0, 0, k] * devices + owners_ref[0, 0, k]
        table = jnp.where(lane == tiles_ref[0, 0, k], block, table)
    table = table.astype(jnp.float32).astype(jnp.bfloat16)
    for first in range(0, width, TILE):
        load_ref[seq:, first : first + TILE] = table
        table_ref[:, first : first + TILE] = table
    for copy in copies:
        copy.wait()
    for k in range(len(vectors)):
        rows_ref[k : k + 1, :] = kept[pl.ds(k * width, width)][None, :]


def pile_kernel(parts, heights, *refs):
    rows = jnp.concatenate(
        [ref[first : first + count, :] for ref, (first, count) in zip(refs, parts)], axis=0
    )
    at = 0
    for ref, height in zip(refs[len(parts) :], heights):
        ref[...] = rows[at : at + height, :]
        at += height


def fetch(ref, slot, sem):
    copy = pltpu.make_async_copy(ref, slot, sem)
    copy.start()
    return copy


def keep_tops(normed, count, halves, bests):
    for w_ref, best in zip(halves, bests):
        for j, top in enumerate(tops_of(normed, w_ref, count)):
            best[j : j + 1, :] = top


def fetch_kernel(count, *refs):
    copies = [fetch(refs[1 + k], refs[1 + count + k], refs[-1].at[k]) for k in range(count)]
    for copy in copies:
        copy.wait()


def first_kernel(seq, shard, masks, count, *refs):
    me_ref, docs, refs = refs[0], refs[1 : 1 + count], refs[1 + count :]
    tables, refs = refs[:count], refs[count:]
    count = len(masks) * shard // seq
    parts, others, refs = refs[:count], refs[count : 2 * count], refs[2 * count :]
    params, halves, refs = refs[0], refs[1:3], refs[3:]
    bests, weight = refs[:2], refs[2]
    me = me_ref[0]
    core = me % 2
    for at in range(0, len(masks) * shard, SLOT_ROWS):
        (k, inside), (part, place) = divmod(at, shard), divmod(at, seq)
        chip = (me // 2) ^ masks[k]
        for whose, sources in ((core, parts), (1 - core, others)):
            to = pl.multiple_of((2 * chip + whose) * shard + inside, SLOT_ROWS)
            weight[pl.ds(to, SLOT_ROWS), :] = sources[part][place : place + SLOT_ROWS, :]
    keep_tops(normed_rows(docs, tables, seq, weight, params), len(docs), halves, bests)


def next_kernel(seq, count, *refs):
    docs, tables, refs = refs[:count], refs[count : 2 * count], refs[2 * count :]
    weight, params, refs = refs[0], refs[1], refs[2:]
    keep_tops(normed_rows(docs, tables, seq, weight, params), count, refs[:2], refs[2:])


def last_kernel(seq, groups, *refs):
    masks = [mask for group in groups for mask in group]
    me_ref, docs, refs = refs[0], refs[1 : 1 + len(groups[-1])], refs[1 + len(groups[-1]) :]
    tables, refs = refs[: len(masks)], refs[len(masks) :]
    weight, params, halves, dbias_ref, refs = refs[0], refs[1], refs[2:4], refs[4], refs[5:]
    earlier, keep_ref, give_ref, send = refs[:-3], *refs[-3:]
    me = me_ref[0]
    core, chip = me % 2, me // 2
    devices = 2 * len(masks)
    tiles = 2 * halves[0].shape[0] // TILE
    normed = normed_rows(docs, docs, seq, weight, params)
    found = []
    for k, w_ref in enumerate(halves):
        parts = [ref[0 : len(group), :] for ref, group in zip(earlier[k::2], groups)]
        parts += tops_of(normed, w_ref, len(docs))
        found.append(jnp.concatenate(parts, axis=0))
    low = jnp.where(core == 0, found[0], found[1])
    high = jnp.where(core == 0, found[1], found[0])
    logits = jnp.concatenate([low, high], axis=1)
    docs_at = [me ^ (2 * mask) for mask in masks]
    bias = dbias_ref[...]
    bias = pltpu.roll(bias, bias.shape[0] - chip * tiles, 0)
    tables = jnp.concatenate([table_of(ref) for ref in tables], axis=0)
    tables = pltpu.roll(tables, TILE - chip * tiles, 1).astype(jnp.int32)
    send[...] = jnp.zeros(send.shape, jnp.float32)
    stride = keep_ref.shape[1]
    target = lax.broadcasted_iota(jnp.int32, (BLK_DEV * devices, TILE), 0)
    for t in range(tiles):
        lanes = slice(t * TILE, (t + 1) * TILE)
        impacts = jnp.log1p(jnp.maximum(logits[:, lanes] + bias[t : t + 1, :], 0.0))
        impacts = impacts.astype(jnp.bfloat16).astype(jnp.float32)
        blocks = jnp.zeros((BLK_DEV * devices, TILE), jnp.float32)
        for n in range(len(masks)):
            row = impacts[n : n + 1, :]
            send[pl.ds(docs_at[n] * stride + t, 1), :] = row
            block = jnp.broadcast_to(tables[n : n + 1, t : t + 1], target.shape)
            blocks = jnp.maximum(blocks, jnp.where(target == block, row, 0.0))
        for s in range(BLK_DEV):
            send[pl.ds((1 + s) * SLOT_ROWS + t, devices, stride=stride), :] = blocks[
                s * devices : (s + 1) * devices
            ]
    for k in range(len(masks)):
        at = pl.multiple_of((2 * k + core) * stride, SLOT_ROWS)
        keep_ref[k] = send[pl.ds(at, stride), :].astype(jnp.bfloat16)
        at = pl.multiple_of((2 * k + 1 - core) * stride + SLOT_ROWS, SLOT_ROWS)
        give_ref[k] = send[pl.ds(at, stride - SLOT_ROWS), :].astype(jnp.bfloat16)


def merge_kernel(keep_ref, got_ref, out_ref):
    out_ref[:, 0:SLOT_ROWS, :] = keep_ref[:, 0:SLOT_ROWS, :]
    mine = keep_ref[:, SLOT_ROWS:, :].astype(jnp.float32)
    theirs = got_ref[...].astype(jnp.float32)
    out_ref[:, SLOT_ROWS:, :] = jnp.maximum(mine, theirs).astype(jnp.bfloat16)


def place_kernel(tiles, rows_ref, impacts_ref, summaries_ref):
    for chip in range(rows_ref.shape[0]):
        rows = rows_ref[chip].astype(jnp.float32)
        lanes = slice(chip * tiles * TILE, (chip + 1) * tiles * TILE)
        lines = [
            jnp.concatenate([rows[first + t : first + t + 1] for t in range(tiles)], axis=1)
            for first in range(0, rows.shape[0], SLOT_ROWS)
        ]
        impacts_ref[:, lanes] = lines[0].astype(jnp.bfloat16)
        summaries_ref[:, lanes] = jnp.concatenate(lines[1:], axis=0).astype(jnp.bfloat16)


def move_tokens(
    hidden_states,
    doc_lengths,
    transform_weight,
    transform_bias,
    norm_gain,
    norm_bias,
    decoder_weight,
    decoder_bias,
    tile_ids,
    owner_ids,
    block_slots,
):
    devices = lax.axis_size("doc")
    chips = devices // 2
    seq, width = hidden_states.shape
    rows = transform_weight.shape[0]
    half = decoder_weight.shape[2]
    tiles = 2 * half // TILE
    me = lax.axis_index("doc").astype(jnp.int32)

    def cross(value, mask):
        return lax.ppermute(value, "doc", [(i, i ^ (2 * mask)) for i in range(devices)])

    def swap(value):
        return lax.ppermute(value, "doc", [(i, i ^ 1) for i in range(devices)])

    smem = pl.BlockSpec(memory_space=pltpu.SMEM)
    vmem = pl.BlockSpec(memory_space=pltpu.VMEM)
    hbm = pl.BlockSpec(memory_space=pltpu.HBM)

    def stay(value):
        return pltpu.with_memory_space_constraint(value, pltpu.HBM)

    limit = pltpu.CompilerParams(vmem_limit_bytes=24 * 1024 * 1024)

    def cost(docs):
        return pl.CostEstimate(flops=docs, bytes_accessed=docs, transcendentals=0)

    def shape(dims, dtype):
        return jax.ShapeDtypeStruct(dims, dtype)

    def after(value, *done):
        return lax.optimization_barrier((value, *done))[0]

    def pile(values, parts, heights=()):
        heights = heights or (sum(count for _, count in parts),)
        piled = pl.pallas_call(
            lambda *refs: pile_kernel(parts, heights, *refs),
            out_shape=[shape((height, width), jnp.bfloat16) for height in heights],
            in_specs=[vmem] * len(values),
            out_specs=[vmem] * len(heights),
            compiler_params=limit,
        )(*values)
        return piled if len(heights) > 1 else piled[0]

    where = me[None]
    weight_rows = jnp.swapaxes(decoder_weight[0], 0, 1)
    block_6 = cross(transform_weight, 6)
    block_2 = cross(transform_weight, 2)
    theirs = swap(weight_rows)
    docs = {1: cross(hidden_states, 1), 2: cross(hidden_states, 2)}
    load, block, table, params = pl.pallas_call(
        start_kernel,
        out_shape=[
            shape((seq + SLOT_ROWS, width), jnp.bfloat16),
            shape((rows, width), jnp.bfloat16),
            shape((SLOT_ROWS, width), jnp.bfloat16),
            shape((8, width), jnp.float32),
        ],
        in_specs=[smem] * 5 + [hbm] * 5,
        out_specs=[vmem] * 4,
        scratch_shapes=[
            pltpu.VMEM((3 * width,), jnp.float32),
            pltpu.SemaphoreType.DMA((5,)),
        ],
        compiler_params=limit,
    )(
        where,
        stay(tile_ids),
        stay(owner_ids[..., 0]),
        stay(block_slots),
        doc_lengths,
        stay(hidden_states),
        stay(transform_weight),
        stay(transform_bias),
        stay(norm_gain),
        stay(norm_bias),
    )
    one, two, below = (0, rows), (0, 2 * rows), (0, SLOT_ROWS)
    near = pile((block, after(block_2, block_6, docs[1]), table), (one, one, below))
    near_pile = cross(near, 1)
    block_4 = cross(pile((block_6, table), (one, below)), 2)
    docs[6] = cross(after(load, block_6), 6)
    docs[3] = cross(after(docs[2], near), 1)
    far_from = [stay(after(weight_rows, table))]
    [mine] = pl.pallas_call(
        lambda *refs: fetch_kernel(1, *refs),
        out_shape=[shape(value.shape, value.dtype) for value in far_from],
        in_specs=[vmem] + [hbm],
        out_specs=[vmem],
        scratch_shapes=[pltpu.SemaphoreType.DMA((1,))],
        compiler_params=limit,
    )(table, *far_from)
    far = (block_6, after(block_4, near_pile, mine, theirs))
    far = pile(far, (one, (0, rows + SLOT_ROWS)))
    far_pile = cross(far, 1)
    docs[4] = cross(after(docs[6], far), 2)
    docs[7] = cross(docs[6], 1)
    sources = (after(block, docs[6], docs[3]), block_2, block_6, block_4, near_pile, far_pile)
    packed = pile(sources, (one, one, one, one, two, two), (seq,) * (chips * rows // seq))
    other_packed = [swap(part) for part in packed]
    block_masks = [0, 2, 6, 4, 1, 3, 7, 5]

    groups = [[6, 7, 0, 1, 2, 3, 4], [5]]
    masks = [mask for group in groups for mask in group]
    docs[0] = load
    docs[5] = cross(after(docs[4], docs[7], *other_packed), 1)
    tables = docs | {1: near_pile, 2: block_4, 3: far_pile}
    best_shape = shape((8, half), jnp.float32)
    *best, weight = pl.pallas_call(
        lambda *refs: first_kernel(seq, rows, block_masks, len(groups[0]), *refs),
        out_shape=[best_shape, best_shape, shape((width, width), jnp.bfloat16)],
        in_specs=[smem] + [vmem] * (2 * len(groups[0]) + 3 + 2 * len(packed)),
        out_specs=[vmem] * 3,
        compiler_params=limit,
        cost_estimate=cost(2),
    )(
        where,
        *[docs[mask] for mask in groups[0]],
        *[tables[mask] for mask in groups[0]],
        *packed,
        *other_packed,
        params,
        mine,
        theirs,
    )
    for group in groups[1:-1]:
        best += pl.pallas_call(
            lambda *refs, count=len(group): next_kernel(seq, count, *refs),
            out_shape=[best_shape] * 2,
            in_specs=[vmem] * (2 * len(group) + 4),
            out_specs=[vmem] * 2,
            compiler_params=limit,
            cost_estimate=cost(len(group)),
        )(
            *[docs[mask] for mask in group],
            *[tables[mask] for mask in group],
            after(weight, best[-1]),
            params,
            mine,
            theirs,
        )
    height = (1 + BLK_DEV) * SLOT_ROWS
    keep, give = pl.pallas_call(
        lambda *refs: last_kernel(seq, groups, *refs),
        out_shape=[
            shape((chips, height, TILE), jnp.bfloat16),
            shape((chips, height - SLOT_ROWS, TILE), jnp.bfloat16),
        ],
        in_specs=[smem] + [vmem] * (len(groups[-1]) + len(masks) + 5 + len(best)),
        out_specs=[vmem] * 2,
        scratch_shapes=[pltpu.VMEM((devices * height, TILE), jnp.float32)],
        compiler_params=limit,
        cost_estimate=cost(2),
    )(
        where,
        *[docs[mask] for mask in groups[-1]],
        *[tables[mask] for mask in masks],
        weight,
        params,
        mine,
        theirs,
        decoder_bias.reshape(-1, TILE),
        *best,
    )
    merged = pl.pallas_call(
        merge_kernel,
        out_shape=shape((chips, height, TILE), jnp.bfloat16),
        in_specs=[vmem] * 2,
        out_specs=vmem,
        compiler_params=limit,
    )(keep, swap(give))
    alike = [list(range(parity, devices, 2)) for parity in range(2)]
    got = lax.all_to_all(
        merged, "doc", split_axis=0, concat_axis=0, axis_index_groups=alike, tiled=True
    )
    return pl.pallas_call(
        lambda *refs: place_kernel(tiles, *refs),
        out_shape=[
            shape((1, chips * tiles * TILE), jnp.bfloat16),
            shape((BLK_DEV, chips * tiles * TILE), jnp.bfloat16),
        ],
        in_specs=[vmem],
        out_specs=[vmem] * 2,
        compiler_params=limit,
    )(got)


def tokens_move(mesh):
    return mesh.shape["term"] == 1 and mesh.shape["doc"] == 16


def solution(mesh):
    placed = (
        P(("groups", "doc"), None),
        P(("groups", "doc")),
        P("doc", "term"),
        P(),
        P(),
        P(),
        P("term", None, "doc"),
        P("term"),
        P("term", ("groups", "doc"), None),
        P("term", ("groups", "doc"), None, None),
        P("term", ("groups", "doc"), None),
    )

    def local(*args):
        pair = 2 * args[6].shape[2]
        tiles = pair * (mesh.shape["doc"] // 2) // TILE
        fits = pair % TILE == 0 and tiles < TILE and pair // TILE <= SLOT_ROWS
        if tokens_move(mesh) and args[1].shape[0] == 1 and fits:
            return move_tokens(*args)
        return move_weights(*args)

    return jax.shard_map(
        local,
        mesh=mesh,
        in_specs=placed,
        out_specs=(P(("groups", "doc"), "term"), P(("groups", "doc"), "term")),
        check_vma=False,
    )
```

```python
import jax
import jax.numpy as jnp
from jax import lax
from jax.experimental import pallas as pl
from jax.experimental.pallas import tpu as pltpu
from jax.sharding import PartitionSpec as P

TILE = 128
BLK_DEV = 2
SLOT_ROWS = 16


def layer_norm(activated, norm_gain, norm_bias):
    values = activated.astype(jnp.float32)
    centre = jnp.mean(values, axis=-1, keepdims=True)
    centred = values - centre
    spread = jnp.mean(centred * centred, axis=-1, keepdims=True)
    return (centred * lax.rsqrt(spread + 1e-05) * norm_gain + norm_bias).astype(jnp.bfloat16)


def pool_docs(logits, keep):
    docs_here = keep.shape[0]
    saturated = jnp.log1p(jnp.maximum(logits, 0.0)).reshape(
        docs_here, keep.shape[1], logits.shape[1]
    )
    return jnp.max(jnp.where(keep[:, :, None], saturated, 0.0), axis=1)


def move_weights(
    hidden_states,
    doc_lengths,
    transform_weight,
    transform_bias,
    norm_gain,
    norm_bias,
    decoder_weight,
    decoder_bias,
    tile_ids,
    owner_ids,
    block_slots,
):
    tok_rows = hidden_states.shape[0]
    docs_here = doc_lengths.shape[0]
    seq_len = tok_rows // docs_here
    cols = transform_weight.shape[1]
    pre_half = jnp.dot(
        hidden_states,
        lax.all_gather(transform_weight, "doc", axis=0, tiled=True),
        preferred_element_type=jnp.float32,
    )
    bias_half = lax.dynamic_slice_in_dim(transform_bias, lax.axis_index("term") * cols, cols, 0)
    act_half = jax.nn.gelu(pre_half + bias_half, approximate=False).astype(jnp.bfloat16)
    activated = lax.all_gather(act_half, "term", axis=1, tiled=True)
    normed = layer_norm(activated, norm_gain, norm_bias)
    keep = jnp.arange(seq_len, dtype=jnp.int32)[None, :] < doc_lengths[:, None]
    logits = jnp.dot(
        normed,
        lax.all_gather(decoder_weight, "doc", axis=2, tiled=True)[0],
        preferred_element_type=jnp.float32,
    )
    logits = logits + decoder_bias
    impacts = pool_docs(logits, keep).astype(jnp.bfloat16)
    tiles_t = impacts.shape[1] // TILE
    slots_total = BLK_DEV * tiles_t
    tiles = impacts.reshape(docs_here * tiles_t, TILE)
    chosen = tile_ids[0]
    doc_index = jnp.arange(docs_here, dtype=jnp.int32)[:, None]
    posted = tiles[(doc_index * tiles_t + chosen).reshape(-1)]
    owners = owner_ids[0, :, :, 0].reshape(-1)
    target = block_slots[0].reshape(-1) * tiles_t + chosen.reshape(-1)
    owner_count = lax.axis_size("doc")
    capacity = max(2, 2 * posted.shape[0] // owner_count)
    onehot = (owners[:, None] == jnp.arange(owner_count, dtype=jnp.int32)[None, :]).astype(
        jnp.int32
    )
    before = jnp.cumsum(onehot, axis=0) - onehot
    position = jnp.sum(before * onehot, axis=1)
    dest = owners * capacity + position
    outgoing = jnp.zeros((owner_count * capacity, TILE), jnp.bfloat16).at[dest].set(posted)
    out_tags = jnp.full((owner_count * capacity,), slots_total, jnp.int32).at[dest].set(target)
    got_vals, got_tags = (
        lax.all_to_all(
            outgoing.reshape(owner_count, capacity, TILE),
            "doc",
            split_axis=0,
            concat_axis=0,
            tiled=True,
        ),
        lax.all_to_all(
            out_tags.reshape(owner_count, capacity), "doc", split_axis=0, concat_axis=0, tiled=True
        ),
    )
    got_vals = got_vals.reshape(-1, TILE)
    local_tags = got_tags.reshape(-1)
    summary = jnp.zeros((slots_total, TILE), jnp.bfloat16).at[local_tags].max(got_vals, mode="drop")
    return (impacts, summary.reshape(BLK_DEV, tiles_t * TILE))


def dot_t(left, right):
    return lax.dot_general(
        left, right, (((1,), (1,)), ((), ())), preferred_element_type=jnp.float32
    )


def table_of(ref):
    return ref[ref.shape[0] - SLOT_ROWS :, 0:TILE].astype(jnp.float32)[0:1, :]


def masked(ref, table_ref, seq):
    here = ref[0:seq, :]
    length = table_of(table_ref)[:, TILE - 1 :]
    keep = lax.broadcasted_iota(jnp.int32, here.shape, 0).astype(jnp.float32) < length
    first = jnp.broadcast_to(here[0:1, :].astype(jnp.float32), here.shape).astype(here.dtype)
    return jnp.where(keep, here, first)


def normed_rows(docs, tables, seq, weight, params):
    rows = [masked(ref, table, seq) for ref, table in zip(docs, tables)]
    rows = jnp.concatenate(rows, axis=0)
    pre = jnp.dot(rows, weight[...], preferred_element_type=jnp.float32) + params[0:1, :]
    act = 0.5 * pre * (1.0 + lax.erf(pre * (0.5**0.5)))
    return layer_norm(act.astype(jnp.bfloat16), params[1:2, :], params[2:3, :])


def tops_of(normed, w_ref, count):
    logits = dot_t(normed, w_ref[...])
    seq = normed.shape[0] // count
    return [
        jnp.max(logits[j * seq : (j + 1) * seq], axis=0, keepdims=True) for j in range(count)
    ]


def start_kernel(me_ref, tiles_ref, owners_ref, slots_ref, length_ref, *refs):
    hidden_ref, weight_ref, vectors = refs[0], refs[1], refs[2:5]
    load_ref, block_ref, table_ref, rows_ref, kept, sems = refs[5:]
    seq, width = hidden_ref.shape
    copies = [
        fetch(hidden_ref, load_ref.at[pl.ds(0, seq), :], sems.at[0]),
        fetch(weight_ref, block_ref, sems.at[1]),
    ]
    for k, ref in enumerate(vectors):
        copies.append(fetch(ref, kept.at[pl.ds(k * width, width)], sems.at[2 + k]))
    lane = lax.broadcasted_iota(jnp.int32, (SLOT_ROWS, TILE), 1)
    table = jnp.where(lane == TILE - 1, length_ref[0], -1)
    devices = lax.axis_size("doc")
    for k in range(tiles_ref.shape[2]):
        block = slots_ref[0, 0, k] * devices + owners_ref[0, 0, k]
        table = jnp.where(lane == tiles_ref[0, 0, k], block, table)
    table = table.astype(jnp.float32).astype(jnp.bfloat16)
    for first in range(0, width, TILE):
        load_ref[seq:, first : first + TILE] = table
        table_ref[:, first : first + TILE] = table
    for copy in copies:
        copy.wait()
    for k in range(len(vectors)):
        rows_ref[k : k + 1, :] = kept[pl.ds(k * width, width)][None, :]


def pile_kernel(parts, heights, *refs):
    rows = jnp.concatenate(
        [ref[first : first + count, :] for ref, (first, count) in zip(refs, parts)], axis=0
    )
    at = 0
    for ref, height in zip(refs[len(parts) :], heights):
        ref[...] = rows[at : at + height, :]
        at += height


def fetch(ref, slot, sem):
    copy = pltpu.make_async_copy(ref, slot, sem)
    copy.start()
    return copy


def keep_tops(normed, count, halves, bests):
    for w_ref, best in zip(halves, bests):
        for j, top in enumerate(tops_of(normed, w_ref, count)):
            best[j : j + 1, :] = top


def fetch_kernel(count, *refs):
    copies = [fetch(refs[1 + k], refs[1 + count + k], refs[-1].at[k]) for k in range(count)]
    for copy in copies:
        copy.wait()


def first_kernel(seq, shard, masks, count, *refs):
    me_ref, docs, refs = refs[0], refs[1 : 1 + count], refs[1 + count :]
    tables, refs = refs[:count], refs[count:]
    count = len(masks) * shard // seq
    parts, others, refs = refs[:count], refs[count : 2 * count], refs[2 * count :]
    params, halves, refs = refs[0], refs[1:3], refs[3:]
    bests, weight = refs[:2], refs[2]
    me = me_ref[0]
    core = me % 2
    for at in range(0, len(masks) * shard, SLOT_ROWS):
        (k, inside), (part, place) = divmod(at, shard), divmod(at, seq)
        chip = (me // 2) ^ masks[k]
        for whose, sources in ((core, parts), (1 - core, others)):
            to = pl.multiple_of((2 * chip + whose) * shard + inside, SLOT_ROWS)
            weight[pl.ds(to, SLOT_ROWS), :] = sources[part][place : place + SLOT_ROWS, :]
    keep_tops(normed_rows(docs, tables, seq, weight, params), len(docs), halves, bests)


def next_kernel(seq, count, *refs):
    docs, tables, refs = refs[:count], refs[count : 2 * count], refs[2 * count :]
    weight, params, refs = refs[0], refs[1], refs[2:]
    keep_tops(normed_rows(docs, tables, seq, weight, params), count, refs[:2], refs[2:])


def last_kernel(seq, groups, *refs):
    masks = [mask for group in groups for mask in group]
    me_ref, docs, refs = refs[0], refs[1 : 1 + len(groups[-1])], refs[1 + len(groups[-1]) :]
    tables, refs = refs[: len(masks)], refs[len(masks) :]
    weight, params, halves, dbias_ref, refs = refs[0], refs[1], refs[2:4], refs[4], refs[5:]
    earlier, keep_ref, give_ref, send = refs[:-3], *refs[-3:]
    me = me_ref[0]
    core, chip = me % 2, me // 2
    devices = 2 * len(masks)
    tiles = 2 * halves[0].shape[0] // TILE
    normed = normed_rows(docs, docs, seq, weight, params)
    found = []
    for k, w_ref in enumerate(halves):
        parts = [ref[0 : len(group), :] for ref, group in zip(earlier[k::2], groups)]
        parts += tops_of(normed, w_ref, len(docs))
        found.append(jnp.concatenate(parts, axis=0))
    low = jnp.where(core == 0, found[0], found[1])
    high = jnp.where(core == 0, found[1], found[0])
    logits = jnp.concatenate([low, high], axis=1)
    docs_at = [me ^ (2 * mask) for mask in masks]
    bias = dbias_ref[...]
    bias = pltpu.roll(bias, bias.shape[0] - chip * tiles, 0)
    tables = jnp.concatenate([table_of(ref) for ref in tables], axis=0)
    tables = pltpu.roll(tables, TILE - chip * tiles, 1).astype(jnp.int32)
    send[...] = jnp.zeros(send.shape, jnp.float32)
    stride = keep_ref.shape[1]
    target = lax.broadcasted_iota(jnp.int32, (BLK_DEV * devices, TILE), 0)
    for t in range(tiles):
        lanes = slice(t * TILE, (t + 1) * TILE)
        impacts = jnp.log1p(jnp.maximum(logits[:, lanes] + bias[t : t + 1, :], 0.0))
        impacts = impacts.astype(jnp.bfloat16).astype(jnp.float32)
        blocks = jnp.zeros((BLK_DEV * devices, TILE), jnp.float32)
        for n in range(len(masks)):
            row = impacts[n : n + 1, :]
            send[pl.ds(docs_at[n] * stride + t, 1), :] = row
            block = jnp.broadcast_to(tables[n : n + 1, t : t + 1], target.shape)
            blocks = jnp.maximum(blocks, jnp.where(target == block, row, 0.0))
        for s in range(BLK_DEV):
            send[pl.ds((1 + s) * SLOT_ROWS + t, devices, stride=stride), :] = blocks[
                s * devices : (s + 1) * devices
            ]
    for k in range(len(masks)):
        at = pl.multiple_of((2 * k + core) * stride, SLOT_ROWS)
        keep_ref[k] = send[pl.ds(at, stride), :].astype(jnp.bfloat16)
        at = pl.multiple_of((2 * k + 1 - core) * stride + SLOT_ROWS, SLOT_ROWS)
        give_ref[k] = send[pl.ds(at, stride - SLOT_ROWS), :].astype(jnp.bfloat16)


def merge_kernel(keep_ref, got_ref, out_ref):
    out_ref[:, 0:SLOT_ROWS, :] = keep_ref[:, 0:SLOT_ROWS, :]
    mine = keep_ref[:, SLOT_ROWS:, :].astype(jnp.float32)
    theirs = got_ref[...].astype(jnp.float32)
    out_ref[:, SLOT_ROWS:, :] = jnp.maximum(mine, theirs).astype(jnp.bfloat16)


def place_kernel(tiles, rows_ref, impacts_ref, summaries_ref):
    for chip in range(rows_ref.shape[0]):
        rows = rows_ref[chip].astype(jnp.float32)
        lanes = slice(chip * tiles * TILE, (chip + 1) * tiles * TILE)
        lines = [
            jnp.concatenate([rows[first + t : first + t + 1] for t in range(tiles)], axis=1)
            for first in range(0, rows.shape[0], SLOT_ROWS)
        ]
        impacts_ref[:, lanes] = lines[0].astype(jnp.bfloat16)
        summaries_ref[:, lanes] = jnp.concatenate(lines[1:], axis=0).astype(jnp.bfloat16)


def move_tokens(
    hidden_states,
    doc_lengths,
    transform_weight,
    transform_bias,
    norm_gain,
    norm_bias,
    decoder_weight,
    decoder_bias,
    tile_ids,
    owner_ids,
    block_slots,
):
    devices = lax.axis_size("doc")
    chips = devices // 2
    seq, width = hidden_states.shape
    rows = transform_weight.shape[0]
    half = decoder_weight.shape[2]
    tiles = 2 * half // TILE
    me = lax.axis_index("doc").astype(jnp.int32)

    def cross(value, mask):
        return lax.ppermute(value, "doc", [(i, i ^ (2 * mask)) for i in range(devices)])

    def swap(value):
        return lax.ppermute(value, "doc", [(i, i ^ 1) for i in range(devices)])

    smem = pl.BlockSpec(memory_space=pltpu.SMEM)
    vmem = pl.BlockSpec(memory_space=pltpu.VMEM)
    hbm = pl.BlockSpec(memory_space=pltpu.HBM)

    def stay(value):
        return pltpu.with_memory_space_constraint(value, pltpu.HBM)

    limit = pltpu.CompilerParams(vmem_limit_bytes=24 * 1024 * 1024)

    def cost(docs):
        return pl.CostEstimate(flops=docs, bytes_accessed=docs, transcendentals=0)

    def shape(dims, dtype):
        return jax.ShapeDtypeStruct(dims, dtype)

    def after(value, *done):
        return lax.optimization_barrier((value, *done))[0]

    def pile(values, parts, heights=()):
        heights = heights or (sum(count for _, count in parts),)
        piled = pl.pallas_call(
            lambda *refs: pile_kernel(parts, heights, *refs),
            out_shape=[shape((height, width), jnp.bfloat16) for height in heights],
            in_specs=[vmem] * len(values),
            out_specs=[vmem] * len(heights),
            compiler_params=limit,
        )(*values)
        return piled if len(heights) > 1 else piled[0]

    where = me[None]
    weight_rows = jnp.swapaxes(decoder_weight[0], 0, 1)
    block_6 = cross(transform_weight, 6)
    block_2 = cross(transform_weight, 2)
    theirs = swap(weight_rows)
    docs = {1: cross(hidden_states, 1), 2: cross(hidden_states, 2)}
    load, block, table, params = pl.pallas_call(
        start_kernel,
        out_shape=[
            shape((seq + SLOT_ROWS, width), jnp.bfloat16),
            shape((rows, width), jnp.bfloat16),
            shape((SLOT_ROWS, width), jnp.bfloat16),
            shape((8, width), jnp.float32),
        ],
        in_specs=[smem] * 5 + [hbm] * 5,
        out_specs=[vmem] * 4,
        scratch_shapes=[
            pltpu.VMEM((3 * width,), jnp.float32),
            pltpu.SemaphoreType.DMA((5,)),
        ],
        compiler_params=limit,
    )(
        where,
        stay(tile_ids),
        stay(owner_ids[..., 0]),
        stay(block_slots),
        doc_lengths,
        stay(hidden_states),
        stay(transform_weight),
        stay(transform_bias),
        stay(norm_gain),
        stay(norm_bias),
    )
    one, two, below = (0, rows), (0, 2 * rows), (0, SLOT_ROWS)
    near = pile((block, after(block_2, block_6, docs[1]), table), (one, one, below))
    near_pile = cross(near, 1)
    block_4 = cross(pile((block_6, table), (one, below)), 2)
    docs[6] = cross(after(load, block_6), 6)
    docs[3] = cross(after(docs[2], near), 1)
    far_from = [stay(after(weight_rows, table))]
    [mine] = pl.pallas_call(
        lambda *refs: fetch_kernel(1, *refs),
        out_shape=[shape(value.shape, value.dtype) for value in far_from],
        in_specs=[vmem] + [hbm],
        out_specs=[vmem],
        scratch_shapes=[pltpu.SemaphoreType.DMA((1,))],
        compiler_params=limit,
    )(table, *far_from)
    far = (block_6, after(block_4, near_pile, mine, theirs))
    far = pile(far, (one, (0, rows + SLOT_ROWS)))
    far_pile = cross(far, 1)
    docs[4] = cross(after(docs[6], far), 2)
    docs[7] = cross(docs[6], 1)
    sources = (after(block, docs[6], docs[3]), block_2, block_6, block_4, near_pile, far_pile)
    packed = pile(sources, (one, one, one, one, two, two), (seq,) * (chips * rows // seq))
    other_packed = [swap(part) for part in packed]
    block_masks = [0, 2, 6, 4, 1, 3, 7, 5]

    groups = [[6, 7, 0, 1, 2, 3], [4, 5]]
    masks = [mask for group in groups for mask in group]
    docs[0] = load
    docs[5] = cross(after(docs[4], docs[7], *other_packed), 1)
    tables = docs | {1: near_pile, 2: block_4, 3: far_pile}
    best_shape = shape((8, half), jnp.float32)
    *best, weight = pl.pallas_call(
        lambda *refs: first_kernel(seq, rows, block_masks, len(groups[0]), *refs),
        out_shape=[best_shape, best_shape, shape((width, width), jnp.bfloat16)],
        in_specs=[smem] + [vmem] * (2 * len(groups[0]) + 3 + 2 * len(packed)),
        out_specs=[vmem] * 3,
        compiler_params=limit,
        cost_estimate=cost(2),
    )(
        where,
        *[docs[mask] for mask in groups[0]],
        *[tables[mask] for mask in groups[0]],
        *packed,
        *other_packed,
        params,
        mine,
        theirs,
    )
    for group in groups[1:-1]:
        best += pl.pallas_call(
            lambda *refs, count=len(group): next_kernel(seq, count, *refs),
            out_shape=[best_shape] * 2,
            in_specs=[vmem] * (2 * len(group) + 4),
            out_specs=[vmem] * 2,
            compiler_params=limit,
            cost_estimate=cost(len(group)),
        )(
            *[docs[mask] for mask in group],
            *[tables[mask] for mask in group],
            after(weight, best[-1]),
            params,
            mine,
            theirs,
        )
    height = (1 + BLK_DEV) * SLOT_ROWS
    keep, give = pl.pallas_call(
        lambda *refs: last_kernel(seq, groups, *refs),
        out_shape=[
            shape((chips, height, TILE), jnp.bfloat16),
            shape((chips, height - SLOT_ROWS, TILE), jnp.bfloat16),
        ],
        in_specs=[smem] + [vmem] * (len(groups[-1]) + len(masks) + 5 + len(best)),
        out_specs=[vmem] * 2,
        scratch_shapes=[pltpu.VMEM((devices * height, TILE), jnp.float32)],
        compiler_params=limit,
        cost_estimate=cost(2),
    )(
        where,
        *[docs[mask] for mask in groups[-1]],
        *[tables[mask] for mask in masks],
        weight,
        params,
        mine,
        theirs,
        decoder_bias.reshape(-1, TILE),
        *best,
    )
    merged = pl.pallas_call(
        merge_kernel,
        out_shape=shape((chips, height, TILE), jnp.bfloat16),
        in_specs=[vmem] * 2,
        out_specs=vmem,
        compiler_params=limit,
    )(keep, swap(give))
    alike = [list(range(parity, devices, 2)) for parity in range(2)]
    got = lax.all_to_all(
        merged, "doc", split_axis=0, concat_axis=0, axis_index_groups=alike, tiled=True
    )
    return pl.pallas_call(
        lambda *refs: place_kernel(tiles, *refs),
        out_shape=[
            shape((1, chips * tiles * TILE), jnp.bfloat16),
            shape((BLK_DEV, chips * tiles * TILE), jnp.bfloat16),
        ],
        in_specs=[vmem],
        out_specs=[vmem] * 2,
        compiler_params=limit,
    )(got)


def tokens_move(mesh):
    return mesh.shape["term"] == 1 and mesh.shape["doc"] == 16


def solution(mesh):
    placed = (
        P(("groups", "doc"), None),
        P(("groups", "doc")),
        P("doc", "term"),
        P(),
        P(),
        P(),
        P("term", None, "doc"),
        P("term"),
        P("term", ("groups", "doc"), None),
        P("term", ("groups", "doc"), None, None),
        P("term", ("groups", "doc"), None),
    )

    def local(*args):
        pair = 2 * args[6].shape[2]
        tiles = pair * (mesh.shape["doc"] // 2) // TILE
        fits = pair % TILE == 0 and tiles < TILE and pair // TILE <= SLOT_ROWS
        if tokens_move(mesh) and args[1].shape[0] == 1 and fits:
            return move_tokens(*args)
        return move_weights(*args)

    return jax.shard_map(
        local,
        mesh=mesh,
        in_specs=placed,
        out_specs=(P(("groups", "doc"), "term"), P(("groups", "doc"), "term")),
        check_vma=False,
    )
```
